32 devices in a mesh: gx: 4 (over x, core), gy: 4 (over z), gz: 2 (over y).
Axes of the slice: x: 2, y: 2, z: 4, core: 2. Of those that a mesh axis runs over, the one named last changes fastest.
Arguments:
- bin_mass: float32 [32, 32, 32, 64], P('gx', 'gy', 'gz'), may hold values from 0.02 to 2
- courant: float32 [3, 32, 32, 32], P(None, 'gx', 'gy', 'gz'), may hold values from 0.05 to 0.3
- sub_courant: float32 [64], replicated, may hold values from 0.3 to 0.9
- fall_steps: int32 [64], replicated, may hold values from 1 to 24, as said below
- frag_gain: bfloat16 [4096, 64], replicated, may hold values from -0.01171875 to 0.01171875
- collide: bfloat16 [64, 64], replicated, may hold values from 0.0019989014 to 0.019897461
Outputs:
- updated_mass: float32 [32, 32, 32, 64], P('gx', 'gy', 'gz')
- rainfall: float32 [32, 32, 64], P('gx', ('gy', 'gz'))
The draws below stay inside these ranges and needn't reach their ends.
Inputs may be any that keep to these rules, and one draw needn't show every extreme that they name: `fall_steps`: some bin takes 24 substeps.
All inputs are finite; a program needn't handle non-finite values.
Results may differ from the reference program's by a relative error of at most 0.003.
Values sent between devices are 32-bit elements; how exact they have to be, the bound alone decides.
No kernel may reach another device: no remote copies, remote signals or barrier semaphores. Data moves between devices by JAX's collectives and lax.ppermute only.
A program may use at most 64 MiB of HBM per device.

```python
import math
import jax
import jax.numpy as jnp
from jax import lax

NB = 64
SUBS = 24
NX = 32
NY = 32
NZ = 32


def draw_fall_steps(key, part):
    first_key, second_key = jax.random.split(jax.random.fold_in(key, 17))
    counts = jax.random.randint(first_key, (NB,), 1, SUBS + 1)
    chosen = jax.random.randint(second_key, (), 0, NB)
    return jnp.where(jnp.arange(NB) == chosen, SUBS, counts).astype(jnp.int32)


def block_levels(own_key, shape, cuts, least, high):
    def one(axis_at, blocks):
        draws = jax.random.uniform(jax.random.fold_in(jax.random.fold_in(own_key, 6), axis_at), (blocks,), jnp.float32, least / len(cuts), high / len(cuts))
        return jnp.repeat(jnp.exp(draws), shape[axis_at] // blocks).reshape((-1,) + (1,) * (len(shape) - axis_at - 1))

    gain = one(*cuts[0])
    for cut in cuts[1:]:
        gain = gain * one(*cut)
    return gain


def noise(own_key, shape, width, most, kind=jnp.bfloat16):
    values = width * jax.random.normal(own_key, shape, jnp.float32)
    return jnp.clip(values, min=-most, max=most).astype(kind)


def setup_inputs(seed: int = 0) -> dict:
    splits = jax.random.split(jax.random.key(seed), 7)
    return {
        "bin_mass": jnp.clip(jnp.exp(math.log(2.0) - 4.6051702 * jax.random.uniform(splits[0], (NX, NY, NZ, NB), jnp.float32) ** block_levels(splits[0], (NX, NY, NZ, NB), ((0, 4), (1, 4), (2, 2)), -0.2, 0.2)), 0.02, 2.0),
        "courant": jnp.clip(0.05 + 0.25 * jax.random.uniform(splits[1], (3, NX, NY, NZ), jnp.float32) ** block_levels(splits[1], (3, NX, NY, NZ), ((1, 4), (2, 4), (3, 2)), -0.2, 0.2), 0.05, 0.3),
        "sub_courant": jnp.clip(jax.random.uniform(splits[2], (NB,), jnp.float32, 0.3, 0.9), 0.3, 0.9),
        "fall_steps": draw_fall_steps(jax.random.fold_in(splits[6], 71), 0),
        "frag_gain": noise(splits[4], (NB * NB, NB), (64 * NB * NB) ** -0.5, 0.01171875),
        "collide": jnp.clip(jnp.exp(jax.random.uniform(splits[5], (NB, NB), jnp.float32, math.log(0.0019989014), math.log(0.019897461))), 0.0019989014, 0.019897461).astype(jnp.bfloat16),
    }


EPS = 1e-6


def face_estimate(far_left, near_left, centre, near_right, far_right):
    left_poly = (2.0 * far_left - 7.0 * near_left + 11.0 * centre) / 6.0
    mid_poly = (-near_left + 5.0 * centre + 2.0 * near_right) / 6.0
    right_poly = (2.0 * centre + 5.0 * near_right - far_right) / 6.0
    left_smooth = 13.0 / 12.0 * jnp.square(far_left - 2.0 * near_left + centre) + 0.25 * jnp.square(far_left - 4.0 * near_left + 3.0 * centre)
    mid_smooth = 13.0 / 12.0 * jnp.square(near_left - 2.0 * centre + near_right) + 0.25 * jnp.square(near_left - near_right)
    right_smooth = 13.0 / 12.0 * jnp.square(centre - 2.0 * near_right + far_right) + 0.25 * jnp.square(3.0 * centre - 4.0 * near_right + far_right)
    left_weight = 0.1 / jnp.square(EPS + left_smooth)
    mid_weight = 0.6 / jnp.square(EPS + mid_smooth)
    right_weight = 0.3 / jnp.square(EPS + right_smooth)
    return (left_weight * left_poly + mid_weight * mid_poly + right_weight * right_poly) / (left_weight + mid_weight + right_weight)


def advect(padded, wind_pad):
    change_sum = None
    for axis_d in range(3):
        values_d = padded
        speed_d = wind_pad[axis_d]
        for other in range(3):
            if other != axis_d:
                values_d = lax.slice_in_dim(values_d, 3, values_d.shape[other] - 3, axis=other)
                speed_d = lax.slice_in_dim(speed_d, 1, speed_d.shape[other] - 1, axis=other)
        length = padded.shape[axis_d] - 6
        stencil = [lax.slice_in_dim(values_d, k, k + length + 1, axis=axis_d) for k in range(5)]
        estimate = face_estimate(stencil[0], stencil[1], stencil[2], stencil[3], stencil[4])
        face_speed = 0.5 * (lax.slice_in_dim(speed_d, 0, length + 1, axis=axis_d) + lax.slice_in_dim(speed_d, 1, length + 2, axis=axis_d))
        face_flux = face_speed[..., None] * estimate
        difference = lax.slice_in_dim(face_flux, 1, length + 1, axis=axis_d) - lax.slice_in_dim(face_flux, 0, length, axis=axis_d)
        change_sum = -difference if change_sum is None else change_sum - difference
    return change_sum


def zero_layer(current):
    return jnp.zeros_like(current[:, :, :1])


def settle(mass, sub_courant, fall_steps, top_layer):
    def substep(step, carry):
        current, rainfall = carry
        fall_rate = jnp.where(step < fall_steps, sub_courant, jnp.float32(0.0))
        upper_cell = jnp.concatenate([current[:, :, 1:], top_layer(current)], axis=2)
        rainfall = rainfall + fall_rate * current[:, :, 0]
        current = current + fall_rate * (upper_cell - current)
        return (current, rainfall)

    empty = jnp.zeros((mass.shape[0], mass.shape[1], mass.shape[3]), jnp.float32)
    return lax.fori_loop(0, SUBS, substep, (mass, empty))


def breakup(settled, frag_gain, collide):
    bins = settled.shape[-1]
    flat = settled.reshape(-1, bins)
    count = flat.shape[0]
    block = 512 if count % 512 == 0 else count

    def block_rows(rows_in):
        rounded = rows_in.astype(jnp.bfloat16)
        widened = rounded.astype(jnp.float32)
        pair_terms = (widened[:, :, None] * widened[:, None, :]).reshape(rows_in.shape[0], bins * bins).astype(jnp.bfloat16)
        gained = jnp.dot(pair_terms, frag_gain, preferred_element_type=jnp.float32)
        breakup_loss = jnp.dot(rounded, collide, preferred_element_type=jnp.float32)
        return rows_in + gained - rows_in * breakup_loss

    blocks = flat.reshape(count // block, block, bins)
    return lax.map(block_rows, blocks).reshape(settled.shape)


def reference(bin_mass, courant, sub_courant, fall_steps, frag_gain, collide):
    wind_pad = jnp.pad(courant, ((0, 0), (1, 1), (1, 1), (1, 1)))

    def tendency(values):
        return advect(jnp.pad(values, ((3, 3), (3, 3), (3, 3), (0, 0))), wind_pad)

    section_one = bin_mass + tendency(bin_mass)
    advected = 0.5 * bin_mass + 0.5 * (section_one + tendency(section_one))
    settled, rainfall = settle(advected, sub_courant, fall_steps, zero_layer)
    updated_mass = breakup(settled, frag_gain, collide)
    return updated_mass, rainfall
```

```python
import functools

import jax
import jax.numpy as jnp
from jax import lax
from jax.experimental import pallas as pl
from jax.experimental.pallas import tpu as pltpu
from jax.sharding import PartitionSpec as P

SUBS = 24
EPS = 1e-06
LO, HI = 3, 2
PAD_LO, PAD_HI = 2 * LO, 2 * HI
ROWS, LANES = 8, 128
F32 = jnp.float32
VMEM = pl.BlockSpec(memory_space=pltpu.VMEM)
SMEM = pl.BlockSpec(memory_space=pltpu.SMEM)


def lane_ids():
    return lax.broadcasted_iota(jnp.int32, (ROWS, LANES), 1)


def pick(tile, ids):
    return jnp.take_along_axis(tile, ids, axis=1, mode="promise_in_bounds")


def rows_of(first, count=1):
    return pl.ds(first * ROWS, count * ROWS)


def swap(ref_a, ref_b, own_first):
    return jnp.where(own_first, ref_a, ref_b), jnp.where(own_first, ref_b, ref_a)


def line_change(cells, winds):
    first = [b - a for a, b in zip(cells, cells[1:])]
    twice = [d + d for d in first]
    second = [b - a for a, b in zip(first, first[1:])]
    third = [a - b for a, b in zip(second, second[1:])]
    curved = [(13.0 / 3.0) * (c * c) + 4.0 * EPS for c in second]
    fluxes = []
    for j in range(len(cells) - 4):
        left = twice[j + 1] + second[j]
        mid = first[j + 1] + first[j + 2]
        right = twice[j + 2] - second[j + 2]
        e0 = curved[j] + left * left
        e1 = curved[j + 1] + mid * mid
        e2 = curved[j + 2] + right * right
        e0 = e0 * e0
        e1 = e1 * e1
        e2 = e2 * e2
        e0 = 3.0 * e0
        e2_twice = e2 + e2
        top = e1 * (e2_twice * third[j] + e0 * third[j + 1])
        low = e1 * (e2 + e0) + e0 * e2_twice
        inverse = pl.reciprocal(low, approx=True)
        inverse = inverse * (2.0 - low * inverse)
        estimate = 6.0 * cells[j + 2] + (first[j + 1] + twice[j + 2]) + top * inverse
        fluxes.append((winds[j] + winds[j + 1]) * estimate)
    return [a - b for a, b in zip(fluxes, fluxes[1:])]


def pack_kernel(own_ref, mass_ref, wind_ref, send_ref, keep_ref):
    gz = own_ref[0]
    nx, ny = mass_ref.shape[:2]
    lanes = lane_ids()
    place = lanes % 64
    low = lanes < 64

    def one(half):
        return (2 * (place // 32) + half) * 32 + place % 32

    keep_ids, send_ids = one(gz), one(1 - gz)
    for x in range(nx // 2):
        for y in range(ny):
            a = jnp.concatenate([mass_ref[x, y, 0:8], mass_ref[x, y, 8:16]], axis=1)
            b = jnp.concatenate([mass_ref[x + nx // 2, y, 0:8], mass_ref[x + nx // 2, y, 8:16]], axis=1)
            at = rows_of(x * ny + y)
            keep_ref[at] = jnp.where(low, pick(a, keep_ids), pick(b, keep_ids))
            send_ref[at] = jnp.where(low, pick(a, send_ids), pick(b, send_ids))
    base = nx // 2 * ny
    for d in range(3):
        send_ref[rows_of(base + d)] = wind_ref[d]
        keep_ref[rows_of(base + d)] = wind_ref[d]


def merge_kernel(own_ref, keep_ref, got_ref, block_ref, right_ref, left_ref):
    first = own_ref[0] == 0
    low = lane_ids() < 64
    n = 8
    for x in range(n // 2):
        for y in range(n):
            at = rows_of(x * n + y)
            a, b = swap(keep_ref[at], got_ref[at], first)
            for xx, tile in (
                (x, jnp.where(low, a, pltpu.roll(b, 64, 1))),
                (x + n // 2, jnp.where(low, pltpu.roll(a, 64, 1), b)),
            ):
                block_ref[rows_of(xx * n + y)] = tile
                if y >= n - PAD_LO:
                    right_ref[rows_of(xx * PAD_LO + y - (n - PAD_LO))] = tile
                if y < PAD_HI:
                    left_ref[rows_of(xx * PAD_HI + y)] = tile
    for d in range(3):
        at = rows_of(n // 2 * n + d)
        a, b = swap(keep_ref[at], got_ref[at], first)
        for ref, base in ((block_ref, n * n), (right_ref, n * PAD_LO), (left_ref, n * PAD_HI)):
            ref[rows_of(base + d)] = a
            ref[rows_of(base + 3 + d)] = b


def side_kernel(n, wind_rows, block_ref, below_ref, above_ref, right_ref, left_ref):
    for ref, start, wide, narrow in ((right_ref, n - PAD_LO, PAD_LO, LO), (left_ref, 0, PAD_HI, HI)):
        for x in range(wide):
            ref[rows_of(x * n, n)] = block_ref[rows_of((start + x) * n, n)]
        start = start + (wide - narrow if start else 0)
        at = wide * n
        for x in range(narrow):
            ref[rows_of(at, LO)] = below_ref[rows_of((start + x) * PAD_LO + PAD_LO - LO, LO)]
            ref[rows_of(at + LO, HI)] = above_ref[rows_of((start + x) * PAD_HI, HI)]
            at += LO + HI
        for part, base in ((block_ref, n * n), (below_ref, n * PAD_LO), (above_ref, n * PAD_HI)):
            ref[rows_of(at, wind_rows)] = part[rows_of(base, wind_rows)]
            at += wind_rows


def main_kernel(
    n,
    parts,
    info_ref,
    rate_ref,
    steps_ref,
    block_ref,
    below_ref,
    above_ref,
    west_ref,
    east_ref,
    *rest,
):
    if parts == 2:
        send_ref, keep_ref = rest[:2]
        cell, one, change, wind_x, wind_y, wind_z, air = rest[2:]
    else:
        settled_ref, rain_ref = rest[:2]
        cell, one, change, wind_x, wind_y, wind_z, air = rest[2:]
    span = n + PAD_LO + PAD_HI
    lanes = lane_ids()
    group = LANES // (2 * parts)
    cuts = 3 * parts

    def at(x, y):
        return (x + PAD_LO) * span + (y + PAD_LO)

    def tile(ref, x, y):
        return ref[rows_of(at(x, y))]

    for x in range(n):
        cell[rows_of(at(x, 0), n)] = block_ref[rows_of(x * n, n)]
        cell[rows_of(at(x, -PAD_LO), PAD_LO)] = below_ref[rows_of(x * PAD_LO, PAD_LO)]
        cell[rows_of(at(x, n), PAD_HI)] = above_ref[rows_of(x * PAD_HI, PAD_HI)]
    for ref, start, wide, narrow_at, narrow in (
        (west_ref, -PAD_LO, PAD_LO, -LO, LO),
        (east_ref, n, PAD_HI, n, HI),
    ):
        for x in range(wide):
            cell[rows_of(at(start + x, 0), n)] = ref[rows_of(x * n, n)]
        for x in range(narrow):
            base = wide * n + x * (LO + HI)
            cell[rows_of(at(narrow_at + x, -LO), LO)] = ref[rows_of(base, LO)]
            cell[rows_of(at(narrow_at + x, n), HI)] = ref[rows_of(base + LO, HI)]

    side = {0: (block_ref, n * n), -1: (below_ref, n * PAD_LO), 1: (above_ref, n * PAD_HI)}
    west_at, east_at = PAD_LO * n + LO * (LO + HI), PAD_HI * n + HI * (LO + HI)

    def wind_part(bx, by):
        if bx == 0:
            return side[by]
        ref, base = (west_ref, west_at) if bx < 0 else (east_ref, east_at)
        return ref, base + cuts * (0, 2, 1)[by]

    for bx in (-1, 0, 1):
        for by in (-1, 0, 1):
            ref, base = wind_part(bx, by)
            for k in range(cuts):
                air[rows_of(((bx + 1) * 3 + by + 1) * cuts + k)] = ref[rows_of(base + k)] * (1.0 / 12.0)

    ids = (lanes // group) % 2
    which = lanes // (2 * group)

    def spread(out, d, xs, ys):
        bx, by = (xs[0] >= n) - (xs[0] < 0), (ys[0] >= n) - (ys[0] < 0)

        def one_x(x):
            for y in ys:
                here = ids + ((x - bx * n) * (2 * n) + (y - by * n) * 2)
                value = None
                for h in range(parts):
                    source = air[rows_of(((bx + 1) * 3 + by + 1) * cuts + h * 3 + d)]
                    part = pick(source, here)
                    value = part if value is None else jnp.where(which == h, part, value)
                out[rows_of(at(x, y))] = value

        if len(xs) > 3:
            pl.loop(xs[0], xs[-1] + 1)(one_x)
        else:
            for x in xs:
                one_x(x)

    lo4, lo3, lo1 = range(-LO - 1, 0), range(-LO, 0), range(-1, 0)
    mid = range(n)
    hi3, hi2, hi1 = range(n, n + HI + 1), range(n, n + HI), range(n, n + 1)
    for xs, ys in ((lo4, mid), (mid, mid), (hi3, mid), (mid, lo3), (mid, hi2), (lo1, lo3), (lo1, hi2), (hi1, lo3), (hi1, hi2)):
        spread(wind_x, 0, xs, ys)
    for xs, ys in ((mid, lo4), (mid, mid), (mid, hi3), (lo3, mid), (hi2, mid), (lo3, lo1), (hi2, lo1), (lo3, hi1), (hi2, hi1)):
        spread(wind_y, 1, xs, ys)
    for xs, ys in ((mid, mid), (mid, lo3), (mid, hi2), (lo3, mid), (hi2, mid)):
        spread(wind_z, 2, xs, ys)

    def pass_x(ref, y, begin, end, add):
        cells = [tile(ref, x, y) for x in range(begin - LO, end + HI)]
        winds = [tile(wind_x, x, y) for x in range(begin - 1, end + 1)]
        for x, value in zip(range(begin, end), line_change(cells, winds)):
            if add:
                value = value + tile(change, x, y)
            change[rows_of(at(x, y))] = value

    def pass_y(ref, x, begin, end, add):
        cells = [tile(ref, x, y) for y in range(begin - LO, end + HI)]
        winds = [tile(wind_y, x, y) for y in range(begin - 1, end + 1)]
        for y, value in zip(range(begin, end), line_change(cells, winds)):
            if add:
                value = value + tile(change, x, y)
            change[rows_of(at(x, y))] = value

    def eight(ref, first, step, level):
        return ref[pl.ds(first * ROWS + level, ROWS, stride=step * ROWS)]

    def from_below(value):
        return jnp.where(lanes < group, 0.0, pltpu.roll(value, group, 1))

    def from_above(value):
        return jnp.where(lanes >= LANES - group, 0.0, pltpu.roll(value, LANES - group, 1))

    def pass_z(ref, first, step):
        cells = [eight(ref, first, step, k) for k in range(ROWS)]
        winds = [eight(wind_z, first, step, k) for k in range(ROWS)]
        long_cells = [from_below(v) for v in cells[ROWS - LO :]] + cells + [from_above(v) for v in cells[:HI]]
        long_winds = [from_below(winds[-1])] + winds + [from_above(winds[0])]
        sums = [eight(change, first, step, k) + v for k, v in enumerate(line_change(long_cells, long_winds))]
        return cells, sums

    halo = (LO, HI)

    @pl.loop(0, n)
    def _(i):
        pass_x(cell, i, -LO, n + HI, False)

    @pl.loop(0, LO + HI)
    def _(i):
        pass_x(cell, jnp.where(i < LO, i - LO, i + n - LO), 0, n, False)

    @pl.loop(0, LO + HI)
    def _(i):
        pass_y(cell, jnp.where(i < LO, i - LO, i + n - LO), 0, n, True)

    @pl.loop(0, n)
    def _(i):
        pass_y(cell, i, -LO, n + HI, True)

    def stage_one(first, step, inside):
        cells, sums = pass_z(cell, first, step)
        for k in range(ROWS):
            one[pl.ds(first * ROWS + k, ROWS, stride=step * ROWS)] = (cells[k] + sums[k]) * inside

    def inside(i, lower, upper):
        return jnp.where(i < 0, info_ref[lower], jnp.where(i >= n, info_ref[upper], 1)).astype(F32)

    @pl.loop(-LO, n + HI)
    def _(x):
        stage_one(at(x, 0), 1, inside(x, 1, 2))

    @pl.loop(0, LO + HI)
    def _(i):
        y = jnp.where(i < LO, i - LO, i + n - LO)
        stage_one(at(0, y), span, inside(y, 3, 4))

    @pl.loop(0, n)
    def _(i):
        pass_x(one, i, 0, n, False)

    @pl.loop(0, n)
    def _(i):
        pass_y(one, i, 0, n, True)

    @pl.loop(0, n)
    def _(x):
        first = at(x, 0)
        cells, sums = pass_z(one, first, 1)
        for k in range(ROWS):
            mass = eight(cell, first, 1, k)
            change[pl.ds(first * ROWS + k, ROWS, stride=ROWS)] = 0.5 * mass + 0.5 * (cells[k] + sums[k])

    rates = jnp.broadcast_to(rate_ref[...], (ROWS, LANES))
    steps = jnp.broadcast_to(steps_ref[...], (ROWS, LANES))
    together = 4
    rains = []
    for half in range(n // together):
        firsts = [at(half * together + i, 0) for i in range(together)]

        def substep(s, carry):
            columns, rain = carry
            rate = jnp.where(s < steps, rates, 0.0)
            new_columns, new_rain = [], []
            for column, drops in zip(columns, rain):
                upper = column[1:] + [from_above(column[0])]
                new_rain.append(drops + rate * column[0])
                new_columns.append([v + rate * (u - v) for v, u in zip(column, upper)])
            return new_columns, new_rain

        columns = [[eight(change, f, 1, k) for k in range(ROWS)] for f in firsts]
        columns, rain = lax.fori_loop(0, SUBS, substep, (columns, [jnp.zeros((ROWS, LANES), F32)] * together))
        for f, column in zip(firsts, columns):
            for k in range(ROWS):
                one[pl.ds(f * ROWS + k, ROWS, stride=ROWS)] = column[k]
        rains += rain

    if parts == 2:
        first = info_ref[0] == 0
        low = lanes < 64
        for x in range(n // 2):
            for y in range(n):
                a, b = tile(one, x, y), tile(one, x + n // 2, y)
                lower = jnp.where(low, a, pltpu.roll(b, 64, 1))
                upper = jnp.where(low, pltpu.roll(a, 64, 1), b)
                keep, send = swap(lower, upper, first)
                keep_ref[rows_of(x * n + y)] = keep
                send_ref[rows_of(x * n + y)] = send
        for j in range(2):
            value = jnp.where(lanes < group, rains[4 * j], 0.0)
            for i in range(1, 4):
                shifted = pltpu.roll(rains[4 * j + i], group * i, 1)
                value = jnp.where(lanes // group == i, shifted, value)
            keep_ref[rows_of(n // 2 * n + j)] = value
            send_ref[rows_of(n // 2 * n + j)] = value
    else:
        for x in range(n):
            settled_ref[rows_of(x * n, n)] = one[rows_of(at(x, 0), n)]
            rain_ref[rows_of(x)] = rains[x]


def matrix_kernel(bins, gain_ref, loss_ref, pairs_ref, lost_ref, wide, tall):
    zero = jnp.zeros((bins, LANES - bins), F32)
    shifts = bins // 2

    @pl.loop(0, bins)
    def _(i):
        rows = gain_ref[pl.ds(i * bins, bins)].astype(F32)
        rows = jnp.concatenate([rows, zero], axis=1)
        wide[pl.ds(i * 2 * bins, bins)] = rows
        wide[pl.ds(i * 2 * bins + bins, bins)] = rows
        tall[pl.ds(i * bins, bins)] = rows

        @pl.when(i < shifts)
        def _():
            tall[pl.ds((i + bins) * bins, bins)] = rows

    for d in range(shifts + 1):
        rows = wide[pl.ds(d, bins, stride=2 * bins + 1)]
        if 0 < d < shifts:
            rows = rows + tall[pl.ds(d * bins, bins, stride=bins + 1)]
        pairs_ref[pl.ds(d * LANES, bins)] = rows.astype(jnp.bfloat16)
        pairs_ref[pl.ds(d * LANES + bins, bins)] = pltpu.roll(rows, bins, 1).astype(jnp.bfloat16)
    rows = jnp.concatenate([loss_ref[...].astype(F32), zero], axis=1)
    lost_ref[pl.ds(0, bins)] = rows.astype(jnp.bfloat16)
    lost_ref[pl.ds(bins, bins)] = pltpu.roll(rows, bins, 1).astype(jnp.bfloat16)


def breakup_rows(mass, pairs_ref, lost_ref, products):
    bins = LANES // 2
    count = mass.shape[0]
    lanes = lax.broadcasted_iota(jnp.int32, (ROWS, LANES), 1)
    rounded = mass.astype(jnp.bfloat16)
    wide = rounded.astype(F32)
    for d in range(bins // 2 + 1):
        ids = lanes // bins * bins + (lanes + d) % bins
        for r in range(0, count, 2 * ROWS):
            halves = [wide[r + ROWS * k : r + ROWS * (k + 1)] for k in range(2)]
            if d:
                halves = [v * pick(v, ids) for v in halves]
            else:
                halves = [v * v for v in halves]
            products[pl.ds(r, 2 * ROWS), d * LANES : (d + 1) * LANES] = jnp.concatenate(halves, axis=0).astype(jnp.bfloat16)
    gained = jnp.dot(products[pl.ds(0, count)], pairs_ref[...], preferred_element_type=F32)
    loss = jnp.dot(rounded, lost_ref[...], preferred_element_type=F32)
    return mass + gained - mass * loss


def breakup_kernel(n, own_ref, keep_ref, got_ref, pairs_ref, lost_ref, mass_ref, rain_ref, columns, products):
    gz = own_ref[0]
    first = gz == 0
    lanes = lane_ids()
    odd = (lanes // 32) % 2 == 1
    half = n // 2
    ids = [lanes // 64 * 32 + lanes % 32 + 64 * k for k in range(2)]
    for x in range(half):
        for y in range(n):
            at = rows_of(x * n + y)
            a, b = swap(keep_ref[at], got_ref[at], first)
            for k in range(2):
                columns[rows_of((x + half * k) * n + y)] = jnp.where(odd, pick(b, ids[k]), pick(a, ids[k]))
    for j in range(2):
        at = rows_of(half * n + j)
        a, b = swap(keep_ref[at], got_ref[at], first)
        a, b = [jnp.where(first, v[: n // 2], v[n // 2 :]) for v in (a, b)]
        for i in range(4):
            rain_ref[4 * j + i] = jnp.concatenate([a[:, 32 * i : 32 * i + 32], b[:, 32 * i : 32 * i + 32]], axis=1)

    count = products.shape[0]

    @pl.loop(0, n * n * ROWS // count)
    def _(i):
        start = pl.multiple_of(i * count, count)
        mass = columns[pl.ds(start, count)]
        columns[pl.ds(start, count)] = breakup_rows(mass, pairs_ref, lost_ref, products)

    for x in range(n):
        for y in range(n):
            value = columns[rows_of(x * n + y)]
            mass_ref[x, y, 0:8] = value[:, :64]
            mass_ref[x, y, 8:16] = value[:, 64:]


def breakup_plain_kernel(mass_ref, pairs_ref, lost_ref, out_ref, products):
    count = products.shape[0]

    @pl.loop(0, mass_ref.shape[0] // count)
    def _(i):
        start = pl.multiple_of(i * count, count)
        out_ref[pl.ds(start, count)] = breakup_rows(mass_ref[pl.ds(start, count)], pairs_ref, lost_ref, products)


def shape(*dims, dtype=F32):
    return jax.ShapeDtypeStruct(dims, dtype)


def call(kernel, out_shape, in_specs, scratch=(), flops=0, moved=1 << 20):
    return pl.pallas_call(
        kernel,
        out_shape=out_shape,
        in_specs=in_specs,
        out_specs=jax.tree.map(lambda _: VMEM, out_shape),
        scratch_shapes=list(scratch),
        compiler_params=pltpu.CompilerParams(vmem_limit_bytes=40 << 20),
        cost_estimate=pl.CostEstimate(flops=flops, bytes_accessed=moved, transcendentals=0),
    )


def to_neighbours(axis, up, down):
    count = lax.axis_size(axis)
    from_lower = lax.ppermute(up, axis, [(i, i + 1) for i in range(count - 1)])
    from_upper = lax.ppermute(down, axis, [(i + 1, i) for i in range(count - 1)])
    return from_lower, from_upper


def per_device(bin_mass, courant, sub_courant, fall_steps, frag_gain, collide):
    nx, ny, nz, bins = bin_mass.shape
    n = nx
    parts = lax.axis_size("gz")
    gz, gx, gy = lax.axis_index("gz"), lax.axis_index("gx"), lax.axis_index("gy")
    width = bins // parts
    pairs_rows = (bins // 2 + 1) * LANES

    pairs, lost = call(
        functools.partial(matrix_kernel, bins),
        (shape(pairs_rows, LANES, dtype=jnp.bfloat16), shape(LANES, LANES, dtype=jnp.bfloat16)),
        [VMEM, VMEM],
        [pltpu.VMEM((2 * bins * bins, LANES), F32), pltpu.VMEM((3 * bins * bins // 2, LANES), F32)],
        flops=1 << 20,
    )(frag_gain, collide)

    wind = courant.reshape(3, nx * ny * nz // ROWS, ROWS).transpose(0, 2, 1)
    own = gz.astype(jnp.int32).reshape(1)
    wind_rows = 3 * parts
    block_shape = shape((n * n + wind_rows) * ROWS, LANES)
    below_shape = shape((n * PAD_LO + wind_rows) * ROWS, LANES)
    above_shape = shape((n * PAD_HI + wind_rows) * ROWS, LANES)
    if parts == 2:
        half = shape((n * n // 2 + 3) * ROWS, LANES)
        send, keep = call(pack_kernel, (half, half), [SMEM, VMEM, VMEM])(own, bin_mass, wind)
        got = lax.ppermute(send, "gz", [(0, 1), (1, 0)])
        block, up, down = call(merge_kernel, (block_shape, below_shape, above_shape), [SMEM, VMEM, VMEM])(own, keep, got)
    else:
        split = bin_mass.reshape(nx, ny, nz // ROWS, ROWS, parts, width).transpose(4, 0, 1, 3, 2, 5)
        split = lax.all_to_all(split, "gz", split_axis=0, concat_axis=0, tiled=True)
        block = split.transpose(1, 2, 3, 0, 4, 5).reshape(-1, LANES)
        winds = lax.all_gather(wind, "gz").reshape(-1, LANES)
        cube = block.reshape(n, n, ROWS, LANES)
        up = jnp.concatenate([cube[:, n - PAD_LO :].reshape(-1, LANES), winds])
        down = jnp.concatenate([cube[:, :PAD_HI].reshape(-1, LANES), winds])
        block = jnp.concatenate([block, winds])

    below, above = to_neighbours("gy", up, down)

    right, left = call(
        functools.partial(side_kernel, n, wind_rows),
        (
            shape((PAD_LO * n + LO * (LO + HI) + 3 * wind_rows) * ROWS, LANES),
            shape((PAD_HI * n + HI * (LO + HI) + 3 * wind_rows) * ROWS, LANES),
        ),
        [VMEM] * 3,
    )(block, below, above)
    west, east = to_neighbours("gx", right, left)

    info = jnp.stack([gz, gx > 0, gx < lax.axis_size("gx") - 1, gy > 0, gy < lax.axis_size("gy") - 1]).astype(jnp.int32)
    rate = jnp.tile(lax.dynamic_slice(sub_courant, (gz * width,), (width,)), 2 * parts).reshape(1, LANES)
    steps = jnp.tile(lax.dynamic_slice(fall_steps, (gz * width,), (width,)), 2 * parts).reshape(1, LANES)
    span = n + PAD_LO + PAD_HI
    if parts == 2:
        half = shape((n * n // 2 + 2) * ROWS, LANES)
        outs = (half, half)
    else:
        outs = (shape(n * n * ROWS, LANES), shape(n * ROWS, LANES))
    outs = call(
        functools.partial(main_kernel, n, parts),
        outs,
        [SMEM] + [VMEM] * 7,
        [pltpu.VMEM((span * span * ROWS, LANES), F32)] * 6 + [pltpu.VMEM((9 * wind_rows * ROWS, LANES), F32)],
        flops=1 << 24,
    )(info, rate, steps, block, below, above, west, east)

    if parts == 2:
        send, keep = outs
        got = lax.ppermute(send, "gz", [(0, 1), (1, 0)])
        return call(
            functools.partial(breakup_kernel, n),
            (shape(nx, ny, nz, bins), shape(nx, ny // parts, bins)),
            [SMEM] + [VMEM] * 4,
            [pltpu.VMEM((n * n * ROWS, LANES), F32), pltpu.VMEM((256, pairs_rows), jnp.bfloat16)],
            flops=1 << 28,
        )(own, keep, got, pairs, lost)

    settled, rain = outs
    rain = rain.reshape(nx, ny, LANES)[:, :, :width]
    rain = lax.all_to_all(rain, "gz", split_axis=1, concat_axis=2, tiled=True)
    settled = settled.reshape(nx, ny, ROWS, parts, nz // ROWS, width).transpose(3, 0, 1, 4, 2, 5)
    settled = lax.all_to_all(settled, "gz", split_axis=0, concat_axis=0, tiled=True)
    settled = settled.transpose(1, 2, 3, 4, 0, 5).reshape(nx * ny, nz // ROWS, ROWS, bins)
    paired = settled.transpose(0, 2, 1, 3).reshape(-1, LANES)
    updated = call(
        breakup_plain_kernel,
        shape(n * n * ROWS, LANES),
        [VMEM] * 3,
        [pltpu.VMEM((256, pairs_rows), jnp.bfloat16)],
        flops=1 << 28,
    )(paired, pairs, lost)
    updated = updated.reshape(nx, ny, ROWS, nz // ROWS, bins).transpose(0, 1, 3, 2, 4).reshape(nx, ny, nz, bins)
    return updated, rain


def solution(mesh):
    in_specs = (P("gx", "gy", "gz", None), P(None, "gx", "gy", "gz"), P(), P(), P(), P())
    out_specs = (P("gx", "gy", "gz", None), P("gx", ("gy", "gz"), None))
    return jax.shard_map(per_device, mesh=mesh, in_specs=in_specs, out_specs=out_specs, check_vma=False)
```

```python
import functools

import jax
import jax.numpy as jnp
from jax import lax
from jax.experimental import pallas as pl
from jax.experimental.pallas import tpu as pltpu
from jax.sharding import PartitionSpec as P

SUBS = 24
EPS = 1e-06
LO, HI = 3, 2
PAD_LO, PAD_HI = 2 * LO, 2 * HI
ROWS, LANES = 8, 128
F32 = jnp.float32
VMEM = pl.BlockSpec(memory_space=pltpu.VMEM)
SMEM = pl.BlockSpec(memory_space=pltpu.SMEM)


def lane_ids():
    return lax.broadcasted_iota(jnp.int32, (ROWS, LANES), 1)


def pick(tile, ids):
    return jnp.take_along_axis(tile, ids, axis=1, mode="promise_in_bounds")


def rows_of(first, count=1):
    return pl.ds(first * ROWS, count * ROWS)


def swap(ref_a, ref_b, own_first):
    return jnp.where(own_first, ref_a, ref_b), jnp.where(own_first, ref_b, ref_a)


def line_change(cells, winds):
    first = [b - a for a, b in zip(cells, cells[1:])]
    twice = [d + d for d in first]
    second = [b - a for a, b in zip(first, first[1:])]
    third = [a - b for a, b in zip(second, second[1:])]
    curved = [(13.0 / 3.0) * (c * c) + 4.0 * EPS for c in second]
    fluxes = []
    for j in range(len(cells) - 4):
        left = twice[j + 1] + second[j]
        mid = first[j + 1] + first[j + 2]
        right = twice[j + 2] - second[j + 2]
        e0 = curved[j] + left * left
        e1 = curved[j + 1] + mid * mid
        e2 = curved[j + 2] + right * right
        e0 = e0 * e0
        e1 = e1 * e1
        e2 = e2 * e2
        e0 = 3.0 * e0
        e2_twice = e2 + e2
        top = e1 * (e2_twice * third[j] + e0 * third[j + 1])
        low = e1 * (e2 + e0) + e0 * e2_twice
        inverse = pl.reciprocal(low, approx=True)
        inverse = inverse * (2.0 - low * inverse)
        estimate = 6.0 * cells[j + 2] + (first[j + 1] + twice[j + 2]) + top * inverse
        fluxes.append((winds[j] + winds[j + 1]) * estimate)
    return [a - b for a, b in zip(fluxes, fluxes[1:])]


def pack_kernel(own_ref, mass_ref, wind_ref, send_ref, keep_ref):
    gz = own_ref[0]
    nx, ny = mass_ref.shape[:2]
    lanes = lane_ids()
    place = lanes % 64
    low = lanes < 64

    def one(half):
        return (2 * (place // 32) + half) * 32 + place % 32

    keep_ids, send_ids = one(gz), one(1 - gz)
    for x in range(nx // 2):
        for y in range(ny):
            a = jnp.concatenate([mass_ref[x, y, 0:8], mass_ref[x, y, 8:16]], axis=1)
            b = jnp.concatenate([mass_ref[x + nx // 2, y, 0:8], mass_ref[x + nx // 2, y, 8:16]], axis=1)
            at = rows_of(x * ny + y)
            keep_ref[at] = jnp.where(low, pick(a, keep_ids), pick(b, keep_ids))
            send_ref[at] = jnp.where(low, pick(a, send_ids), pick(b, send_ids))
    base = nx // 2 * ny
    for d in range(3):
        send_ref[rows_of(base + d)] = wind_ref[d]
        keep_ref[rows_of(base + d)] = wind_ref[d]


def by_parity(even, body):
    pl.when(even)(lambda: body(0, 1))
    pl.when(jnp.logical_not(even))(lambda: body(1, 0))


def merge_kernel(own_ref, keep_ref, got_ref, block_ref, *messages):
    by_parity(
        own_ref[1] == 0,
        lambda up, down: merge_body(own_ref, keep_ref, got_ref, block_ref, messages[up], messages[down]),
    )


def merge_body(own_ref, keep_ref, got_ref, block_ref, right_ref, left_ref):
    first = own_ref[0] == 0
    low = lane_ids() < 64
    n = 8
    for x in range(n // 2):
        for y in range(n):
            at = rows_of(x * n + y)
            a, b = swap(keep_ref[at], got_ref[at], first)
            for xx, tile in (
                (x, jnp.where(low, a, pltpu.roll(b, 64, 1))),
                (x + n // 2, jnp.where(low, pltpu.roll(a, 64, 1), b)),
            ):
                block_ref[rows_of(xx * n + y)] = tile
                if y >= n - PAD_LO:
                    right_ref[rows_of(xx * PAD_LO + y - (n - PAD_LO))] = tile
                if y < PAD_HI:
                    left_ref[rows_of(xx * PAD_HI + y)] = tile
    for d in range(3):
        at = rows_of(n // 2 * n + d)
        a, b = swap(keep_ref[at], got_ref[at], first)
        for ref, base in ((block_ref, n * n), (right_ref, n * PAD_LO), (left_ref, n * PAD_HI)):
            ref[rows_of(base + d)] = a
            ref[rows_of(base + 3 + d)] = b


def side_kernel(n, wind_rows, own_ref, block_ref, first_ref, second_ref, *messages):
    def along_x(above_ref, below_ref):
        by_parity(
            own_ref[2] == 0,
            lambda up, down: side_body(n, wind_rows, block_ref, below_ref, above_ref, messages[up], messages[down]),
        )

    got = (first_ref, second_ref)
    by_parity(own_ref[1] == 0, lambda up, down: along_x(got[up], got[down]))


def side_body(n, wind_rows, block_ref, below_ref, above_ref, right_ref, left_ref):
    for ref, start, wide, narrow in ((right_ref, n - PAD_LO, PAD_LO, LO), (left_ref, 0, PAD_HI, HI)):
        for x in range(wide):
            ref[rows_of(x * n, n)] = block_ref[rows_of((start + x) * n, n)]
        start = start + (wide - narrow if start else 0)
        at = wide * n
        for x in range(narrow):
            ref[rows_of(at, LO)] = below_ref[rows_of((start + x) * PAD_LO + PAD_LO - LO, LO)]
            ref[rows_of(at + LO, HI)] = above_ref[rows_of((start + x) * PAD_HI, HI)]
            at += LO + HI
        for part, base in ((block_ref, n * n), (below_ref, n * PAD_LO), (above_ref, n * PAD_HI)):
            ref[rows_of(at, wind_rows)] = part[rows_of(base, wind_rows)]
            at += wind_rows


def main_kernel(
    n,
    parts,
    info_ref,
    rate_ref,
    steps_ref,
    block_ref,
    y_first_ref,
    y_second_ref,
    x_first_ref,
    x_second_ref,
    *rest,
):
    if parts == 2:
        send_ref, keep_ref = rest[:2]
        cell, one, change, wind_x, wind_y, wind_z, air, *halos = rest[2:]
    else:
        settled_ref, rain_ref = rest[:2]
        cell, one, change, wind_x, wind_y, wind_z, air, *halos = rest[2:]
    below_ref, above_ref, west_ref, east_ref = halos
    for (first_ref, second_ref), even, lower_ref, upper_ref in (
        ((y_first_ref, y_second_ref), info_ref[5] == 0, below_ref, above_ref),
        ((x_first_ref, x_second_ref), info_ref[6] == 0, west_ref, east_ref),
    ):
        upper_ref[...], lower_ref[...] = swap(first_ref[...], second_ref[...], even)
    span = n + PAD_LO + PAD_HI
    lanes = lane_ids()
    group = LANES // (2 * parts)
    cuts = 3 * parts

    def at(x, y):
        return (x + PAD_LO) * span + (y + PAD_LO)

    def tile(ref, x, y):
        return ref[rows_of(at(x, y))]

    for x in range(n):
        cell[rows_of(at(x, 0), n)] = block_ref[rows_of(x * n, n)]
        cell[rows_of(at(x, -PAD_LO), PAD_LO)] = below_ref[rows_of(x * PAD_LO, PAD_LO)]
        cell[rows_of(at(x, n), PAD_HI)] = above_ref[rows_of(x * PAD_HI, PAD_HI)]
    for ref, start, wide, narrow_at, narrow in (
        (west_ref, -PAD_LO, PAD_LO, -LO, LO),
        (east_ref, n, PAD_HI, n, HI),
    ):
        for x in range(wide):
            cell[rows_of(at(start + x, 0), n)] = ref[rows_of(x * n, n)]
        for x in range(narrow):
            base = wide * n + x * (LO + HI)
            cell[rows_of(at(narrow_at + x, -LO), LO)] = ref[rows_of(base, LO)]
            cell[rows_of(at(narrow_at + x, n), HI)] = ref[rows_of(base + LO, HI)]

    side = {0: (block_ref, n * n), -1: (below_ref, n * PAD_LO), 1: (above_ref, n * PAD_HI)}
    west_at, east_at = PAD_LO * n + LO * (LO + HI), PAD_HI * n + HI * (LO + HI)

    def wind_part(bx, by):
        if bx == 0:
            return side[by]
        ref, base = (west_ref, west_at) if bx < 0 else (east_ref, east_at)
        return ref, base + cuts * (0, 2, 1)[by]

    for bx in (-1, 0, 1):
        for by in (-1, 0, 1):
            ref, base = wind_part(bx, by)
            for k in range(cuts):
                air[rows_of(((bx + 1) * 3 + by + 1) * cuts + k)] = ref[rows_of(base + k)] * (1.0 / 12.0)

    ids = (lanes // group) % 2
    which = lanes // (2 * group)

    def spread(out, d, xs, ys):
        bx, by = (xs[0] >= n) - (xs[0] < 0), (ys[0] >= n) - (ys[0] < 0)

        def one_x(x):
            for y in ys:
                here = ids + ((x - bx * n) * (2 * n) + (y - by * n) * 2)
                value = None
                for h in range(parts):
                    source = air[rows_of(((bx + 1) * 3 + by + 1) * cuts + h * 3 + d)]
                    part = pick(source, here)
                    value = part if value is None else jnp.where(which == h, part, value)
                out[rows_of(at(x, y))] = value

        if len(xs) > 3:
            pl.loop(xs[0], xs[-1] + 1)(one_x)
        else:
            for x in xs:
                one_x(x)

    lo4, lo3, lo1 = range(-LO - 1, 0), range(-LO, 0), range(-1, 0)
    mid = range(n)
    hi3, hi2, hi1 = range(n, n + HI + 1), range(n, n + HI), range(n, n + 1)
    for xs, ys in ((lo4, mid), (mid, mid), (hi3, mid), (mid, lo3), (mid, hi2), (lo1, lo3), (lo1, hi2), (hi1, lo3), (hi1, hi2)):
        spread(wind_x, 0, xs, ys)
    for xs, ys in ((mid, lo4), (mid, mid), (mid, hi3), (lo3, mid), (hi2, mid), (lo3, lo1), (hi2, lo1), (lo3, hi1), (hi2, hi1)):
        spread(wind_y, 1, xs, ys)
    for xs, ys in ((mid, mid), (mid, lo3), (mid, hi2), (lo3, mid), (hi2, mid)):
        spread(wind_z, 2, xs, ys)

    def pass_x(ref, y, begin, end, add):
        cells = [tile(ref, x, y) for x in range(begin - LO, end + HI)]
        winds = [tile(wind_x, x, y) for x in range(begin - 1, end + 1)]
        for x, value in zip(range(begin, end), line_change(cells, winds)):
            if add:
                value = value + tile(change, x, y)
            change[rows_of(at(x, y))] = value

    def pass_y(ref, x, begin, end, add):
        cells = [tile(ref, x, y) for y in range(begin - LO, end + HI)]
        winds = [tile(wind_y, x, y) for y in range(begin - 1, end + 1)]
        for y, value in zip(range(begin, end), line_change(cells, winds)):
            if add:
                value = value + tile(change, x, y)
            change[rows_of(at(x, y))] = value

    def eight(ref, first, step, level):
        return ref[pl.ds(first * ROWS + level, ROWS, stride=step * ROWS)]

    def from_below(value):
        return jnp.where(lanes < group, 0.0, pltpu.roll(value, group, 1))

    def from_above(value):
        return jnp.where(lanes >= LANES - group, 0.0, pltpu.roll(value, LANES - group, 1))

    def pass_z(ref, first, step):
        cells = [eight(ref, first, step, k) for k in range(ROWS)]
        winds = [eight(wind_z, first, step, k) for k in range(ROWS)]
        long_cells = [from_below(v) for v in cells[ROWS - LO :]] + cells + [from_above(v) for v in cells[:HI]]
        long_winds = [from_below(winds[-1])] + winds + [from_above(winds[0])]
        sums = [eight(change, first, step, k) + v for k, v in enumerate(line_change(long_cells, long_winds))]
        return cells, sums

    halo = (LO, HI)

    @pl.loop(0, n)
    def _(i):
        pass_x(cell, i, -LO, n + HI, False)

    @pl.loop(0, LO + HI)
    def _(i):
        pass_x(cell, jnp.where(i < LO, i - LO, i + n - LO), 0, n, False)

    @pl.loop(0, LO + HI)
    def _(i):
        pass_y(cell, jnp.where(i < LO, i - LO, i + n - LO), 0, n, True)

    @pl.loop(0, n)
    def _(i):
        pass_y(cell, i, -LO, n + HI, True)

    def stage_one(first, step, inside):
        cells, sums = pass_z(cell, first, step)
        for k in range(ROWS):
            one[pl.ds(first * ROWS + k, ROWS, stride=step * ROWS)] = (cells[k] + sums[k]) * inside

    def inside(i, lower, upper):
        return jnp.where(i < 0, info_ref[lower], jnp.where(i >= n, info_ref[upper], 1)).astype(F32)

    @pl.loop(-LO, n + HI)
    def _(x):
        stage_one(at(x, 0), 1, inside(x, 1, 2))

    @pl.loop(0, LO + HI)
    def _(i):
        y = jnp.where(i < LO, i - LO, i + n - LO)
        stage_one(at(0, y), span, inside(y, 3, 4))

    @pl.loop(0, n)
    def _(i):
        pass_x(one, i, 0, n, False)

    @pl.loop(0, n)
    def _(i):
        pass_y(one, i, 0, n, True)

    @pl.loop(0, n)
    def _(x):
        first = at(x, 0)
        cells, sums = pass_z(one, first, 1)
        for k in range(ROWS):
            mass = eight(cell, first, 1, k)
            change[pl.ds(first * ROWS + k, ROWS, stride=ROWS)] = 0.5 * mass + 0.5 * (cells[k] + sums[k])

    rates = jnp.broadcast_to(rate_ref[...], (ROWS, LANES))
    steps = jnp.broadcast_to(steps_ref[...], (ROWS, LANES))
    together = 4
    rains = []
    for half in range(n // together):
        firsts = [at(half * together + i, 0) for i in range(together)]

        def substep(s, carry):
            columns, rain = carry
            rate = jnp.where(s < steps, rates, 0.0)
            new_columns, new_rain = [], []
            for column, drops in zip(columns, rain):
                upper = column[1:] + [from_above(column[0])]
                new_rain.append(drops + rate * column[0])
                new_columns.append([v + rate * (u - v) for v, u in zip(column, upper)])
            return new_columns, new_rain

        columns = [[eight(change, f, 1, k) for k in range(ROWS)] for f in firsts]
        columns, rain = lax.fori_loop(0, SUBS, substep, (columns, [jnp.zeros((ROWS, LANES), F32)] * together))
        for f, column in zip(firsts, columns):
            for k in range(ROWS):
                one[pl.ds(f * ROWS + k, ROWS, stride=ROWS)] = column[k]
        rains += rain

    if parts == 2:
        first = info_ref[0] == 0
        low = lanes < 64
        for x in range(n // 2):
            for y in range(n):
                a, b = tile(one, x, y), tile(one, x + n // 2, y)
                lower = jnp.where(low, a, pltpu.roll(b, 64, 1))
                upper = jnp.where(low, pltpu.roll(a, 64, 1), b)
                keep, send = swap(lower, upper, first)
                keep_ref[rows_of(x * n + y)] = keep
                send_ref[rows_of(x * n + y)] = send
        for j in range(2):
            value = jnp.where(lanes < group, rains[4 * j], 0.0)
            for i in range(1, 4):
                shifted = pltpu.roll(rains[4 * j + i], group * i, 1)
                value = jnp.where(lanes // group == i, shifted, value)
            keep_ref[rows_of(n // 2 * n + j)] = value
            send_ref[rows_of(n // 2 * n + j)] = value
    else:
        for x in range(n):
            settled_ref[rows_of(x * n, n)] = one[rows_of(at(x, 0), n)]
            rain_ref[rows_of(x)] = rains[x]


def matrix_kernel(bins, gain_ref, loss_ref, pairs_ref, lost_ref, wide, tall):
    zero = jnp.zeros((bins, LANES - bins), F32)
    shifts = bins // 2

    @pl.loop(0, bins)
    def _(i):
        rows = gain_ref[pl.ds(i * bins, bins)].astype(F32)
        rows = jnp.concatenate([rows, zero], axis=1)
        wide[pl.ds(i * 2 * bins, bins)] = rows
        wide[pl.ds(i * 2 * bins + bins, bins)] = rows
        tall[pl.ds(i * bins, bins)] = rows

        @pl.when(i < shifts)
        def _():
            tall[pl.ds((i + bins) * bins, bins)] = rows

    for d in range(shifts + 1):
        rows = wide[pl.ds(d, bins, stride=2 * bins + 1)]
        if 0 < d < shifts:
            rows = rows + tall[pl.ds(d * bins, bins, stride=bins + 1)]
        pairs_ref[pl.ds(d * LANES, bins)] = rows.astype(jnp.bfloat16)
        pairs_ref[pl.ds(d * LANES + bins, bins)] = pltpu.roll(rows, bins, 1).astype(jnp.bfloat16)
    rows = jnp.concatenate([loss_ref[...].astype(F32), zero], axis=1)
    lost_ref[pl.ds(0, bins)] = rows.astype(jnp.bfloat16)
    lost_ref[pl.ds(bins, bins)] = pltpu.roll(rows, bins, 1).astype(jnp.bfloat16)


def breakup_rows(mass, pairs_ref, lost_ref, products):
    bins = LANES // 2
    count = mass.shape[0]
    lanes = lax.broadcasted_iota(jnp.int32, (ROWS, LANES), 1)
    rounded = mass.astype(jnp.bfloat16)
    wide = rounded.astype(F32)
    for d in range(bins // 2 + 1):
        ids = lanes // bins * bins + (lanes + d) % bins
        for r in range(0, count, 2 * ROWS):
            halves = [wide[r + ROWS * k : r + ROWS * (k + 1)] for k in range(2)]
            if d:
                halves = [v * pick(v, ids) for v in halves]
            else:
                halves = [v * v for v in halves]
            products[pl.ds(r, 2 * ROWS), d * LANES : (d + 1) * LANES] = jnp.concatenate(halves, axis=0).astype(jnp.bfloat16)
    gained = jnp.dot(products[pl.ds(0, count)], pairs_ref[...], preferred_element_type=F32)
    loss = jnp.dot(rounded, lost_ref[...], preferred_element_type=F32)
    return mass + gained - mass * loss


def breakup_kernel(n, own_ref, keep_ref, got_ref, pairs_ref, lost_ref, mass_ref, rain_ref, columns, products):
    gz = own_ref[0]
    first = gz == 0
    lanes = lane_ids()
    odd = (lanes // 32) % 2 == 1
    half = n // 2
    ids = [lanes // 64 * 32 + lanes % 32 + 64 * k for k in range(2)]
    for x in range(half):
        for y in range(n):
            at = rows_of(x * n + y)
            a, b = swap(keep_ref[at], got_ref[at], first)
            for k in range(2):
                columns[rows_of((x + half * k) * n + y)] = jnp.where(odd, pick(b, ids[k]), pick(a, ids[k]))
    for j in range(2):
        at = rows_of(half * n + j)
        a, b = swap(keep_ref[at], got_ref[at], first)
        a, b = [jnp.where(first, v[: n // 2], v[n // 2 :]) for v in (a, b)]
        for i in range(4):
            rain_ref[4 * j + i] = jnp.concatenate([a[:, 32 * i : 32 * i + 32], b[:, 32 * i : 32 * i + 32]], axis=1)

    count = products.shape[0]

    @pl.loop(0, n * n * ROWS // count)
    def _(i):
        start = pl.multiple_of(i * count, count)
        mass = columns[pl.ds(start, count)]
        columns[pl.ds(start, count)] = breakup_rows(mass, pairs_ref, lost_ref, products)

    for x in range(n):
        for y in range(n):
            value = columns[rows_of(x * n + y)]
            mass_ref[x, y, 0:8] = value[:, :64]
            mass_ref[x, y, 8:16] = value[:, 64:]


def breakup_plain_kernel(mass_ref, pairs_ref, lost_ref, out_ref, products):
    count = products.shape[0]

    @pl.loop(0, mass_ref.shape[0] // count)
    def _(i):
        start = pl.multiple_of(i * count, count)
        out_ref[pl.ds(start, count)] = breakup_rows(mass_ref[pl.ds(start, count)], pairs_ref, lost_ref, products)


def shape(*dims, dtype=F32):
    return jax.ShapeDtypeStruct(dims, dtype)


def call(kernel, out_shape, in_specs, scratch=(), flops=0, moved=1 << 20):
    return pl.pallas_call(
        kernel,
        out_shape=out_shape,
        in_specs=in_specs,
        out_specs=jax.tree.map(lambda _: VMEM, out_shape),
        scratch_shapes=list(scratch),
        compiler_params=pltpu.CompilerParams(vmem_limit_bytes=40 << 20),
        cost_estimate=pl.CostEstimate(flops=flops, bytes_accessed=moved, transcendentals=0),
    )


def to_neighbours(axis, first, second):
    count = lax.axis_size(axis)
    got = []
    for begin, message in ((0, first), (1, second)):
        pairs = [(i, i + 1) for i in range(begin, count - 1, 2)]
        got.append(lax.ppermute(message, axis, pairs + [(b, a) for a, b in pairs]))
    return got


def per_device(bin_mass, courant, sub_courant, fall_steps, frag_gain, collide):
    nx, ny, nz, bins = bin_mass.shape
    n = nx
    parts = lax.axis_size("gz")
    gz, gx, gy = lax.axis_index("gz"), lax.axis_index("gx"), lax.axis_index("gy")
    width = bins // parts
    pairs_rows = (bins // 2 + 1) * LANES

    pairs, lost = call(
        functools.partial(matrix_kernel, bins),
        (shape(pairs_rows, LANES, dtype=jnp.bfloat16), shape(LANES, LANES, dtype=jnp.bfloat16)),
        [VMEM, VMEM],
        [pltpu.VMEM((2 * bins * bins, LANES), F32), pltpu.VMEM((3 * bins * bins // 2, LANES), F32)],
        flops=1 << 20,
    )(frag_gain, collide)

    wind = courant.reshape(3, nx * ny * nz // ROWS, ROWS).transpose(0, 2, 1)
    own = jnp.stack([gz, gy % 2, gx % 2]).astype(jnp.int32)
    wind_rows = 3 * parts
    block_shape = shape((n * n + wind_rows) * ROWS, LANES)
    below_shape = shape((n * PAD_LO + wind_rows) * ROWS, LANES)
    if parts == 2:
        half = shape((n * n // 2 + 3) * ROWS, LANES)
        send, keep = call(pack_kernel, (half, half), [SMEM, VMEM, VMEM])(own, bin_mass, wind)
        got = lax.ppermute(send, "gz", [(0, 1), (1, 0)])
        block, first, second = call(merge_kernel, (block_shape, below_shape, below_shape), [SMEM, VMEM, VMEM])(own, keep, got)
    else:
        split = bin_mass.reshape(nx, ny, nz // ROWS, ROWS, parts, width).transpose(4, 0, 1, 3, 2, 5)
        split = lax.all_to_all(split, "gz", split_axis=0, concat_axis=0, tiled=True)
        block = split.transpose(1, 2, 3, 0, 4, 5).reshape(-1, LANES)
        winds = lax.all_gather(wind, "gz").reshape(-1, LANES)
        cube = block.reshape(n, n, ROWS, LANES)
        up = jnp.concatenate([cube[:, n - PAD_LO :].reshape(-1, LANES), winds])
        down = jnp.concatenate([cube[:, :PAD_HI].reshape(-1, LANES), winds])
        block = jnp.concatenate([block, winds])
        down = jnp.pad(down, ((0, up.shape[0] - down.shape[0]), (0, 0)))
        first, second = swap(up, down, gy % 2 == 0)

    from_y = to_neighbours("gy", first, second)

    side_shape = shape((PAD_LO * n + LO * (LO + HI) + 3 * wind_rows) * ROWS, LANES)
    first, second = call(
        functools.partial(side_kernel, n, wind_rows),
        (side_shape, side_shape),
        [SMEM] + [VMEM] * 3,
    )(own, block, *from_y)
    from_x = to_neighbours("gx", first, second)

    info = jnp.stack([gz, gx > 0, gx < lax.axis_size("gx") - 1, gy > 0, gy < lax.axis_size("gy") - 1, gy % 2, gx % 2]).astype(jnp.int32)
    rate = jnp.tile(lax.dynamic_slice(sub_courant, (gz * width,), (width,)), 2 * parts).reshape(1, LANES)
    steps = jnp.tile(lax.dynamic_slice(fall_steps, (gz * width,), (width,)), 2 * parts).reshape(1, LANES)
    span = n + PAD_LO + PAD_HI
    if parts == 2:
        half = shape((n * n // 2 + 2) * ROWS, LANES)
        outs = (half, half)
    else:
        outs = (shape(n * n * ROWS, LANES), shape(n * ROWS, LANES))
    outs = call(
        functools.partial(main_kernel, n, parts),
        outs,
        [SMEM] + [VMEM] * 7,
        [pltpu.VMEM((span * span * ROWS, LANES), F32)] * 6
        + [pltpu.VMEM((9 * wind_rows * ROWS, LANES), F32)]
        + [pltpu.VMEM(s.shape, F32) for s in (below_shape, below_shape, side_shape, side_shape)],
        flops=1 << 24,
    )(info, rate, steps, block, *from_y, *from_x)

    if parts == 2:
        send, keep = outs
        got = lax.ppermute(send, "gz", [(0, 1), (1, 0)])
        return call(
            functools.partial(breakup_kernel, n),
            (shape(nx, ny, nz, bins), shape(nx, ny // parts, bins)),
            [SMEM] + [VMEM] * 4,
            [pltpu.VMEM((n * n * ROWS, LANES), F32), pltpu.VMEM((256, pairs_rows), jnp.bfloat16)],
            flops=1 << 28,
        )(own, keep, got, pairs, lost)

    settled, rain = outs
    rain = rain.reshape(nx, ny, LANES)[:, :, :width]
    rain = lax.all_to_all(rain, "gz", split_axis=1, concat_axis=2, tiled=True)
    settled = settled.reshape(nx, ny, ROWS, parts, nz // ROWS, width).transpose(3, 0, 1, 4, 2, 5)
    settled = lax.all_to_all(settled, "gz", split_axis=0, concat_axis=0, tiled=True)
    settled = settled.transpose(1, 2, 3, 4, 0, 5).reshape(nx * ny, nz // ROWS, ROWS, bins)
    paired = settled.transpose(0, 2, 1, 3).reshape(-1, LANES)
    updated = call(
        breakup_plain_kernel,
        shape(n * n * ROWS, LANES),
        [VMEM] * 3,
        [pltpu.VMEM((256, pairs_rows), jnp.bfloat16)],
        flops=1 << 28,
    )(paired, pairs, lost)
    updated = updated.reshape(nx, ny, ROWS, nz // ROWS, bins).transpose(0, 1, 3, 2, 4).reshape(nx, ny, nz, bins)
    return updated, rain


def solution(mesh):
    in_specs = (P("gx", "gy", "gz", None), P(None, "gx", "gy", "gz"), P(), P(), P(), P())
    out_specs = (P("gx", "gy", "gz", None), P("gx", ("gy", "gz"), None))
    return jax.shard_map(per_device, mesh=mesh, in_specs=in_specs, out_specs=out_specs, check_vma=False)
```

```python
import functools

import jax
import jax.numpy as jnp
from jax import lax
from jax.experimental import pallas as pl
from jax.experimental.pallas import tpu as pltpu
from jax.sharding import PartitionSpec as P

SUBS = 24
EPS = 1e-06
LO, HI = 3, 2
PAD_LO, PAD_HI = 2 * LO, 2 * HI
LINES = LO + HI
ROWS, LANES = 8, 128
AHEAD = 4
F32 = jnp.float32
VMEM = pl.BlockSpec(memory_space=pltpu.VMEM)


def lane_ids():
    return lax.broadcasted_iota(jnp.int32, (ROWS, LANES), 1)


def pick(tile, ids):
    return jnp.take_along_axis(tile, ids, axis=1, mode="promise_in_bounds")


def turn(tile, lanes):
    lanes %= LANES
    return pltpu.roll(tile, lanes, 1) if lanes else tile


def rows_of(first, count=1):
    return pl.ds(first * ROWS, count * ROWS)


def eight(first, level, step=1):
    return pl.ds(first * ROWS + level, ROWS, stride=step * ROWS)


def order(a, b, straight):
    return jnp.where(straight, a, b), jnp.where(straight, b, a)


def is_even(axis):
    return lax.axis_index(axis) % 2 == 0


def by_quarter(parts):
    quarter = lane_ids() // (LANES // 4)
    return jnp.where(quarter < 2, jnp.where(quarter == 0, parts[0], parts[1]), jnp.where(quarter == 2, parts[2], parts[3]))


def groups(parts):
    width = LANES // (2 * parts)
    return width, width // ROWS, ROWS * ROWS // width


def spread(tile, x, y, parts):
    width, deep, _ = groups(parts)
    return pick(turn(tile, -(x % deep * ROWS + y)), lane_ids() // width * width)


def halo_line(i, n):
    return jnp.where(i < LO, i - LO, i - LO + n)


def line_change(cells, winds):
    first = [b - a for a, b in zip(cells, cells[1:])]
    twice = [d + d for d in first]
    second = [b - a for a, b in zip(first, first[1:])]
    third = [a - b for a, b in zip(second, second[1:])]
    curved = [(13.0 / 3.0) * (c * c) + 4.0 * EPS for c in second]
    fluxes = []
    for j in range(len(cells) - 4):
        left = twice[j + 1] + second[j]
        mid = first[j + 1] + first[j + 2]
        right = twice[j + 2] - second[j + 2]
        e0 = curved[j] + left * left
        e1 = curved[j + 1] + mid * mid
        e2 = curved[j + 2] + right * right
        e0 = e0 * e0
        e1 = e1 * e1
        e2 = e2 * e2
        e0 = 3.0 * e0
        e2_twice = e2 + e2
        top = e1 * (e2_twice * third[j] + e0 * third[j + 1])
        low = e1 * (e2 + e0) + e0 * e2_twice
        inverse = pl.reciprocal(low, approx=True)
        inverse = inverse * (2.0 - low * inverse)
        estimate = 6.0 * cells[j + 2] + (first[j + 1] + twice[j + 2]) + top * inverse
        fluxes.append((winds[j] + winds[j + 1]) * estimate)
    return [a - b for a, b in zip(fluxes, fluxes[1:])]


def from_below(value, width):
    return jnp.where(lane_ids() < width, 0.0, turn(value, width))


def from_above(value, width):
    return jnp.where(lane_ids() >= LANES - width, 0.0, turn(value, -width))


def level_change(cells, winds, width):
    long_cells = [from_below(v, width) for v in cells[ROWS - LO :]] + cells + [from_above(v, width) for v in cells[:HI]]
    long_winds = [from_below(winds[-1], width)] + winds + [from_above(winds[0], width)]
    return line_change(long_cells, long_winds)


def pack_kernel(mass_ref, wind_ref, send_ref, keep_ref):
    lower = is_even("gz")
    n = mass_ref.shape[0]
    zero = jnp.zeros((ROWS, LANES // 2), F32)
    for x in range(n // 2):
        for y in range(n):
            tiles = [
                jnp.concatenate([mass_ref[xx, y, z : z + ROWS], zero], axis=1) for xx in (x, x + n // 2) for z in (0, ROWS)
            ]
            low = by_quarter([turn(v, 32 * k) for k, v in enumerate(tiles)])
            high = by_quarter([turn(v, 32 * k - 32) for k, v in enumerate(tiles)])
            at = rows_of(x * n + y)
            keep_ref[at], send_ref[at] = order(low, high, lower)
    for d in range(3):
        levels = wind_ref[d].reshape(n * n, 2 * ROWS).T * (1.0 / 12.0)
        tile = jnp.concatenate([levels[:ROWS], levels[ROWS:]], axis=1)
        at = rows_of(n // 2 * n + d)
        send_ref[at] = tile
        keep_ref[at] = tile


def by_parity(axis, body):
    even = is_even(axis)
    pl.when(even)(lambda: body(0, 1))
    pl.when(jnp.logical_not(even))(lambda: body(1, 0))


def merge_kernel(keep_ref, got_ref, block_ref, *messages):
    n = 8
    lower = is_even("gz")
    low = lane_ids() < 64

    def body(up, down):
        up_ref, down_ref = messages[up], messages[down]
        for x in range(n // 2):
            for y in range(n):
                at = rows_of(x * n + y)
                a, b = order(keep_ref[at], got_ref[at], lower)
                for xx, tile in (
                    (x, jnp.where(low, a, turn(b, 64))),
                    (x + n // 2, jnp.where(low, turn(a, 64), b)),
                ):
                    block_ref[rows_of(xx * n + y)] = tile
                    if y >= n - PAD_LO:
                        up_ref[rows_of(xx * PAD_LO + y - (n - PAD_LO))] = tile
                    if y < PAD_HI:
                        down_ref[rows_of(xx * PAD_HI + y)] = tile
        for d in range(3):
            at = rows_of(n // 2 * n + d)
            a, b = order(keep_ref[at], got_ref[at], lower)
            for half, tile in enumerate(
                (
                    by_quarter([a, turn(a, -32), turn(b, 64), turn(b, 32)]),
                    by_quarter([turn(a, -32), turn(a, -64), turn(b, 32), b]),
                )
            ):
                for ref, base in ((block_ref, n * n), (up_ref, n * PAD_LO), (down_ref, n * PAD_HI)):
                    ref[rows_of(base + 2 * d + half)] = tile

    by_parity("gy", body)


def side_kernel(n, parts, block_ref, *refs):
    got, messages = refs[:2], refs[2:]
    tiles = groups(parts)[2]
    half = tiles // 2

    def body(above_ref, below_ref, up_ref, down_ref):
        for ref, start, wide, narrow_at, narrow, part in (
            (up_ref, n - PAD_LO, PAD_LO, n - LO, LO, half),
            (down_ref, 0, PAD_HI, 0, HI, 0),
        ):
            for x in range(wide):
                ref[rows_of(x * n, n)] = block_ref[rows_of((start + x) * n, n)]
            at = wide * n
            for x in range(narrow):
                xx = narrow_at + x
                ref[rows_of(at, LO)] = below_ref[rows_of(xx * PAD_LO + PAD_LO - LO, LO)]
                ref[rows_of(at + LO, HI)] = above_ref[rows_of(xx * PAD_HI, HI)]
                at += LINES
            for d in range(3):
                ref[rows_of(at, half)] = block_ref[rows_of(n * n + d * tiles + part, half)]
                at += half
            for side_ref, base in ((below_ref, n * PAD_LO), (above_ref, n * PAD_HI)):
                ref[rows_of(at)] = side_ref[rows_of(base + (tiles - 1 if part else 0))]
                ref[rows_of(at + 1, half)] = side_ref[rows_of(base + tiles + part, half)]
                at += 1 + half

    by_parity(
        "gy", lambda y_up, y_down: by_parity("gx", lambda up, down: body(got[y_up], got[y_down], messages[up], messages[down]))
    )


def own_kernel(n, parts, block_ref, wind_x, wind_y, wind_z, change):
    width, deep, tiles = groups(parts)
    for d, out in enumerate((wind_x, wind_y, wind_z)):
        for x in range(n):
            tile = block_ref[rows_of(n * n + d * tiles + x // deep)]
            for y in range(n):
                out[rows_of(x * n + y)] = spread(tile, x, y, parts)

    @pl.loop(0, n)
    def _(x):
        cells = [block_ref[eight(x * n, k)] for k in range(ROWS)]
        winds = [wind_z[eight(x * n, k)] for k in range(ROWS)]
        for k, value in enumerate(level_change(cells, winds, width)):
            change[eight(x * n, k)] = value


def y_kernel(n, parts, block_ref, first_ref, second_ref, wind_y, own_change, *refs):
    width, deep, tiles = groups(parts)
    cell, change, wind_x, far_y, wind_z, halo_change = refs
    even = is_even("gy")
    span, reach = n + PAD_LO + PAD_HI, n + LINES

    def below(at):
        return jnp.where(even, second_ref[at], first_ref[at])

    def above(at):
        return jnp.where(even, first_ref[at], second_ref[at])

    for x in range(n):
        cell[rows_of(x * span, PAD_LO)] = below(rows_of(x * PAD_LO, PAD_LO))
        cell[rows_of(x * span + PAD_LO, n)] = block_ref[rows_of(x * n, n)]
        cell[rows_of(x * span + PAD_LO + n, PAD_HI)] = above(rows_of(x * PAD_HI, PAD_HI))
    for d in range(3):
        for t in range(tiles):
            low, high = below(rows_of(n * PAD_LO + d * tiles + t)), above(rows_of(n * PAD_HI + d * tiles + t))
            for x in range(t * deep, (t + 1) * deep):
                if d == 1:
                    for y in range(LO + 1):
                        far_y[rows_of(x * (LINES + 2) + y)] = spread(low, x, n - LO - 1 + y, parts)
                    for y in range(HI + 1):
                        far_y[rows_of(x * (LINES + 2) + LO + 1 + y)] = spread(high, x, y, parts)
                else:
                    out = wind_z if d else wind_x
                    for y in range(LO):
                        out[rows_of(y * n + x)] = spread(low, x, n - LO + y, parts)
                    for y in range(HI):
                        out[rows_of((LO + y) * n + x)] = spread(high, x, y, parts)

    @pl.loop(0, LINES)
    def _(i):
        first = halo_line(i, n) + PAD_LO
        cells = [cell[eight(first, k, span)] for k in range(ROWS)]
        winds = [wind_z[eight(i * n, k)] for k in range(ROWS)]
        for k, value in enumerate(level_change(cells, winds, width)):
            halo_change[eight(i * n, k)] = value

    @pl.loop(0, n)
    def _(x):
        cells = [cell[rows_of(x * span + y)] for y in range(span)]
        far = [far_y[rows_of(x * (LINES + 2) + y)] for y in range(LINES + 2)]
        winds = far[: LO + 1] + [wind_y[rows_of(x * n + y)] for y in range(n)] + far[LO + 1 :]
        for y, value in enumerate(line_change(cells, winds)):
            if LO <= y < LO + n:
                value = value + own_change[rows_of(x * n + y - LO)]
            else:
                value = value + halo_change[rows_of((y if y < LO else y - n) * n + x)]
            change[rows_of(x * reach + y)] = value


def main_kernel(n, parts, *refs):
    cell, change, wind_x, wind_y, wind_z, halo_wind_x, far_wind_y, first_ref, second_ref, rate_ref, steps_ref = refs[:11]
    out_refs, scratch = refs[11:13], refs[13:]
    far, side, far_wind_x, corner_wind_x, side_wind_y, side_wind_z, side_change, one, change_two = scratch
    width, deep, tiles = groups(parts)
    half = tiles // 2
    even = is_even("gx")
    span, reach = n + PAD_LO + PAD_HI, n + LINES

    def west(at):
        return jnp.where(even, second_ref[at], first_ref[at])

    def east(at):
        return jnp.where(even, first_ref[at], second_ref[at])

    for take, wide, narrow, far_at, side_at, far_from, side_from in (
        (west, PAD_LO, LO, 0, 0, 0, LO),
        (east, PAD_HI, HI, LO, LO, HI, 0),
    ):
        for i in range(narrow):
            far[rows_of((far_at + i) * n, n)] = take(rows_of((far_from + i) * n, n))
            line = (side_at + i) * reach
            corner = wide * n + i * LINES
            side[rows_of(line, LO)] = take(rows_of(corner, LO))
            side[rows_of(line + LO, n)] = take(rows_of((side_from + i) * n, n))
            side[rows_of(line + LO + n, HI)] = take(rows_of(corner + LO, HI))
        at = wide * n + narrow * LINES
        layers = range(n - narrow, n) if narrow == LO else range(narrow)
        wider = range(n - narrow - 1, n) if narrow == LO else range(narrow + 1)
        shift = half if narrow == LO else 0

        def winds_of(base, x):
            return take(rows_of(base + x // deep - shift))

        for i, x in enumerate(wider):
            tile = winds_of(at, x)
            for y in range(n):
                far_wind_x[rows_of((far_at + bool(far_at) + i) * n + y)] = spread(tile, x, y, parts)
        below, above = at + 3 * half, at + 3 * half + 1 + half
        x = wider[-1] if narrow == LO else wider[0]
        for y in range(LINES):
            tile = take(rows_of(below if y < LO else above))
            corner_wind_x[rows_of(bool(far_at) * LINES + y)] = spread(tile, x, n - LO + y if y < LO else y - LO, parts)
        for i, x in enumerate(layers):
            line = (side_at + i) * (n + 2)
            side_wind_y[rows_of(line)] = spread(winds_of(below + 1, x), x, n - 1, parts)
            side_wind_y[rows_of(line + n + 1)] = spread(winds_of(above + 1, x), x, 0, parts)
            for y in range(n):
                side_wind_y[rows_of(line + 1 + y)] = spread(winds_of(at + half, x), x, y, parts)
                side_wind_z[rows_of((side_at + i) * n + y)] = spread(winds_of(at + 2 * half, x), x, y, parts)

    @pl.loop(0, LINES)
    def _(i):
        cells = [side[eight(i * reach + LO, k)] for k in range(ROWS)]
        winds = [side_wind_z[eight(i * n, k)] for k in range(ROWS)]
        for k, value in enumerate(level_change(cells, winds, width)):
            side_change[eight(i * n, k)] = value

    @pl.loop(0, LINES)
    def _(i):
        cells = [side[rows_of(i * reach + y)] for y in range(reach)]
        winds = [side_wind_y[rows_of(i * (n + 2) + y)] for y in range(n + 2)]
        for y, value in enumerate(line_change(cells, winds)):
            at = rows_of(i * n + y)
            side_change[at] = side_change[at] + value

    last = lax.axis_size("gx") - 1, lax.axis_size("gy") - 1

    def inside(axis, count, lower):
        place = lax.axis_index(axis)
        return jnp.where(place > 0 if lower else place < count, 1.0, 0.0)

    west_in, east_in = inside("gx", last[0], True), inside("gx", last[0], False)
    south_in, north_in = inside("gy", last[1], True), inside("gy", last[1], False)

    @pl.loop(0, n)
    def _(y):
        outer = [far[rows_of(i * n + y)] for i in range(LINES)]
        near = [side[rows_of(i * reach + LO + y)] for i in range(LINES)]
        cells = outer[:LO] + near[:LO] + [cell[rows_of(x * span + PAD_LO + y)] for x in range(n)] + near[LO:] + outer[LO:]
        winds = [far_wind_x[rows_of(i * n + y)] for i in range(LINES + 2)]
        winds = winds[: LO + 1] + [wind_x[rows_of(x * n + y)] for x in range(n)] + winds[LO + 1 :]
        for i, value in enumerate(line_change(cells, winds)):
            if LO <= i < LO + n:
                value = cells[i + LO] + (value + change[rows_of((i - LO) * reach + LO + y)])
            else:
                value = cells[i + LO] + (value + side_change[rows_of((i if i < LO else i - n) * n + y)])
                value = value * (west_in if i < LO else east_in)
            one[rows_of(i * reach + LO + y)] = value

    @pl.loop(0, LINES)
    def _(i):
        line = halo_line(i, n) + LO
        near = [side[rows_of(k * reach + line)] for k in range(LINES)]
        cells = near[:LO] + [cell[rows_of(x * span + LO + line)] for x in range(n)] + near[LO:]
        winds = [halo_wind_x[rows_of(i * n + x)] for x in range(n)]
        winds = [corner_wind_x[rows_of(i)]] + winds + [corner_wind_x[rows_of(LINES + i)]]
        keep = jnp.where(i < LO, south_in, north_in)
        for x, value in enumerate(line_change(cells, winds)):
            one[rows_of((x + LO) * reach + line)] = (cells[x + LO] + (value + change[rows_of(x * reach + line)])) * keep

    @pl.loop(0, n)
    def _(y):
        cells = [one[rows_of(x * reach + LO + y)] for x in range(reach)]
        winds = [far_wind_x[rows_of(LO * n + y)]] + [wind_x[rows_of(x * n + y)] for x in range(n)]
        winds += [far_wind_x[rows_of((LO + 1) * n + y)]]
        for x, value in enumerate(line_change(cells, winds)):
            change_two[rows_of(x * n + y)] = value

    @pl.loop(0, n)
    def _(x):
        cells = [one[rows_of((x + LO) * reach + y)] for y in range(reach)]
        winds = [far_wind_y[rows_of(x * (LINES + 2) + LO)]] + [wind_y[rows_of(x * n + y)] for y in range(n)]
        winds += [far_wind_y[rows_of(x * (LINES + 2) + LO + 1)]]
        for y, value in enumerate(line_change(cells, winds)):
            at = rows_of(x * n + y)
            change_two[at] = change_two[at] + value

    @pl.loop(0, n)
    def _(x):
        cells = [one[eight((x + LO) * reach + LO, k)] for k in range(ROWS)]
        winds = [wind_z[eight(x * n, k)] for k in range(ROWS)]
        for k, value in enumerate(level_change(cells, winds, width)):
            at = eight(x * n, k)
            change_two[at] = 0.5 * cell[eight(x * span + PAD_LO, k)] + 0.5 * (cells[k] + (value + change_two[at]))

    rates = jnp.broadcast_to(rate_ref[...], (ROWS, LANES))
    steps = jnp.broadcast_to(steps_ref[...], (ROWS, LANES))
    together = 4
    rains = []
    for begin in range(0, n, together):
        xs = range(begin, begin + together)

        def fall(block, carry):
            columns, rain = carry
            columns = [column + [from_above(v, width) for v in column[:AHEAD]] for column in columns]
            rain = list(rain)
            for s in range(AHEAD):
                rate = jnp.where(block * AHEAD + s < steps, rates, 0.0)
                for i, column in enumerate(columns):
                    rain[i] = rain[i] + rate * column[0]
                    columns[i] = [v + rate * (u - v) for v, u in zip(column, column[1:])]
            return columns, rain

        columns = [[change_two[eight(x * n, k)] for k in range(ROWS)] for x in xs]
        columns, rain = lax.fori_loop(0, SUBS // AHEAD, fall, (columns, [jnp.zeros((ROWS, LANES), F32)] * together))
        for x, column in zip(xs, columns):
            for k in range(ROWS):
                change_two[eight(x * n, k)] = column[k]
        rains += rain

    if parts == 2:
        send_ref, keep_ref = out_refs
        lower = is_even("gz")
        low = lane_ids() < 64
        for x in range(n // 2):
            for y in range(n):
                a, b = change_two[rows_of(x * n + y)], change_two[rows_of((x + n // 2) * n + y)]
                at = rows_of(x * n + y)
                keep_ref[at], send_ref[at] = order(jnp.where(low, a, turn(b, 64)), jnp.where(low, turn(a, 64), b), lower)
        for j in range(2):
            value = by_quarter([turn(rains[4 * j + i], 32 * i) for i in range(4)])
            keep_ref[rows_of(n // 2 * n + j)] = value
            send_ref[rows_of(n // 2 * n + j)] = value
    else:
        settled_ref, rain_ref = out_refs
        settled_ref[...] = change_two[...]
        for x in range(n):
            rain_ref[rows_of(x)] = rains[x]


def matrix_kernel(bins, gain_ref, loss_ref, pairs_ref, lost_ref, wide, tall):
    zero = jnp.zeros((bins, LANES - bins), F32)
    shifts = bins // 2

    @pl.loop(0, bins)
    def _(i):
        rows = gain_ref[pl.ds(i * bins, bins)].astype(F32)
        rows = jnp.concatenate([rows, zero], axis=1)
        wide[pl.ds(i * 2 * bins, bins)] = rows
        wide[pl.ds(i * 2 * bins + bins, bins)] = rows
        tall[pl.ds(i * bins, bins)] = rows

        @pl.when(i < shifts)
        def _():
            tall[pl.ds((i + bins) * bins, bins)] = rows

    for d in range(shifts + 1):
        rows = wide[pl.ds(d, bins, stride=2 * bins + 1)]
        if 0 < d < shifts:
            rows = rows + tall[pl.ds(d * bins, bins, stride=bins + 1)]
        pairs_ref[pl.ds(d * LANES, bins)] = rows.astype(jnp.bfloat16)
        pairs_ref[pl.ds(d * LANES + bins, bins)] = pltpu.roll(rows, bins, 1).astype(jnp.bfloat16)
    rows = jnp.concatenate([loss_ref[...].astype(F32), zero], axis=1)
    lost_ref[pl.ds(0, bins)] = rows.astype(jnp.bfloat16)
    lost_ref[pl.ds(bins, bins)] = pltpu.roll(rows, bins, 1).astype(jnp.bfloat16)


def breakup_rows(mass, pairs_ref, lost_ref, products):
    bins = LANES // 2
    count = mass.shape[0]
    lanes = lane_ids()
    rounded = mass.astype(jnp.bfloat16)
    wide = rounded.astype(F32)
    for d in range(bins // 2 + 1):
        ids = lanes // bins * bins + (lanes + d) % bins
        for r in range(0, count, 2 * ROWS):
            halves = [wide[r + ROWS * k : r + ROWS * (k + 1)] for k in range(2)]
            halves = [v * pick(v, ids) if d else v * v for v in halves]
            products[pl.ds(r, 2 * ROWS), d * LANES : (d + 1) * LANES] = jnp.concatenate(halves, axis=0).astype(jnp.bfloat16)
    gained = jnp.dot(products[pl.ds(0, count)], pairs_ref[...], preferred_element_type=F32)
    loss = jnp.dot(rounded, lost_ref[...], preferred_element_type=F32)
    return mass + gained - mass * loss


def breakup_kernel(n, keep_ref, got_ref, pairs_ref, lost_ref, mass_ref, rain_ref, columns, products):
    first = is_even("gz")
    half = n // 2
    for x in range(half):
        for y in range(n):
            at = rows_of(x * n + y)
            a, b = order(keep_ref[at], got_ref[at], first)
            columns[rows_of(x * n + y)] = by_quarter([a, turn(b, 32), turn(a, 32), turn(b, 64)])
            columns[rows_of((x + half) * n + y)] = by_quarter([turn(a, -64), turn(b, -32), turn(a, -32), b])
    for j in range(2):
        at = rows_of(half * n + j)
        a, b = order(keep_ref[at], got_ref[at], first)
        a, b = [jnp.where(first, v[: n // 2], v[n // 2 :]) for v in (a, b)]
        for i in range(4):
            rain_ref[4 * j + i] = jnp.concatenate([a[:, 32 * i : 32 * i + 32], b[:, 32 * i : 32 * i + 32]], axis=1)

    count = products.shape[0]

    @pl.loop(0, n * n * ROWS // count)
    def _(i):
        start = pl.multiple_of(i * count, count)
        mass = columns[pl.ds(start, count)]
        columns[pl.ds(start, count)] = breakup_rows(mass, pairs_ref, lost_ref, products)

    for x in range(n):
        for y in range(n):
            value = columns[rows_of(x * n + y)]
            mass_ref[x, y, 0:ROWS] = value[:, :64]
            mass_ref[x, y, ROWS : 2 * ROWS] = value[:, 64:]


def breakup_plain_kernel(mass_ref, pairs_ref, lost_ref, out_ref, products):
    count = products.shape[0]

    @pl.loop(0, mass_ref.shape[0] // count)
    def _(i):
        start = pl.multiple_of(i * count, count)
        out_ref[pl.ds(start, count)] = breakup_rows(mass_ref[pl.ds(start, count)], pairs_ref, lost_ref, products)


def shape(*dims, dtype=F32):
    return jax.ShapeDtypeStruct(dims, dtype)


def tiles_of(count):
    return shape(count * ROWS, LANES)


def call(kernel, outs, args, scratch=(), flops=1 << 22):
    return pl.pallas_call(
        kernel,
        out_shape=outs,
        in_specs=[VMEM] * len(args),
        out_specs=jax.tree.map(lambda _: VMEM, outs),
        scratch_shapes=[pltpu.VMEM(s.shape, s.dtype) for s in scratch],
        compiler_params=pltpu.CompilerParams(vmem_limit_bytes=40 << 20),
        cost_estimate=pl.CostEstimate(flops=flops, bytes_accessed=1 << 20, transcendentals=0),
    )(*args)


def swap_neighbours(axis, first, second, order_of=(0, 1)):
    count = lax.axis_size(axis)
    got = {}
    for begin in order_of:
        pairs = [(i, i + 1) for i in range(begin, count - 1, 2)]
        got[begin] = lax.ppermute((first, second)[begin], axis, pairs + [(b, a) for a, b in pairs])
    return got[0], got[1]


def per_device(bin_mass, courant, sub_courant, fall_steps, frag_gain, collide):
    nx, ny, nz, bins = bin_mass.shape
    n = nx
    parts = lax.axis_size("gz")
    gz, gy = lax.axis_index("gz"), lax.axis_index("gy")
    width = bins // parts
    tiles = groups(parts)[2]
    winds = 3 * tiles

    pair_rows = (bins // 2 + 1) * LANES
    pairs, lost = call(
        functools.partial(matrix_kernel, bins),
        (shape(pair_rows, LANES, dtype=jnp.bfloat16), shape(LANES, LANES, dtype=jnp.bfloat16)),
        (frag_gain, collide),
        [shape(2 * bins * bins, LANES), shape(3 * bins * bins // 2, LANES)],
    )

    if parts == 2:
        half = tiles_of(n * n // 2 + 3)
        send, keep = call(pack_kernel, (half, half), (bin_mass, courant))
        got = lax.ppermute(send, "gz", [(0, 1), (1, 0)])
        message = tiles_of(n * PAD_LO + winds)
        block, first, second = call(merge_kernel, (tiles_of(n * n + winds), message, message), (keep, got))
    else:
        split = bin_mass.reshape(nx, ny, nz // ROWS, ROWS, parts, width).transpose(4, 0, 1, 3, 2, 5)
        split = lax.all_to_all(split, "gz", split_axis=0, concat_axis=0, tiled=True)
        cube = split.transpose(1, 2, 3, 0, 4, 5).reshape(n, n, ROWS, LANES)
        air = courant.reshape(3, nx, ny, nz // ROWS, ROWS).transpose(0, 4, 3, 1, 2) * (1.0 / 12.0)
        air = lax.all_gather(air, "gz").reshape(parts, 3, ROWS, nz // ROWS, tiles, nx // tiles, ny)
        air = air.transpose(1, 4, 2, 0, 3, 5, 6).reshape(-1, LANES)
        block = jnp.concatenate([cube.reshape(-1, LANES), air])
        up = jnp.concatenate([cube[:, n - PAD_LO :].reshape(-1, LANES), air])
        down = jnp.concatenate([cube[:, :PAD_HI].reshape(-1, LANES), air])
        down = jnp.pad(down, ((0, up.shape[0] - down.shape[0]), (0, 0)))
        first, second = order(up, down, gy % 2 == 0)

    from_y = swap_neighbours("gy", first, second)
    wind_x, wind_y, wind_z, own_change = call(
        functools.partial(own_kernel, n, parts), [tiles_of(n * n)] * 4, (block,), flops=1 << 23
    )
    message = tiles_of(PAD_LO * n + LO * LINES + 3 * tiles // 2 + 2 + tiles)
    first, second = call(functools.partial(side_kernel, n, parts), (message, message), (block, *from_y))
    from_x = swap_neighbours("gx", first, second, (1, 0))
    cell, change, halo_wind_x, far_wind_y = call(
        functools.partial(y_kernel, n, parts),
        [tiles_of(n * (n + PAD_LO + PAD_HI)), tiles_of(n * (n + LINES)), tiles_of(LINES * n), tiles_of(n * (LINES + 2))],
        (block, *from_y, wind_y, own_change),
        [tiles_of(LINES * n)] * 2,
        flops=1 << 24,
    )
    rate = jnp.tile(lax.dynamic_slice(sub_courant, (gz * width,), (width,)), 2 * parts).reshape(1, LANES)
    steps = jnp.tile(lax.dynamic_slice(fall_steps, (gz * width,), (width,)), 2 * parts).reshape(1, LANES)
    reach = n + LINES
    outs = call(
        functools.partial(main_kernel, n, parts),
        [tiles_of(n * n // 2 + 2)] * 2 if parts == 2 else [tiles_of(n * n), tiles_of(n)],
        (cell, change, wind_x, wind_y, wind_z, halo_wind_x, far_wind_y, *from_x, rate, steps),
        [
            tiles_of(count)
            for count in (
                LINES * n,
                LINES * reach,
                (LINES + 2) * n,
                2 * LINES,
                LINES * (n + 2),
                LINES * n,
                LINES * n,
                reach * reach,
                n * n,
            )
        ],
        flops=1 << 25,
    )

    products = shape(256, pair_rows, dtype=jnp.bfloat16)
    if parts == 2:
        send, keep = outs
        got = lax.ppermute(send, "gz", [(0, 1), (1, 0)])
        return tuple(
            call(
                functools.partial(breakup_kernel, n),
                [shape(nx, ny, nz, bins), shape(nx, ny // parts, bins)],
                (keep, got, pairs, lost),
                [tiles_of(n * n), products],
                flops=1 << 28,
            )
        )

    settled, rain = outs
    rain = rain.reshape(nx, ny, LANES)[:, :, :width]
    rain = lax.all_to_all(rain, "gz", split_axis=1, concat_axis=2, tiled=True)
    settled = settled.reshape(nx, ny, ROWS, parts, nz // ROWS, width).transpose(3, 0, 1, 4, 2, 5)
    settled = lax.all_to_all(settled, "gz", split_axis=0, concat_axis=0, tiled=True)
    settled = settled.transpose(1, 2, 3, 4, 0, 5).reshape(nx * ny, nz // ROWS, ROWS, bins)
    paired = settled.transpose(0, 2, 1, 3).reshape(-1, LANES)
    updated = call(breakup_plain_kernel, tiles_of(n * n), (paired, pairs, lost), [products], flops=1 << 28)
    updated = updated.reshape(nx, ny, ROWS, nz // ROWS, bins).transpose(0, 1, 3, 2, 4).reshape(nx, ny, nz, bins)
    return updated, rain


def solution(mesh):
    in_specs = (P("gx", "gy", "gz", None), P(None, "gx", "gy", "gz"), P(), P(), P(), P())
    out_specs = (P("gx", "gy", "gz", None), P("gx", ("gy", "gz"), None))
    return jax.shard_map(per_device, mesh=mesh, in_specs=in_specs, out_specs=out_specs, check_vma=False)
```

```python
import functools

import jax
import jax.numpy as jnp
from jax import lax
from jax.experimental import pallas as pl
from jax.experimental.pallas import tpu as pltpu
from jax.sharding import PartitionSpec as P

SUBS = 24
EPS = 1e-06
LO, HI = 3, 2
PAD_LO, PAD_HI = 2 * LO, 2 * HI
LINES = LO + HI
ROWS, LANES = 8, 128
AHEAD = 4
F32 = jnp.float32
VMEM = pl.BlockSpec(memory_space=pltpu.VMEM)


def lane_ids():
    return lax.broadcasted_iota(jnp.int32, (ROWS, LANES), 1)


def pick(tile, ids):
    return jnp.take_along_axis(tile, ids, axis=1, mode="promise_in_bounds")


def turn(tile, lanes):
    lanes %= LANES
    return pltpu.roll(tile, lanes, 1) if lanes else tile


def rows_of(first, count=1):
    return pl.ds(first * ROWS, count * ROWS)


def eight(first, level, step=1):
    return pl.ds(first * ROWS + level, ROWS, stride=step * ROWS)


def order(a, b, straight):
    return jnp.where(straight, a, b), jnp.where(straight, b, a)


def is_even(axis):
    return lax.axis_index(axis) % 2 == 0


def by_quarter(parts):
    quarter = lane_ids() // (LANES // 4)
    return jnp.where(quarter < 2, jnp.where(quarter == 0, parts[0], parts[1]), jnp.where(quarter == 2, parts[2], parts[3]))


def groups(parts):
    width = LANES // (2 * parts)
    return width, width // ROWS, ROWS * ROWS // width


def spread(tile, x, y, parts):
    width, deep, _ = groups(parts)
    return pick(turn(tile, -(x % deep * ROWS + y)), lane_ids() // width * width)


def halo_line(i, n):
    return jnp.where(i < LO, i - LO, i - LO + n)


def line_change(cells, winds):
    first = [b - a for a, b in zip(cells, cells[1:])]
    twice = [d + d for d in first]
    second = [b - a for a, b in zip(first, first[1:])]
    third = [a - b for a, b in zip(second, second[1:])]
    curved = [(13.0 / 3.0) * (c * c) + 4.0 * EPS for c in second]
    fluxes = []
    for j in range(len(cells) - 4):
        left = twice[j + 1] + second[j]
        mid = first[j + 1] + first[j + 2]
        right = twice[j + 2] - second[j + 2]
        e0 = curved[j] + left * left
        e1 = curved[j + 1] + mid * mid
        e2 = curved[j + 2] + right * right
        e0 = e0 * e0
        e1 = e1 * e1
        e2 = e2 * e2
        e0 = 3.0 * e0
        e2_twice = e2 + e2
        top = e1 * (e2_twice * third[j] + e0 * third[j + 1])
        low = e1 * (e2 + e0) + e0 * e2_twice
        inverse = pl.reciprocal(low, approx=True)
        inverse = inverse * (2.0 - low * inverse)
        estimate = 6.0 * cells[j + 2] + (first[j + 1] + twice[j + 2]) + top * inverse
        fluxes.append((winds[j] + winds[j + 1]) * estimate)
    return [a - b for a, b in zip(fluxes, fluxes[1:])]


def from_below(value, width):
    return jnp.where(lane_ids() < width, 0.0, turn(value, width))


def from_above(value, width):
    return jnp.where(lane_ids() >= LANES - width, 0.0, turn(value, -width))


def level_change(cells, winds, width):
    long_cells = [from_below(v, width) for v in cells[ROWS - LO :]] + cells + [from_above(v, width) for v in cells[:HI]]
    long_winds = [from_below(winds[-1], width)] + winds + [from_above(winds[0], width)]
    return line_change(long_cells, long_winds)


def pack_kernel(mass_hbm, wind_hbm, send_ref, keep_ref, mass_ref, wind_ref, mass_sem, wind_sem):
    mass_copy = pltpu.make_async_copy(mass_hbm, mass_ref, mass_sem)
    wind_copy = pltpu.make_async_copy(wind_hbm, wind_ref, wind_sem)
    mass_copy.start()
    wind_copy.start()
    lower = is_even("gz")
    n = mass_ref.shape[0]
    wind_copy.wait()
    for d in range(3):
        levels = wind_ref[d].reshape(n * n, 2 * ROWS).T * (1.0 / 12.0)
        tile = jnp.concatenate([levels[:ROWS], levels[ROWS:]], axis=1)
        at = rows_of(n // 2 * n + d)
        send_ref[at] = tile
        keep_ref[at] = tile
    mass_copy.wait()
    zero = jnp.zeros((ROWS, LANES // 2), F32)
    for x in range(n // 2):
        for y in range(n):
            tiles = [
                jnp.concatenate([mass_ref[xx, y, z : z + ROWS], zero], axis=1) for xx in (x, x + n // 2) for z in (0, ROWS)
            ]
            low = by_quarter([turn(v, 32 * k) for k, v in enumerate(tiles)])
            high = by_quarter([turn(v, 32 * k - 32) for k, v in enumerate(tiles)])
            at = rows_of(x * n + y)
            keep_ref[at], send_ref[at] = order(low, high, lower)


def sides(axis, first_ref, second_ref):
    even, place = is_even(axis), lax.axis_index(axis)
    inner_low, inner_high = place > 0, place < lax.axis_size(axis) - 1

    def below(at):
        return jnp.where(inner_low, jnp.where(even, second_ref[at], first_ref[at]), 0.0)

    def above(at):
        return jnp.where(inner_high, jnp.where(even, first_ref[at], second_ref[at]), 0.0)

    return below, above


def by_parity(axis, body):
    even = is_even(axis)
    pl.when(even)(lambda: body(0, 1))
    pl.when(jnp.logical_not(even))(lambda: body(1, 0))


def merge_kernel(keep_ref, got_ref, block_ref, *messages):
    n = 8
    lower = is_even("gz")
    low = lane_ids() < 64

    def body(up, down):
        up_ref, down_ref = messages[up], messages[down]
        for x in range(n // 2):
            for y in range(n):
                at = rows_of(x * n + y)
                a, b = order(keep_ref[at], got_ref[at], lower)
                for xx, tile in (
                    (x, jnp.where(low, a, turn(b, 64))),
                    (x + n // 2, jnp.where(low, turn(a, 64), b)),
                ):
                    block_ref[rows_of(xx * n + y)] = tile
                    if y >= n - PAD_LO:
                        up_ref[rows_of(xx * PAD_LO + y - (n - PAD_LO))] = tile
                    if y < PAD_HI:
                        down_ref[rows_of(xx * PAD_HI + y)] = tile
        for d in range(3):
            at = rows_of(n // 2 * n + d)
            a, b = order(keep_ref[at], got_ref[at], lower)
            for half, tile in enumerate(
                (
                    by_quarter([a, turn(a, -32), turn(b, 64), turn(b, 32)]),
                    by_quarter([turn(a, -32), turn(a, -64), turn(b, 32), b]),
                )
            ):
                for ref, base in ((block_ref, n * n), (up_ref, n * PAD_LO), (down_ref, n * PAD_HI)):
                    ref[rows_of(base + 2 * d + half)] = tile

    by_parity("gy", body)


def side_kernel(n, parts, block_ref, first_ref, second_ref, own_change, *messages):
    del own_change
    tiles = groups(parts)[2]
    half = tiles // 2
    below, above = sides("gy", first_ref, second_ref)

    def body(up, down):
        for ref, start, wide, narrow_at, narrow, part in (
            (messages[up], n - PAD_LO, PAD_LO, n - LO, LO, half),
            (messages[down], 0, PAD_HI, 0, HI, 0),
        ):
            for x in range(wide):
                ref[rows_of(x * n, n)] = block_ref[rows_of((start + x) * n, n)]
            at = wide * n
            for x in range(narrow):
                xx = narrow_at + x
                ref[rows_of(at, LO)] = below(rows_of(xx * PAD_LO + PAD_LO - LO, LO))
                ref[rows_of(at + LO, HI)] = above(rows_of(xx * PAD_HI, HI))
                at += LINES
            for d in range(3):
                ref[rows_of(at, half)] = block_ref[rows_of(n * n + d * tiles + part, half)]
                at += half
            for side, base in ((below, n * PAD_LO), (above, n * PAD_HI)):
                ref[rows_of(at)] = side(rows_of(base + (tiles - 1 if part else 0)))
                ref[rows_of(at + 1, half)] = side(rows_of(base + tiles + part, half))
                at += 1 + half

    by_parity("gx", body)


def own_kernel(n, parts, block_ref, wind_x, wind_y, wind_z, change):
    width, deep, tiles = groups(parts)
    for d, out in enumerate((wind_x, wind_y, wind_z)):
        for x in range(n):
            tile = block_ref[rows_of(n * n + d * tiles + x // deep)]
            for y in range(n):
                out[rows_of(x * n + y)] = spread(tile, x, y, parts)

    @pl.loop(0, n)
    def _(x):
        cells = [block_ref[eight(x * n, k)] for k in range(ROWS)]
        winds = [wind_z[eight(x * n, k)] for k in range(ROWS)]
        for k, value in enumerate(level_change(cells, winds, width)):
            change[eight(x * n, k)] = value


def y_kernel(n, parts, block_ref, first_ref, second_ref, wind_y, own_change, *refs):
    width, deep, tiles = groups(parts)
    cell, change, wind_x, far_y, wind_z, halo_change = refs
    below, above = sides("gy", first_ref, second_ref)
    span, reach = n + PAD_LO + PAD_HI, n + LINES

    for x in range(n):
        cell[rows_of(x * span, PAD_LO)] = below(rows_of(x * PAD_LO, PAD_LO))
        cell[rows_of(x * span + PAD_LO, n)] = block_ref[rows_of(x * n, n)]
        cell[rows_of(x * span + PAD_LO + n, PAD_HI)] = above(rows_of(x * PAD_HI, PAD_HI))
    for d in range(3):
        for t in range(tiles):
            low, high = below(rows_of(n * PAD_LO + d * tiles + t)), above(rows_of(n * PAD_HI + d * tiles + t))
            for x in range(t * deep, (t + 1) * deep):
                if d == 1:
                    for y in range(LO + 1):
                        far_y[rows_of(x * (LINES + 2) + y)] = spread(low, x, n - LO - 1 + y, parts)
                    for y in range(HI + 1):
                        far_y[rows_of(x * (LINES + 2) + LO + 1 + y)] = spread(high, x, y, parts)
                else:
                    out = wind_z if d else wind_x
                    for y in range(LO):
                        out[rows_of(y * n + x)] = spread(low, x, n - LO + y, parts)
                    for y in range(HI):
                        out[rows_of((LO + y) * n + x)] = spread(high, x, y, parts)

    @pl.loop(0, LINES)
    def _(i):
        first = halo_line(i, n) + PAD_LO
        cells = [cell[eight(first, k, span)] for k in range(ROWS)]
        winds = [wind_z[eight(i * n, k)] for k in range(ROWS)]
        for k, value in enumerate(level_change(cells, winds, width)):
            halo_change[eight(i * n, k)] = value

    @pl.loop(0, n)
    def _(x):
        cells = [cell[rows_of(x * span + y)] for y in range(span)]
        far = [far_y[rows_of(x * (LINES + 2) + y)] for y in range(LINES + 2)]
        winds = far[: LO + 1] + [wind_y[rows_of(x * n + y)] for y in range(n)] + far[LO + 1 :]
        for y, value in enumerate(line_change(cells, winds)):
            if LO <= y < LO + n:
                value = value + own_change[rows_of(x * n + y - LO)]
            else:
                value = value + halo_change[rows_of((y if y < LO else y - n) * n + x)]
            change[rows_of(x * reach + y)] = value


def hand_on_kernel(held_ref, got_ref, message_ref):
    del got_ref
    message_ref[...] = held_ref[...]


def main_kernel(n, parts, *refs):
    cell, change, wind_x, wind_y, wind_z, halo_wind_x, far_wind_y, first_ref, second_ref, rate_ref, steps_ref = refs[:11]
    out_refs, scratch = refs[11:13], refs[13:]
    far, side, far_wind_x, corner_wind_x, side_wind_y, side_wind_z, side_change, one, change_two = scratch
    width, deep, tiles = groups(parts)
    half = tiles // 2
    west, east = sides("gx", first_ref, second_ref)
    span, reach = n + PAD_LO + PAD_HI, n + LINES

    for take, wide, narrow, far_at, side_at, far_from, side_from in (
        (west, PAD_LO, LO, 0, 0, 0, LO),
        (east, PAD_HI, HI, LO, LO, HI, 0),
    ):
        for i in range(narrow):
            far[rows_of((far_at + i) * n, n)] = take(rows_of((far_from + i) * n, n))
            line = (side_at + i) * reach
            corner = wide * n + i * LINES
            side[rows_of(line, LO)] = take(rows_of(corner, LO))
            side[rows_of(line + LO, n)] = take(rows_of((side_from + i) * n, n))
            side[rows_of(line + LO + n, HI)] = take(rows_of(corner + LO, HI))
        at = wide * n + narrow * LINES
        layers = range(n - narrow, n) if narrow == LO else range(narrow)
        wider = range(n - narrow - 1, n) if narrow == LO else range(narrow + 1)
        shift = half if narrow == LO else 0

        def winds_of(base, x):
            return take(rows_of(base + x // deep - shift))

        for i, x in enumerate(wider):
            tile = winds_of(at, x)
            for y in range(n):
                far_wind_x[rows_of((far_at + bool(far_at) + i) * n + y)] = spread(tile, x, y, parts)
        below, above = at + 3 * half, at + 3 * half + 1 + half
        x = wider[-1] if narrow == LO else wider[0]
        for y in range(LINES):
            tile = take(rows_of(below if y < LO else above))
            corner_wind_x[rows_of(bool(far_at) * LINES + y)] = spread(tile, x, n - LO + y if y < LO else y - LO, parts)
        for i, x in enumerate(layers):
            line = (side_at + i) * (n + 2)
            side_wind_y[rows_of(line)] = spread(winds_of(below + 1, x), x, n - 1, parts)
            side_wind_y[rows_of(line + n + 1)] = spread(winds_of(above + 1, x), x, 0, parts)
            for y in range(n):
                side_wind_y[rows_of(line + 1 + y)] = spread(winds_of(at + half, x), x, y, parts)
                side_wind_z[rows_of((side_at + i) * n + y)] = spread(winds_of(at + 2 * half, x), x, y, parts)

    @pl.loop(0, LINES)
    def _(i):
        cells = [side[eight(i * reach + LO, k)] for k in range(ROWS)]
        winds = [side_wind_z[eight(i * n, k)] for k in range(ROWS)]
        for k, value in enumerate(level_change(cells, winds, width)):
            side_change[eight(i * n, k)] = value

    @pl.loop(0, LINES)
    def _(i):
        cells = [side[rows_of(i * reach + y)] for y in range(reach)]
        winds = [side_wind_y[rows_of(i * (n + 2) + y)] for y in range(n + 2)]
        for y, value in enumerate(line_change(cells, winds)):
            at = rows_of(i * n + y)
            side_change[at] = side_change[at] + value

    last = lax.axis_size("gx") - 1, lax.axis_size("gy") - 1

    def inside(axis, count, lower):
        place = lax.axis_index(axis)
        return jnp.where(place > 0 if lower else place < count, 1.0, 0.0)

    west_in, east_in = inside("gx", last[0], True), inside("gx", last[0], False)
    south_in, north_in = inside("gy", last[1], True), inside("gy", last[1], False)

    @pl.loop(0, n)
    def _(y):
        outer = [far[rows_of(i * n + y)] for i in range(LINES)]
        near = [side[rows_of(i * reach + LO + y)] for i in range(LINES)]
        cells = outer[:LO] + near[:LO] + [cell[rows_of(x * span + PAD_LO + y)] for x in range(n)] + near[LO:] + outer[LO:]
        winds = [far_wind_x[rows_of(i * n + y)] for i in range(LINES + 2)]
        winds = winds[: LO + 1] + [wind_x[rows_of(x * n + y)] for x in range(n)] + winds[LO + 1 :]
        for i, value in enumerate(line_change(cells, winds)):
            if LO <= i < LO + n:
                value = cells[i + LO] + (value + change[rows_of((i - LO) * reach + LO + y)])
            else:
                value = cells[i + LO] + (value + side_change[rows_of((i if i < LO else i - n) * n + y)])
                value = value * (west_in if i < LO else east_in)
            one[rows_of(i * reach + LO + y)] = value

    @pl.loop(0, LINES)
    def _(i):
        line = halo_line(i, n) + LO
        near = [side[rows_of(k * reach + line)] for k in range(LINES)]
        cells = near[:LO] + [cell[rows_of(x * span + LO + line)] for x in range(n)] + near[LO:]
        winds = [halo_wind_x[rows_of(i * n + x)] for x in range(n)]
        winds = [corner_wind_x[rows_of(i)]] + winds + [corner_wind_x[rows_of(LINES + i)]]
        keep = jnp.where(i < LO, south_in, north_in)
        for x, value in enumerate(line_change(cells, winds)):
            one[rows_of((x + LO) * reach + line)] = (cells[x + LO] + (value + change[rows_of(x * reach + line)])) * keep

    @pl.loop(0, n)
    def _(y):
        cells = [one[rows_of(x * reach + LO + y)] for x in range(reach)]
        winds = [far_wind_x[rows_of(LO * n + y)]] + [wind_x[rows_of(x * n + y)] for x in range(n)]
        winds += [far_wind_x[rows_of((LO + 1) * n + y)]]
        for x, value in enumerate(line_change(cells, winds)):
            change_two[rows_of(x * n + y)] = value

    @pl.loop(0, n)
    def _(x):
        cells = [one[rows_of((x + LO) * reach + y)] for y in range(reach)]
        winds = [far_wind_y[rows_of(x * (LINES + 2) + LO)]] + [wind_y[rows_of(x * n + y)] for y in range(n)]
        winds += [far_wind_y[rows_of(x * (LINES + 2) + LO + 1)]]
        for y, value in enumerate(line_change(cells, winds)):
            at = rows_of(x * n + y)
            change_two[at] = change_two[at] + value

    @pl.loop(0, n)
    def _(x):
        cells = [one[eight((x + LO) * reach + LO, k)] for k in range(ROWS)]
        winds = [wind_z[eight(x * n, k)] for k in range(ROWS)]
        for k, value in enumerate(level_change(cells, winds, width)):
            at = eight(x * n, k)
            change_two[at] = 0.5 * cell[eight(x * span + PAD_LO, k)] + 0.5 * (cells[k] + (value + change_two[at]))

    bins = LANES // 2 // parts
    ids = lax.axis_index("gz") * bins + lane_ids() % bins
    rates, steps = [
        pick(jnp.broadcast_to(jnp.concatenate([ref[...]] * 2, axis=1), (ROWS, LANES)), ids) for ref in (rate_ref, steps_ref)
    ]
    together = 4
    rains = []
    for begin in range(0, n, together):
        xs = range(begin, begin + together)

        def fall(block, carry):
            columns, rain = carry
            columns = [column + [from_above(v, width) for v in column[:AHEAD]] for column in columns]
            rain = list(rain)
            for s in range(AHEAD):
                rate = jnp.where(block * AHEAD + s < steps, rates, 0.0)
                for i, column in enumerate(columns):
                    rain[i] = rain[i] + rate * column[0]
                    columns[i] = [v + rate * (u - v) for v, u in zip(column, column[1:])]
            return columns, rain

        columns = [[change_two[eight(x * n, k)] for k in range(ROWS)] for x in xs]
        columns, rain = lax.fori_loop(0, SUBS // AHEAD, fall, (columns, [jnp.zeros((ROWS, LANES), F32)] * together))
        for x, column in zip(xs, columns):
            for k in range(ROWS):
                change_two[eight(x * n, k)] = column[k]
        rains += rain

    if parts == 2:
        send_ref, keep_ref = out_refs
        lower = is_even("gz")
        low = lane_ids() < 64
        for x in range(n // 2):
            for y in range(n):
                a, b = change_two[rows_of(x * n + y)], change_two[rows_of((x + n // 2) * n + y)]
                at = rows_of(x * n + y)
                keep_ref[at], send_ref[at] = order(jnp.where(low, a, turn(b, 64)), jnp.where(low, turn(a, 64), b), lower)
        for j in range(2):
            value = by_quarter([turn(rains[4 * j + i], 32 * i) for i in range(4)])
            keep_ref[rows_of(n // 2 * n + j)] = value
            send_ref[rows_of(n // 2 * n + j)] = value
    else:
        settled_ref, rain_ref = out_refs
        settled_ref[...] = change_two[...]
        for x in range(n):
            rain_ref[rows_of(x)] = rains[x]


def matrix_kernel(bins, gain_ref, loss_ref, pairs_ref, lost_ref, wide, tall):
    zero = jnp.zeros((bins, LANES - bins), F32)
    shifts = bins // 2

    @pl.loop(0, bins)
    def _(i):
        rows = gain_ref[pl.ds(i * bins, bins)].astype(F32)
        rows = jnp.concatenate([rows, zero], axis=1)
        wide[pl.ds(i * 2 * bins, bins)] = rows
        wide[pl.ds(i * 2 * bins + bins, bins)] = rows
        tall[pl.ds(i * bins, bins)] = rows

        @pl.when(i < shifts)
        def _():
            tall[pl.ds((i + bins) * bins, bins)] = rows

    for d in range(shifts + 1):
        rows = wide[pl.ds(d, bins, stride=2 * bins + 1)]
        if 0 < d < shifts:
            rows = rows + tall[pl.ds(d * bins, bins, stride=bins + 1)]
        pairs_ref[pl.ds(d * LANES, bins)] = rows.astype(jnp.bfloat16)
        pairs_ref[pl.ds(d * LANES + bins, bins)] = pltpu.roll(rows, bins, 1).astype(jnp.bfloat16)
    rows = jnp.concatenate([loss_ref[...].astype(F32), zero], axis=1)
    lost_ref[pl.ds(0, bins)] = rows.astype(jnp.bfloat16)
    lost_ref[pl.ds(bins, bins)] = pltpu.roll(rows, bins, 1).astype(jnp.bfloat16)


def breakup_rows(mass, pairs_ref, lost_ref, products):
    bins = LANES // 2
    count = mass.shape[0]
    lanes = lane_ids()
    rounded = mass.astype(jnp.bfloat16)
    wide = rounded.astype(F32)
    for d in range(bins // 2 + 1):
        ids = lanes // bins * bins + (lanes + d) % bins
        for r in range(0, count, 2 * ROWS):
            halves = [wide[r + ROWS * k : r + ROWS * (k + 1)] for k in range(2)]
            halves = [v * pick(v, ids) if d else v * v for v in halves]
            products[pl.ds(r, 2 * ROWS), d * LANES : (d + 1) * LANES] = jnp.concatenate(halves, axis=0).astype(jnp.bfloat16)
    gained = jnp.dot(products[pl.ds(0, count)], pairs_ref[...], preferred_element_type=F32)
    loss = jnp.dot(rounded, lost_ref[...], preferred_element_type=F32)
    return mass + gained - mass * loss


def breakup_kernel(n, keep_ref, got_ref, pairs_ref, lost_ref, mass_ref, rain_ref, columns, products):
    first = is_even("gz")
    half = n // 2
    for x in range(half):
        for y in range(n):
            at = rows_of(x * n + y)
            a, b = order(keep_ref[at], got_ref[at], first)
            columns[rows_of(x * n + y)] = by_quarter([a, turn(b, 32), turn(a, 32), turn(b, 64)])
            columns[rows_of((x + half) * n + y)] = by_quarter([turn(a, -64), turn(b, -32), turn(a, -32), b])
    for j in range(2):
        at = rows_of(half * n + j)
        a, b = order(keep_ref[at], got_ref[at], first)
        a, b = [jnp.where(first, v[: n // 2], v[n // 2 :]) for v in (a, b)]
        for i in range(4):
            rain_ref[4 * j + i] = jnp.concatenate([a[:, 32 * i : 32 * i + 32], b[:, 32 * i : 32 * i + 32]], axis=1)

    count = products.shape[0]

    @pl.loop(0, n * n * ROWS // count)
    def _(i):
        start = pl.multiple_of(i * count, count)
        mass = columns[pl.ds(start, count)]
        columns[pl.ds(start, count)] = breakup_rows(mass, pairs_ref, lost_ref, products)

    for x in range(n):
        for y in range(n):
            value = columns[rows_of(x * n + y)]
            mass_ref[x, y, 0:ROWS] = value[:, :64]
            mass_ref[x, y, ROWS : 2 * ROWS] = value[:, 64:]


def breakup_plain_kernel(mass_ref, pairs_ref, lost_ref, out_ref, products):
    count = products.shape[0]

    @pl.loop(0, mass_ref.shape[0] // count)
    def _(i):
        start = pl.multiple_of(i * count, count)
        out_ref[pl.ds(start, count)] = breakup_rows(mass_ref[pl.ds(start, count)], pairs_ref, lost_ref, products)


def shape(*dims, dtype=F32):
    return jax.ShapeDtypeStruct(dims, dtype)


def tiles_of(count):
    return shape(count * ROWS, LANES)


def call(kernel, outs, args, scratch=(), micros=1.0, place=pltpu.VMEM, copies=0):
    return pl.pallas_call(
        kernel,
        out_shape=outs,
        in_specs=[pl.BlockSpec(memory_space=place)] * len(args),
        out_specs=jax.tree.map(lambda _: VMEM, outs),
        scratch_shapes=[pltpu.VMEM(s.shape, s.dtype) for s in scratch] + [pltpu.SemaphoreType.DMA] * copies,
        compiler_params=pltpu.CompilerParams(vmem_limit_bytes=40 << 20),
        cost_estimate=pl.CostEstimate(
            flops=int(micros * 1.1e9), bytes_accessed=int(micros * 3.6e6), transcendentals=0
        ),
    )(*args)


def swap_neighbours(axis, begin, message):
    count = lax.axis_size(axis)
    partner = {i: i for i in range(count)}
    for i in range(begin, count - 1, 2):
        partner[i], partner[i + 1] = i + 1, i
    return lax.ppermute(message, axis, list(partner.items()))


def per_device(bin_mass, courant, sub_courant, fall_steps, frag_gain, collide):
    nx, ny, nz, bins = bin_mass.shape
    n = nx
    parts = lax.axis_size("gz")
    gz, gy = lax.axis_index("gz"), lax.axis_index("gy")
    width = bins // parts
    tiles = groups(parts)[2]
    winds = 3 * tiles

    pair_rows = (bins // 2 + 1) * LANES
    pairs, lost = call(
        functools.partial(matrix_kernel, bins),
        (shape(pair_rows, LANES, dtype=jnp.bfloat16), shape(LANES, LANES, dtype=jnp.bfloat16)),
        (frag_gain, collide),
        [shape(2 * bins * bins, LANES), shape(3 * bins * bins // 2, LANES)],
    )

    if parts == 2:
        half = tiles_of(n * n // 2 + 3)
        send, keep = call(pack_kernel, (half, half), (bin_mass, courant), [bin_mass, courant], place=pltpu.HBM, copies=2)
        got = lax.ppermute(send, "gz", [(0, 1), (1, 0)])
        message = tiles_of(n * PAD_LO + winds)
        block, first, second = call(merge_kernel, (tiles_of(n * n + winds), message, message), (keep, got))
    else:
        split = bin_mass.reshape(nx, ny, nz // ROWS, ROWS, parts, width).transpose(4, 0, 1, 3, 2, 5)
        split = lax.all_to_all(split, "gz", split_axis=0, concat_axis=0, tiled=True)
        cube = split.transpose(1, 2, 3, 0, 4, 5).reshape(n, n, ROWS, LANES)
        air = courant.reshape(3, nx, ny, nz // ROWS, ROWS).transpose(0, 4, 3, 1, 2) * (1.0 / 12.0)
        air = lax.all_gather(air, "gz").reshape(parts, 3, ROWS, nz // ROWS, tiles, nx // tiles, ny)
        air = air.transpose(1, 4, 2, 0, 3, 5, 6).reshape(-1, LANES)
        block = jnp.concatenate([cube.reshape(-1, LANES), air])
        up = jnp.concatenate([cube[:, n - PAD_LO :].reshape(-1, LANES), air])
        down = jnp.concatenate([cube[:, :PAD_HI].reshape(-1, LANES), air])
        down = jnp.pad(down, ((0, up.shape[0] - down.shape[0]), (0, 0)))
        first, second = order(up, down, gy % 2 == 0)

    from_y = swap_neighbours("gy", 0, first), swap_neighbours("gy", 1, second)
    wind_x, wind_y, wind_z, own_change = call(
        functools.partial(own_kernel, n, parts), [tiles_of(n * n)] * 4, (block,), micros=1.7
    )
    message = tiles_of(PAD_LO * n + LO * LINES + 3 * tiles // 2 + 2 + tiles)
    held, second = call(functools.partial(side_kernel, n, parts), (message, message), (block, *from_y, own_change))
    second = swap_neighbours("gx", 1, second)
    cell, change, halo_wind_x, far_wind_y = call(
        functools.partial(y_kernel, n, parts),
        [tiles_of(n * (n + PAD_LO + PAD_HI)), tiles_of(n * (n + LINES)), tiles_of(LINES * n), tiles_of(n * (LINES + 2))],
        (block, *from_y, wind_y, own_change),
        [tiles_of(LINES * n)] * 2,
        micros=2.0,
    )
    first = swap_neighbours("gx", 0, call(hand_on_kernel, message, (held, second), micros=0.05))
    reach = n + LINES
    outs = call(
        functools.partial(main_kernel, n, parts),
        [tiles_of(n * n // 2 + 2)] * 2 if parts == 2 else [tiles_of(n * n), tiles_of(n)],
        (cell, change, wind_x, wind_y, wind_z, halo_wind_x, far_wind_y, first, second, sub_courant.reshape(1, bins), fall_steps.reshape(1, bins)),
        [
            tiles_of(count)
            for count in (
                LINES * n,
                LINES * reach,
                (LINES + 2) * n,
                2 * LINES,
                LINES * (n + 2),
                LINES * n,
                LINES * n,
                reach * reach,
                n * n,
            )
        ],
        micros=6.0,
    )

    products = shape(256, pair_rows, dtype=jnp.bfloat16)
    if parts == 2:
        send, keep = outs
        got = lax.ppermute(send, "gz", [(0, 1), (1, 0)])
        return tuple(
            call(
                functools.partial(breakup_kernel, n),
                [shape(nx, ny, nz, bins), shape(nx, ny // parts, bins)],
                (keep, got, pairs, lost),
                [tiles_of(n * n), products],
                micros=3.0,
            )
        )

    settled, rain = outs
    rain = rain.reshape(nx, ny, LANES)[:, :, :width]
    rain = lax.all_to_all(rain, "gz", split_axis=1, concat_axis=2, tiled=True)
    settled = settled.reshape(nx, ny, ROWS, parts, nz // ROWS, width).transpose(3, 0, 1, 4, 2, 5)
    settled = lax.all_to_all(settled, "gz", split_axis=0, concat_axis=0, tiled=True)
    settled = settled.transpose(1, 2, 3, 4, 0, 5).reshape(nx * ny, nz // ROWS, ROWS, bins)
    paired = settled.transpose(0, 2, 1, 3).reshape(-1, LANES)
    updated = call(breakup_plain_kernel, tiles_of(n * n), (paired, pairs, lost), [products], micros=3.0)
    updated = updated.reshape(nx, ny, ROWS, nz // ROWS, bins).transpose(0, 1, 3, 2, 4).reshape(nx, ny, nz, bins)
    return updated, rain


def solution(mesh):
    in_specs = (P("gx", "gy", "gz", None), P(None, "gx", "gy", "gz"), P(), P(), P(), P())
    out_specs = (P("gx", "gy", "gz", None), P("gx", ("gy", "gz"), None))
    return jax.shard_map(per_device, mesh=mesh, in_specs=in_specs, out_specs=out_specs, check_vma=False)
```

```python
import functools

import jax
import jax.numpy as jnp
from jax import lax
from jax.experimental import pallas as pl
from jax.experimental.pallas import tpu as pltpu
from jax.sharding import PartitionSpec as P

SUBS = 24
EPS = 1e-06
LO, HI = 3, 2
PAD_LO, PAD_HI = 2 * LO, 2 * HI
LINES = LO + HI
ROWS, LANES = 8, 128
AHEAD = 4
F32 = jnp.float32
VMEM = pl.BlockSpec(memory_space=pltpu.VMEM)


def lane_ids():
    return lax.broadcasted_iota(jnp.int32, (ROWS, LANES), 1)


def pick(tile, ids):
    return jnp.take_along_axis(tile, ids, axis=1, mode="promise_in_bounds")


def turn(tile, lanes):
    lanes %= LANES
    return pltpu.roll(tile, lanes, 1) if lanes else tile


def rows_of(first, count=1):
    return pl.ds(first * ROWS, count * ROWS)


def eight(first, level, step=1):
    return pl.ds(first * ROWS + level, ROWS, stride=step * ROWS)


def order(a, b, straight):
    return jnp.where(straight, a, b), jnp.where(straight, b, a)


def is_even(axis):
    return lax.axis_index(axis) % 2 == 0


def by_quarter(parts):
    quarter = lane_ids() // (LANES // 4)
    return jnp.where(quarter < 2, jnp.where(quarter == 0, parts[0], parts[1]), jnp.where(quarter == 2, parts[2], parts[3]))


def groups(parts):
    width = LANES // (2 * parts)
    return width, width // ROWS, ROWS * ROWS // width


def spread(tile, x, y, parts):
    width, deep, _ = groups(parts)
    return pick(turn(tile, -(x % deep * ROWS + y)), lane_ids() // width * width)


def halo_line(i, n):
    return jnp.where(i < LO, i - LO, i - LO + n)


def line_change(cells, winds):
    first = [b - a for a, b in zip(cells, cells[1:])]
    twice = [d + d for d in first]
    second = [b - a for a, b in zip(first, first[1:])]
    third = [a - b for a, b in zip(second, second[1:])]
    curved = [(13.0 / 3.0) * (c * c) + 4.0 * EPS for c in second]
    fluxes = []
    for j in range(len(cells) - 4):
        left = twice[j + 1] + second[j]
        mid = first[j + 1] + first[j + 2]
        right = twice[j + 2] - second[j + 2]
        e0 = curved[j] + left * left
        e1 = curved[j + 1] + mid * mid
        e2 = curved[j + 2] + right * right
        e0 = e0 * e0
        e1 = e1 * e1
        e2 = e2 * e2
        e0 = 3.0 * e0
        e2_twice = e2 + e2
        top = e1 * (e2_twice * third[j] + e0 * third[j + 1])
        low = e1 * (e2 + e0) + e0 * e2_twice
        inverse = pl.reciprocal(low, approx=True)
        inverse = inverse * (2.0 - low * inverse)
        estimate = 6.0 * cells[j + 2] + (first[j + 1] + twice[j + 2]) + top * inverse
        fluxes.append((winds[j] + winds[j + 1]) * estimate)
    return [a - b for a, b in zip(fluxes, fluxes[1:])]


def from_below(value, width):
    return jnp.where(lane_ids() < width, 0.0, turn(value, width))


def from_above(value, width):
    return jnp.where(lane_ids() >= LANES - width, 0.0, turn(value, -width))


def level_change(cells, winds, width):
    long_cells = [from_below(v, width) for v in cells[ROWS - LO :]] + cells + [from_above(v, width) for v in cells[:HI]]
    long_winds = [from_below(winds[-1], width)] + winds + [from_above(winds[0], width)]
    return line_change(long_cells, long_winds)


def pack_kernel(mass_ref, send_ref, keep_ref):
    lower = is_even("gz")
    n = mass_ref.shape[0]
    zero = jnp.zeros((ROWS, LANES // 2), F32)
    for x in range(n // 2):
        for y in range(n):
            tiles = [
                jnp.concatenate([mass_ref[xx, y, z : z + ROWS], zero], axis=1) for xx in (x, x + n // 2) for z in (0, ROWS)
            ]
            low = by_quarter([turn(v, 32 * k) for k, v in enumerate(tiles)])
            high = by_quarter([turn(v, 32 * k - 32) for k, v in enumerate(tiles)])
            at = rows_of(x * n + y)
            keep_ref[at], send_ref[at] = order(low, high, lower)


def wind_kernel(wind_ref, out_ref):
    n = wind_ref.shape[1]
    for d in range(3):
        levels = wind_ref[d].reshape(n * n, 2 * ROWS).T * (1.0 / 12.0)
        out_ref[rows_of(d)] = jnp.concatenate([levels[:ROWS], levels[ROWS:]], axis=1)


def sides(axis, first_ref, second_ref):
    even, place = is_even(axis), lax.axis_index(axis)
    inner_low, inner_high = place > 0, place < lax.axis_size(axis) - 1

    def below(at):
        return jnp.where(inner_low, jnp.where(even, second_ref[at], first_ref[at]), 0.0)

    def above(at):
        return jnp.where(inner_high, jnp.where(even, first_ref[at], second_ref[at]), 0.0)

    return below, above


def by_parity(axis, body):
    even = is_even(axis)
    pl.when(even)(lambda: body(0, 1))
    pl.when(jnp.logical_not(even))(lambda: body(1, 0))


def merge_kernel(keep_ref, got_ref, own_wind_ref, got_wind_ref, block_ref, *messages):
    n = 8
    lower = is_even("gz")
    low = lane_ids() < 64

    def body(up, down):
        up_ref, down_ref = messages[up], messages[down]
        for x in range(n // 2):
            for y in range(n):
                at = rows_of(x * n + y)
                a, b = order(keep_ref[at], got_ref[at], lower)
                for xx, tile in (
                    (x, jnp.where(low, a, turn(b, 64))),
                    (x + n // 2, jnp.where(low, turn(a, 64), b)),
                ):
                    block_ref[rows_of(xx * n + y)] = tile
                    if y >= n - PAD_LO:
                        up_ref[rows_of(xx * PAD_LO + y - (n - PAD_LO))] = tile
                    if y < PAD_HI:
                        down_ref[rows_of(xx * PAD_HI + y)] = tile
        for d in range(3):
            a, b = order(own_wind_ref[rows_of(d)], got_wind_ref[rows_of(d)], lower)
            for half, tile in enumerate(
                (
                    by_quarter([a, turn(a, -32), turn(b, 64), turn(b, 32)]),
                    by_quarter([turn(a, -32), turn(a, -64), turn(b, 32), b]),
                )
            ):
                for ref, base in ((block_ref, n * n), (up_ref, n * PAD_LO), (down_ref, n * PAD_HI)):
                    ref[rows_of(base + 2 * d + half)] = tile

    by_parity("gy", body)


def side_kernel(n, parts, block_ref, first_ref, second_ref, own_change, *messages):
    del own_change
    tiles = groups(parts)[2]
    half = tiles // 2
    below, above = sides("gy", first_ref, second_ref)

    def body(up, down):
        for ref, start, wide, narrow_at, narrow, part in (
            (messages[up], n - PAD_LO, PAD_LO, n - LO, LO, half),
            (messages[down], 0, PAD_HI, 0, HI, 0),
        ):
            for x in range(wide):
                ref[rows_of(x * n, n)] = block_ref[rows_of((start + x) * n, n)]
            at = wide * n
            for x in range(narrow):
                xx = narrow_at + x
                ref[rows_of(at, LO)] = below(rows_of(xx * PAD_LO + PAD_LO - LO, LO))
                ref[rows_of(at + LO, HI)] = above(rows_of(xx * PAD_HI, HI))
                at += LINES
            for d in range(3):
                ref[rows_of(at, half)] = block_ref[rows_of(n * n + d * tiles + part, half)]
                at += half
            for side, base in ((below, n * PAD_LO), (above, n * PAD_HI)):
                ref[rows_of(at)] = side(rows_of(base + (tiles - 1 if part else 0)))
                ref[rows_of(at + 1, half)] = side(rows_of(base + tiles + part, half))
                at += 1 + half

    by_parity("gx", body)


def own_kernel(n, parts, block_ref, wind_x, wind_y, wind_z, change):
    width, deep, tiles = groups(parts)
    for d, out in enumerate((wind_x, wind_y, wind_z)):
        for x in range(n):
            tile = block_ref[rows_of(n * n + d * tiles + x // deep)]
            for y in range(n):
                out[rows_of(x * n + y)] = spread(tile, x, y, parts)

    @pl.loop(0, n)
    def _(x):
        cells = [block_ref[eight(x * n, k)] for k in range(ROWS)]
        winds = [wind_z[eight(x * n, k)] for k in range(ROWS)]
        for k, value in enumerate(level_change(cells, winds, width)):
            change[eight(x * n, k)] = value


def y_kernel(n, parts, block_ref, first_ref, second_ref, wind_y, own_change, *refs):
    width, deep, tiles = groups(parts)
    cell, change, wind_x, far_y, wind_z, halo_change = refs
    below, above = sides("gy", first_ref, second_ref)
    span, reach = n + PAD_LO + PAD_HI, n + LINES

    for x in range(n):
        cell[rows_of(x * span, PAD_LO)] = below(rows_of(x * PAD_LO, PAD_LO))
        cell[rows_of(x * span + PAD_LO, n)] = block_ref[rows_of(x * n, n)]
        cell[rows_of(x * span + PAD_LO + n, PAD_HI)] = above(rows_of(x * PAD_HI, PAD_HI))
    for d in range(3):
        for t in range(tiles):
            low, high = below(rows_of(n * PAD_LO + d * tiles + t)), above(rows_of(n * PAD_HI + d * tiles + t))
            for x in range(t * deep, (t + 1) * deep):
                if d == 1:
                    for y in range(LO + 1):
                        far_y[rows_of(x * (LINES + 2) + y)] = spread(low, x, n - LO - 1 + y, parts)
                    for y in range(HI + 1):
                        far_y[rows_of(x * (LINES + 2) + LO + 1 + y)] = spread(high, x, y, parts)
                else:
                    out = wind_z if d else wind_x
                    for y in range(LO):
                        out[rows_of(y * n + x)] = spread(low, x, n - LO + y, parts)
                    for y in range(HI):
                        out[rows_of((LO + y) * n + x)] = spread(high, x, y, parts)

    @pl.loop(0, LINES)
    def _(i):
        first = halo_line(i, n) + PAD_LO
        cells = [cell[eight(first, k, span)] for k in range(ROWS)]
        winds = [wind_z[eight(i * n, k)] for k in range(ROWS)]
        for k, value in enumerate(level_change(cells, winds, width)):
            halo_change[eight(i * n, k)] = value

    @pl.loop(0, n)
    def _(x):
        cells = [cell[rows_of(x * span + y)] for y in range(span)]
        far = [far_y[rows_of(x * (LINES + 2) + y)] for y in range(LINES + 2)]
        winds = far[: LO + 1] + [wind_y[rows_of(x * n + y)] for y in range(n)] + far[LO + 1 :]
        for y, value in enumerate(line_change(cells, winds)):
            if LO <= y < LO + n:
                value = value + own_change[rows_of(x * n + y - LO)]
            else:
                value = value + halo_change[rows_of((y if y < LO else y - n) * n + x)]
            change[rows_of(x * reach + y)] = value


def main_kernel(n, parts, *refs):
    cell, change, wind_x, wind_y, wind_z, halo_wind_x, far_wind_y, first_ref, second_ref, rate_ref, steps_ref = refs[:11]
    out_refs, scratch = refs[11:13], refs[13:]
    far, side, far_wind_x, corner_wind_x, side_wind_y, side_wind_z, side_change, one, change_two = scratch
    width, deep, tiles = groups(parts)
    half = tiles // 2
    west, east = sides("gx", first_ref, second_ref)
    span, reach = n + PAD_LO + PAD_HI, n + LINES

    for take, wide, narrow, far_at, side_at, far_from, side_from in (
        (west, PAD_LO, LO, 0, 0, 0, LO),
        (east, PAD_HI, HI, LO, LO, HI, 0),
    ):
        for i in range(narrow):
            far[rows_of((far_at + i) * n, n)] = take(rows_of((far_from + i) * n, n))
            line = (side_at + i) * reach
            corner = wide * n + i * LINES
            side[rows_of(line, LO)] = take(rows_of(corner, LO))
            side[rows_of(line + LO, n)] = take(rows_of((side_from + i) * n, n))
            side[rows_of(line + LO + n, HI)] = take(rows_of(corner + LO, HI))
        at = wide * n + narrow * LINES
        layers = range(n - narrow, n) if narrow == LO else range(narrow)
        wider = range(n - narrow - 1, n) if narrow == LO else range(narrow + 1)
        shift = half if narrow == LO else 0

        def winds_of(base, x):
            return take(rows_of(base + x // deep - shift))

        for i, x in enumerate(wider):
            tile = winds_of(at, x)
            for y in range(n):
                far_wind_x[rows_of((far_at + bool(far_at) + i) * n + y)] = spread(tile, x, y, parts)
        below, above = at + 3 * half, at + 3 * half + 1 + half
        x = wider[-1] if narrow == LO else wider[0]
        for y in range(LINES):
            tile = take(rows_of(below if y < LO else above))
            corner_wind_x[rows_of(bool(far_at) * LINES + y)] = spread(tile, x, n - LO + y if y < LO else y - LO, parts)
        for i, x in enumerate(layers):
            line = (side_at + i) * (n + 2)
            side_wind_y[rows_of(line)] = spread(winds_of(below + 1, x), x, n - 1, parts)
            side_wind_y[rows_of(line + n + 1)] = spread(winds_of(above + 1, x), x, 0, parts)
            for y in range(n):
                side_wind_y[rows_of(line + 1 + y)] = spread(winds_of(at + half, x), x, y, parts)
                side_wind_z[rows_of((side_at + i) * n + y)] = spread(winds_of(at + 2 * half, x), x, y, parts)

    @pl.loop(0, LINES)
    def _(i):
        cells = [side[eight(i * reach + LO, k)] for k in range(ROWS)]
        winds = [side_wind_z[eight(i * n, k)] for k in range(ROWS)]
        for k, value in enumerate(level_change(cells, winds, width)):
            side_change[eight(i * n, k)] = value

    @pl.loop(0, LINES)
    def _(i):
        cells = [side[rows_of(i * reach + y)] for y in range(reach)]
        winds = [side_wind_y[rows_of(i * (n + 2) + y)] for y in range(n + 2)]
        for y, value in enumerate(line_change(cells, winds)):
            at = rows_of(i * n + y)
            side_change[at] = side_change[at] + value

    last = lax.axis_size("gx") - 1, lax.axis_size("gy") - 1

    def inside(axis, count, lower):
        place = lax.axis_index(axis)
        return jnp.where(place > 0 if lower else place < count, 1.0, 0.0)

    west_in, east_in = inside("gx", last[0], True), inside("gx", last[0], False)
    south_in, north_in = inside("gy", last[1], True), inside("gy", last[1], False)

    @pl.loop(0, n)
    def _(y):
        outer = [far[rows_of(i * n + y)] for i in range(LINES)]
        near = [side[rows_of(i * reach + LO + y)] for i in range(LINES)]
        cells = outer[:LO] + near[:LO] + [cell[rows_of(x * span + PAD_LO + y)] for x in range(n)] + near[LO:] + outer[LO:]
        winds = [far_wind_x[rows_of(i * n + y)] for i in range(LINES + 2)]
        winds = winds[: LO + 1] + [wind_x[rows_of(x * n + y)] for x in range(n)] + winds[LO + 1 :]
        for i, value in enumerate(line_change(cells, winds)):
            if LO <= i < LO + n:
                value = cells[i + LO] + (value + change[rows_of((i - LO) * reach + LO + y)])
            else:
                value = cells[i + LO] + (value + side_change[rows_of((i if i < LO else i - n) * n + y)])
                value = value * (west_in if i < LO else east_in)
            one[rows_of(i * reach + LO + y)] = value

    @pl.loop(0, LINES)
    def _(i):
        line = halo_line(i, n) + LO
        near = [side[rows_of(k * reach + line)] for k in range(LINES)]
        cells = near[:LO] + [cell[rows_of(x * span + LO + line)] for x in range(n)] + near[LO:]
        winds = [halo_wind_x[rows_of(i * n + x)] for x in range(n)]
        winds = [corner_wind_x[rows_of(i)]] + winds + [corner_wind_x[rows_of(LINES + i)]]
        keep = jnp.where(i < LO, south_in, north_in)
        for x, value in enumerate(line_change(cells, winds)):
            one[rows_of((x + LO) * reach + line)] = (cells[x + LO] + (value + change[rows_of(x * reach + line)])) * keep

    @pl.loop(0, n)
    def _(y):
        cells = [one[rows_of(x * reach + LO + y)] for x in range(reach)]
        winds = [far_wind_x[rows_of(LO * n + y)]] + [wind_x[rows_of(x * n + y)] for x in range(n)]
        winds += [far_wind_x[rows_of((LO + 1) * n + y)]]
        for x, value in enumerate(line_change(cells, winds)):
            change_two[rows_of(x * n + y)] = value

    @pl.loop(0, n)
    def _(x):
        cells = [one[rows_of((x + LO) * reach + y)] for y in range(reach)]
        winds = [far_wind_y[rows_of(x * (LINES + 2) + LO)]] + [wind_y[rows_of(x * n + y)] for y in range(n)]
        winds += [far_wind_y[rows_of(x * (LINES + 2) + LO + 1)]]
        for y, value in enumerate(line_change(cells, winds)):
            at = rows_of(x * n + y)
            change_two[at] = change_two[at] + value

    @pl.loop(0, n)
    def _(x):
        cells = [one[eight((x + LO) * reach + LO, k)] for k in range(ROWS)]
        winds = [wind_z[eight(x * n, k)] for k in range(ROWS)]
        for k, value in enumerate(level_change(cells, winds, width)):
            at = eight(x * n, k)
            change_two[at] = 0.5 * cell[eight(x * span + PAD_LO, k)] + 0.5 * (cells[k] + (value + change_two[at]))

    bins = LANES // 2 // parts
    ids = lax.axis_index("gz") * bins + lane_ids() % bins
    rates, steps = [
        pick(jnp.broadcast_to(jnp.concatenate([ref[...]] * 2, axis=1), (ROWS, LANES)), ids) for ref in (rate_ref, steps_ref)
    ]
    together = 4
    rains = []
    for begin in range(0, n, together):
        xs = range(begin, begin + together)

        def fall(block, carry):
            columns, rain = carry
            columns = [column + [from_above(v, width) for v in column[:AHEAD]] for column in columns]
            rain = list(rain)
            for s in range(AHEAD):
                rate = jnp.where(block * AHEAD + s < steps, rates, 0.0)
                for i, column in enumerate(columns):
                    rain[i] = rain[i] + rate * column[0]
                    columns[i] = [v + rate * (u - v) for v, u in zip(column, column[1:])]
            return columns, rain

        columns = [[change_two[eight(x * n, k)] for k in range(ROWS)] for x in xs]
        columns, rain = lax.fori_loop(0, SUBS // AHEAD, fall, (columns, [jnp.zeros((ROWS, LANES), F32)] * together))
        for x, column in zip(xs, columns):
            for k in range(ROWS):
                change_two[eight(x * n, k)] = column[k]
        rains += rain

    if parts == 2:
        send_ref, keep_ref = out_refs
        lower = is_even("gz")
        low = lane_ids() < 64
        for x in range(n // 2):
            for y in range(n):
                a, b = change_two[rows_of(x * n + y)], change_two[rows_of((x + n // 2) * n + y)]
                at = rows_of(x * n + y)
                keep_ref[at], send_ref[at] = order(jnp.where(low, a, turn(b, 64)), jnp.where(low, turn(a, 64), b), lower)
        for j in range(2):
            value = by_quarter([turn(rains[4 * j + i], 32 * i) for i in range(4)])
            keep_ref[rows_of(n // 2 * n + j)] = value
            send_ref[rows_of(n // 2 * n + j)] = value
    else:
        settled_ref, rain_ref = out_refs
        settled_ref[...] = change_two[...]
        for x in range(n):
            rain_ref[rows_of(x)] = rains[x]


def matrix_kernel(bins, gain_ref, loss_ref, pairs_ref, lost_ref, wide, tall):
    zero = jnp.zeros((bins, LANES - bins), F32)
    shifts = bins // 2

    @pl.loop(0, bins)
    def _(i):
        rows = gain_ref[pl.ds(i * bins, bins)].astype(F32)
        rows = jnp.concatenate([rows, zero], axis=1)
        wide[pl.ds(i * 2 * bins, bins)] = rows
        wide[pl.ds(i * 2 * bins + bins, bins)] = rows
        tall[pl.ds(i * bins, bins)] = rows

        @pl.when(i < shifts)
        def _():
            tall[pl.ds((i + bins) * bins, bins)] = rows

    for d in range(shifts + 1):
        rows = wide[pl.ds(d, bins, stride=2 * bins + 1)]
        if 0 < d < shifts:
            rows = rows + tall[pl.ds(d * bins, bins, stride=bins + 1)]
        pairs_ref[pl.ds(d * LANES, bins)] = rows.astype(jnp.bfloat16)
        pairs_ref[pl.ds(d * LANES + bins, bins)] = pltpu.roll(rows, bins, 1).astype(jnp.bfloat16)
    rows = jnp.concatenate([loss_ref[...].astype(F32), zero], axis=1)
    lost_ref[pl.ds(0, bins)] = rows.astype(jnp.bfloat16)
    lost_ref[pl.ds(bins, bins)] = pltpu.roll(rows, bins, 1).astype(jnp.bfloat16)


def breakup_rows(mass, pairs_ref, lost_ref, products):
    bins = LANES // 2
    count = mass.shape[0]
    lanes = lane_ids()
    rounded = mass.astype(jnp.bfloat16)
    wide = rounded.astype(F32)
    for d in range(bins // 2 + 1):
        ids = lanes // bins * bins + (lanes + d) % bins
        for r in range(0, count, 2 * ROWS):
            halves = [wide[r + ROWS * k : r + ROWS * (k + 1)] for k in range(2)]
            halves = [v * pick(v, ids) if d else v * v for v in halves]
            products[pl.ds(r, 2 * ROWS), d * LANES : (d + 1) * LANES] = jnp.concatenate(halves, axis=0).astype(jnp.bfloat16)
    gained = jnp.dot(products[pl.ds(0, count)], pairs_ref[...], preferred_element_type=F32)
    loss = jnp.dot(rounded, lost_ref[...], preferred_element_type=F32)
    return mass + gained - mass * loss


def breakup_kernel(n, keep_ref, got_ref, pairs_ref, lost_ref, mass_ref, rain_ref, columns, products):
    first = is_even("gz")
    half = n // 2
    for x in range(half):
        for y in range(n):
            at = rows_of(x * n + y)
            a, b = order(keep_ref[at], got_ref[at], first)
            columns[rows_of(x * n + y)] = by_quarter([a, turn(b, 32), turn(a, 32), turn(b, 64)])
            columns[rows_of((x + half) * n + y)] = by_quarter([turn(a, -64), turn(b, -32), turn(a, -32), b])
    for j in range(2):
        at = rows_of(half * n + j)
        a, b = order(keep_ref[at], got_ref[at], first)
        a, b = [jnp.where(first, v[: n // 2], v[n // 2 :]) for v in (a, b)]
        for i in range(4):
            rain_ref[4 * j + i] = jnp.concatenate([a[:, 32 * i : 32 * i + 32], b[:, 32 * i : 32 * i + 32]], axis=1)

    count = products.shape[0]

    @pl.loop(0, n * n * ROWS // count)
    def _(i):
        start = pl.multiple_of(i * count, count)
        mass = columns[pl.ds(start, count)]
        columns[pl.ds(start, count)] = breakup_rows(mass, pairs_ref, lost_ref, products)

    for x in range(n):
        for y in range(n):
            value = columns[rows_of(x * n + y)]
            mass_ref[x, y, 0:ROWS] = value[:, :64]
            mass_ref[x, y, ROWS : 2 * ROWS] = value[:, 64:]


def breakup_plain_kernel(mass_ref, pairs_ref, lost_ref, out_ref, products):
    count = products.shape[0]

    @pl.loop(0, mass_ref.shape[0] // count)
    def _(i):
        start = pl.multiple_of(i * count, count)
        out_ref[pl.ds(start, count)] = breakup_rows(mass_ref[pl.ds(start, count)], pairs_ref, lost_ref, products)


def shape(*dims, dtype=F32):
    return jax.ShapeDtypeStruct(dims, dtype)


def tiles_of(count):
    return shape(count * ROWS, LANES)


def call(kernel, outs, args, scratch=(), micros=1.0):
    return pl.pallas_call(
        kernel,
        out_shape=outs,
        in_specs=[VMEM] * len(args),
        out_specs=jax.tree.map(lambda _: VMEM, outs),
        scratch_shapes=[pltpu.VMEM(s.shape, s.dtype) for s in scratch],
        compiler_params=pltpu.CompilerParams(vmem_limit_bytes=40 << 20),
        cost_estimate=pl.CostEstimate(
            flops=int(micros * 1.1e9), bytes_accessed=int(micros * 3.6e6), transcendentals=0
        ),
    )(*args)


def swap_neighbours(axis, begin, message):
    axes = ("gx", "gy")
    sizes = [lax.axis_size(a) for a in axes]
    along = axes.index(axis)

    def partner(place, start, count):
        to = start + ((place - start) ^ 1)
        return to if start <= place and to < count else place

    pairs = []
    for here in range(sizes[0] * sizes[1]):
        place = list(divmod(here, sizes[1]))
        to = partner(place[along], begin, sizes[along])
        if to == place[along]:
            place[1 - along] = partner(place[1 - along], 0, sizes[1 - along])
        place[along] = to
        pairs.append((here, place[0] * sizes[1] + place[1]))
    return lax.ppermute(message, axes, pairs)


def per_device(bin_mass, courant, sub_courant, fall_steps, frag_gain, collide):
    nx, ny, nz, bins = bin_mass.shape
    n = nx
    parts = lax.axis_size("gz")
    gz, gy = lax.axis_index("gz"), lax.axis_index("gy")
    width = bins // parts
    tiles = groups(parts)[2]
    winds = 3 * tiles

    pair_rows = (bins // 2 + 1) * LANES
    pairs, lost = call(
        functools.partial(matrix_kernel, bins),
        (shape(pair_rows, LANES, dtype=jnp.bfloat16), shape(LANES, LANES, dtype=jnp.bfloat16)),
        (frag_gain, collide),
        [shape(2 * bins * bins, LANES), shape(3 * bins * bins // 2, LANES)],
    )

    if parts == 2:
        half = tiles_of(n * n // 2)
        send, keep = call(pack_kernel, (half, half), (bin_mass,), micros=0.3)
        got = lax.ppermute(send, "gz", [(0, 1), (1, 0)])
        own_wind = call(wind_kernel, tiles_of(3), (courant,), micros=0.1)
        got_wind = lax.ppermute(own_wind, "gz", [(0, 1), (1, 0)])
        message = tiles_of(n * PAD_LO + winds)
        block, first, second = call(
            merge_kernel, (tiles_of(n * n + winds), message, message), (keep, got, own_wind, got_wind), micros=0.2
        )
    else:
        split = bin_mass.reshape(nx, ny, nz // ROWS, ROWS, parts, width).transpose(4, 0, 1, 3, 2, 5)
        split = lax.all_to_all(split, "gz", split_axis=0, concat_axis=0, tiled=True)
        cube = split.transpose(1, 2, 3, 0, 4, 5).reshape(n, n, ROWS, LANES)
        air = courant.reshape(3, nx, ny, nz // ROWS, ROWS).transpose(0, 4, 3, 1, 2) * (1.0 / 12.0)
        air = lax.all_gather(air, "gz").reshape(parts, 3, ROWS, nz // ROWS, tiles, nx // tiles, ny)
        air = air.transpose(1, 4, 2, 0, 3, 5, 6).reshape(-1, LANES)
        block = jnp.concatenate([cube.reshape(-1, LANES), air])
        up = jnp.concatenate([cube[:, n - PAD_LO :].reshape(-1, LANES), air])
        down = jnp.concatenate([cube[:, :PAD_HI].reshape(-1, LANES), air])
        down = jnp.pad(down, ((0, up.shape[0] - down.shape[0]), (0, 0)))
        first, second = order(up, down, gy % 2 == 0)

    from_y = swap_neighbours("gy", 0, first), swap_neighbours("gy", 1, second)
    wind_x, wind_y, wind_z, own_change = call(
        functools.partial(own_kernel, n, parts), [tiles_of(n * n)] * 4, (block,), micros=1.7
    )
    message = tiles_of(PAD_LO * n + LO * LINES + 3 * tiles // 2 + 2 + tiles)
    first, second = call(
        functools.partial(side_kernel, n, parts), (message, message), (block, *from_y, own_change), micros=0.1
    )
    second = swap_neighbours("gx", 1, second)
    first = swap_neighbours("gx", 0, first)
    cell, change, halo_wind_x, far_wind_y = call(
        functools.partial(y_kernel, n, parts),
        [tiles_of(n * (n + PAD_LO + PAD_HI)), tiles_of(n * (n + LINES)), tiles_of(LINES * n), tiles_of(n * (LINES + 2))],
        (block, *from_y, wind_y, own_change),
        [tiles_of(LINES * n)] * 2,
        micros=2.0,
    )
    reach = n + LINES
    outs = call(
        functools.partial(main_kernel, n, parts),
        [tiles_of(n * n // 2 + 2)] * 2 if parts == 2 else [tiles_of(n * n), tiles_of(n)],
        (cell, change, wind_x, wind_y, wind_z, halo_wind_x, far_wind_y, first, second, sub_courant.reshape(1, bins), fall_steps.reshape(1, bins)),
        [
            tiles_of(count)
            for count in (
                LINES * n,
                LINES * reach,
                (LINES + 2) * n,
                2 * LINES,
                LINES * (n + 2),
                LINES * n,
                LINES * n,
                reach * reach,
                n * n,
            )
        ],
        micros=6.0,
    )

    products = shape(256, pair_rows, dtype=jnp.bfloat16)
    if parts == 2:
        send, keep = outs
        got = lax.ppermute(send, "gz", [(0, 1), (1, 0)])
        return tuple(
            call(
                functools.partial(breakup_kernel, n),
                [shape(nx, ny, nz, bins), shape(nx, ny // parts, bins)],
                (keep, got, pairs, lost),
                [tiles_of(n * n), products],
                micros=3.0,
            )
        )

    settled, rain = outs
    rain = rain.reshape(nx, ny, LANES)[:, :, :width]
    rain = lax.all_to_all(rain, "gz", split_axis=1, concat_axis=2, tiled=True)
    settled = settled.reshape(nx, ny, ROWS, parts, nz // ROWS, width).transpose(3, 0, 1, 4, 2, 5)
    settled = lax.all_to_all(settled, "gz", split_axis=0, concat_axis=0, tiled=True)
    settled = settled.transpose(1, 2, 3, 4, 0, 5).reshape(nx * ny, nz // ROWS, ROWS, bins)
    paired = settled.transpose(0, 2, 1, 3).reshape(-1, LANES)
    updated = call(breakup_plain_kernel, tiles_of(n * n), (paired, pairs, lost), [products], micros=3.0)
    updated = updated.reshape(nx, ny, ROWS, nz // ROWS, bins).transpose(0, 1, 3, 2, 4).reshape(nx, ny, nz, bins)
    return updated, rain


def solution(mesh):
    in_specs = (P("gx", "gy", "gz", None), P(None, "gx", "gy", "gz"), P(), P(), P(), P())
    out_specs = (P("gx", "gy", "gz", None), P("gx", ("gy", "gz"), None))
    return jax.shard_map(per_device, mesh=mesh, in_specs=in_specs, out_specs=out_specs, check_vma=False)
```

```python
import functools

import jax
import jax.numpy as jnp
from jax import lax
from jax.experimental import pallas as pl
from jax.experimental.pallas import tpu as pltpu
from jax.sharding import PartitionSpec as P

SUBS = 24
EPS = 1e-06
LO, HI = 3, 2
PAD_LO, PAD_HI = 2 * LO, 2 * HI
LINES = LO + HI
ROWS, LANES = 8, 128
AHEAD = 4
F32 = jnp.float32
VMEM = pl.BlockSpec(memory_space=pltpu.VMEM)


def lane_ids():
    return lax.broadcasted_iota(jnp.int32, (ROWS, LANES), 1)


def pick(tile, ids):
    return jnp.take_along_axis(tile, ids, axis=1, mode="promise_in_bounds")


def turn(tile, lanes):
    lanes %= LANES
    return pltpu.roll(tile, lanes, 1) if lanes else tile


def rows_of(first, count=1):
    return pl.ds(first * ROWS, count * ROWS)


def eight(first, level, step=1):
    return pl.ds(first * ROWS + level, ROWS, stride=step * ROWS)


def order(a, b, straight):
    return jnp.where(straight, a, b), jnp.where(straight, b, a)


def is_even(axis):
    return lax.axis_index(axis) % 2 == 0


def by_quarter(parts):
    quarter = lane_ids() // (LANES // 4)
    return jnp.where(quarter < 2, jnp.where(quarter == 0, parts[0], parts[1]), jnp.where(quarter == 2, parts[2], parts[3]))


def groups(parts):
    width = LANES // (2 * parts)
    return width, width // ROWS, ROWS * ROWS // width


def aim(tile, x, y, parts):
    deep = groups(parts)[1]
    return turn(tile, -(x % deep * ROWS + y))


def spread(ref, parts):
    width = groups(parts)[0]
    ids = lane_ids() // width * width
    count = ref.shape[0] // ROWS
    step = max(k for k in range(1, 17) if count % k == 0)

    @pl.loop(0, count // step)
    def _(i):
        for k in range(step):
            at = rows_of(i * step + k)
            ref[at] = pick(ref[at], ids)


def halo_line(i, n):
    return jnp.where(i < LO, i - LO, i - LO + n)


def line_change(cells, winds):
    first = [b - a for a, b in zip(cells, cells[1:])]
    twice = [d + d for d in first]
    second = [b - a for a, b in zip(first, first[1:])]
    third = [a - b for a, b in zip(second, second[1:])]
    curved = [(13.0 / 3.0) * (c * c) + 4.0 * EPS for c in second]
    fluxes = []
    for j in range(len(cells) - 4):
        left = twice[j + 1] + second[j]
        mid = first[j + 1] + first[j + 2]
        right = twice[j + 2] - second[j + 2]
        e0 = curved[j] + left * left
        e1 = curved[j + 1] + mid * mid
        e2 = curved[j + 2] + right * right
        e0 = e0 * e0
        e1 = e1 * e1
        e2 = e2 * e2
        e0 = 3.0 * e0
        e2_twice = e2 + e2
        top = e1 * (e2_twice * third[j] + e0 * third[j + 1])
        low = e1 * (e2 + e0) + e0 * e2_twice
        inverse = pl.reciprocal(low, approx=True)
        estimate = 6.0 * cells[j + 2] + (first[j + 1] + twice[j + 2]) + top * inverse
        fluxes.append((winds[j] + winds[j + 1]) * estimate)
    return [a - b for a, b in zip(fluxes, fluxes[1:])]


def from_below(value, width):
    return jnp.where(lane_ids() < width, 0.0, turn(value, width))


def from_above(value, width):
    return jnp.where(lane_ids() >= LANES - width, 0.0, turn(value, -width))


def level_change(cells, winds, width):
    long_cells = [from_below(v, width) for v in cells[ROWS - LO :]] + cells + [from_above(v, width) for v in cells[:HI]]
    long_winds = [from_below(winds[-1], width)] + winds + [from_above(winds[0], width)]
    return line_change(long_cells, long_winds)


def pack_kernel(mass_ref, send_ref, keep_ref):
    lower = is_even("gz")
    n = mass_ref.shape[0]
    zero = jnp.zeros((ROWS, LANES // 2), F32)
    for x in range(n // 2):
        for y in range(n):
            tiles = [
                jnp.concatenate([mass_ref[xx, y, z : z + ROWS], zero], axis=1) for xx in (x, x + n // 2) for z in (0, ROWS)
            ]
            low = by_quarter([turn(v, 32 * k) for k, v in enumerate(tiles)])
            high = by_quarter([turn(v, 32 * k - 32) for k, v in enumerate(tiles)])
            at = rows_of(x * n + y)
            keep_ref[at], send_ref[at] = order(low, high, lower)


def wind_kernel(wind_ref, out_ref):
    n = wind_ref.shape[1]
    for d in range(3):
        levels = wind_ref[d].reshape(n * n, 2 * ROWS).T * (1.0 / 12.0)
        out_ref[rows_of(d)] = jnp.concatenate([levels[:ROWS], levels[ROWS:]], axis=1)


def sides(axis, first_ref, second_ref):
    even, place = is_even(axis), lax.axis_index(axis)
    inner_low, inner_high = place > 0, place < lax.axis_size(axis) - 1

    def below(at):
        return jnp.where(inner_low, jnp.where(even, second_ref[at], first_ref[at]), 0.0)

    def above(at):
        return jnp.where(inner_high, jnp.where(even, first_ref[at], second_ref[at]), 0.0)

    return below, above


def by_parity(axis, body):
    even = is_even(axis)
    pl.when(even)(lambda: body(0, 1))
    pl.when(jnp.logical_not(even))(lambda: body(1, 0))


def merge_kernel(keep_ref, got_ref, own_wind_ref, got_wind_ref, block_ref, *messages):
    n = 8
    lower = is_even("gz")
    low = lane_ids() < 64

    def body(up, down):
        up_ref, down_ref = messages[up], messages[down]
        for x in range(n // 2):
            for y in range(n):
                at = rows_of(x * n + y)
                a, b = order(keep_ref[at], got_ref[at], lower)
                for xx, tile in (
                    (x, jnp.where(low, a, turn(b, 64))),
                    (x + n // 2, jnp.where(low, turn(a, 64), b)),
                ):
                    block_ref[rows_of(xx * n + y)] = tile
                    if y >= n - PAD_LO:
                        up_ref[rows_of(xx * PAD_LO + y - (n - PAD_LO))] = tile
                    if y < PAD_HI:
                        down_ref[rows_of(xx * PAD_HI + y)] = tile
        for d in range(3):
            a, b = order(own_wind_ref[rows_of(d)], got_wind_ref[rows_of(d)], lower)
            for half, tile in enumerate(
                (
                    by_quarter([a, turn(a, -32), turn(b, 64), turn(b, 32)]),
                    by_quarter([turn(a, -32), turn(a, -64), turn(b, 32), b]),
                )
            ):
                for ref, base in ((block_ref, n * n), (up_ref, n * PAD_LO), (down_ref, n * PAD_HI)):
                    ref[rows_of(base + 2 * d + half)] = tile

    by_parity("gy", body)


def side_kernel(n, parts, block_ref, first_ref, second_ref, own_change, pairs_ref, *messages):
    del own_change, pairs_ref
    tiles = groups(parts)[2]
    half = tiles // 2
    below, above = sides("gy", first_ref, second_ref)

    def body(up, down):
        for ref, start, wide, narrow_at, narrow, part in (
            (messages[up], n - PAD_LO, PAD_LO, n - LO, LO, half),
            (messages[down], 0, PAD_HI, 0, HI, 0),
        ):
            for x in range(wide):
                ref[rows_of(x * n, n)] = block_ref[rows_of((start + x) * n, n)]
            at = wide * n
            for x in range(narrow):
                xx = narrow_at + x
                ref[rows_of(at, LO)] = below(rows_of(xx * PAD_LO + PAD_LO - LO, LO))
                ref[rows_of(at + LO, HI)] = above(rows_of(xx * PAD_HI, HI))
                at += LINES
            for d in range(3):
                ref[rows_of(at, half)] = block_ref[rows_of(n * n + d * tiles + part, half)]
                at += half
            for side, base in ((below, n * PAD_LO), (above, n * PAD_HI)):
                ref[rows_of(at)] = side(rows_of(base + (tiles - 1 if part else 0)))
                ref[rows_of(at + 1, half)] = side(rows_of(base + tiles + part, half))
                at += 1 + half

    by_parity("gx", body)


def own_kernel(n, parts, block_ref, wind_x, wind_y, wind_z, change):
    width, deep, tiles = groups(parts)
    for d, out in enumerate((wind_x, wind_y, wind_z)):
        for x in range(n):
            tile = block_ref[rows_of(n * n + d * tiles + x // deep)]
            for y in range(n):
                out[rows_of(x * n + y)] = aim(tile, x, y, parts)
        spread(out, parts)

    @pl.loop(0, n)
    def _(x):
        cells = [block_ref[eight(x * n, k)] for k in range(ROWS)]
        winds = [wind_z[eight(x * n, k)] for k in range(ROWS)]
        for k, value in enumerate(level_change(cells, winds, width)):
            change[eight(x * n, k)] = value


def y_kernel(n, parts, block_ref, first_ref, second_ref, wind_y, own_change, *refs):
    width, deep, tiles = groups(parts)
    cell, change, wind_x, far_y, wind_z, halo_change = refs
    below, above = sides("gy", first_ref, second_ref)
    span, reach = n + PAD_LO + PAD_HI, n + LINES

    for x in range(n):
        cell[rows_of(x * span, PAD_LO)] = below(rows_of(x * PAD_LO, PAD_LO))
        cell[rows_of(x * span + PAD_LO, n)] = block_ref[rows_of(x * n, n)]
        cell[rows_of(x * span + PAD_LO + n, PAD_HI)] = above(rows_of(x * PAD_HI, PAD_HI))
    for d in range(3):
        for t in range(tiles):
            low, high = below(rows_of(n * PAD_LO + d * tiles + t)), above(rows_of(n * PAD_HI + d * tiles + t))
            for x in range(t * deep, (t + 1) * deep):
                if d == 1:
                    for y in range(LO + 1):
                        far_y[rows_of(x * (LINES + 2) + y)] = aim(low, x, n - LO - 1 + y, parts)
                    for y in range(HI + 1):
                        far_y[rows_of(x * (LINES + 2) + LO + 1 + y)] = aim(high, x, y, parts)
                else:
                    out = wind_z if d else wind_x
                    for y in range(LO):
                        out[rows_of(y * n + x)] = aim(low, x, n - LO + y, parts)
                    for y in range(HI):
                        out[rows_of((LO + y) * n + x)] = aim(high, x, y, parts)
    for out in (far_y, wind_x, wind_z):
        spread(out, parts)

    @pl.loop(0, LINES)
    def _(i):
        first = halo_line(i, n) + PAD_LO
        cells = [cell[eight(first, k, span)] for k in range(ROWS)]
        winds = [wind_z[eight(i * n, k)] for k in range(ROWS)]
        for k, value in enumerate(level_change(cells, winds, width)):
            halo_change[eight(i * n, k)] = value

    @pl.loop(0, n)
    def _(x):
        cells = [cell[rows_of(x * span + y)] for y in range(span)]
        far = [far_y[rows_of(x * (LINES + 2) + y)] for y in range(LINES + 2)]
        winds = far[: LO + 1] + [wind_y[rows_of(x * n + y)] for y in range(n)] + far[LO + 1 :]
        for y, value in enumerate(line_change(cells, winds)):
            if LO <= y < LO + n:
                value = value + own_change[rows_of(x * n + y - LO)]
            else:
                value = value + halo_change[rows_of((y if y < LO else y - n) * n + x)]
            change[rows_of(x * reach + y)] = value


def main_kernel(n, parts, *refs):
    cell, change, wind_x, wind_y, wind_z, halo_wind_x, far_wind_y, first_ref, second_ref, rate_ref, steps_ref = refs[:11]
    one, change_two, *out_refs = refs[11:15]
    far, side, far_wind_x, corner_wind_x, side_wind_y, side_wind_z, side_change, fallen = refs[15:]
    width, deep, tiles = groups(parts)
    half = tiles // 2
    west, east = sides("gx", first_ref, second_ref)
    span, reach = n + PAD_LO + PAD_HI, n + LINES

    for take, wide, narrow, far_at, side_at, far_from, side_from in (
        (west, PAD_LO, LO, 0, 0, 0, LO),
        (east, PAD_HI, HI, LO, LO, HI, 0),
    ):
        for i in range(narrow):
            far[rows_of((far_at + i) * n, n)] = take(rows_of((far_from + i) * n, n))
            line = (side_at + i) * reach
            corner = wide * n + i * LINES
            side[rows_of(line, LO)] = take(rows_of(corner, LO))
            side[rows_of(line + LO, n)] = take(rows_of((side_from + i) * n, n))
            side[rows_of(line + LO + n, HI)] = take(rows_of(corner + LO, HI))
        at = wide * n + narrow * LINES
        layers = range(n - narrow, n) if narrow == LO else range(narrow)
        wider = range(n - narrow - 1, n) if narrow == LO else range(narrow + 1)
        shift = half if narrow == LO else 0

        def winds_of(base, x):
            return take(rows_of(base + x // deep - shift))

        for i, x in enumerate(wider):
            tile = winds_of(at, x)
            for y in range(n):
                far_wind_x[rows_of((far_at + bool(far_at) + i) * n + y)] = aim(tile, x, y, parts)
        below, above = at + 3 * half, at + 3 * half + 1 + half
        x = wider[-1] if narrow == LO else wider[0]
        for y in range(LINES):
            tile = take(rows_of(below if y < LO else above))
            corner_wind_x[rows_of(bool(far_at) * LINES + y)] = aim(tile, x, n - LO + y if y < LO else y - LO, parts)
        for i, x in enumerate(layers):
            line = (side_at + i) * (n + 2)
            side_wind_y[rows_of(line)] = aim(winds_of(below + 1, x), x, n - 1, parts)
            side_wind_y[rows_of(line + n + 1)] = aim(winds_of(above + 1, x), x, 0, parts)
            for y in range(n):
                side_wind_y[rows_of(line + 1 + y)] = aim(winds_of(at + half, x), x, y, parts)
                side_wind_z[rows_of((side_at + i) * n + y)] = aim(winds_of(at + 2 * half, x), x, y, parts)

    for out in (far_wind_x, corner_wind_x, side_wind_y, side_wind_z):
        spread(out, parts)

    @pl.loop(0, LINES)
    def _(i):
        cells = [side[eight(i * reach + LO, k)] for k in range(ROWS)]
        winds = [side_wind_z[eight(i * n, k)] for k in range(ROWS)]
        for k, value in enumerate(level_change(cells, winds, width)):
            side_change[eight(i * n, k)] = value

    @pl.loop(0, LINES)
    def _(i):
        cells = [side[rows_of(i * reach + y)] for y in range(reach)]
        winds = [side_wind_y[rows_of(i * (n + 2) + y)] for y in range(n + 2)]
        for y, value in enumerate(line_change(cells, winds)):
            at = rows_of(i * n + y)
            side_change[at] = side_change[at] + value

    last = lax.axis_size("gx") - 1, lax.axis_size("gy") - 1

    def inside(axis, count, lower):
        place = lax.axis_index(axis)
        return jnp.where(place > 0 if lower else place < count, 1.0, 0.0)

    west_in, east_in = inside("gx", last[0], True), inside("gx", last[0], False)
    south_in, north_in = inside("gy", last[1], True), inside("gy", last[1], False)

    @pl.loop(0, n)
    def _(y):
        outer = [far[rows_of(i * n + y)] for i in range(LINES)]
        near = [side[rows_of(i * reach + LO + y)] for i in range(LINES)]
        cells = outer[:LO] + near[:LO] + [cell[rows_of(x * span + PAD_LO + y)] for x in range(n)] + near[LO:] + outer[LO:]
        winds = [far_wind_x[rows_of(i * n + y)] for i in range(LINES + 2)]
        winds = winds[: LO + 1] + [wind_x[rows_of(x * n + y)] for x in range(n)] + winds[LO + 1 :]
        for i, value in enumerate(line_change(cells, winds)):
            if LO <= i < LO + n:
                value = cells[i + LO] + (value + change[rows_of((i - LO) * reach + LO + y)])
            else:
                value = cells[i + LO] + (value + side_change[rows_of((i if i < LO else i - n) * n + y)])
                value = value * (west_in if i < LO else east_in)
            one[rows_of(i * reach + LO + y)] = value

    @pl.loop(0, LINES)
    def _(i):
        line = halo_line(i, n) + LO
        near = [side[rows_of(k * reach + line)] for k in range(LINES)]
        cells = near[:LO] + [cell[rows_of(x * span + LO + line)] for x in range(n)] + near[LO:]
        winds = [halo_wind_x[rows_of(i * n + x)] for x in range(n)]
        winds = [corner_wind_x[rows_of(i)]] + winds + [corner_wind_x[rows_of(LINES + i)]]
        keep = jnp.where(i < LO, south_in, north_in)
        for x, value in enumerate(line_change(cells, winds)):
            one[rows_of((x + LO) * reach + line)] = (cells[x + LO] + (value + change[rows_of(x * reach + line)])) * keep

    @pl.loop(0, n)
    def _(y):
        cells = [one[rows_of(x * reach + LO + y)] for x in range(reach)]
        winds = [far_wind_x[rows_of(LO * n + y)]] + [wind_x[rows_of(x * n + y)] for x in range(n)]
        winds += [far_wind_x[rows_of((LO + 1) * n + y)]]
        for x, value in enumerate(line_change(cells, winds)):
            change_two[rows_of(x * n + y)] = value

    @pl.loop(0, n)
    def _(x):
        cells = [one[rows_of((x + LO) * reach + y)] for y in range(reach)]
        winds = [far_wind_y[rows_of(x * (LINES + 2) + LO)]] + [wind_y[rows_of(x * n + y)] for y in range(n)]
        winds += [far_wind_y[rows_of(x * (LINES + 2) + LO + 1)]]
        for y, value in enumerate(line_change(cells, winds)):
            at = rows_of(x * n + y)
            change_two[at] = change_two[at] + value

    fall_half(n, parts, 0, one, change_two, wind_z, cell, rate_ref, steps_ref, out_refs, fallen)


def late_kernel(n, parts, one, change_two, wind_z, cell, rate_ref, steps_ref, *refs):
    fall_half(n, parts, n // 2, one, change_two, wind_z, cell, rate_ref, steps_ref, refs[:2], refs[2])


def fall_half(n, parts, begin, one, change_two, wind_z, cell, rate_ref, steps_ref, out_refs, fallen):
    width = groups(parts)[0]
    span, reach, half = n + PAD_LO + PAD_HI, n + LINES, n // 2

    @pl.loop(0, half)
    def _(i):
        x = begin + i
        cells = [one[eight((x + LO) * reach + LO, k)] for k in range(ROWS)]
        winds = [wind_z[eight(x * n, k)] for k in range(ROWS)]
        for k, value in enumerate(level_change(cells, winds, width)):
            value = cells[k] + (value + change_two[eight(x * n, k)])
            fallen[eight(i * n, k)] = 0.5 * cell[eight(x * span + PAD_LO, k)] + 0.5 * value

    bins = LANES // 2 // parts
    ids = lax.axis_index("gz") * bins + lane_ids() % bins
    rates, steps = [
        pick(jnp.broadcast_to(jnp.concatenate([ref[...]] * 2, axis=1), (ROWS, LANES)), ids) for ref in (rate_ref, steps_ref)
    ]

    def fall(block, carry):
        columns, rain = carry
        columns = [column + [from_above(v, width) for v in column[:AHEAD]] for column in columns]
        rain = list(rain)
        for s in range(AHEAD):
            rate = jnp.where(block * AHEAD + s < steps, rates, 0.0)
            for i, column in enumerate(columns):
                rain[i] = rain[i] + rate * column[0]
                columns[i] = [v + rate * (u - v) for v, u in zip(column, column[1:])]
        return columns, rain

    columns = [[fallen[eight(i * n, k)] for k in range(ROWS)] for i in range(half)]
    columns, rain = lax.fori_loop(0, SUBS // AHEAD, fall, (columns, [jnp.zeros((ROWS, LANES), F32)] * half))
    for i, column in enumerate(columns):
        for k in range(ROWS):
            fallen[eight(i * n, k)] = column[k]

    if parts == 2:
        send_ref, keep_ref = out_refs
        lower = is_even("gz")
        low = lane_ids() < 64
        count = half * n // 2
        for c in range(count):
            a, b = fallen[rows_of(c)], fallen[rows_of(count + c)]
            at = rows_of(c)
            keep_ref[at], send_ref[at] = order(jnp.where(low, a, turn(b, 64)), jnp.where(low, turn(a, 64), b), lower)
        value = by_quarter([turn(rain[i], 32 * i) for i in range(4)])
        keep_ref[rows_of(count)] = value
        send_ref[rows_of(count)] = value
    else:
        settled_ref, rain_ref = out_refs
        settled_ref[...] = fallen[...]
        for i in range(half):
            rain_ref[rows_of(i)] = rain[i]


def matrix_kernel(bins, gain_ref, loss_ref, pairs_ref, lost_ref, wide, tall):
    zero = jnp.zeros((bins, LANES - bins), F32)
    shifts = bins // 2

    @pl.loop(0, bins)
    def _(i):
        rows = gain_ref[pl.ds(i * bins, bins)].astype(F32)
        rows = jnp.concatenate([rows, zero], axis=1)
        wide[pl.ds(i * 2 * bins, bins)] = rows
        wide[pl.ds(i * 2 * bins + bins, bins)] = rows
        tall[pl.ds(i * bins, bins)] = rows

        @pl.when(i < shifts)
        def _():
            tall[pl.ds((i + bins) * bins, bins)] = rows

    for d in range(shifts + 1):
        rows = wide[pl.ds(d, bins, stride=2 * bins + 1)]
        if 0 < d < shifts:
            rows = rows + tall[pl.ds(d * bins, bins, stride=bins + 1)]
        pairs_ref[pl.ds(d * LANES, bins)] = rows.astype(jnp.bfloat16)
        pairs_ref[pl.ds(d * LANES + bins, bins)] = pltpu.roll(rows, bins, 1).astype(jnp.bfloat16)
    rows = jnp.concatenate([loss_ref[...].astype(F32), zero], axis=1)
    lost_ref[pl.ds(0, bins)] = rows.astype(jnp.bfloat16)
    lost_ref[pl.ds(bins, bins)] = pltpu.roll(rows, bins, 1).astype(jnp.bfloat16)


def breakup_rows(mass, pairs_ref, lost_ref, products):
    bins = LANES // 2
    count = mass.shape[0]
    lanes = lane_ids()
    rounded = mass.astype(jnp.bfloat16)
    wide = rounded.astype(F32)
    gained = None
    shifts = bins // 2 + 1
    for begin in range(0, shifts, 12):
        end = min(begin + 12, shifts)
        for d in range(begin, end):
            ids = lanes // bins * bins + (lanes + d) % bins
            for r in range(0, count, 2 * ROWS):
                halves = [wide[r + ROWS * k : r + ROWS * (k + 1)] for k in range(2)]
                halves = [v * pick(v, ids) if d else v * v for v in halves]
                both = jnp.concatenate(halves, axis=0).astype(jnp.bfloat16)
                products[pl.ds(r, 2 * ROWS), d * LANES : (d + 1) * LANES] = both
        part = jnp.dot(
            products[pl.ds(0, count), begin * LANES : end * LANES],
            pairs_ref[pl.ds(begin * LANES, (end - begin) * LANES)],
            preferred_element_type=F32,
        )
        gained = part if gained is None else gained + part
    loss = jnp.dot(rounded, lost_ref[...], preferred_element_type=F32)
    return mass + gained - mass * loss


def breakup_half(n, keep_ref, got_ref, pairs_ref, lost_ref, columns, products):
    first = is_even("gz")
    count = n * n // 4
    for c in range(count):
        a, b = order(keep_ref[rows_of(c)], got_ref[rows_of(c)], first)
        columns[rows_of(c)] = by_quarter([a, turn(b, 32), turn(a, 32), turn(b, 64)])
        columns[rows_of(count + c)] = by_quarter([turn(a, -64), turn(b, -32), turn(a, -32), b])
    a, b = order(keep_ref[rows_of(count)], got_ref[rows_of(count)], first)
    a, b = [jnp.where(first, v[: n // 2], v[n // 2 :]) for v in (a, b)]
    columns[...] = breakup_rows(columns[...], pairs_ref, lost_ref, products)
    return [jnp.concatenate([a[:, 32 * i : 32 * i + 32], b[:, 32 * i : 32 * i + 32]], axis=1) for i in range(4)]


def breakup_first_kernel(n, keep_ref, got_ref, pairs_ref, lost_ref, columns, rain_ref, products):
    for i, value in enumerate(breakup_half(n, keep_ref, got_ref, pairs_ref, lost_ref, columns, products)):
        rain_ref[i] = value


def breakup_last_kernel(
    n, keep_ref, got_ref, pairs_ref, lost_ref, early, early_rain, mass_out, rain_out, columns, products, mass, rain, sems
):
    half = n // 2

    def lay_out(ref, begin):
        for x in range(half):
            for y in range(n):
                value = ref[rows_of(x * n + y)]
                mass[begin + x, y, 0:ROWS] = value[:, :64]
                mass[begin + x, y, ROWS : 2 * ROWS] = value[:, 64:]
        copy = pltpu.make_async_copy(mass.at[pl.ds(begin, half)], mass_out.at[pl.ds(begin, half)], sems.at[begin // half])
        copy.start()
        return copy

    copies = [lay_out(early, 0)]
    late_rain = breakup_half(n, keep_ref, got_ref, pairs_ref, lost_ref, columns, products)
    for i in range(half):
        rain[i] = early_rain[i]
        rain[half + i] = late_rain[i]
    rain_copy = pltpu.make_async_copy(rain, rain_out, sems.at[2])
    rain_copy.start()
    copies.append(lay_out(columns, half))
    for copy in copies + [rain_copy]:
        copy.wait()


def breakup_plain_kernel(mass_ref, pairs_ref, lost_ref, out_ref, products):
    count = products.shape[0]

    @pl.loop(0, mass_ref.shape[0] // count)
    def _(i):
        start = pl.multiple_of(i * count, count)
        out_ref[pl.ds(start, count)] = breakup_rows(mass_ref[pl.ds(start, count)], pairs_ref, lost_ref, products)


def shape(*dims, dtype=F32):
    return jax.ShapeDtypeStruct(dims, dtype)


def tiles_of(count):
    return shape(count * ROWS, LANES)


def call(kernel, outs, args, scratch=(), micros=1.0, out_place=pltpu.VMEM, copies=0):
    scratch = [pltpu.VMEM(s.shape, s.dtype) for s in scratch]
    if copies:
        scratch.append(pltpu.SemaphoreType.DMA((copies,)))
    return pl.pallas_call(
        kernel,
        out_shape=outs,
        in_specs=[VMEM] * len(args),
        out_specs=jax.tree.map(lambda _: pl.BlockSpec(memory_space=out_place), outs),
        scratch_shapes=scratch,
        compiler_params=pltpu.CompilerParams(vmem_limit_bytes=40 << 20),
        cost_estimate=pl.CostEstimate(
            flops=int(micros * 1.1e9), bytes_accessed=int(micros * 3.6e6), transcendentals=0
        ),
    )(*args)


def swap_neighbours(axis, begin, message):
    axes = ("gx", "gy")
    sizes = [lax.axis_size(a) for a in axes]
    along = axes.index(axis)

    def partner(place, start, count):
        to = start + ((place - start) ^ 1)
        return to if start <= place and to < count else place

    pairs = []
    for here in range(sizes[0] * sizes[1]):
        place = list(divmod(here, sizes[1]))
        to = partner(place[along], begin, sizes[along])
        if to == place[along]:
            place[1 - along] = partner(place[1 - along], 0, sizes[1 - along])
        place[along] = to
        pairs.append((here, place[0] * sizes[1] + place[1]))
    return lax.ppermute(message, axes, pairs)


def per_device(bin_mass, courant, sub_courant, fall_steps, frag_gain, collide):
    nx, ny, nz, bins = bin_mass.shape
    n = nx
    parts = lax.axis_size("gz")
    gz, gy = lax.axis_index("gz"), lax.axis_index("gy")
    width = bins // parts
    tiles = groups(parts)[2]
    winds = 3 * tiles

    pair_rows = (bins // 2 + 1) * LANES
    pairs, lost = call(
        functools.partial(matrix_kernel, bins),
        (shape(pair_rows, LANES, dtype=jnp.bfloat16), shape(LANES, LANES, dtype=jnp.bfloat16)),
        (frag_gain, collide),
        [shape(2 * bins * bins, LANES), shape(3 * bins * bins // 2, LANES)],
        micros=1.4,
    )

    if parts == 2:
        half = tiles_of(n * n // 2)
        send, keep = call(pack_kernel, (half, half), (bin_mass,), micros=0.3)
        got = lax.ppermute(send, "gz", [(0, 1), (1, 0)])
        own_wind = call(wind_kernel, tiles_of(3), (courant,), micros=0.1)
        got_wind = lax.ppermute(own_wind, "gz", [(0, 1), (1, 0)])
        message = tiles_of(n * PAD_LO + winds)
        block, first, second = call(
            merge_kernel, (tiles_of(n * n + winds), message, message), (keep, got, own_wind, got_wind), micros=0.2
        )
    else:
        split = bin_mass.reshape(nx, ny, nz // ROWS, ROWS, parts, width).transpose(4, 0, 1, 3, 2, 5)
        split = lax.all_to_all(split, "gz", split_axis=0, concat_axis=0, tiled=True)
        cube = split.transpose(1, 2, 3, 0, 4, 5).reshape(n, n, ROWS, LANES)
        air = courant.reshape(3, nx, ny, nz // ROWS, ROWS).transpose(0, 4, 3, 1, 2) * (1.0 / 12.0)
        air = lax.all_gather(air, "gz").reshape(parts, 3, ROWS, nz // ROWS, tiles, nx // tiles, ny)
        air = air.transpose(1, 4, 2, 0, 3, 5, 6).reshape(-1, LANES)
        block = jnp.concatenate([cube.reshape(-1, LANES), air])
        up = jnp.concatenate([cube[:, n - PAD_LO :].reshape(-1, LANES), air])
        down = jnp.concatenate([cube[:, :PAD_HI].reshape(-1, LANES), air])
        down = jnp.pad(down, ((0, up.shape[0] - down.shape[0]), (0, 0)))
        first, second = order(up, down, gy % 2 == 0)

    from_y = swap_neighbours("gy", 0, first), swap_neighbours("gy", 1, second)
    wind_x, wind_y, wind_z, own_change = call(
        functools.partial(own_kernel, n, parts), [tiles_of(n * n)] * 4, (block,), micros=1.7
    )
    message = tiles_of(PAD_LO * n + LO * LINES + 3 * tiles // 2 + 2 + tiles)
    first, second = call(
        functools.partial(side_kernel, n, parts), (message, message), (block, *from_y, own_change, pairs), micros=0.1
    )
    second = swap_neighbours("gx", 1, second)
    first = swap_neighbours("gx", 0, first)
    cell, change, halo_wind_x, far_wind_y = call(
        functools.partial(y_kernel, n, parts),
        [tiles_of(n * (n + PAD_LO + PAD_HI)), tiles_of(n * (n + LINES)), tiles_of(LINES * n), tiles_of(n * (LINES + 2))],
        (block, *from_y, wind_y, own_change),
        [tiles_of(LINES * n)] * 2,
        micros=2.0,
    )
    reach, half = n + LINES, n // 2
    fall = sub_courant.reshape(1, bins), fall_steps.reshape(1, bins)
    message = [tiles_of(n * half // 2 + 1)] * 2 if parts == 2 else [tiles_of(n * half), tiles_of(half)]
    one, change_two, *early = call(
        functools.partial(main_kernel, n, parts),
        [tiles_of(reach * reach), tiles_of(n * n)] + message,
        (cell, change, wind_x, wind_y, wind_z, halo_wind_x, far_wind_y, first, second, *fall),
        [
            tiles_of(count)
            for count in (
                LINES * n,
                LINES * reach,
                (LINES + 2) * n,
                2 * LINES,
                LINES * (n + 2),
                LINES * n,
                LINES * n,
                n * half,
            )
        ],
        micros=5.0,
    )
    if parts == 2:
        early_got = lax.ppermute(early[0], "gz", [(0, 1), (1, 0)])
    late = call(
        functools.partial(late_kernel, n, parts),
        message,
        (one, change_two, wind_z, cell, *fall),
        [tiles_of(n * half)],
    )

    products = shape(n * half * ROWS, pair_rows, dtype=jnp.bfloat16)
    if parts == 2:
        late_got = lax.ppermute(late[0], "gz", [(0, 1), (1, 0)])
        early = call(
            functools.partial(breakup_first_kernel, n),
            [tiles_of(n * half), shape(half, ny // parts, bins)],
            (early[1], early_got, pairs, lost),
            [products],
            micros=1.5,
        )
        outs = [shape(nx, ny, nz, bins), shape(nx, ny // parts, bins)]
        return tuple(
            call(
                functools.partial(breakup_last_kernel, n),
                outs,
                (late[1], late_got, pairs, lost, *early),
                [tiles_of(n * half), products, *outs],
                micros=1.5,
                out_place=pl.ANY,
                copies=3,
            )
        )

    settled, rain = [jnp.concatenate(halves) for halves in zip(early, late)]
    rain = rain.reshape(nx, ny, LANES)[:, :, :width]
    rain = lax.all_to_all(rain, "gz", split_axis=1, concat_axis=2, tiled=True)
    settled = settled.reshape(nx, ny, ROWS, parts, nz // ROWS, width).transpose(3, 0, 1, 4, 2, 5)
    settled = lax.all_to_all(settled, "gz", split_axis=0, concat_axis=0, tiled=True)
    settled = settled.transpose(1, 2, 3, 4, 0, 5).reshape(nx * ny, nz // ROWS, ROWS, bins)
    paired = settled.transpose(0, 2, 1, 3).reshape(-1, LANES)
    updated = call(breakup_plain_kernel, tiles_of(n * n), (paired, pairs, lost), [products], micros=3.0)
    updated = updated.reshape(nx, ny, ROWS, nz // ROWS, bins).transpose(0, 1, 3, 2, 4).reshape(nx, ny, nz, bins)
    return updated, rain


def solution(mesh):
    in_specs = (P("gx", "gy", "gz", None), P(None, "gx", "gy", "gz"), P(), P(), P(), P())
    out_specs = (P("gx", "gy", "gz", None), P("gx", ("gy", "gz"), None))
    return jax.shard_map(per_device, mesh=mesh, in_specs=in_specs, out_specs=out_specs, check_vma=False)
```

```python
import functools

import jax
import jax.numpy as jnp
from jax import lax
from jax.experimental import pallas as pl
from jax.experimental.pallas import tpu as pltpu
from jax.sharding import PartitionSpec as P

SUBS = 24
EPS = 1e-06
LO, HI = 3, 2
PAD_LO, PAD_HI = 2 * LO, 2 * HI
LINES = LO + HI
ROWS, LANES = 8, 128
AHEAD = 4
F32 = jnp.float32
VMEM = pl.BlockSpec(memory_space=pltpu.VMEM)


def lane_ids():
    return lax.broadcasted_iota(jnp.int32, (ROWS, LANES), 1)


def pick(tile, ids):
    return jnp.take_along_axis(tile, ids, axis=1, mode="promise_in_bounds")


def turn(tile, lanes):
    lanes %= LANES
    return pltpu.roll(tile, lanes, 1) if lanes else tile


def rows_of(first, count=1):
    return pl.ds(first * ROWS, count * ROWS)


def eight(first, level, step=1):
    return pl.ds(first * ROWS + level, ROWS, stride=step * ROWS)


def order(a, b, straight):
    return jnp.where(straight, a, b), jnp.where(straight, b, a)


def is_even(axis):
    return lax.axis_index(axis) % 2 == 0


def by_quarter(parts):
    quarter = lane_ids() // (LANES // 4)
    return jnp.where(quarter < 2, jnp.where(quarter == 0, parts[0], parts[1]), jnp.where(quarter == 2, parts[2], parts[3]))


def groups(parts):
    width = LANES // (2 * parts)
    return width, width // ROWS, ROWS * ROWS // width


def spread(tile, x, y, parts):
    width, deep, _ = groups(parts)
    return pick(turn(tile, -(x % deep * ROWS + y)), lane_ids() // width * width)


def halo_line(i, n):
    return jnp.where(i < LO, i - LO, i - LO + n)


def line_change(cells, winds):
    return changes(line_fluxes(cells, winds))


def changes(fluxes):
    return [a - b for a, b in zip(fluxes, fluxes[1:])]


def line_fluxes(cells, winds):
    first = [b - a for a, b in zip(cells, cells[1:])]
    twice = [d + d for d in first]
    second = [b - a for a, b in zip(first, first[1:])]
    third = [a - b for a, b in zip(second, second[1:])]
    curved = [(13.0 / 3.0) * (c * c) + 4.0 * EPS for c in second]
    fluxes = []
    for j in range(len(cells) - 4):
        left = twice[j + 1] + second[j]
        mid = first[j + 1] + first[j + 2]
        right = twice[j + 2] - second[j + 2]
        e0 = curved[j] + left * left
        e1 = curved[j + 1] + mid * mid
        e2 = curved[j + 2] + right * right
        e0 = e0 * e0
        e1 = e1 * e1
        e2 = e2 * e2
        e0 = 3.0 * e0
        e2_twice = e2 + e2
        top = e1 * (e2_twice * third[j] + e0 * third[j + 1])
        low = e1 * (e2 + e0) + e0 * e2_twice
        inverse = pl.reciprocal(low, approx=True)
        estimate = 6.0 * cells[j + 2] + (first[j + 1] + twice[j + 2]) + top * inverse
        fluxes.append((winds[j] + winds[j + 1]) * estimate)
    return fluxes


def from_below(value, width):
    return jnp.where(lane_ids() < width, 0.0, turn(value, width))


def from_above(value, width):
    return jnp.where(lane_ids() >= LANES - width, 0.0, turn(value, -width))


def level_change(cells, winds, width):
    long_cells = [from_below(v, width) for v in cells[ROWS - LO :]] + cells + [from_above(v, width) for v in cells[:HI]]
    long_winds = [from_below(winds[-1], width)] + winds + [from_above(winds[0], width)]
    return line_change(long_cells, long_winds)


def pack_kernel(mass_ref, send_ref, keep_ref):
    lower = is_even("gz")
    n = mass_ref.shape[0]
    zero = jnp.zeros((ROWS, LANES // 2), F32)
    for x in range(n // 2):
        for y in range(n):
            tiles = [
                jnp.concatenate([mass_ref[xx, y, z : z + ROWS], zero], axis=1) for xx in (x, x + n // 2) for z in (0, ROWS)
            ]
            low = by_quarter([turn(v, 32 * k) for k, v in enumerate(tiles)])
            high = by_quarter([turn(v, 32 * k - 32) for k, v in enumerate(tiles)])
            at = rows_of(x * n + y)
            keep_ref[at], send_ref[at] = order(low, high, lower)


def wind_kernel(wind_ref, out_ref):
    n = wind_ref.shape[1]
    for d in range(3):
        levels = wind_ref[d].reshape(n * n, 2 * ROWS).T * (1.0 / 12.0)
        out_ref[rows_of(d)] = jnp.concatenate([levels[:ROWS], levels[ROWS:]], axis=1)


def sides(axis, first_ref, second_ref):
    even, place = is_even(axis), lax.axis_index(axis)
    inner_low, inner_high = place > 0, place < lax.axis_size(axis) - 1

    def below(at):
        return jnp.where(inner_low, jnp.where(even, second_ref[at], first_ref[at]), 0.0)

    def above(at):
        return jnp.where(inner_high, jnp.where(even, first_ref[at], second_ref[at]), 0.0)

    return below, above


def by_parity(axis, body):
    even = is_even(axis)
    pl.when(even)(lambda: body(0, 1))
    pl.when(jnp.logical_not(even))(lambda: body(1, 0))


def merge_kernel(keep_ref, got_ref, own_wind_ref, got_wind_ref, block_ref, *messages):
    n = 8
    lower = is_even("gz")
    low = lane_ids() < 64

    def body(up, down):
        up_ref, down_ref = messages[up], messages[down]
        for x in range(n // 2):
            for y in range(n):
                at = rows_of(x * n + y)
                a, b = order(keep_ref[at], got_ref[at], lower)
                for xx, tile in (
                    (x, jnp.where(low, a, turn(b, 64))),
                    (x + n // 2, jnp.where(low, turn(a, 64), b)),
                ):
                    block_ref[rows_of(xx * n + y)] = tile
                    if y >= n - PAD_LO:
                        up_ref[rows_of(xx * PAD_LO + y - (n - PAD_LO))] = tile
                    if y < PAD_HI:
                        down_ref[rows_of(xx * PAD_HI + y)] = tile
        for d in range(3):
            a, b = order(own_wind_ref[rows_of(d)], got_wind_ref[rows_of(d)], lower)
            for half, tile in enumerate(
                (
                    by_quarter([a, turn(a, -32), turn(b, 64), turn(b, 32)]),
                    by_quarter([turn(a, -32), turn(a, -64), turn(b, 32), b]),
                )
            ):
                for ref, base in ((block_ref, n * n), (up_ref, n * PAD_LO), (down_ref, n * PAD_HI)):
                    ref[rows_of(base + 2 * d + half)] = tile

    by_parity("gy", body)


def side_kernel(n, parts, block_ref, first_ref, second_ref, own_change, pairs_ref, *messages):
    del own_change, pairs_ref
    tiles = groups(parts)[2]
    half = tiles // 2
    below, above = sides("gy", first_ref, second_ref)

    def body(up, down):
        for ref, start, wide, narrow_at, narrow, part in (
            (messages[up], n - PAD_LO, PAD_LO, n - LO, LO, half),
            (messages[down], 0, PAD_HI, 0, HI, 0),
        ):
            for x in range(wide):
                ref[rows_of(x * n, n)] = block_ref[rows_of((start + x) * n, n)]
            at = wide * n
            for x in range(narrow):
                xx = narrow_at + x
                ref[rows_of(at, LO)] = below(rows_of(xx * PAD_LO + PAD_LO - LO, LO))
                ref[rows_of(at + LO, HI)] = above(rows_of(xx * PAD_HI, HI))
                at += LINES
            for d in range(3):
                ref[rows_of(at, half)] = block_ref[rows_of(n * n + d * tiles + part, half)]
                at += half
            for side, base in ((below, n * PAD_LO), (above, n * PAD_HI)):
                ref[rows_of(at)] = side(rows_of(base + (tiles - 1 if part else 0)))
                ref[rows_of(at + 1, half)] = side(rows_of(base + tiles + part, half))
                at += 1 + half

    by_parity("gx", body)


def own_kernel(n, parts, block_ref, wind_x, wind_y, wind_z, change):
    width, deep, tiles = groups(parts)
    for d, out in enumerate((wind_x, wind_y, wind_z)):
        for x in range(n):
            tile = block_ref[rows_of(n * n + d * tiles + x // deep)]
            for y in range(n):
                out[rows_of(x * n + y)] = spread(tile, x, y, parts)

    @pl.loop(0, n)
    def _(x):
        cells = [block_ref[eight(x * n, k)] for k in range(ROWS)]
        winds = [wind_z[eight(x * n, k)] for k in range(ROWS)]
        for k, value in enumerate(level_change(cells, winds, width)):
            change[eight(x * n, k)] = value


def y_kernel(n, parts, block_ref, first_ref, second_ref, wind_y, own_change, *refs):
    width, deep, tiles = groups(parts)
    cell, change, wind_x, far_y, wind_z, halo_change = refs
    below, above = sides("gy", first_ref, second_ref)
    span, reach = n + PAD_LO + PAD_HI, n + LINES

    for x in range(n):
        cell[rows_of(x * span, PAD_LO)] = below(rows_of(x * PAD_LO, PAD_LO))
        cell[rows_of(x * span + PAD_LO, n)] = block_ref[rows_of(x * n, n)]
        cell[rows_of(x * span + PAD_LO + n, PAD_HI)] = above(rows_of(x * PAD_HI, PAD_HI))
    for d in range(3):
        for t in range(tiles):
            low, high = below(rows_of(n * PAD_LO + d * tiles + t)), above(rows_of(n * PAD_HI + d * tiles + t))
            for x in range(t * deep, (t + 1) * deep):
                if d == 1:
                    for y in range(LO + 1):
                        far_y[rows_of(x * (LINES + 2) + y)] = spread(low, x, n - LO - 1 + y, parts)
                    for y in range(HI + 1):
                        far_y[rows_of(x * (LINES + 2) + LO + 1 + y)] = spread(high, x, y, parts)
                else:
                    out = wind_z if d else wind_x
                    for y in range(LO):
                        out[rows_of(y * n + x)] = spread(low, x, n - LO + y, parts)
                    for y in range(HI):
                        out[rows_of((LO + y) * n + x)] = spread(high, x, y, parts)

    @pl.loop(0, LINES)
    def _(i):
        first = halo_line(i, n) + PAD_LO
        cells = [cell[eight(first, k, span)] for k in range(ROWS)]
        winds = [wind_z[eight(i * n, k)] for k in range(ROWS)]
        for k, value in enumerate(level_change(cells, winds, width)):
            halo_change[eight(i * n, k)] = value

    @pl.loop(0, n)
    def _(x):
        cells = [cell[rows_of(x * span + y)] for y in range(span)]
        far = [far_y[rows_of(x * (LINES + 2) + y)] for y in range(LINES + 2)]
        winds = far[: LO + 1] + [wind_y[rows_of(x * n + y)] for y in range(n)] + far[LO + 1 :]
        for y, value in enumerate(line_change(cells, winds)):
            if LO <= y < LO + n:
                value = value + own_change[rows_of(x * n + y - LO)]
            else:
                value = value + halo_change[rows_of((y if y < LO else y - n) * n + x)]
            change[rows_of(x * reach + y)] = value


def inside(axis):
    place = lax.axis_index(axis)
    return [jnp.where(ok, 1.0, 0.0) for ok in (place > 0, place < lax.axis_size(axis) - 1)]


def inner_kernel(n, parts, cell, change, wind_x, halo_wind_x, wind_y, far_wind_y, wind_z, one, edge, second):
    width = groups(parts)[0]
    span, reach = n + PAD_LO + PAD_HI, n + LINES
    begin, end = LO, n - HI
    south_in, north_in = inside("gy")

    def line(at, winds, keep):
        cells = [cell[rows_of(x * span + LO + at)] for x in range(n)]
        fluxes = line_fluxes(cells, winds)
        edge[rows_of(at)] = fluxes[0]
        edge[rows_of(reach + at)] = fluxes[-1]
        for i, value in enumerate(changes(fluxes)):
            x = begin + i
            value = cells[x] + (value + change[rows_of(x * reach + at)])
            one[rows_of(i * reach + at)] = value if keep is None else value * keep

    @pl.loop(0, n)
    def _(y):
        line(LO + y, [wind_x[rows_of(x * n + y)] for x in range(begin - 1, end + 1)], None)

    @pl.loop(0, LINES)
    def _(i):
        winds = [halo_wind_x[rows_of(i * n + x)] for x in range(begin - 1, end + 1)]
        line(halo_line(i, n) + LO, winds, jnp.where(i < LO, south_in, north_in))

    @pl.loop(0, end - begin)
    def _(i):
        second_y_z(n, width, begin + i, one, i, wind_y, far_wind_y, wind_z, second, i)


def second_y_z(n, width, x, one, one_x, wind_y, far_wind_y, wind_z, second, second_x):
    reach = n + LINES
    cells = [one[rows_of(one_x * reach + y)] for y in range(reach)]
    winds = [far_wind_y[rows_of(x * (LINES + 2) + LO)]] + [wind_y[rows_of(x * n + y)] for y in range(n)]
    winds += [far_wind_y[rows_of(x * (LINES + 2) + LO + 1)]]
    for y, value in enumerate(line_change(cells, winds)):
        second[rows_of(second_x * n + y)] = value
    cells = [one[eight(one_x * reach + LO, k)] for k in range(ROWS)]
    winds = [wind_z[eight(x * n, k)] for k in range(ROWS)]
    for k, value in enumerate(level_change(cells, winds, width)):
        at = eight(second_x * n, k)
        second[at] = second[at] + value


def main_kernel(n, parts, *refs):
    cell, change, wind_x, wind_y, wind_z, halo_wind_x, far_wind_y, inner, edge, inner_second = refs[:10]
    second_ref, first_ref, rate_ref, steps_ref = refs[10:14]
    one, far_wind_x, *out_refs = refs[14:18]
    far, side, corner_wind_x, side_wind_y, side_wind_z, side_change, second, fallen = refs[18:]
    width, deep, tiles = groups(parts)
    half = tiles // 2
    west, east = sides("gx", first_ref, second_ref)
    span, reach = n + PAD_LO + PAD_HI, n + LINES

    for take, wide, narrow, far_at, side_at, far_from, side_from in (
        (west, PAD_LO, LO, 0, 0, 0, LO),
        (east, PAD_HI, HI, LO, LO, HI, 0),
    ):
        for i in range(narrow):
            far[rows_of((far_at + i) * n, n)] = take(rows_of((far_from + i) * n, n))
            line = (side_at + i) * reach
            corner = wide * n + i * LINES
            side[rows_of(line, LO)] = take(rows_of(corner, LO))
            side[rows_of(line + LO, n)] = take(rows_of((side_from + i) * n, n))
            side[rows_of(line + LO + n, HI)] = take(rows_of(corner + LO, HI))
        at = wide * n + narrow * LINES
        layers = range(n - narrow, n) if narrow == LO else range(narrow)
        wider = range(n - narrow - 1, n) if narrow == LO else range(narrow + 1)
        shift = half if narrow == LO else 0

        def winds_of(base, x):
            return take(rows_of(base + x // deep - shift))

        for i, x in enumerate(wider):
            tile = winds_of(at, x)
            for y in range(n):
                far_wind_x[rows_of((far_at + bool(far_at) + i) * n + y)] = spread(tile, x, y, parts)
        below, above = at + 3 * half, at + 3 * half + 1 + half
        x = wider[-1] if narrow == LO else wider[0]
        for y in range(LINES):
            tile = take(rows_of(below if y < LO else above))
            corner_wind_x[rows_of(bool(far_at) * LINES + y)] = spread(tile, x, n - LO + y if y < LO else y - LO, parts)
        for i, x in enumerate(layers):
            line = (side_at + i) * (n + 2)
            side_wind_y[rows_of(line)] = spread(winds_of(below + 1, x), x, n - 1, parts)
            side_wind_y[rows_of(line + n + 1)] = spread(winds_of(above + 1, x), x, 0, parts)
            for y in range(n):
                side_wind_y[rows_of(line + 1 + y)] = spread(winds_of(at + half, x), x, y, parts)
                side_wind_z[rows_of((side_at + i) * n + y)] = spread(winds_of(at + 2 * half, x), x, y, parts)

    @pl.loop(0, LINES)
    def _(i):
        cells = [side[eight(i * reach + LO, k)] for k in range(ROWS)]
        winds = [side_wind_z[eight(i * n, k)] for k in range(ROWS)]
        for k, value in enumerate(level_change(cells, winds, width)):
            side_change[eight(i * n, k)] = value

    @pl.loop(0, LINES)
    def _(i):
        cells = [side[rows_of(i * reach + y)] for y in range(reach)]
        winds = [side_wind_y[rows_of(i * (n + 2) + y)] for y in range(n + 2)]
        for y, value in enumerate(line_change(cells, winds)):
            at = rows_of(i * n + y)
            side_change[at] = side_change[at] + value

    west_in, east_in = inside("gx")
    south_in, north_in = inside("gy")
    begin, end = LO, n - HI
    one[rows_of((begin + LO) * reach, (end - begin) * reach)] = inner[...]

    @pl.loop(0, n)
    def _(y):
        outer = [far[rows_of(i * n + y)] for i in range(LINES)]
        near = [side[rows_of(i * reach + LO + y)] for i in range(LINES)]
        cells = outer[:LO] + near[:LO] + [cell[rows_of(x * span + PAD_LO + y)] for x in range(n)] + near[LO:] + outer[LO:]
        winds = [far_wind_x[rows_of(i * n + y)] for i in range(LINES + 2)]
        winds = winds[: LO + 1] + [wind_x[rows_of(x * n + y)] for x in range(n)] + winds[LO + 1 :]
        low = line_fluxes(cells[: PAD_LO + begin + 1], winds[: LO + 1 + begin]) + [edge[rows_of(LO + y)]]
        high = [edge[rows_of(reach + LO + y)]] + line_fluxes(cells[PAD_LO + end - HI :], winds[LO + 1 + end :])
        values = dict(zip(range(-LO, begin), changes(low))) | dict(zip(range(end, n + HI), changes(high)))
        for x, value in values.items():
            mass = cells[PAD_LO + x]
            if 0 <= x < n:
                value = mass + (value + change[rows_of(x * reach + LO + y)])
            else:
                value = mass + (value + side_change[rows_of((x + LO if x < 0 else x + LO - n) * n + y)])
                value = value * (west_in if x < 0 else east_in)
            one[rows_of((x + LO) * reach + LO + y)] = value

    @pl.loop(0, LINES)
    def _(i):
        line = halo_line(i, n) + LO
        near = [side[rows_of(k * reach + line)] for k in range(LINES)]
        cells = near[:LO] + [cell[rows_of(x * span + LO + line)] for x in range(n)] + near[LO:]
        winds = [halo_wind_x[rows_of(i * n + x)] for x in range(n)]
        winds = [corner_wind_x[rows_of(i)]] + winds + [corner_wind_x[rows_of(LINES + i)]]
        keep = jnp.where(i < LO, south_in, north_in)
        low = line_fluxes(cells[: LO + begin + 1], winds[: begin + 1]) + [edge[rows_of(line)]]
        high = [edge[rows_of(reach + line)]] + line_fluxes(cells[LO + end - HI :], winds[end + 1 :])
        values = dict(zip(range(begin), changes(low))) | dict(zip(range(end, n), changes(high)))
        for x, value in values.items():
            one[rows_of((x + LO) * reach + line)] = (cells[x + LO] + (value + change[rows_of(x * reach + line)])) * keep

    fall_half(
        n, parts, 0, one, cell, wind_x, far_wind_x, wind_y, far_wind_y, wind_z, inner_second, rate_ref, steps_ref,
        out_refs, second, fallen,
    )


def late_kernel(
    n, parts, one, cell, wind_x, far_wind_x, wind_y, far_wind_y, wind_z, inner_second, rate_ref, steps_ref, *refs
):
    fall_half(
        n, parts, n // 2, one, cell, wind_x, far_wind_x, wind_y, far_wind_y, wind_z, inner_second, rate_ref, steps_ref,
        refs[:2], *refs[2:],
    )


def fall_half(
    n, parts, begin, one, cell, wind_x, far_wind_x, wind_y, far_wind_y, wind_z, inner_second, rate_ref, steps_ref,
    out_refs, second, fallen,
):
    width = groups(parts)[0]
    span, reach, half = n + PAD_LO + PAD_HI, n + LINES, n // 2
    end = begin + half
    ready = [x for x in range(LO, n - HI) if begin <= x < end]
    left = [x for x in range(begin, end) if x not in ready]
    second[rows_of((ready[0] - begin) * n, len(ready) * n)] = inner_second[rows_of((ready[0] - LO) * n, len(ready) * n)]

    @pl.loop(left[0], left[-1] + 1)
    def _(x):
        second_y_z(n, width, x, one, x + LO, wind_y, far_wind_y, wind_z, second, x - begin)

    @pl.loop(0, n)
    def _(y):
        cells = [one[rows_of(x * reach + LO + y)] for x in range(begin, end + LINES)]
        winds = [wind_x[rows_of(x * n + y)] for x in range(max(begin - 1, 0), min(end + 1, n))]
        if begin == 0:
            winds = [far_wind_x[rows_of(LO * n + y)]] + winds
        else:
            winds = winds + [far_wind_x[rows_of((LO + 1) * n + y)]]
        for i, value in enumerate(line_change(cells, winds)):
            value = cells[i + LO] + (value + second[rows_of(i * n + y)])
            fallen[rows_of(i * n + y)] = 0.5 * cell[rows_of((begin + i) * span + PAD_LO + y)] + 0.5 * value

    bins = LANES // 2 // parts
    ids = lax.axis_index("gz") * bins + lane_ids() % bins
    rates, steps = [
        pick(jnp.broadcast_to(jnp.concatenate([ref[...]] * 2, axis=1), (ROWS, LANES)), ids) for ref in (rate_ref, steps_ref)
    ]

    columns = [[fallen[eight(i * n, k)] for k in range(ROWS)] for i in range(half)]
    rain = [jnp.zeros((ROWS, LANES), F32)] * half
    for block in range(SUBS // AHEAD):
        columns = [column + [from_above(v, width) for v in column[:AHEAD]] for column in columns]
        for s in range(AHEAD):
            rate = jnp.where(block * AHEAD + s < steps, rates, 0.0)
            for i, column in enumerate(columns):
                rain[i] = rain[i] + rate * column[0]
                columns[i] = [v + rate * (u - v) for v, u in zip(column, column[1:])]
    for i, column in enumerate(columns):
        for k in range(ROWS):
            fallen[eight(i * n, k)] = column[k]

    if parts == 2:
        send_ref, keep_ref = out_refs
        lower = is_even("gz")
        low = lane_ids() < 64
        count = half * n // 2
        for c in range(count):
            a, b = fallen[rows_of(c)], fallen[rows_of(count + c)]
            at = rows_of(c)
            keep_ref[at], send_ref[at] = order(jnp.where(low, a, turn(b, 64)), jnp.where(low, turn(a, 64), b), lower)
        value = by_quarter([turn(rain[i], 32 * i) for i in range(4)])
        keep_ref[rows_of(count)] = value
        send_ref[rows_of(count)] = value
    else:
        settled_ref, rain_ref = out_refs
        settled_ref[...] = fallen[...]
        for i in range(half):
            rain_ref[rows_of(i)] = rain[i]


def matrix_kernel(bins, gain_ref, loss_ref, pairs_ref, lost_ref, wide, tall):
    zero = jnp.zeros((bins, LANES - bins), F32)
    shifts = bins // 2

    @pl.loop(0, bins)
    def _(i):
        rows = gain_ref[pl.ds(i * bins, bins)].astype(F32)
        rows = jnp.concatenate([rows, zero], axis=1)
        wide[pl.ds(i * 2 * bins, bins)] = rows
        wide[pl.ds(i * 2 * bins + bins, bins)] = rows
        tall[pl.ds(i * bins, bins)] = rows

        @pl.when(i < shifts)
        def _():
            tall[pl.ds((i + bins) * bins, bins)] = rows

    for d in range(shifts + 1):
        rows = wide[pl.ds(d, bins, stride=2 * bins + 1)]
        if 0 < d < shifts:
            rows = rows + tall[pl.ds(d * bins, bins, stride=bins + 1)]
        pairs_ref[pl.ds(d * LANES, bins)] = rows.astype(jnp.bfloat16)
        pairs_ref[pl.ds(d * LANES + bins, bins)] = pltpu.roll(rows, bins, 1).astype(jnp.bfloat16)
    rows = jnp.concatenate([loss_ref[...].astype(F32), zero], axis=1)
    lost_ref[pl.ds(0, bins)] = rows.astype(jnp.bfloat16)
    lost_ref[pl.ds(bins, bins)] = pltpu.roll(rows, bins, 1).astype(jnp.bfloat16)


def breakup_rows(mass, pairs_ref, lost_ref, products):
    bins = LANES // 2
    count = mass.shape[0]
    lanes = lane_ids()
    rounded = mass.astype(jnp.bfloat16)
    wide = rounded.astype(F32)
    gained = None
    shifts = bins // 2 + 1
    for begin in range(0, shifts, 12):
        end = min(begin + 12, shifts)
        for d in range(begin, end):
            ids = lanes // bins * bins + (lanes + d) % bins
            for r in range(0, count, 2 * ROWS):
                halves = [wide[r + ROWS * k : r + ROWS * (k + 1)] for k in range(2)]
                halves = [v * pick(v, ids) if d else v * v for v in halves]
                both = jnp.concatenate(halves, axis=0).astype(jnp.bfloat16)
                products[pl.ds(r, 2 * ROWS), d * LANES : (d + 1) * LANES] = both
        part = jnp.dot(
            products[pl.ds(0, count), begin * LANES : end * LANES],
            pairs_ref[pl.ds(begin * LANES, (end - begin) * LANES)],
            preferred_element_type=F32,
        )
        gained = part if gained is None else gained + part
    loss = jnp.dot(rounded, lost_ref[...], preferred_element_type=F32)
    return mass + gained - mass * loss


def breakup_half(n, keep_ref, got_ref, pairs_ref, lost_ref, columns, products):
    first = is_even("gz")
    count = n * n // 4
    for c in range(count):
        a, b = order(keep_ref[rows_of(c)], got_ref[rows_of(c)], first)
        columns[rows_of(c)] = by_quarter([a, turn(b, 32), turn(a, 32), turn(b, 64)])
        columns[rows_of(count + c)] = by_quarter([turn(a, -64), turn(b, -32), turn(a, -32), b])
    a, b = order(keep_ref[rows_of(count)], got_ref[rows_of(count)], first)
    a, b = [jnp.where(first, v[: n // 2], v[n // 2 :]) for v in (a, b)]
    columns[...] = breakup_rows(columns[...], pairs_ref, lost_ref, products)
    return [jnp.concatenate([a[:, 32 * i : 32 * i + 32], b[:, 32 * i : 32 * i + 32]], axis=1) for i in range(4)]


def breakup_first_kernel(n, keep_ref, got_ref, pairs_ref, lost_ref, columns, rain_ref, products):
    for i, value in enumerate(breakup_half(n, keep_ref, got_ref, pairs_ref, lost_ref, columns, products)):
        rain_ref[i] = value


def breakup_last_kernel(
    n, keep_ref, got_ref, pairs_ref, lost_ref, early, early_rain, mass_out, rain_out, columns, products, mass, rain, sems
):
    half = n // 2

    def lay_out(ref, begin):
        for x in range(half):
            for y in range(n):
                value = ref[rows_of(x * n + y)]
                mass[begin + x, y, 0:ROWS] = value[:, :64]
                mass[begin + x, y, ROWS : 2 * ROWS] = value[:, 64:]
        copy = pltpu.make_async_copy(mass.at[pl.ds(begin, half)], mass_out.at[pl.ds(begin, half)], sems.at[begin // half])
        copy.start()
        return copy

    copies = [lay_out(early, 0)]
    late_rain = breakup_half(n, keep_ref, got_ref, pairs_ref, lost_ref, columns, products)
    for i in range(half):
        rain[i] = early_rain[i]
        rain[half + i] = late_rain[i]
    rain_copy = pltpu.make_async_copy(rain, rain_out, sems.at[2])
    rain_copy.start()
    copies.append(lay_out(columns, half))
    for copy in copies + [rain_copy]:
        copy.wait()


def breakup_plain_kernel(mass_ref, pairs_ref, lost_ref, out_ref, products):
    count = products.shape[0]

    @pl.loop(0, mass_ref.shape[0] // count)
    def _(i):
        start = pl.multiple_of(i * count, count)
        out_ref[pl.ds(start, count)] = breakup_rows(mass_ref[pl.ds(start, count)], pairs_ref, lost_ref, products)


def shape(*dims, dtype=F32):
    return jax.ShapeDtypeStruct(dims, dtype)


def tiles_of(count):
    return shape(count * ROWS, LANES)


def call(kernel, outs, args, scratch=(), micros=1.0, out_place=pltpu.VMEM, copies=0):
    scratch = [pltpu.VMEM(s.shape, s.dtype) for s in scratch]
    if copies:
        scratch.append(pltpu.SemaphoreType.DMA((copies,)))
    return pl.pallas_call(
        kernel,
        out_shape=outs,
        in_specs=[VMEM] * len(args),
        out_specs=jax.tree.map(lambda _: pl.BlockSpec(memory_space=out_place), outs),
        scratch_shapes=scratch,
        compiler_params=pltpu.CompilerParams(vmem_limit_bytes=40 << 20),
        cost_estimate=pl.CostEstimate(
            flops=int(micros * 1.1e9), bytes_accessed=int(micros * 3.6e6), transcendentals=0
        ),
    )(*args)


def swap_neighbours(axis, begin, message):
    axes = ("gx", "gy")
    sizes = [lax.axis_size(a) for a in axes]
    along = axes.index(axis)

    def partner(place, start, count):
        to = start + ((place - start) ^ 1)
        return to if start <= place and to < count else place

    pairs = []
    for here in range(sizes[0] * sizes[1]):
        place = list(divmod(here, sizes[1]))
        to = partner(place[along], begin, sizes[along])
        if to == place[along]:
            place[1 - along] = partner(place[1 - along], 0, sizes[1 - along])
        place[along] = to
        pairs.append((here, place[0] * sizes[1] + place[1]))
    return lax.ppermute(message, axes, pairs)


def per_device(bin_mass, courant, sub_courant, fall_steps, frag_gain, collide):
    nx, ny, nz, bins = bin_mass.shape
    n = nx
    parts = lax.axis_size("gz")
    gz, gy = lax.axis_index("gz"), lax.axis_index("gy")
    width = bins // parts
    tiles = groups(parts)[2]
    winds = 3 * tiles

    pair_rows = (bins // 2 + 1) * LANES
    pairs, lost = call(
        functools.partial(matrix_kernel, bins),
        (shape(pair_rows, LANES, dtype=jnp.bfloat16), shape(LANES, LANES, dtype=jnp.bfloat16)),
        (frag_gain, collide),
        [shape(2 * bins * bins, LANES), shape(3 * bins * bins // 2, LANES)],
        micros=1.4,
    )

    if parts == 2:
        half = tiles_of(n * n // 2)
        send, keep = call(pack_kernel, (half, half), (bin_mass,), micros=0.3)
        got = lax.ppermute(send, "gz", [(0, 1), (1, 0)])
        own_wind = call(wind_kernel, tiles_of(3), (courant,), micros=0.1)
        got_wind = lax.ppermute(own_wind, "gz", [(0, 1), (1, 0)])
        message = tiles_of(n * PAD_LO + winds)
        block, first, second = call(
            merge_kernel, (tiles_of(n * n + winds), message, message), (keep, got, own_wind, got_wind), micros=0.2
        )
    else:
        split = bin_mass.reshape(nx, ny, nz // ROWS, ROWS, parts, width).transpose(4, 0, 1, 3, 2, 5)
        split = lax.all_to_all(split, "gz", split_axis=0, concat_axis=0, tiled=True)
        cube = split.transpose(1, 2, 3, 0, 4, 5).reshape(n, n, ROWS, LANES)
        air = courant.reshape(3, nx, ny, nz // ROWS, ROWS).transpose(0, 4, 3, 1, 2) * (1.0 / 12.0)
        air = lax.all_gather(air, "gz").reshape(parts, 3, ROWS, nz // ROWS, tiles, nx // tiles, ny)
        air = air.transpose(1, 4, 2, 0, 3, 5, 6).reshape(-1, LANES)
        block = jnp.concatenate([cube.reshape(-1, LANES), air])
        up = jnp.concatenate([cube[:, n - PAD_LO :].reshape(-1, LANES), air])
        down = jnp.concatenate([cube[:, :PAD_HI].reshape(-1, LANES), air])
        down = jnp.pad(down, ((0, up.shape[0] - down.shape[0]), (0, 0)))
        first, second = order(up, down, gy % 2 == 0)

    from_y = swap_neighbours("gy", 0, first), swap_neighbours("gy", 1, second)
    wind_x, wind_y, wind_z, own_change = call(
        functools.partial(own_kernel, n, parts), [tiles_of(n * n)] * 4, (block,), micros=1.7
    )
    message = tiles_of(PAD_LO * n + LO * LINES + 3 * tiles // 2 + 2 + tiles)
    first, second = call(
        functools.partial(side_kernel, n, parts), (message, message), (block, *from_y, own_change, pairs), micros=0.1
    )
    second = swap_neighbours("gx", 1, second)
    first = swap_neighbours("gx", 0, first)
    cell, change, halo_wind_x, far_wind_y = call(
        functools.partial(y_kernel, n, parts),
        [tiles_of(n * (n + PAD_LO + PAD_HI)), tiles_of(n * (n + LINES)), tiles_of(LINES * n), tiles_of(n * (LINES + 2))],
        (block, *from_y, wind_y, own_change),
        [tiles_of(LINES * n)] * 2,
        micros=2.0,
    )
    reach, half, inner = n + LINES, n // 2, n - LINES
    near = call(
        functools.partial(inner_kernel, n, parts),
        [tiles_of(inner * reach), tiles_of(2 * reach), tiles_of(inner * n)],
        (cell, change, wind_x, halo_wind_x, wind_y, far_wind_y, wind_z),
        micros=0.9,
    )
    fall = sub_courant.reshape(1, bins), fall_steps.reshape(1, bins)
    message = [tiles_of(n * half // 2 + 1)] * 2 if parts == 2 else [tiles_of(n * half), tiles_of(half)]
    one, far_wind_x, *early = call(
        functools.partial(main_kernel, n, parts),
        [tiles_of(reach * reach), tiles_of((LINES + 2) * n)] + message,
        (cell, change, wind_x, wind_y, wind_z, halo_wind_x, far_wind_y, *near, second, first, *fall),
        [
            tiles_of(count)
            for count in (LINES * n, LINES * reach, 2 * LINES, LINES * (n + 2), LINES * n, LINES * n, n * half, n * half)
        ],
        micros=4.0,
    )
    if parts == 2:
        early_got = lax.ppermute(early[0], "gz", [(0, 1), (1, 0)])
    late = call(
        functools.partial(late_kernel, n, parts),
        message,
        (one, cell, wind_x, far_wind_x, wind_y, far_wind_y, wind_z, near[2], *fall),
        [tiles_of(n * half)] * 2,
        micros=1.5,
    )

    products = shape(n * half * ROWS, pair_rows, dtype=jnp.bfloat16)
    if parts == 2:
        late_got = lax.ppermute(late[0], "gz", [(0, 1), (1, 0)])
        early = call(
            functools.partial(breakup_first_kernel, n),
            [tiles_of(n * half), shape(half, ny // parts, bins)],
            (early[1], early_got, pairs, lost),
            [products],
            micros=1.5,
        )
        outs = [shape(nx, ny, nz, bins), shape(nx, ny // parts, bins)]
        return tuple(
            call(
                functools.partial(breakup_last_kernel, n),
                outs,
                (late[1], late_got, pairs, lost, *early),
                [tiles_of(n * half), products, *outs],
                micros=1.5,
                out_place=pl.ANY,
                copies=3,
            )
        )

    settled, rain = [jnp.concatenate(halves) for halves in zip(early, late)]
    rain = rain.reshape(nx, ny, LANES)[:, :, :width]
    rain = lax.all_to_all(rain, "gz", split_axis=1, concat_axis=2, tiled=True)
    settled = settled.reshape(nx, ny, ROWS, parts, nz // ROWS, width).transpose(3, 0, 1, 4, 2, 5)
    settled = lax.all_to_all(settled, "gz", split_axis=0, concat_axis=0, tiled=True)
    settled = settled.transpose(1, 2, 3, 4, 0, 5).reshape(nx * ny, nz // ROWS, ROWS, bins)
    paired = settled.transpose(0, 2, 1, 3).reshape(-1, LANES)
    updated = call(breakup_plain_kernel, tiles_of(n * n), (paired, pairs, lost), [products], micros=3.0)
    updated = updated.reshape(nx, ny, ROWS, nz // ROWS, bins).transpose(0, 1, 3, 2, 4).reshape(nx, ny, nz, bins)
    return updated, rain


def solution(mesh):
    in_specs = (P("gx", "gy", "gz", None), P(None, "gx", "gy", "gz"), P(), P(), P(), P())
    out_specs = (P("gx", "gy", "gz", None), P("gx", ("gy", "gz"), None))
    return jax.shard_map(per_device, mesh=mesh, in_specs=in_specs, out_specs=out_specs, check_vma=False)
```

```python
import functools

import jax
import jax.numpy as jnp
from jax import lax
from jax.experimental import pallas as pl
from jax.experimental.pallas import tpu as pltpu
from jax.sharding import PartitionSpec as P

SUBS = 24
EPS = 1e-06
LO, HI = 3, 2
PAD_LO, PAD_HI = 2 * LO, 2 * HI
LINES = LO + HI
ROWS, LANES = 8, 128
AHEAD = 4
F32 = jnp.float32
VMEM = pl.BlockSpec(memory_space=pltpu.VMEM)


def lane_ids():
    return lax.broadcasted_iota(jnp.int32, (ROWS, LANES), 1)


def pick(tile, ids):
    return jnp.take_along_axis(tile, ids, axis=1, mode="promise_in_bounds")


def turn(tile, lanes):
    lanes %= LANES
    return pltpu.roll(tile, lanes, 1) if lanes else tile


def rows_of(first, count=1):
    return pl.ds(first * ROWS, count * ROWS)


def eight(first, level, step=1):
    return pl.ds(first * ROWS + level, ROWS, stride=step * ROWS)


def order(a, b, straight):
    return jnp.where(straight, a, b), jnp.where(straight, b, a)


def is_even(axis):
    return lax.axis_index(axis) % 2 == 0


def by_quarter(parts):
    quarter = lane_ids() // (LANES // 4)
    return jnp.where(quarter < 2, jnp.where(quarter == 0, parts[0], parts[1]), jnp.where(quarter == 2, parts[2], parts[3]))


def groups(parts):
    width = LANES // (2 * parts)
    return width, width // ROWS, ROWS * ROWS // width


def spread(tile, x, y, parts):
    width, deep, _ = groups(parts)
    return pick(turn(tile, -(x % deep * ROWS + y)), lane_ids() // width * width)


def halo_line(i, n):
    return jnp.where(i < LO, i - LO, i - LO + n)


def line_change(cells, winds):
    return changes(line_fluxes(cells, winds))


def changes(fluxes):
    return [a - b for a, b in zip(fluxes, fluxes[1:])]


def line_fluxes(cells, winds):
    first = [b - a for a, b in zip(cells, cells[1:])]
    twice = [d + d for d in first]
    second = [b - a for a, b in zip(first, first[1:])]
    third = [a - b for a, b in zip(second, second[1:])]
    curved = [(13.0 / 3.0) * (c * c) + 4.0 * EPS for c in second]
    fluxes = []
    for j in range(len(cells) - 4):
        left = twice[j + 1] + second[j]
        mid = first[j + 1] + first[j + 2]
        right = twice[j + 2] - second[j + 2]
        e0 = curved[j] + left * left
        e1 = curved[j + 1] + mid * mid
        e2 = curved[j + 2] + right * right
        e0 = e0 * e0
        e1 = e1 * e1
        e2 = e2 * e2
        e0 = 3.0 * e0
        e2_twice = e2 + e2
        top = e1 * (e2_twice * third[j] + e0 * third[j + 1])
        low = e1 * (e2 + e0) + e0 * e2_twice
        inverse = pl.reciprocal(low, approx=True)
        estimate = 6.0 * cells[j + 2] + (first[j + 1] + twice[j + 2]) + top * inverse
        fluxes.append((winds[j] + winds[j + 1]) * estimate)
    return fluxes


def from_below(value, width):
    return jnp.where(lane_ids() < width, 0.0, turn(value, width))


def from_above(value, width):
    return jnp.where(lane_ids() >= LANES - width, 0.0, turn(value, -width))


def level_change(cells, winds, width):
    long_cells = [from_below(v, width) for v in cells[ROWS - LO :]] + cells + [from_above(v, width) for v in cells[:HI]]
    long_winds = [from_below(winds[-1], width)] + winds + [from_above(winds[0], width)]
    return line_change(long_cells, long_winds)


def pack_kernel(mass_ref, send_ref, keep_ref):
    lower = is_even("gz")
    n = mass_ref.shape[0]
    zero = jnp.zeros((ROWS, LANES // 2), F32)
    for x in range(n // 2):
        for y in range(n):
            tiles = [
                jnp.concatenate([mass_ref[xx, y, z : z + ROWS], zero], axis=1) for xx in (x, x + n // 2) for z in (0, ROWS)
            ]
            low = by_quarter([turn(v, 32 * k) for k, v in enumerate(tiles)])
            high = by_quarter([turn(v, 32 * k - 32) for k, v in enumerate(tiles)])
            at = rows_of(x * n + y)
            keep_ref[at], send_ref[at] = order(low, high, lower)


def wind_kernel(wind_ref, keep_ref, out_ref):
    del keep_ref
    n = wind_ref.shape[1]
    for d in range(3):
        levels = wind_ref[d].reshape(n * n, 2 * ROWS).T * (1.0 / 12.0)
        out_ref[rows_of(d)] = jnp.concatenate([levels[:ROWS], levels[ROWS:]], axis=1)


def sides(axis, first_ref, second_ref):
    even, place = is_even(axis), lax.axis_index(axis)
    inner_low, inner_high = place > 0, place < lax.axis_size(axis) - 1

    def below(at):
        return jnp.where(inner_low, jnp.where(even, second_ref[at], first_ref[at]), 0.0)

    def above(at):
        return jnp.where(inner_high, jnp.where(even, first_ref[at], second_ref[at]), 0.0)

    return below, above


def by_parity(axis, body):
    even = is_even(axis)
    pl.when(even)(lambda: body(0, 1))
    pl.when(jnp.logical_not(even))(lambda: body(1, 0))


def merge_kernel(keep_ref, got_ref, own_wind_ref, got_wind_ref, block_ref, y_first, y_second, x_first, x_second):
    n = 8
    lower = is_even("gz")
    low = lane_ids() < 64
    for x in range(n // 2):
        for y in range(n):
            at = rows_of(x * n + y)
            a, b = order(keep_ref[at], got_ref[at], lower)
            block_ref[at] = jnp.where(low, a, turn(b, 64))
            block_ref[rows_of((x + n // 2) * n + y)] = jnp.where(low, turn(a, 64), b)
    for d in range(3):
        a, b = order(own_wind_ref[rows_of(d)], got_wind_ref[rows_of(d)], lower)
        block_ref[rows_of(n * n + 2 * d)] = by_quarter([a, turn(a, -32), turn(b, 64), turn(b, 32)])
        block_ref[rows_of(n * n + 2 * d + 1)] = by_quarter([turn(a, -32), turn(a, -64), turn(b, 32), b])

    def along_y(up, down):
        for ref, start, wide in (((y_first, y_second)[up], n - PAD_LO, PAD_LO), ((y_first, y_second)[down], 0, PAD_HI)):
            for x in range(n):
                ref[rows_of(x * wide, wide)] = block_ref[rows_of(x * n + start, wide)]
            ref[rows_of(n * wide, 6)] = block_ref[rows_of(n * n, 6)]

    def along_x(up, down):
        for ref, start, wide, part in (((x_first, x_second)[up], n - PAD_LO, PAD_LO, 1), ((x_first, x_second)[down], 0, PAD_HI, 0)):
            ref[rows_of(0, wide * n)] = block_ref[rows_of(start * n, wide * n)]
            for d in range(3):
                ref[rows_of(wide * n + d)] = block_ref[rows_of(n * n + 2 * d + part)]

    by_parity("gy", along_y)
    by_parity("gx", along_x)


def corner_kernel(n, parts, first_ref, second_ref, own_change, pairs_ref, *messages):
    del own_change, pairs_ref
    tiles = groups(parts)[2]
    half = tiles // 2
    below, above = sides("gy", first_ref, second_ref)

    def body(up, down):
        for ref, start, narrow, part in ((messages[up], n - LO, LO, half), (messages[down], 0, HI, 0)):
            at = 0
            for x in range(start, start + narrow):
                ref[rows_of(at, LO)] = below(rows_of(x * PAD_LO + PAD_LO - LO, LO))
                ref[rows_of(at + LO, HI)] = above(rows_of(x * PAD_HI, HI))
                at += LINES
            for side, base in ((below, n * PAD_LO), (above, n * PAD_HI)):
                ref[rows_of(at)] = side(rows_of(base + (tiles - 1 if part else 0)))
                ref[rows_of(at + 1, half)] = side(rows_of(base + tiles + part, half))
                at += 1 + half

    by_parity("gx", body)


def own_kernel(n, parts, block_ref, wind_x, wind_y, wind_z, change):
    width, deep, tiles = groups(parts)
    for d, out in enumerate((wind_x, wind_y, wind_z)):
        for x in range(n):
            tile = block_ref[rows_of(n * n + d * tiles + x // deep)]
            for y in range(n):
                out[rows_of(x * n + y)] = spread(tile, x, y, parts)

    @pl.loop(0, n)
    def _(x):
        cells = [block_ref[eight(x * n, k)] for k in range(ROWS)]
        winds = [wind_z[eight(x * n, k)] for k in range(ROWS)]
        for k, value in enumerate(level_change(cells, winds, width)):
            change[eight(x * n, k)] = value


def y_kernel(n, parts, block_ref, first_ref, second_ref, wind_y, own_change, *refs):
    width, deep, tiles = groups(parts)
    cell, change, wind_x, far_y, wind_z, halo_change = refs
    below, above = sides("gy", first_ref, second_ref)
    span, reach = n + PAD_LO + PAD_HI, n + LINES

    for x in range(n):
        cell[rows_of(x * span, PAD_LO)] = below(rows_of(x * PAD_LO, PAD_LO))
        cell[rows_of(x * span + PAD_LO, n)] = block_ref[rows_of(x * n, n)]
        cell[rows_of(x * span + PAD_LO + n, PAD_HI)] = above(rows_of(x * PAD_HI, PAD_HI))
    for d in range(3):
        for t in range(tiles):
            low, high = below(rows_of(n * PAD_LO + d * tiles + t)), above(rows_of(n * PAD_HI + d * tiles + t))
            for x in range(t * deep, (t + 1) * deep):
                if d == 1:
                    for y in range(LO + 1):
                        far_y[rows_of(x * (LINES + 2) + y)] = spread(low, x, n - LO - 1 + y, parts)
                    for y in range(HI + 1):
                        far_y[rows_of(x * (LINES + 2) + LO + 1 + y)] = spread(high, x, y, parts)
                else:
                    out = wind_z if d else wind_x
                    for y in range(LO):
                        out[rows_of(y * n + x)] = spread(low, x, n - LO + y, parts)
                    for y in range(HI):
                        out[rows_of((LO + y) * n + x)] = spread(high, x, y, parts)

    @pl.loop(0, LINES)
    def _(i):
        first = halo_line(i, n) + PAD_LO
        cells = [cell[eight(first, k, span)] for k in range(ROWS)]
        winds = [wind_z[eight(i * n, k)] for k in range(ROWS)]
        for k, value in enumerate(level_change(cells, winds, width)):
            halo_change[eight(i * n, k)] = value

    @pl.loop(0, n)
    def _(x):
        cells = [cell[rows_of(x * span + y)] for y in range(span)]
        far = [far_y[rows_of(x * (LINES + 2) + y)] for y in range(LINES + 2)]
        winds = far[: LO + 1] + [wind_y[rows_of(x * n + y)] for y in range(n)] + far[LO + 1 :]
        for y, value in enumerate(line_change(cells, winds)):
            if LO <= y < LO + n:
                value = value + own_change[rows_of(x * n + y - LO)]
            else:
                value = value + halo_change[rows_of((y if y < LO else y - n) * n + x)]
            change[rows_of(x * reach + y)] = value


def inside(axis):
    place = lax.axis_index(axis)
    return [jnp.where(ok, 1.0, 0.0) for ok in (place > 0, place < lax.axis_size(axis) - 1)]


def inner_kernel(n, parts, cell, change, wind_x, halo_wind_x, wind_y, far_wind_y, wind_z, one, edge, second):
    width = groups(parts)[0]
    span, reach = n + PAD_LO + PAD_HI, n + LINES
    begin, end = LO, n - HI
    south_in, north_in = inside("gy")

    def line(at, winds, keep):
        cells = [cell[rows_of(x * span + LO + at)] for x in range(n)]
        fluxes = line_fluxes(cells, winds)
        edge[rows_of(at)] = fluxes[0]
        edge[rows_of(reach + at)] = fluxes[-1]
        for i, value in enumerate(changes(fluxes)):
            x = begin + i
            value = cells[x] + (value + change[rows_of(x * reach + at)])
            one[rows_of(i * reach + at)] = value if keep is None else value * keep

    @pl.loop(0, n)
    def _(y):
        line(LO + y, [wind_x[rows_of(x * n + y)] for x in range(begin - 1, end + 1)], None)

    @pl.loop(0, LINES)
    def _(i):
        winds = [halo_wind_x[rows_of(i * n + x)] for x in range(begin - 1, end + 1)]
        line(halo_line(i, n) + LO, winds, jnp.where(i < LO, south_in, north_in))

    @pl.loop(0, end - begin)
    def _(i):
        second_y_z(n, width, begin + i, one, i, wind_y, far_wind_y, wind_z, second, i)


def second_y_z(n, width, x, one, one_x, wind_y, far_wind_y, wind_z, second, second_x):
    reach = n + LINES
    cells = [one[rows_of(one_x * reach + y)] for y in range(reach)]
    winds = [far_wind_y[rows_of(x * (LINES + 2) + LO)]] + [wind_y[rows_of(x * n + y)] for y in range(n)]
    winds += [far_wind_y[rows_of(x * (LINES + 2) + LO + 1)]]
    for y, value in enumerate(line_change(cells, winds)):
        second[rows_of(second_x * n + y)] = value
    cells = [one[eight(one_x * reach + LO, k)] for k in range(ROWS)]
    winds = [wind_z[eight(x * n, k)] for k in range(ROWS)]
    for k, value in enumerate(level_change(cells, winds, width)):
        at = eight(second_x * n, k)
        second[at] = second[at] + value


def x_kernel(n, parts, cell, change, wind_x, edge, second_ref, first_ref, mid, far_wind_x, side, side_wind_y, *scratch):
    far, side_wind_z, side_change = scratch
    width, deep, tiles = groups(parts)
    half = tiles // 2
    west, east = sides("gx", first_ref, second_ref)
    span, reach = n + PAD_LO + PAD_HI, n + LINES

    for take, wide, near_from, far_from, line in ((west, PAD_LO, LO, 0, 0), (east, PAD_HI, 0, HI, LO)):
        narrow = wide // 2
        side[rows_of(line * n, narrow * n)] = take(rows_of(near_from * n, narrow * n))
        far[rows_of(line * n, narrow * n)] = take(rows_of(far_from * n, narrow * n))
        layers, shift = (range(n - narrow, n), half) if line == 0 else (range(narrow), 0)
        wider = range(n - narrow - 1, n) if line == 0 else range(narrow + 1)

        def winds_of(d, x):
            return take(rows_of(wide * n + d * half + x // deep - shift))

        for i, x in enumerate(wider):
            for y in range(n):
                far_wind_x[rows_of((line + bool(line) + i) * n + y)] = spread(winds_of(0, x), x, y, parts)
        for i, x in enumerate(layers):
            for y in range(n):
                at = rows_of((line + i) * n + y)
                side_wind_y[at] = spread(winds_of(1, x), x, y, parts)
                side_wind_z[at] = spread(winds_of(2, x), x, y, parts)

    @pl.loop(0, LINES)
    def _(i):
        cells = [side[eight(i * n, k)] for k in range(ROWS)]
        winds = [side_wind_z[eight(i * n, k)] for k in range(ROWS)]
        for k, value in enumerate(level_change(cells, winds, width)):
            side_change[eight(i * n, k)] = value

    begin, end = LO, n - HI

    @pl.loop(0, n)
    def _(y):
        outer = [far[rows_of(i * n + y)] for i in range(LINES)]
        near = [side[rows_of(i * n + y)] for i in range(LINES)]
        cells = outer[:LO] + near[:LO] + [cell[rows_of(x * span + PAD_LO + y)] for x in range(n)] + near[LO:] + outer[LO:]
        winds = [far_wind_x[rows_of(i * n + y)] for i in range(LINES + 2)]
        winds = winds[: LO + 1] + [wind_x[rows_of(x * n + y)] for x in range(n)] + winds[LO + 1 :]
        low = line_fluxes(cells[: PAD_LO + begin + 1], winds[: LO + 1 + begin]) + [edge[rows_of(LO + y)]]
        high = [edge[rows_of(reach + LO + y)]] + line_fluxes(cells[PAD_LO + end - HI :], winds[LO + 1 + end :])
        values = dict(zip(range(-LO, begin), changes(low))) | dict(zip(range(end, n + HI), changes(high)))
        for x, value in values.items():
            if 0 <= x < n:
                value = value + change[rows_of(x * reach + LO + y)]
            else:
                value = value + side_change[rows_of((x + LO if x < 0 else x + LO - n) * n + y)]
            mid[rows_of((x + LO) * n + y)] = cells[PAD_LO + x] + value


def main_kernel(n, parts, *refs):
    cell, change, wind_x, wind_y, wind_z, halo_wind_x, far_wind_y, inner, edge, inner_second = refs[:10]
    mid, far_wind_x, side, side_wind_y, second_ref, first_ref, rate_ref, steps_ref = refs[10:18]
    one, *out_refs = refs[18:21]
    corner, corner_wind_x, edge_wind_y, second, fallen = refs[21:]
    deep, tiles = groups(parts)[1:]
    half = tiles // 2
    west, east = sides("gx", first_ref, second_ref)
    span, reach = n + PAD_LO + PAD_HI, n + LINES

    for take, narrow, line in ((west, LO, 0), (east, HI, LO)):
        at = narrow * LINES
        corner[rows_of(line * LINES, at)] = take(rows_of(0, at))
        below, above = at, at + 1 + half
        layers, shift = (range(n - narrow, n), half) if line == 0 else (range(narrow), 0)
        for y in range(LINES):
            tile = take(rows_of(below if y < LO else above))
            value = spread(tile, layers[-1] if line == 0 else layers[0], n - LO + y if y < LO else y - LO, parts)
            corner_wind_x[rows_of(bool(line) * LINES + y)] = value
        for i, x in enumerate(layers):
            tile = x // deep - shift
            edge_wind_y[rows_of(2 * (line + i))] = spread(take(rows_of(below + 1 + tile)), x, n - 1, parts)
            edge_wind_y[rows_of(2 * (line + i) + 1)] = spread(take(rows_of(above + 1 + tile)), x, 0, parts)

    west_in, east_in = inside("gx")
    south_in, north_in = inside("gy")
    begin, end = LO, n - HI
    one[rows_of((begin + LO) * reach, (end - begin) * reach)] = inner[...]
    for x in [x for x in range(n) if not begin <= x < end]:
        one[rows_of((x + LO) * reach + LO, n)] = mid[rows_of((x + LO) * n, n)]

    @pl.loop(0, LINES)
    def _(i):
        corners = [corner[rows_of(i * LINES + y)] for y in range(LINES)]
        cells = corners[:LO] + [side[rows_of(i * n + y)] for y in range(n)] + corners[LO:]
        winds = [side_wind_y[rows_of(i * n + y)] for y in range(n)]
        winds = [edge_wind_y[rows_of(2 * i)]] + winds + [edge_wind_y[rows_of(2 * i + 1)]]
        keep = jnp.where(i < LO, west_in, east_in)
        line = halo_line(i, n) + LO
        for y, value in enumerate(line_change(cells, winds)):
            one[rows_of(line * reach + LO + y)] = (mid[rows_of(line * n + y)] + value) * keep

    @pl.loop(0, LINES)
    def _(i):
        line = halo_line(i, n) + LO
        near = [corner[rows_of(k * LINES + i)] for k in range(LINES)]
        cells = near[:LO] + [cell[rows_of(x * span + LO + line)] for x in range(n)] + near[LO:]
        winds = [halo_wind_x[rows_of(i * n + x)] for x in range(n)]
        winds = [corner_wind_x[rows_of(i)]] + winds + [corner_wind_x[rows_of(LINES + i)]]
        keep = jnp.where(i < LO, south_in, north_in)
        low = line_fluxes(cells[: LO + begin + 1], winds[: begin + 1]) + [edge[rows_of(line)]]
        high = [edge[rows_of(reach + line)]] + line_fluxes(cells[LO + end - HI :], winds[end + 1 :])
        values = dict(zip(range(begin), changes(low))) | dict(zip(range(end, n), changes(high)))
        for x, value in values.items():
            one[rows_of((x + LO) * reach + line)] = (cells[x + LO] + (value + change[rows_of(x * reach + line)])) * keep

    fall_half(
        n, parts, 0, one, cell, wind_x, far_wind_x, wind_y, far_wind_y, wind_z, inner_second, rate_ref, steps_ref,
        out_refs, second, fallen,
    )


def late_kernel(
    n, parts, one, cell, wind_x, far_wind_x, wind_y, far_wind_y, wind_z, inner_second, rate_ref, steps_ref, *refs
):
    fall_half(
        n, parts, n // 2, one, cell, wind_x, far_wind_x, wind_y, far_wind_y, wind_z, inner_second, rate_ref, steps_ref,
        refs[:2], *refs[2:],
    )


def fall_half(
    n, parts, begin, one, cell, wind_x, far_wind_x, wind_y, far_wind_y, wind_z, inner_second, rate_ref, steps_ref,
    out_refs, second, fallen,
):
    width = groups(parts)[0]
    span, reach, half = n + PAD_LO + PAD_HI, n + LINES, n // 2
    end = begin + half
    ready = [x for x in range(LO, n - HI) if begin <= x < end]
    left = [x for x in range(begin, end) if x not in ready]
    second[rows_of((ready[0] - begin) * n, len(ready) * n)] = inner_second[rows_of((ready[0] - LO) * n, len(ready) * n)]

    @pl.loop(left[0], left[-1] + 1)
    def _(x):
        second_y_z(n, width, x, one, x + LO, wind_y, far_wind_y, wind_z, second, x - begin)

    @pl.loop(0, n)
    def _(y):
        cells = [one[rows_of(x * reach + LO + y)] for x in range(begin, end + LINES)]
        winds = [wind_x[rows_of(x * n + y)] for x in range(max(begin - 1, 0), min(end + 1, n))]
        if begin == 0:
            winds = [far_wind_x[rows_of(LO * n + y)]] + winds
        else:
            winds = winds + [far_wind_x[rows_of((LO + 1) * n + y)]]
        for i, value in enumerate(line_change(cells, winds)):
            value = cells[i + LO] + (value + second[rows_of(i * n + y)])
            fallen[rows_of(i * n + y)] = 0.5 * cell[rows_of((begin + i) * span + PAD_LO + y)] + 0.5 * value

    bins = LANES // 2 // parts
    ids = lax.axis_index("gz") * bins + lane_ids() % bins
    rates, steps = [
        pick(jnp.broadcast_to(jnp.concatenate([ref[...]] * 2, axis=1), (ROWS, LANES)), ids) for ref in (rate_ref, steps_ref)
    ]

    columns = [[fallen[eight(i * n, k)] for k in range(ROWS)] for i in range(half)]
    rain = [jnp.zeros((ROWS, LANES), F32)] * half
    for block in range(SUBS // AHEAD):
        columns = [column + [from_above(v, width) for v in column[:AHEAD]] for column in columns]
        for s in range(AHEAD):
            rate = jnp.where(block * AHEAD + s < steps, rates, 0.0)
            for i, column in enumerate(columns):
                rain[i] = rain[i] + rate * column[0]
                columns[i] = [v + rate * (u - v) for v, u in zip(column, column[1:])]
    for i, column in enumerate(columns):
        for k in range(ROWS):
            fallen[eight(i * n, k)] = column[k]

    if parts == 2:
        send_ref, keep_ref = out_refs
        lower = is_even("gz")
        low = lane_ids() < 64
        count = half * n // 2
        for c in range(count):
            a, b = fallen[rows_of(c)], fallen[rows_of(count + c)]
            at = rows_of(c)
            keep_ref[at], send_ref[at] = order(jnp.where(low, a, turn(b, 64)), jnp.where(low, turn(a, 64), b), lower)
        value = by_quarter([turn(rain[i], 32 * i) for i in range(4)])
        keep_ref[rows_of(count)] = value
        send_ref[rows_of(count)] = value
    else:
        settled_ref, rain_ref = out_refs
        settled_ref[...] = fallen[...]
        for i in range(half):
            rain_ref[rows_of(i)] = rain[i]


def matrix_kernel(bins, gain_ref, loss_ref, pairs_ref, lost_ref, wide, tall):
    zero = jnp.zeros((bins, LANES - bins), F32)
    shifts = bins // 2

    @pl.loop(0, bins)
    def _(i):
        rows = gain_ref[pl.ds(i * bins, bins)].astype(F32)
        rows = jnp.concatenate([rows, zero], axis=1)
        wide[pl.ds(i * 2 * bins, bins)] = rows
        wide[pl.ds(i * 2 * bins + bins, bins)] = rows
        tall[pl.ds(i * bins, bins)] = rows

        @pl.when(i < shifts)
        def _():
            tall[pl.ds((i + bins) * bins, bins)] = rows

    for d in range(shifts + 1):
        rows = wide[pl.ds(d, bins, stride=2 * bins + 1)]
        if 0 < d < shifts:
            rows = rows + tall[pl.ds(d * bins, bins, stride=bins + 1)]
        pairs_ref[pl.ds(d * LANES, bins)] = rows.astype(jnp.bfloat16)
        pairs_ref[pl.ds(d * LANES + bins, bins)] = pltpu.roll(rows, bins, 1).astype(jnp.bfloat16)
    rows = jnp.concatenate([loss_ref[...].astype(F32), zero], axis=1)
    lost_ref[pl.ds(0, bins)] = rows.astype(jnp.bfloat16)
    lost_ref[pl.ds(bins, bins)] = pltpu.roll(rows, bins, 1).astype(jnp.bfloat16)


def breakup_rows(mass, pairs_ref, lost_ref, products):
    bins = LANES // 2
    count = mass.shape[0]
    lanes = lane_ids()
    rounded = mass.astype(jnp.bfloat16)
    wide = rounded.astype(F32)
    gained = None
    shifts = bins // 2 + 1
    for begin in range(0, shifts, 12):
        end = min(begin + 12, shifts)
        for d in range(begin, end):
            ids = lanes // bins * bins + (lanes + d) % bins
            for r in range(0, count, 2 * ROWS):
                halves = [wide[r + ROWS * k : r + ROWS * (k + 1)] for k in range(2)]
                halves = [v * pick(v, ids) if d else v * v for v in halves]
                both = jnp.concatenate(halves, axis=0).astype(jnp.bfloat16)
                products[pl.ds(r, 2 * ROWS), d * LANES : (d + 1) * LANES] = both
        part = jnp.dot(
            products[pl.ds(0, count), begin * LANES : end * LANES],
            pairs_ref[pl.ds(begin * LANES, (end - begin) * LANES)],
            preferred_element_type=F32,
        )
        gained = part if gained is None else gained + part
    loss = jnp.dot(rounded, lost_ref[...], preferred_element_type=F32)
    return mass + gained - mass * loss


def breakup_half(n, keep_ref, got_ref, pairs_ref, lost_ref, columns, products):
    first = is_even("gz")
    count = n * n // 4
    for c in range(count):
        a, b = order(keep_ref[rows_of(c)], got_ref[rows_of(c)], first)
        columns[rows_of(c)] = by_quarter([a, turn(b, 32), turn(a, 32), turn(b, 64)])
        columns[rows_of(count + c)] = by_quarter([turn(a, -64), turn(b, -32), turn(a, -32), b])
    a, b = order(keep_ref[rows_of(count)], got_ref[rows_of(count)], first)
    a, b = [jnp.where(first, v[: n // 2], v[n // 2 :]) for v in (a, b)]
    columns[...] = breakup_rows(columns[...], pairs_ref, lost_ref, products)
    return [jnp.concatenate([a[:, 32 * i : 32 * i + 32], b[:, 32 * i : 32 * i + 32]], axis=1) for i in range(4)]


def breakup_first_kernel(n, keep_ref, got_ref, pairs_ref, lost_ref, columns, rain_ref, products):
    for i, value in enumerate(breakup_half(n, keep_ref, got_ref, pairs_ref, lost_ref, columns, products)):
        rain_ref[i] = value


def breakup_last_kernel(
    n, keep_ref, got_ref, pairs_ref, lost_ref, early, early_rain, mass_out, rain_out, columns, products, mass, rain, sems
):
    half = n // 2

    def lay_out(ref, begin):
        for x in range(half):
            for y in range(n):
                value = ref[rows_of(x * n + y)]
                mass[begin + x, y, 0:ROWS] = value[:, :64]
                mass[begin + x, y, ROWS : 2 * ROWS] = value[:, 64:]
        copy = pltpu.make_async_copy(mass.at[pl.ds(begin, half)], mass_out.at[pl.ds(begin, half)], sems.at[begin // half])
        copy.start()
        return copy

    copies = [lay_out(early, 0)]
    late_rain = breakup_half(n, keep_ref, got_ref, pairs_ref, lost_ref, columns, products)
    for i in range(half):
        rain[i] = early_rain[i]
        rain[half + i] = late_rain[i]
    rain_copy = pltpu.make_async_copy(rain, rain_out, sems.at[2])
    rain_copy.start()
    copies.append(lay_out(columns, half))
    for copy in copies + [rain_copy]:
        copy.wait()


def breakup_plain_kernel(mass_ref, pairs_ref, lost_ref, out_ref, products):
    count = products.shape[0]

    @pl.loop(0, mass_ref.shape[0] // count)
    def _(i):
        start = pl.multiple_of(i * count, count)
        out_ref[pl.ds(start, count)] = breakup_rows(mass_ref[pl.ds(start, count)], pairs_ref, lost_ref, products)


def shape(*dims, dtype=F32):
    return jax.ShapeDtypeStruct(dims, dtype)


def tiles_of(count):
    return shape(count * ROWS, LANES)


def call(kernel, outs, args, scratch=(), micros=1.0, out_place=pltpu.VMEM, copies=0):
    scratch = [pltpu.VMEM(s.shape, s.dtype) for s in scratch]
    if copies:
        scratch.append(pltpu.SemaphoreType.DMA((copies,)))
    return pl.pallas_call(
        kernel,
        out_shape=outs,
        in_specs=[VMEM] * len(args),
        out_specs=jax.tree.map(lambda _: pl.BlockSpec(memory_space=out_place), outs),
        scratch_shapes=scratch,
        compiler_params=pltpu.CompilerParams(vmem_limit_bytes=40 << 20),
        cost_estimate=pl.CostEstimate(
            flops=int(micros * 1.1e9), bytes_accessed=int(micros * 3.6e6), transcendentals=0
        ),
    )(*args)


def swap_neighbours(axis, begin, message):
    axes = ("gx", "gy")
    sizes = [lax.axis_size(a) for a in axes]
    along = axes.index(axis)

    def partner(place, start, count):
        to = start + ((place - start) ^ 1)
        return to if start <= place and to < count else place

    pairs = []
    for here in range(sizes[0] * sizes[1]):
        place = list(divmod(here, sizes[1]))
        to = partner(place[along], begin, sizes[along])
        if to == place[along]:
            place[1 - along] = partner(place[1 - along], 0, sizes[1 - along])
        place[along] = to
        pairs.append((here, place[0] * sizes[1] + place[1]))
    return lax.ppermute(message, axes, pairs)


def per_device(bin_mass, courant, sub_courant, fall_steps, frag_gain, collide):
    nx, ny, nz, bins = bin_mass.shape
    n = nx
    parts = lax.axis_size("gz")
    gz, gy = lax.axis_index("gz"), lax.axis_index("gy")
    width = bins // parts
    tiles = groups(parts)[2]
    winds = 3 * tiles

    pair_rows = (bins // 2 + 1) * LANES
    pairs, lost = call(
        functools.partial(matrix_kernel, bins),
        (shape(pair_rows, LANES, dtype=jnp.bfloat16), shape(LANES, LANES, dtype=jnp.bfloat16)),
        (frag_gain, collide),
        [shape(2 * bins * bins, LANES), shape(3 * bins * bins // 2, LANES)],
        micros=1.4,
    )

    y_message = tiles_of(n * PAD_LO + winds)
    x_message = tiles_of(n * PAD_LO + winds // 2)
    if parts == 2:
        half = tiles_of(n * n // 2)
        send, keep = call(pack_kernel, (half, half), (bin_mass,), micros=0.3)
        got = lax.ppermute(send, "gz", [(0, 1), (1, 0)])
        own_wind = call(wind_kernel, tiles_of(3), (courant, keep), micros=0.1)
        got_wind = lax.ppermute(own_wind, "gz", [(0, 1), (1, 0)])
        block, *messages = call(
            merge_kernel,
            [tiles_of(n * n + winds), y_message, y_message, x_message, x_message],
            (keep, got, own_wind, got_wind),
            micros=0.2,
        )
    else:
        split = bin_mass.reshape(nx, ny, nz // ROWS, ROWS, parts, width).transpose(4, 0, 1, 3, 2, 5)
        split = lax.all_to_all(split, "gz", split_axis=0, concat_axis=0, tiled=True)
        cube = split.transpose(1, 2, 3, 0, 4, 5).reshape(n, n, ROWS, LANES)
        air = courant.reshape(3, nx, ny, nz // ROWS, ROWS).transpose(0, 4, 3, 1, 2) * (1.0 / 12.0)
        air = lax.all_gather(air, "gz").reshape(parts, 3, ROWS, nz // ROWS, tiles, nx // tiles, ny)
        air = air.transpose(1, 4, 2, 0, 3, 5, 6).reshape(3, tiles, ROWS, LANES)
        block = jnp.concatenate([cube.reshape(-1, LANES), air.reshape(-1, LANES)])
        messages = []
        for layers, low_air, high_air, message, even in (
            (cube.transpose(1, 0, 2, 3), air, air, y_message, gy % 2 == 0),
            (cube, air[:, : tiles // 2], air[:, tiles // 2 :], x_message, lax.axis_index("gx") % 2 == 0),
        ):
            up, down = layers[n - PAD_LO :], layers[:PAD_HI]
            if message is y_message:
                up, down = up.transpose(1, 0, 2, 3), down.transpose(1, 0, 2, 3)
            up = jnp.concatenate([up.reshape(-1, LANES), high_air.reshape(-1, LANES)])
            down = jnp.concatenate([down.reshape(-1, LANES), low_air.reshape(-1, LANES)])
            messages += order(up, jnp.pad(down, ((0, up.shape[0] - down.shape[0]), (0, 0))), even)

    from_y = swap_neighbours("gy", 0, messages[0]), swap_neighbours("gy", 1, messages[1])
    from_x = swap_neighbours("gx", 1, messages[3]), swap_neighbours("gx", 0, messages[2])
    wind_x, wind_y, wind_z, own_change = call(
        functools.partial(own_kernel, n, parts), [tiles_of(n * n)] * 4, (block,), micros=1.7
    )
    message = tiles_of(LO * LINES + 2 + tiles)
    corners = call(functools.partial(corner_kernel, n, parts), (message, message), (*from_y, own_change, pairs), micros=0.1)
    corners = swap_neighbours("gx", 1, corners[1]), swap_neighbours("gx", 0, corners[0])
    cell, change, halo_wind_x, far_wind_y = call(
        functools.partial(y_kernel, n, parts),
        [tiles_of(n * (n + PAD_LO + PAD_HI)), tiles_of(n * (n + LINES)), tiles_of(LINES * n), tiles_of(n * (LINES + 2))],
        (block, *from_y, wind_y, own_change),
        [tiles_of(LINES * n)] * 2,
        micros=2.0,
    )
    reach, half, inner = n + LINES, n // 2, n - LINES
    near = call(
        functools.partial(inner_kernel, n, parts),
        [tiles_of(inner * reach), tiles_of(2 * reach), tiles_of(inner * n)],
        (cell, change, wind_x, halo_wind_x, wind_y, far_wind_y, wind_z),
        micros=0.9,
    )
    mid, far_wind_x, side, side_wind_y = call(
        functools.partial(x_kernel, n, parts),
        [tiles_of(count) for count in (reach * n, (LINES + 2) * n, LINES * n, LINES * n)],
        (cell, change, wind_x, near[1], *from_x),
        [tiles_of(LINES * n)] * 3,
        micros=1.7,
    )
    fall = sub_courant.reshape(1, bins), fall_steps.reshape(1, bins)
    message = [tiles_of(n * half // 2 + 1)] * 2 if parts == 2 else [tiles_of(n * half), tiles_of(half)]
    one, *early = call(
        functools.partial(main_kernel, n, parts),
        [tiles_of(reach * reach)] + message,
        (
            *(cell, change, wind_x, wind_y, wind_z, halo_wind_x, far_wind_y, *near),
            *(mid, far_wind_x, side, side_wind_y, *corners, *fall),
        ),
        [tiles_of(count) for count in (LINES * LINES, 2 * LINES, 2 * LINES, n * half, n * half)],
        micros=2.0,
    )
    if parts == 2:
        early_got = lax.ppermute(early[0], "gz", [(0, 1), (1, 0)])
    late = call(
        functools.partial(late_kernel, n, parts),
        message,
        (one, cell, wind_x, far_wind_x, wind_y, far_wind_y, wind_z, near[2], *fall),
        [tiles_of(n * half)] * 2,
        micros=1.5,
    )

    products = shape(n * half * ROWS, pair_rows, dtype=jnp.bfloat16)
    if parts == 2:
        late_got = lax.ppermute(late[0], "gz", [(0, 1), (1, 0)])
        early = call(
            functools.partial(breakup_first_kernel, n),
            [tiles_of(n * half), shape(half, ny // parts, bins)],
            (early[1], early_got, pairs, lost),
            [products],
            micros=1.5,
        )
        outs = [shape(nx, ny, nz, bins), shape(nx, ny // parts, bins)]
        return tuple(
            call(
                functools.partial(breakup_last_kernel, n),
                outs,
                (late[1], late_got, pairs, lost, *early),
                [tiles_of(n * half), products, *outs],
                micros=1.5,
                out_place=pl.ANY,
                copies=3,
            )
        )

    settled, rain = [jnp.concatenate(halves) for halves in zip(early, late)]
    rain = rain.reshape(nx, ny, LANES)[:, :, :width]
    rain = lax.all_to_all(rain, "gz", split_axis=1, concat_axis=2, tiled=True)
    settled = settled.reshape(nx, ny, ROWS, parts, nz // ROWS, width).transpose(3, 0, 1, 4, 2, 5)
    settled = lax.all_to_all(settled, "gz", split_axis=0, concat_axis=0, tiled=True)
    settled = settled.transpose(1, 2, 3, 4, 0, 5).reshape(nx * ny, nz // ROWS, ROWS, bins)
    paired = settled.transpose(0, 2, 1, 3).reshape(-1, LANES)
    updated = call(breakup_plain_kernel, tiles_of(n * n), (paired, pairs, lost), [products], micros=3.0)
    updated = updated.reshape(nx, ny, ROWS, nz // ROWS, bins).transpose(0, 1, 3, 2, 4).reshape(nx, ny, nz, bins)
    return updated, rain


def solution(mesh):
    in_specs = (P("gx", "gy", "gz", None), P(None, "gx", "gy", "gz"), P(), P(), P(), P())
    out_specs = (P("gx", "gy", "gz", None), P("gx", ("gy", "gz"), None))
    return jax.shard_map(per_device, mesh=mesh, in_specs=in_specs, out_specs=out_specs, check_vma=False)
```

```python
import functools

import jax
import jax.numpy as jnp
from jax import lax
from jax.experimental import pallas as pl
from jax.experimental.pallas import tpu as pltpu
from jax.sharding import PartitionSpec as P

SUBS = 24
EPS = 1e-06
LO, HI = 3, 2
PAD_LO, PAD_HI = 2 * LO, 2 * HI
LINES = LO + HI
ROWS, LANES = 8, 128
AHEAD = 4
F32 = jnp.float32
VMEM = pl.BlockSpec(memory_space=pltpu.VMEM)


def lane_ids():
    return lax.broadcasted_iota(jnp.int32, (ROWS, LANES), 1)


def pick(tile, ids):
    return jnp.take_along_axis(tile, ids, axis=1, mode="promise_in_bounds")


def turn(tile, lanes):
    lanes %= LANES
    return pltpu.roll(tile, lanes, 1) if lanes else tile


def rows_of(first, count=1):
    return pl.ds(first * ROWS, count * ROWS)


def eight(first, level, step=1):
    return pl.ds(first * ROWS + level, ROWS, stride=step * ROWS)


def order(a, b, straight):
    return jnp.where(straight, a, b), jnp.where(straight, b, a)


def is_even(axis):
    return lax.axis_index(axis) % 2 == 0


def by_quarter(parts):
    quarter = lane_ids() // (LANES // 4)
    return jnp.where(quarter < 2, jnp.where(quarter == 0, parts[0], parts[1]), jnp.where(quarter == 2, parts[2], parts[3]))


def groups(parts):
    width = LANES // (2 * parts)
    return width, width // ROWS, ROWS * ROWS // width


def spread(jobs, parts):
    width, deep, _ = groups(parts)
    place = lane_ids() % width
    rows = [[], []]
    for tile, x, y, _, _ in jobs:
        top = tile.astype(jnp.bfloat16).astype(F32)
        here = place == x % deep * ROWS + y
        for out, term in zip(rows, (top, tile - top)):
            out.append(jnp.where(here, term, 0.0))
    terms = jnp.concatenate([jnp.concatenate(r, axis=0).astype(jnp.bfloat16) for r in rows], axis=1)
    source, target = [lax.broadcasted_iota(jnp.int32, (2 * LANES, LANES), k) for k in range(2)]
    same = jnp.where(source % LANES // width == target // width, 1.0, 0.0).astype(jnp.bfloat16)
    out = jnp.dot(terms, same, preferred_element_type=F32)
    for k, (_, _, _, ref, at) in enumerate(jobs):
        ref[rows_of(at)] = out[k * ROWS : (k + 1) * ROWS]


def halo_line(i, n):
    return jnp.where(i < LO, i - LO, i - LO + n)


def line_change(cells, winds):
    return changes(line_fluxes(cells, winds))


def changes(fluxes):
    return [a - b for a, b in zip(fluxes, fluxes[1:])]


def line_fluxes(cells, winds):
    first = [b - a for a, b in zip(cells, cells[1:])]
    twice = [d + d for d in first]
    second = [b - a for a, b in zip(first, first[1:])]
    third = [a - b for a, b in zip(second, second[1:])]
    curved = [(13.0 / 3.0) * (c * c) + 4.0 * EPS for c in second]
    fluxes = []
    for j in range(len(cells) - 4):
        left = twice[j + 1] + second[j]
        mid = first[j + 1] + first[j + 2]
        right = twice[j + 2] - second[j + 2]
        e0 = curved[j] + left * left
        e1 = curved[j + 1] + mid * mid
        e2 = curved[j + 2] + right * right
        e0 = e0 * e0
        e1 = e1 * e1
        e2 = e2 * e2
        e0 = 3.0 * e0
        e2_twice = e2 + e2
        top = e1 * (e2_twice * third[j] + e0 * third[j + 1])
        low = e1 * (e2 + e0) + e0 * e2_twice
        inverse = pl.reciprocal(low, approx=True)
        estimate = 6.0 * cells[j + 2] + (first[j + 1] + twice[j + 2]) + top * inverse
        fluxes.append((winds[j] + winds[j + 1]) * estimate)
    return fluxes


def from_below(value, width):
    return jnp.where(lane_ids() < width, 0.0, turn(value, width))


def from_above(value, width):
    return jnp.where(lane_ids() >= LANES - width, 0.0, turn(value, -width))


def level_change(cells, winds, width):
    long_cells = [from_below(v, width) for v in cells[ROWS - LO :]] + cells + [from_above(v, width) for v in cells[:HI]]
    long_winds = [from_below(winds[-1], width)] + winds + [from_above(winds[0], width)]
    return line_change(long_cells, long_winds)


def pack_kernel(mass_ref, send_ref, keep_ref):
    lower = is_even("gz")
    n = mass_ref.shape[0]
    zero = jnp.zeros((ROWS, LANES // 2), F32)
    for x in range(n // 2):
        for y in range(n):
            tiles = [
                jnp.concatenate([mass_ref[xx, y, z : z + ROWS], zero], axis=1) for xx in (x, x + n // 2) for z in (0, ROWS)
            ]
            low = by_quarter([turn(v, 32 * k) for k, v in enumerate(tiles)])
            high = by_quarter([turn(v, 32 * k - 32) for k, v in enumerate(tiles)])
            at = rows_of(x * n + y)
            keep_ref[at], send_ref[at] = order(low, high, lower)


def wind_kernel(wind_ref, keep_ref, out_ref):
    del keep_ref
    n = wind_ref.shape[1]
    for d in range(3):
        levels = wind_ref[d].reshape(n * n, 2 * ROWS).T * (1.0 / 12.0)
        out_ref[rows_of(d)] = jnp.concatenate([levels[:ROWS], levels[ROWS:]], axis=1)


def sides(axis, first_ref, second_ref):
    even, place = is_even(axis), lax.axis_index(axis)
    inner_low, inner_high = place > 0, place < lax.axis_size(axis) - 1

    def below(at):
        return jnp.where(inner_low, jnp.where(even, second_ref[at], first_ref[at]), 0.0)

    def above(at):
        return jnp.where(inner_high, jnp.where(even, first_ref[at], second_ref[at]), 0.0)

    return below, above


def by_parity(axis, body):
    even = is_even(axis)
    pl.when(even)(lambda: body(0, 1))
    pl.when(jnp.logical_not(even))(lambda: body(1, 0))


def merge_kernel(keep_ref, got_ref, own_wind_ref, got_wind_ref, block_ref, y_first, y_second, x_first, x_second):
    n = 8
    lower = is_even("gz")
    low = lane_ids() < 64
    for x in range(n // 2):
        for y in range(n):
            at = rows_of(x * n + y)
            a, b = order(keep_ref[at], got_ref[at], lower)
            block_ref[at] = jnp.where(low, a, turn(b, 64))
            block_ref[rows_of((x + n // 2) * n + y)] = jnp.where(low, turn(a, 64), b)
    for d in range(3):
        a, b = order(own_wind_ref[rows_of(d)], got_wind_ref[rows_of(d)], lower)
        block_ref[rows_of(n * n + 2 * d)] = by_quarter([a, turn(a, -32), turn(b, 64), turn(b, 32)])
        block_ref[rows_of(n * n + 2 * d + 1)] = by_quarter([turn(a, -32), turn(a, -64), turn(b, 32), b])

    def along_y(up, down):
        for ref, start, wide in (((y_first, y_second)[up], n - PAD_LO, PAD_LO), ((y_first, y_second)[down], 0, PAD_HI)):
            for x in range(n):
                ref[rows_of(x * wide, wide)] = block_ref[rows_of(x * n + start, wide)]
            ref[rows_of(n * wide, 6)] = block_ref[rows_of(n * n, 6)]

    def along_x(up, down):
        for ref, start, wide, part in (((x_first, x_second)[up], n - PAD_LO, PAD_LO, 1), ((x_first, x_second)[down], 0, PAD_HI, 0)):
            ref[rows_of(0, wide * n)] = block_ref[rows_of(start * n, wide * n)]
            for d in range(3):
                ref[rows_of(wide * n + d)] = block_ref[rows_of(n * n + 2 * d + part)]

    by_parity("gy", along_y)
    by_parity("gx", along_x)


def corner_kernel(n, parts, first_ref, second_ref, own_change, pairs_ref, *messages):
    del own_change, pairs_ref
    tiles = groups(parts)[2]
    half = tiles // 2
    below, above = sides("gy", first_ref, second_ref)

    def body(up, down):
        for ref, start, narrow, part in ((messages[up], n - LO, LO, half), (messages[down], 0, HI, 0)):
            at = 0
            for x in range(start, start + narrow):
                ref[rows_of(at, LO)] = below(rows_of(x * PAD_LO + PAD_LO - LO, LO))
                ref[rows_of(at + LO, HI)] = above(rows_of(x * PAD_HI, HI))
                at += LINES
            for side, base in ((below, n * PAD_LO), (above, n * PAD_HI)):
                ref[rows_of(at)] = side(rows_of(base + (tiles - 1 if part else 0)))
                ref[rows_of(at + 1, half)] = side(rows_of(base + tiles + part, half))
                at += 1 + half

    by_parity("gx", body)


def own_kernel(n, parts, block_ref, wind_x, wind_y, wind_z, change):
    width, deep, tiles = groups(parts)
    for d, out in enumerate((wind_x, wind_y, wind_z)):
        jobs = []
        for x in range(n):
            tile = block_ref[rows_of(n * n + d * tiles + x // deep)]
            jobs += [(tile, x, y, out, x * n + y) for y in range(n)]
        spread(jobs, parts)

    @pl.loop(0, n)
    def _(x):
        cells = [block_ref[eight(x * n, k)] for k in range(ROWS)]
        winds = [wind_z[eight(x * n, k)] for k in range(ROWS)]
        for k, value in enumerate(level_change(cells, winds, width)):
            change[eight(x * n, k)] = value


def y_kernel(n, parts, block_ref, first_ref, second_ref, wind_y, own_change, *refs):
    width, deep, tiles = groups(parts)
    cell, change, wind_x, far_y, wind_z, halo_change = refs
    below, above = sides("gy", first_ref, second_ref)
    span, reach = n + PAD_LO + PAD_HI, n + LINES

    for x in range(n):
        cell[rows_of(x * span, PAD_LO)] = below(rows_of(x * PAD_LO, PAD_LO))
        cell[rows_of(x * span + PAD_LO, n)] = block_ref[rows_of(x * n, n)]
        cell[rows_of(x * span + PAD_LO + n, PAD_HI)] = above(rows_of(x * PAD_HI, PAD_HI))
    jobs = []
    for d in range(3):
        for t in range(tiles):
            low, high = below(rows_of(n * PAD_LO + d * tiles + t)), above(rows_of(n * PAD_HI + d * tiles + t))
            for x in range(t * deep, (t + 1) * deep):
                if d == 1:
                    jobs += [(low, x, n - LO - 1 + y, far_y, x * (LINES + 2) + y) for y in range(LO + 1)]
                    jobs += [(high, x, y, far_y, x * (LINES + 2) + LO + 1 + y) for y in range(HI + 1)]
                else:
                    out = wind_z if d else wind_x
                    jobs += [(low, x, n - LO + y, out, y * n + x) for y in range(LO)]
                    jobs += [(high, x, y, out, (LO + y) * n + x) for y in range(HI)]
    spread(jobs, parts)

    @pl.loop(0, LINES)
    def _(i):
        first = halo_line(i, n) + PAD_LO
        cells = [cell[eight(first, k, span)] for k in range(ROWS)]
        winds = [wind_z[eight(i * n, k)] for k in range(ROWS)]
        for k, value in enumerate(level_change(cells, winds, width)):
            halo_change[eight(i * n, k)] = value

    @pl.loop(0, n)
    def _(x):
        cells = [cell[rows_of(x * span + y)] for y in range(span)]
        far = [far_y[rows_of(x * (LINES + 2) + y)] for y in range(LINES + 2)]
        winds = far[: LO + 1] + [wind_y[rows_of(x * n + y)] for y in range(n)] + far[LO + 1 :]
        for y, value in enumerate(line_change(cells, winds)):
            if LO <= y < LO + n:
                value = value + own_change[rows_of(x * n + y - LO)]
            else:
                value = value + halo_change[rows_of((y if y < LO else y - n) * n + x)]
            change[rows_of(x * reach + y)] = value


def inside(axis):
    place = lax.axis_index(axis)
    return [jnp.where(ok, 1.0, 0.0) for ok in (place > 0, place < lax.axis_size(axis) - 1)]


def inner_kernel(n, parts, cell, change, wind_x, halo_wind_x, wind_y, far_wind_y, wind_z, one, edge, second):
    width = groups(parts)[0]
    span, reach = n + PAD_LO + PAD_HI, n + LINES
    begin, end = LO, n - HI
    south_in, north_in = inside("gy")

    def line(at, winds, keep):
        cells = [cell[rows_of(x * span + LO + at)] for x in range(n)]
        fluxes = line_fluxes(cells, winds)
        edge[rows_of(at)] = fluxes[0]
        edge[rows_of(reach + at)] = fluxes[-1]
        for i, value in enumerate(changes(fluxes)):
            x = begin + i
            value = cells[x] + (value + change[rows_of(x * reach + at)])
            one[rows_of(i * reach + at)] = value if keep is None else value * keep

    @pl.loop(0, n)
    def _(y):
        line(LO + y, [wind_x[rows_of(x * n + y)] for x in range(begin - 1, end + 1)], None)

    @pl.loop(0, LINES)
    def _(i):
        winds = [halo_wind_x[rows_of(i * n + x)] for x in range(begin - 1, end + 1)]
        line(halo_line(i, n) + LO, winds, jnp.where(i < LO, south_in, north_in))

    @pl.loop(0, end - begin)
    def _(i):
        second_y_z(n, width, begin + i, one, i, wind_y, far_wind_y, wind_z, second, i)


def second_y_z(n, width, x, one, one_x, wind_y, far_wind_y, wind_z, second, second_x):
    reach = n + LINES
    cells = [one[rows_of(one_x * reach + y)] for y in range(reach)]
    winds = [far_wind_y[rows_of(x * (LINES + 2) + LO)]] + [wind_y[rows_of(x * n + y)] for y in range(n)]
    winds += [far_wind_y[rows_of(x * (LINES + 2) + LO + 1)]]
    for y, value in enumerate(line_change(cells, winds)):
        second[rows_of(second_x * n + y)] = value
    cells = [one[eight(one_x * reach + LO, k)] for k in range(ROWS)]
    winds = [wind_z[eight(x * n, k)] for k in range(ROWS)]
    for k, value in enumerate(level_change(cells, winds, width)):
        at = eight(second_x * n, k)
        second[at] = second[at] + value


def x_kernel(n, parts, cell, change, wind_x, edge, second_ref, first_ref, mid, far_wind_x, side, side_wind_y, *scratch):
    far, side_wind_z, side_change = scratch
    width, deep, tiles = groups(parts)
    half = tiles // 2
    west, east = sides("gx", first_ref, second_ref)
    span, reach = n + PAD_LO + PAD_HI, n + LINES

    jobs = []
    for take, wide, near_from, far_from, line in ((west, PAD_LO, LO, 0, 0), (east, PAD_HI, 0, HI, LO)):
        narrow = wide // 2
        side[rows_of(line * n, narrow * n)] = take(rows_of(near_from * n, narrow * n))
        far[rows_of(line * n, narrow * n)] = take(rows_of(far_from * n, narrow * n))
        layers, shift = (range(n - narrow, n), half) if line == 0 else (range(narrow), 0)
        wider = range(n - narrow - 1, n) if line == 0 else range(narrow + 1)

        def winds_of(d, x):
            return take(rows_of(wide * n + d * half + x // deep - shift))

        for i, x in enumerate(wider):
            jobs += [(winds_of(0, x), x, y, far_wind_x, (line + bool(line) + i) * n + y) for y in range(n)]
        for d, out in ((1, side_wind_y), (2, side_wind_z)):
            for i, x in enumerate(layers):
                jobs += [(winds_of(d, x), x, y, out, (line + i) * n + y) for y in range(n)]
    spread(jobs, parts)

    @pl.loop(0, LINES)
    def _(i):
        cells = [side[eight(i * n, k)] for k in range(ROWS)]
        winds = [side_wind_z[eight(i * n, k)] for k in range(ROWS)]
        for k, value in enumerate(level_change(cells, winds, width)):
            side_change[eight(i * n, k)] = value

    begin, end = LO, n - HI

    @pl.loop(0, n)
    def _(y):
        outer = [far[rows_of(i * n + y)] for i in range(LINES)]
        near = [side[rows_of(i * n + y)] for i in range(LINES)]
        cells = outer[:LO] + near[:LO] + [cell[rows_of(x * span + PAD_LO + y)] for x in range(n)] + near[LO:] + outer[LO:]
        winds = [far_wind_x[rows_of(i * n + y)] for i in range(LINES + 2)]
        winds = winds[: LO + 1] + [wind_x[rows_of(x * n + y)] for x in range(n)] + winds[LO + 1 :]
        low = line_fluxes(cells[: PAD_LO + begin + 1], winds[: LO + 1 + begin]) + [edge[rows_of(LO + y)]]
        high = [edge[rows_of(reach + LO + y)]] + line_fluxes(cells[PAD_LO + end - HI :], winds[LO + 1 + end :])
        values = dict(zip(range(-LO, begin), changes(low))) | dict(zip(range(end, n + HI), changes(high)))
        for x, value in values.items():
            if 0 <= x < n:
                value = value + change[rows_of(x * reach + LO + y)]
            else:
                value = value + side_change[rows_of((x + LO if x < 0 else x + LO - n) * n + y)]
            mid[rows_of((x + LO) * n + y)] = cells[PAD_LO + x] + value


def main_kernel(n, parts, *refs):
    cell, change, wind_x, wind_y, wind_z, halo_wind_x, far_wind_y, inner, edge, inner_second = refs[:10]
    mid, far_wind_x, side, side_wind_y, second_ref, first_ref, rate_ref, steps_ref = refs[10:18]
    one, *out_refs = refs[18:21]
    corner, corner_wind_x, edge_wind_y, second, fallen = refs[21:]
    deep, tiles = groups(parts)[1:]
    half = tiles // 2
    west, east = sides("gx", first_ref, second_ref)
    span, reach = n + PAD_LO + PAD_HI, n + LINES

    jobs = []
    for take, narrow, line in ((west, LO, 0), (east, HI, LO)):
        at = narrow * LINES
        corner[rows_of(line * LINES, at)] = take(rows_of(0, at))
        below, above = at, at + 1 + half
        layers, shift = (range(n - narrow, n), half) if line == 0 else (range(narrow), 0)
        for y in range(LINES):
            tile = take(rows_of(below if y < LO else above))
            x = layers[-1] if line == 0 else layers[0]
            jobs.append((tile, x, n - LO + y if y < LO else y - LO, corner_wind_x, bool(line) * LINES + y))
        for i, x in enumerate(layers):
            tile = x // deep - shift
            jobs.append((take(rows_of(below + 1 + tile)), x, n - 1, edge_wind_y, 2 * (line + i)))
            jobs.append((take(rows_of(above + 1 + tile)), x, 0, edge_wind_y, 2 * (line + i) + 1))
    spread(jobs, parts)

    west_in, east_in = inside("gx")
    south_in, north_in = inside("gy")
    begin, end = LO, n - HI
    one[rows_of((begin + LO) * reach, (end - begin) * reach)] = inner[...]
    for x in [x for x in range(n) if not begin <= x < end]:
        one[rows_of((x + LO) * reach + LO, n)] = mid[rows_of((x + LO) * n, n)]

    @pl.loop(0, LINES)
    def _(i):
        corners = [corner[rows_of(i * LINES + y)] for y in range(LINES)]
        cells = corners[:LO] + [side[rows_of(i * n + y)] for y in range(n)] + corners[LO:]
        winds = [side_wind_y[rows_of(i * n + y)] for y in range(n)]
        winds = [edge_wind_y[rows_of(2 * i)]] + winds + [edge_wind_y[rows_of(2 * i + 1)]]
        keep = jnp.where(i < LO, west_in, east_in)
        line = halo_line(i, n) + LO
        for y, value in enumerate(line_change(cells, winds)):
            one[rows_of(line * reach + LO + y)] = (mid[rows_of(line * n + y)] + value) * keep

    @pl.loop(0, LINES)
    def _(i):
        line = halo_line(i, n) + LO
        near = [corner[rows_of(k * LINES + i)] for k in range(LINES)]
        cells = near[:LO] + [cell[rows_of(x * span + LO + line)] for x in range(n)] + near[LO:]
        winds = [halo_wind_x[rows_of(i * n + x)] for x in range(n)]
        winds = [corner_wind_x[rows_of(i)]] + winds + [corner_wind_x[rows_of(LINES + i)]]
        keep = jnp.where(i < LO, south_in, north_in)
        low = line_fluxes(cells[: LO + begin + 1], winds[: begin + 1]) + [edge[rows_of(line)]]
        high = [edge[rows_of(reach + line)]] + line_fluxes(cells[LO + end - HI :], winds[end + 1 :])
        values = dict(zip(range(begin), changes(low))) | dict(zip(range(end, n), changes(high)))
        for x, value in values.items():
            one[rows_of((x + LO) * reach + line)] = (cells[x + LO] + (value + change[rows_of(x * reach + line)])) * keep

    fall_half(
        n, parts, 0, one, cell, wind_x, far_wind_x, wind_y, far_wind_y, wind_z, inner_second, rate_ref, steps_ref,
        out_refs, second, fallen,
    )


def late_kernel(
    n, parts, one, cell, wind_x, far_wind_x, wind_y, far_wind_y, wind_z, inner_second, rate_ref, steps_ref, *refs
):
    fall_half(
        n, parts, n // 2, one, cell, wind_x, far_wind_x, wind_y, far_wind_y, wind_z, inner_second, rate_ref, steps_ref,
        refs[:2], *refs[2:],
    )


def fall_half(
    n, parts, begin, one, cell, wind_x, far_wind_x, wind_y, far_wind_y, wind_z, inner_second, rate_ref, steps_ref,
    out_refs, second, fallen,
):
    width = groups(parts)[0]
    span, reach, half = n + PAD_LO + PAD_HI, n + LINES, n // 2
    end = begin + half
    ready = [x for x in range(LO, n - HI) if begin <= x < end]
    left = [x for x in range(begin, end) if x not in ready]
    second[rows_of((ready[0] - begin) * n, len(ready) * n)] = inner_second[rows_of((ready[0] - LO) * n, len(ready) * n)]

    @pl.loop(left[0], left[-1] + 1)
    def _(x):
        second_y_z(n, width, x, one, x + LO, wind_y, far_wind_y, wind_z, second, x - begin)

    @pl.loop(0, n)
    def _(y):
        cells = [one[rows_of(x * reach + LO + y)] for x in range(begin, end + LINES)]
        winds = [wind_x[rows_of(x * n + y)] for x in range(max(begin - 1, 0), min(end + 1, n))]
        if begin == 0:
            winds = [far_wind_x[rows_of(LO * n + y)]] + winds
        else:
            winds = winds + [far_wind_x[rows_of((LO + 1) * n + y)]]
        for i, value in enumerate(line_change(cells, winds)):
            value = cells[i + LO] + (value + second[rows_of(i * n + y)])
            fallen[rows_of(i * n + y)] = 0.5 * cell[rows_of((begin + i) * span + PAD_LO + y)] + 0.5 * value

    bins = LANES // 2 // parts
    ids = lax.axis_index("gz") * bins + lane_ids() % bins
    rates, steps = [
        pick(jnp.broadcast_to(jnp.concatenate([ref[...]] * 2, axis=1), (ROWS, LANES)), ids) for ref in (rate_ref, steps_ref)
    ]

    columns = [[fallen[eight(i * n, k)] for k in range(ROWS)] for i in range(half)]
    rain = [jnp.zeros((ROWS, LANES), F32)] * half
    for block in range(SUBS // AHEAD):
        columns = [column + [from_above(v, width) for v in column[:AHEAD]] for column in columns]
        for s in range(AHEAD):
            rate = jnp.where(block * AHEAD + s < steps, rates, 0.0)
            for i, column in enumerate(columns):
                rain[i] = rain[i] + rate * column[0]
                columns[i] = [v + rate * (u - v) for v, u in zip(column, column[1:])]
    for i, column in enumerate(columns):
        for k in range(ROWS):
            fallen[eight(i * n, k)] = column[k]

    if parts == 2:
        send_ref, keep_ref = out_refs
        lower = is_even("gz")
        low = lane_ids() < 64
        count = half * n // 2
        for c in range(count):
            a, b = fallen[rows_of(c)], fallen[rows_of(count + c)]
            at = rows_of(c)
            keep_ref[at], send_ref[at] = order(jnp.where(low, a, turn(b, 64)), jnp.where(low, turn(a, 64), b), lower)
        value = by_quarter([turn(rain[i], 32 * i) for i in range(4)])
        keep_ref[rows_of(count)] = value
        send_ref[rows_of(count)] = value
    else:
        settled_ref, rain_ref = out_refs
        settled_ref[...] = fallen[...]
        for i in range(half):
            rain_ref[rows_of(i)] = rain[i]


def matrix_kernel(bins, gain_ref, loss_ref, pairs_ref, lost_ref, wide, tall):
    zero = jnp.zeros((bins, LANES - bins), F32)
    shifts = bins // 2

    @pl.loop(0, bins)
    def _(i):
        rows = gain_ref[pl.ds(i * bins, bins)].astype(F32)
        rows = jnp.concatenate([rows, zero], axis=1)
        wide[pl.ds(i * 2 * bins, bins)] = rows
        wide[pl.ds(i * 2 * bins + bins, bins)] = rows
        tall[pl.ds(i * bins, bins)] = rows

        @pl.when(i < shifts)
        def _():
            tall[pl.ds((i + bins) * bins, bins)] = rows

    for d in range(shifts + 1):
        rows = wide[pl.ds(d, bins, stride=2 * bins + 1)]
        if 0 < d < shifts:
            rows = rows + tall[pl.ds(d * bins, bins, stride=bins + 1)]
        pairs_ref[pl.ds(d * LANES, bins)] = rows.astype(jnp.bfloat16)
        pairs_ref[pl.ds(d * LANES + bins, bins)] = pltpu.roll(rows, bins, 1).astype(jnp.bfloat16)
    rows = jnp.concatenate([loss_ref[...].astype(F32), zero], axis=1)
    lost_ref[pl.ds(0, bins)] = rows.astype(jnp.bfloat16)
    lost_ref[pl.ds(bins, bins)] = pltpu.roll(rows, bins, 1).astype(jnp.bfloat16)


def breakup_rows(mass, pairs_ref, lost_ref, products):
    bins = LANES // 2
    count = mass.shape[0]
    lanes = lane_ids()
    rounded = mass.astype(jnp.bfloat16)
    wide = rounded.astype(F32)
    gained = None
    shifts = bins // 2 + 1
    for begin in range(0, shifts, 4):
        end = min(begin + 4, shifts)
        for d in range(begin, end):
            ids = lanes // bins * bins + (lanes + d) % bins
            for r in range(0, count, 2 * ROWS):
                halves = [wide[r + ROWS * k : r + ROWS * (k + 1)] for k in range(2)]
                halves = [v * pick(v, ids) if d else v * v for v in halves]
                both = jnp.concatenate(halves, axis=0).astype(jnp.bfloat16)
                products[pl.ds(r, 2 * ROWS), d * LANES : (d + 1) * LANES] = both
        part = jnp.dot(
            products[pl.ds(0, count), begin * LANES : end * LANES],
            pairs_ref[pl.ds(begin * LANES, (end - begin) * LANES)],
            preferred_element_type=F32,
        )
        gained = part if gained is None else gained + part
    loss = jnp.dot(rounded, lost_ref[...], preferred_element_type=F32)
    return mass + gained - mass * loss


def breakup_half(n, keep_ref, got_ref, pairs_ref, lost_ref, columns, products):
    first = is_even("gz")
    count = n * n // 4
    for c in range(count):
        a, b = order(keep_ref[rows_of(c)], got_ref[rows_of(c)], first)
        columns[rows_of(c)] = by_quarter([a, turn(b, 32), turn(a, 32), turn(b, 64)])
        columns[rows_of(count + c)] = by_quarter([turn(a, -64), turn(b, -32), turn(a, -32), b])
    a, b = order(keep_ref[rows_of(count)], got_ref[rows_of(count)], first)
    a, b = [jnp.where(first, v[: n // 2], v[n // 2 :]) for v in (a, b)]
    columns[...] = breakup_rows(columns[...], pairs_ref, lost_ref, products)
    return [jnp.concatenate([a[:, 32 * i : 32 * i + 32], b[:, 32 * i : 32 * i + 32]], axis=1) for i in range(4)]


def lay_out(columns, mass, n, begin):
    for x in range(n // 2):
        for y in range(n):
            value = columns[rows_of(x * n + y)]
            mass[begin + x, y, 0:ROWS] = value[:, :64]
            mass[begin + x, y, ROWS : 2 * ROWS] = value[:, 64:]


def breakup_first_kernel(n, keep_ref, got_ref, pairs_ref, lost_ref, mass_ref, rain_ref, columns, products):
    for i, value in enumerate(breakup_half(n, keep_ref, got_ref, pairs_ref, lost_ref, columns, products)):
        rain_ref[i] = value
    lay_out(columns, mass_ref, n, 0)


def breakup_last_kernel(
    n, keep_ref, got_ref, pairs_ref, lost_ref, early, early_rain, mass_out, rain_out, columns, products, mass, rain, sems
):
    half = n // 2
    early_copy = pltpu.make_async_copy(early, mass_out.at[pl.ds(0, half)], sems.at[0])
    early_copy.start()
    late_rain = breakup_half(n, keep_ref, got_ref, pairs_ref, lost_ref, columns, products)
    for i in range(half):
        rain[i] = early_rain[i]
        rain[half + i] = late_rain[i]
    rain_copy = pltpu.make_async_copy(rain, rain_out, sems.at[2])
    rain_copy.start()
    lay_out(columns, mass, n, 0)
    late_copy = pltpu.make_async_copy(mass, mass_out.at[pl.ds(half, half)], sems.at[1])
    late_copy.start()
    for copy in (early_copy, rain_copy, late_copy):
        copy.wait()


def breakup_plain_kernel(mass_ref, pairs_ref, lost_ref, out_ref, products):
    count = products.shape[0]

    @pl.loop(0, mass_ref.shape[0] // count)
    def _(i):
        start = pl.multiple_of(i * count, count)
        out_ref[pl.ds(start, count)] = breakup_rows(mass_ref[pl.ds(start, count)], pairs_ref, lost_ref, products)


def shape(*dims, dtype=F32):
    return jax.ShapeDtypeStruct(dims, dtype)


def tiles_of(count):
    return shape(count * ROWS, LANES)


def call(kernel, outs, args, scratch=(), micros=1.0, out_place=pltpu.VMEM, copies=0):
    scratch = [pltpu.VMEM(s.shape, s.dtype) for s in scratch]
    if copies:
        scratch.append(pltpu.SemaphoreType.DMA((copies,)))
    return pl.pallas_call(
        kernel,
        out_shape=outs,
        in_specs=[VMEM] * len(args),
        out_specs=jax.tree.map(lambda _: pl.BlockSpec(memory_space=out_place), outs),
        scratch_shapes=scratch,
        compiler_params=pltpu.CompilerParams(vmem_limit_bytes=40 << 20),
        cost_estimate=pl.CostEstimate(
            flops=int(micros * 1.1e9), bytes_accessed=int(micros * 3.6e6), transcendentals=0
        ),
    )(*args)


def swap_neighbours(axis, begin, message):
    axes = ("gx", "gy")
    sizes = [lax.axis_size(a) for a in axes]
    along = axes.index(axis)

    def partner(place, start, count):
        to = start + ((place - start) ^ 1)
        return to if start <= place and to < count else place

    pairs = []
    for here in range(sizes[0] * sizes[1]):
        place = list(divmod(here, sizes[1]))
        to = partner(place[along], begin, sizes[along])
        if to == place[along]:
            place[1 - along] = partner(place[1 - along], 0, sizes[1 - along])
        place[along] = to
        pairs.append((here, place[0] * sizes[1] + place[1]))
    return lax.ppermute(message, axes, pairs)


def per_device(bin_mass, courant, sub_courant, fall_steps, frag_gain, collide):
    nx, ny, nz, bins = bin_mass.shape
    n = nx
    parts = lax.axis_size("gz")
    gz, gy = lax.axis_index("gz"), lax.axis_index("gy")
    width = bins // parts
    tiles = groups(parts)[2]
    winds = 3 * tiles

    pair_rows = (bins // 2 + 1) * LANES
    pairs, lost = call(
        functools.partial(matrix_kernel, bins),
        (shape(pair_rows, LANES, dtype=jnp.bfloat16), shape(LANES, LANES, dtype=jnp.bfloat16)),
        (frag_gain, collide),
        [shape(2 * bins * bins, LANES), shape(3 * bins * bins // 2, LANES)],
        micros=1.4,
    )

    y_message = tiles_of(n * PAD_LO + winds)
    x_message = tiles_of(n * PAD_LO + winds // 2)
    if parts == 2:
        half = tiles_of(n * n // 2)
        send, keep = call(pack_kernel, (half, half), (bin_mass,), micros=0.3)
        got = lax.ppermute(send, "gz", [(0, 1), (1, 0)])
        own_wind = call(wind_kernel, tiles_of(3), (courant, keep), micros=0.1)
        got_wind = lax.ppermute(own_wind, "gz", [(0, 1), (1, 0)])
        block, *messages = call(
            merge_kernel,
            [tiles_of(n * n + winds), y_message, y_message, x_message, x_message],
            (keep, got, own_wind, got_wind),
            micros=0.2,
        )
    else:
        split = bin_mass.reshape(nx, ny, nz // ROWS, ROWS, parts, width).transpose(4, 0, 1, 3, 2, 5)
        split = lax.all_to_all(split, "gz", split_axis=0, concat_axis=0, tiled=True)
        cube = split.transpose(1, 2, 3, 0, 4, 5).reshape(n, n, ROWS, LANES)
        air = courant.reshape(3, nx, ny, nz // ROWS, ROWS).transpose(0, 4, 3, 1, 2) * (1.0 / 12.0)
        air = lax.all_gather(air, "gz").reshape(parts, 3, ROWS, nz // ROWS, tiles, nx // tiles, ny)
        air = air.transpose(1, 4, 2, 0, 3, 5, 6).reshape(3, tiles, ROWS, LANES)
        block = jnp.concatenate([cube.reshape(-1, LANES), air.reshape(-1, LANES)])
        messages = []
        for layers, low_air, high_air, message, even in (
            (cube.transpose(1, 0, 2, 3), air, air, y_message, gy % 2 == 0),
            (cube, air[:, : tiles // 2], air[:, tiles // 2 :], x_message, lax.axis_index("gx") % 2 == 0),
        ):
            up, down = layers[n - PAD_LO :], layers[:PAD_HI]
            if message is y_message:
                up, down = up.transpose(1, 0, 2, 3), down.transpose(1, 0, 2, 3)
            up = jnp.concatenate([up.reshape(-1, LANES), high_air.reshape(-1, LANES)])
            down = jnp.concatenate([down.reshape(-1, LANES), low_air.reshape(-1, LANES)])
            messages += order(up, jnp.pad(down, ((0, up.shape[0] - down.shape[0]), (0, 0))), even)

    from_y = swap_neighbours("gy", 0, messages[0]), swap_neighbours("gy", 1, messages[1])
    from_x = swap_neighbours("gx", 1, messages[3]), swap_neighbours("gx", 0, messages[2])
    wind_x, wind_y, wind_z, own_change = call(
        functools.partial(own_kernel, n, parts), [tiles_of(n * n)] * 4, (block,), micros=1.7
    )
    message = tiles_of(LO * LINES + 2 + tiles)
    corners = call(functools.partial(corner_kernel, n, parts), (message, message), (*from_y, own_change, pairs), micros=0.1)
    corners = swap_neighbours("gx", 1, corners[1]), swap_neighbours("gx", 0, corners[0])
    cell, change, halo_wind_x, far_wind_y = call(
        functools.partial(y_kernel, n, parts),
        [tiles_of(n * (n + PAD_LO + PAD_HI)), tiles_of(n * (n + LINES)), tiles_of(LINES * n), tiles_of(n * (LINES + 2))],
        (block, *from_y, wind_y, own_change),
        [tiles_of(LINES * n)] * 2,
        micros=2.0,
    )
    reach, half, inner = n + LINES, n // 2, n - LINES
    near = call(
        functools.partial(inner_kernel, n, parts),
        [tiles_of(inner * reach), tiles_of(2 * reach), tiles_of(inner * n)],
        (cell, change, wind_x, halo_wind_x, wind_y, far_wind_y, wind_z),
        micros=0.9,
    )
    mid, far_wind_x, side, side_wind_y = call(
        functools.partial(x_kernel, n, parts),
        [tiles_of(count) for count in (reach * n, (LINES + 2) * n, LINES * n, LINES * n)],
        (cell, change, wind_x, near[1], *from_x),
        [tiles_of(LINES * n)] * 3,
        micros=1.7,
    )
    fall = sub_courant.reshape(1, bins), fall_steps.reshape(1, bins)
    message = [tiles_of(n * half // 2 + 1)] * 2 if parts == 2 else [tiles_of(n * half), tiles_of(half)]
    one, *early = call(
        functools.partial(main_kernel, n, parts),
        [tiles_of(reach * reach)] + message,
        (
            *(cell, change, wind_x, wind_y, wind_z, halo_wind_x, far_wind_y, *near),
            *(mid, far_wind_x, side, side_wind_y, *corners, *fall),
        ),
        [tiles_of(count) for count in (LINES * LINES, 2 * LINES, 2 * LINES, n * half, n * half)],
        micros=2.0,
    )
    if parts == 2:
        early_got = lax.ppermute(early[0], "gz", [(0, 1), (1, 0)])
    late = call(
        functools.partial(late_kernel, n, parts),
        message,
        (one, cell, wind_x, far_wind_x, wind_y, far_wind_y, wind_z, near[2], *fall),
        [tiles_of(n * half)] * 2,
        micros=1.5,
    )

    products = shape(n * half * ROWS, pair_rows, dtype=jnp.bfloat16)
    if parts == 2:
        late_got = lax.ppermute(late[0], "gz", [(0, 1), (1, 0)])
        early = call(
            functools.partial(breakup_first_kernel, n),
            [shape(half, ny, nz, bins), shape(half, ny // parts, bins)],
            (early[1], early_got, pairs, lost),
            [tiles_of(n * half), products],
            micros=1.5,
        )
        outs = [shape(nx, ny, nz, bins), shape(nx, ny // parts, bins)]
        return tuple(
            call(
                functools.partial(breakup_last_kernel, n),
                outs,
                (late[1], late_got, pairs, lost, *early),
                [tiles_of(n * half), products, shape(half, ny, nz, bins), outs[1]],
                micros=1.5,
                out_place=pl.ANY,
                copies=3,
            )
        )

    settled, rain = [jnp.concatenate(halves) for halves in zip(early, late)]
    rain = rain.reshape(nx, ny, LANES)[:, :, :width]
    rain = lax.all_to_all(rain, "gz", split_axis=1, concat_axis=2, tiled=True)
    settled = settled.reshape(nx, ny, ROWS, parts, nz // ROWS, width).transpose(3, 0, 1, 4, 2, 5)
    settled = lax.all_to_all(settled, "gz", split_axis=0, concat_axis=0, tiled=True)
    settled = settled.transpose(1, 2, 3, 4, 0, 5).reshape(nx * ny, nz // ROWS, ROWS, bins)
    paired = settled.transpose(0, 2, 1, 3).reshape(-1, LANES)
    updated = call(breakup_plain_kernel, tiles_of(n * n), (paired, pairs, lost), [products], micros=3.0)
    updated = updated.reshape(nx, ny, ROWS, nz // ROWS, bins).transpose(0, 1, 3, 2, 4).reshape(nx, ny, nz, bins)
    return updated, rain


def solution(mesh):
    in_specs = (P("gx", "gy", "gz", None), P(None, "gx", "gy", "gz"), P(), P(), P(), P())
    out_specs = (P("gx", "gy", "gz", None), P("gx", ("gy", "gz"), None))
    return jax.shard_map(per_device, mesh=mesh, in_specs=in_specs, out_specs=out_specs, check_vma=False)
```

```python
import functools
import itertools

import jax
import jax.numpy as jnp
from jax import lax
from jax.experimental import pallas as pl
from jax.experimental.pallas import tpu as pltpu
from jax.sharding import PartitionSpec as P

SUBS = 24
EPS = 1e-06
LO, HI = 3, 2
PAD_LO, PAD_HI = 2 * LO, 2 * HI
LINES = LO + HI
ROWS, LANES = 8, 128
AHEAD = 4
F32 = jnp.float32
VMEM = pl.BlockSpec(memory_space=pltpu.VMEM)


def lane_ids():
    return lax.broadcasted_iota(jnp.int32, (ROWS, LANES), 1)


def pick(tile, ids):
    return jnp.take_along_axis(tile, ids, axis=1, mode="promise_in_bounds")


def turn(tile, lanes):
    lanes %= LANES
    return pltpu.roll(tile, lanes, 1) if lanes else tile


def rows_of(first, count=1):
    return pl.ds(first * ROWS, count * ROWS)


def eight(first, level, step=1):
    return pl.ds(first * ROWS + level, ROWS, stride=step * ROWS)


def order(a, b, straight):
    return jnp.where(straight, a, b), jnp.where(straight, b, a)


def is_even(axis):
    return lax.axis_index(axis) % 2 == 0


def by_quarter(parts):
    quarter = lane_ids() // (LANES // 4)
    return jnp.where(quarter < 2, jnp.where(quarter == 0, parts[0], parts[1]), jnp.where(quarter == 2, parts[2], parts[3]))


def groups(parts):
    width = LANES // (2 * parts)
    return width, width // ROWS, ROWS * ROWS // width


def spread(jobs, parts):
    width, deep, _ = groups(parts)
    place = lane_ids() % width
    rows = [[], []]
    for tile, x, y, _, _ in jobs:
        top = tile.astype(jnp.bfloat16).astype(F32)
        here = place == x % deep * ROWS + y
        for out, term in zip(rows, (top, tile - top)):
            out.append(jnp.where(here, term, 0.0))
    terms = jnp.concatenate([jnp.concatenate(r, axis=0).astype(jnp.bfloat16) for r in rows], axis=1)
    source, target = [lax.broadcasted_iota(jnp.int32, (2 * LANES, LANES), k) for k in range(2)]
    same = jnp.where(source % LANES // width == target // width, 1.0, 0.0).astype(jnp.bfloat16)
    out = jnp.dot(terms, same, preferred_element_type=F32)
    for k, (_, _, _, ref, at) in enumerate(jobs):
        ref[rows_of(at)] = out[k * ROWS : (k + 1) * ROWS]


def halo_line(i, n):
    return jnp.where(i < LO, i - LO, i - LO + n)


def line_change(cells, winds):
    return changes(line_fluxes(cells, winds))


def changes(fluxes):
    return [a - b for a, b in zip(fluxes, fluxes[1:])]


def long_line(cells, winds, low_edge, high_edge, n):
    begin, end = LO, n - HI
    low = line_fluxes(cells[: PAD_LO + begin + 1], winds[: LO + 1 + begin]) + [low_edge]
    high = [high_edge] + line_fluxes(cells[PAD_LO + end - HI :], winds[LO + 1 + end :])
    return dict(zip(range(-LO, begin), changes(low))) | dict(zip(range(end, n + HI), changes(high)))


def line_fluxes(cells, winds):
    first = [b - a for a, b in zip(cells, cells[1:])]
    twice = [d + d for d in first]
    second = [b - a for a, b in zip(first, first[1:])]
    third = [a - b for a, b in zip(second, second[1:])]
    curved = [(13.0 / 3.0) * (c * c) + 4.0 * EPS for c in second]
    fluxes = []
    for j in range(len(cells) - 4):
        left = twice[j + 1] + second[j]
        mid = first[j + 1] + first[j + 2]
        right = twice[j + 2] - second[j + 2]
        e0 = curved[j] + left * left
        e1 = curved[j + 1] + mid * mid
        e2 = curved[j + 2] + right * right
        e0 = e0 * e0
        e1 = e1 * e1
        e2 = e2 * e2
        e0 = 3.0 * e0
        e2_twice = e2 + e2
        top = e1 * (e2_twice * third[j] + e0 * third[j + 1])
        low = e1 * (e2 + e0) + e0 * e2_twice
        inverse = pl.reciprocal(low, approx=True)
        estimate = 6.0 * cells[j + 2] + (first[j + 1] + twice[j + 2]) + top * inverse
        fluxes.append((winds[j] + winds[j + 1]) * estimate)
    return fluxes


def from_below(value, width):
    return jnp.where(lane_ids() < width, 0.0, turn(value, width))


def from_above(value, width):
    return jnp.where(lane_ids() >= LANES - width, 0.0, turn(value, -width))


def level_change(cells, winds, width):
    long_cells = [from_below(v, width) for v in cells[ROWS - LO :]] + cells + [from_above(v, width) for v in cells[:HI]]
    long_winds = [from_below(winds[-1], width)] + winds + [from_above(winds[0], width)]
    return line_change(long_cells, long_winds)


def pack_kernel(mass_ref, send_ref, keep_ref):
    lower = is_even("gz")
    n = mass_ref.shape[0]
    zero = jnp.zeros((ROWS, LANES // 2), F32)
    for x in range(n // 2):
        for y in range(n):
            tiles = [
                jnp.concatenate([mass_ref[xx, y, z : z + ROWS], zero], axis=1) for xx in (x, x + n // 2) for z in (0, ROWS)
            ]
            low = by_quarter([turn(v, 32 * k) for k, v in enumerate(tiles)])
            high = by_quarter([turn(v, 32 * k - 32) for k, v in enumerate(tiles)])
            at = rows_of(x * n + y)
            keep_ref[at], send_ref[at] = order(low, high, lower)


def wind_kernel(wind_ref, keep_ref, out_ref):
    del keep_ref
    n = wind_ref.shape[1]
    for d in range(3):
        levels = wind_ref[d].reshape(n * n, 2 * ROWS).T * (1.0 / 12.0)
        out_ref[rows_of(d)] = jnp.concatenate([levels[:ROWS], levels[ROWS:]], axis=1)


def sides(axis, first_ref, second_ref):
    even, place = is_even(axis), lax.axis_index(axis)
    inner_low, inner_high = place > 0, place < lax.axis_size(axis) - 1

    def below(at):
        return jnp.where(inner_low, jnp.where(even, second_ref[at], first_ref[at]), 0.0)

    def above(at):
        return jnp.where(inner_high, jnp.where(even, first_ref[at], second_ref[at]), 0.0)

    return below, above


def by_parity(axis, body):
    even = is_even(axis)
    pl.when(even)(lambda: body(0, 1))
    pl.when(jnp.logical_not(even))(lambda: body(1, 0))


def merge_kernel(keep_ref, got_ref, own_wind_ref, got_wind_ref, lost_ref, block_ref, y_first, y_second, x_first, x_second):
    del lost_ref
    n = 8
    lower = is_even("gz")
    low = lane_ids() < 64
    for x in range(n // 2):
        for y in range(n):
            at = rows_of(x * n + y)
            a, b = order(keep_ref[at], got_ref[at], lower)
            block_ref[at] = jnp.where(low, a, turn(b, 64))
            block_ref[rows_of((x + n // 2) * n + y)] = jnp.where(low, turn(a, 64), b)
    for d in range(3):
        a, b = order(own_wind_ref[rows_of(d)], got_wind_ref[rows_of(d)], lower)
        block_ref[rows_of(n * n + 2 * d)] = by_quarter([a, turn(a, -32), turn(b, 64), turn(b, 32)])
        block_ref[rows_of(n * n + 2 * d + 1)] = by_quarter([turn(a, -32), turn(a, -64), turn(b, 32), b])

    def along_y(up, down):
        for ref, start, wide in (((y_first, y_second)[up], n - PAD_LO, PAD_LO), ((y_first, y_second)[down], 0, PAD_HI)):
            for x in range(n):
                ref[rows_of(x * wide, wide)] = block_ref[rows_of(x * n + start, wide)]
            ref[rows_of(n * wide, 6)] = block_ref[rows_of(n * n, 6)]

    def along_x(up, down):
        for ref, start, wide, part in (((x_first, x_second)[up], n - PAD_LO, PAD_LO, 1), ((x_first, x_second)[down], 0, PAD_HI, 0)):
            ref[rows_of(0, wide * n)] = block_ref[rows_of(start * n, wide * n)]
            for d in range(3):
                ref[rows_of(wide * n + d)] = block_ref[rows_of(n * n + 2 * d + part)]

    by_parity("gy", along_y)
    by_parity("gx", along_x)


def corner_kernel(n, parts, first_ref, second_ref, own_change, *messages):
    del own_change
    tiles = groups(parts)[2]
    half = tiles // 2
    below, above = sides("gy", first_ref, second_ref)

    def body(up, down):
        for ref, start, narrow, part in ((messages[up], n - LO, LO, half), (messages[down], 0, HI, 0)):
            at = 0
            for x in range(start, start + narrow):
                ref[rows_of(at, LO)] = below(rows_of(x * PAD_LO + PAD_LO - LO, LO))
                ref[rows_of(at + LO, HI)] = above(rows_of(x * PAD_HI, HI))
                at += LINES
            for side, base in ((below, n * PAD_LO), (above, n * PAD_HI)):
                ref[rows_of(at)] = side(rows_of(base + (tiles - 1 if part else 0)))
                ref[rows_of(at + 1, half)] = side(rows_of(base + tiles + part, half))
                at += 1 + half

    by_parity("gx", body)


def own_kernel(n, parts, block_ref, wind_x, wind_y, wind_z, change, edge_x, edge_y):
    width, deep, tiles = groups(parts)
    for d, out in enumerate((wind_x, wind_y, wind_z)):
        jobs = []
        for x in range(n):
            tile = block_ref[rows_of(n * n + d * tiles + x // deep)]
            jobs += [(tile, x, y, out, x * n + y) for y in range(n)]
        spread(jobs, parts)

    @pl.loop(0, n)
    def _(x):
        cells = [block_ref[eight(x * n, k)] for k in range(ROWS)]
        winds = [wind_z[eight(x * n, k)] for k in range(ROWS)]
        for k, value in enumerate(level_change(cells, winds, width)):
            change[eight(x * n, k)] = value

    begin, end = LO, n - HI
    for wind, edge, place in ((wind_x, edge_x, lambda i, k: k * n + i), (wind_y, edge_y, lambda i, k: i * n + k)):

        @pl.loop(0, n)
        def _(i):
            cells = [block_ref[rows_of(place(i, k))] for k in range(n)]
            fluxes = line_fluxes(cells, [wind[rows_of(place(i, k))] for k in range(begin - 1, end + 1)])
            edge[rows_of(i)] = fluxes[0]
            edge[rows_of(n + i)] = fluxes[-1]
            for k, value in zip(range(begin, end), changes(fluxes)):
                at = rows_of(place(i, k))
                change[at] = change[at] + value


def y_kernel(n, parts, block_ref, first_ref, second_ref, wind_y, own_change, edge_y, *refs):
    width, deep, tiles = groups(parts)
    cell, change, wind_x, far_y, wind_z, halo_change = refs
    below, above = sides("gy", first_ref, second_ref)
    span, reach = n + PAD_LO + PAD_HI, n + LINES

    for x in range(n):
        cell[rows_of(x * span, PAD_LO)] = below(rows_of(x * PAD_LO, PAD_LO))
        cell[rows_of(x * span + PAD_LO, n)] = block_ref[rows_of(x * n, n)]
        cell[rows_of(x * span + PAD_LO + n, PAD_HI)] = above(rows_of(x * PAD_HI, PAD_HI))
    jobs = []
    for d in range(3):
        for t in range(tiles):
            low, high = below(rows_of(n * PAD_LO + d * tiles + t)), above(rows_of(n * PAD_HI + d * tiles + t))
            for x in range(t * deep, (t + 1) * deep):
                if d == 1:
                    jobs += [(low, x, n - LO - 1 + y, far_y, x * (LINES + 2) + y) for y in range(LO + 1)]
                    jobs += [(high, x, y, far_y, x * (LINES + 2) + LO + 1 + y) for y in range(HI + 1)]
                else:
                    out = wind_z if d else wind_x
                    jobs += [(low, x, n - LO + y, out, y * n + x) for y in range(LO)]
                    jobs += [(high, x, y, out, (LO + y) * n + x) for y in range(HI)]
    spread(jobs, parts)

    @pl.loop(0, LINES)
    def _(i):
        first = halo_line(i, n) + PAD_LO
        cells = [cell[eight(first, k, span)] for k in range(ROWS)]
        winds = [wind_z[eight(i * n, k)] for k in range(ROWS)]
        for k, value in enumerate(level_change(cells, winds, width)):
            halo_change[eight(i * n, k)] = value

    @pl.loop(0, n)
    def _(x):
        cells = [cell[rows_of(x * span + y)] for y in range(span)]
        far = [far_y[rows_of(x * (LINES + 2) + y)] for y in range(LINES + 2)]
        winds = far[: LO + 1] + [wind_y[rows_of(x * n + y)] for y in range(n)] + far[LO + 1 :]
        for y, value in long_line(cells, winds, edge_y[rows_of(x)], edge_y[rows_of(n + x)], n).items():
            if 0 <= y < n:
                value = value + own_change[rows_of(x * n + y)]
            else:
                value = value + halo_change[rows_of((y + LO if y < 0 else y + LO - n) * n + x)]
            change[rows_of(x * reach + y + LO)] = value
        for y in range(LO, n - HI):
            change[rows_of(x * reach + y + LO)] = own_change[rows_of(x * n + y)]


def inside(axis):
    place = lax.axis_index(axis)
    return [jnp.where(ok, 1.0, 0.0) for ok in (place > 0, place < lax.axis_size(axis) - 1)]


def inner_kernel(n, parts, cell, change, halo_wind_x, wind_y, far_wind_y, wind_z, edge_x, one, edge, second):
    width = groups(parts)[0]
    span, reach = n + PAD_LO + PAD_HI, n + LINES
    begin, end = LO, n - HI
    south_in, north_in = inside("gy")

    for k in range(2):
        edge[rows_of(k * reach + LO, n)] = edge_x[rows_of(k * n, n)]
    for i in range(end - begin):
        x = begin + i
        one[rows_of(i * reach + LO, n)] = cell[rows_of(x * span + PAD_LO, n)] + change[rows_of(x * reach + LO, n)]

    @pl.loop(0, LINES)
    def _(i):
        at = halo_line(i, n) + LO
        cells = [cell[rows_of(x * span + LO + at)] for x in range(n)]
        fluxes = line_fluxes(cells, [halo_wind_x[rows_of(i * n + x)] for x in range(begin - 1, end + 1)])
        edge[rows_of(at)] = fluxes[0]
        edge[rows_of(reach + at)] = fluxes[-1]
        keep = jnp.where(i < LO, south_in, north_in)
        for k, value in enumerate(changes(fluxes)):
            x = begin + k
            one[rows_of(k * reach + at)] = (cells[x] + (value + change[rows_of(x * reach + at)])) * keep

    @pl.loop(0, end - begin)
    def _(i):
        second_y_z(n, width, begin + i, one, i, wind_y, far_wind_y, wind_z, second, i)


def second_y_z(n, width, x, one, one_x, wind_y, far_wind_y, wind_z, second, second_x):
    reach = n + LINES
    cells = [one[rows_of(one_x * reach + y)] for y in range(reach)]
    winds = [far_wind_y[rows_of(x * (LINES + 2) + LO)]] + [wind_y[rows_of(x * n + y)] for y in range(n)]
    winds += [far_wind_y[rows_of(x * (LINES + 2) + LO + 1)]]
    for y, value in enumerate(line_change(cells, winds)):
        second[rows_of(second_x * n + y)] = value
    cells = [one[eight(one_x * reach + LO, k)] for k in range(ROWS)]
    winds = [wind_z[eight(x * n, k)] for k in range(ROWS)]
    for k, value in enumerate(level_change(cells, winds, width)):
        at = eight(second_x * n, k)
        second[at] = second[at] + value


def x_kernel(n, parts, cell, change, wind_x, edge, second_ref, first_ref, mid, far_wind_x, side, side_wind_y, *scratch):
    far, side_wind_z, side_change = scratch
    width, deep, tiles = groups(parts)
    half = tiles // 2
    west, east = sides("gx", first_ref, second_ref)
    span, reach = n + PAD_LO + PAD_HI, n + LINES

    jobs = []
    for take, wide, near_from, far_from, line in ((west, PAD_LO, LO, 0, 0), (east, PAD_HI, 0, HI, LO)):
        narrow = wide // 2
        side[rows_of(line * n, narrow * n)] = take(rows_of(near_from * n, narrow * n))
        far[rows_of(line * n, narrow * n)] = take(rows_of(far_from * n, narrow * n))
        layers, shift = (range(n - narrow, n), half) if line == 0 else (range(narrow), 0)
        wider = range(n - narrow - 1, n) if line == 0 else range(narrow + 1)

        def winds_of(d, x):
            return take(rows_of(wide * n + d * half + x // deep - shift))

        for i, x in enumerate(wider):
            jobs += [(winds_of(0, x), x, y, far_wind_x, (line + bool(line) + i) * n + y) for y in range(n)]
        for d, out in ((1, side_wind_y), (2, side_wind_z)):
            for i, x in enumerate(layers):
                jobs += [(winds_of(d, x), x, y, out, (line + i) * n + y) for y in range(n)]
    spread(jobs, parts)

    @pl.loop(0, LINES)
    def _(i):
        cells = [side[eight(i * n, k)] for k in range(ROWS)]
        winds = [side_wind_z[eight(i * n, k)] for k in range(ROWS)]
        for k, value in enumerate(level_change(cells, winds, width)):
            side_change[eight(i * n, k)] = value

    @pl.loop(0, n)
    def _(y):
        outer = [far[rows_of(i * n + y)] for i in range(LINES)]
        near = [side[rows_of(i * n + y)] for i in range(LINES)]
        cells = outer[:LO] + near[:LO] + [cell[rows_of(x * span + PAD_LO + y)] for x in range(n)] + near[LO:] + outer[LO:]
        winds = [far_wind_x[rows_of(i * n + y)] for i in range(LINES + 2)]
        winds = winds[: LO + 1] + [wind_x[rows_of(x * n + y)] for x in range(n)] + winds[LO + 1 :]
        for x, value in long_line(cells, winds, edge[rows_of(LO + y)], edge[rows_of(reach + LO + y)], n).items():
            if 0 <= x < n:
                value = value + change[rows_of(x * reach + LO + y)]
            else:
                value = value + side_change[rows_of((x + LO if x < 0 else x + LO - n) * n + y)]
            mid[rows_of((x + LO) * n + y)] = cells[PAD_LO + x] + value


def main_kernel(n, parts, *refs):
    cell, change, wind_x, wind_y, wind_z, halo_wind_x, far_wind_y, inner, edge, inner_second = refs[:10]
    mid, far_wind_x, side, side_wind_y, second_ref, first_ref, rate_ref, steps_ref = refs[10:18]
    one, *out_refs = refs[18:21]
    corner, corner_wind_x, edge_wind_y, second, fallen = refs[21:]
    deep, tiles = groups(parts)[1:]
    half = tiles // 2
    west, east = sides("gx", first_ref, second_ref)
    span, reach = n + PAD_LO + PAD_HI, n + LINES

    jobs = []
    for take, narrow, line in ((west, LO, 0), (east, HI, LO)):
        at = narrow * LINES
        corner[rows_of(line * LINES, at)] = take(rows_of(0, at))
        below, above = at, at + 1 + half
        layers, shift = (range(n - narrow, n), half) if line == 0 else (range(narrow), 0)
        for y in range(LINES):
            tile = take(rows_of(below if y < LO else above))
            x = layers[-1] if line == 0 else layers[0]
            jobs.append((tile, x, n - LO + y if y < LO else y - LO, corner_wind_x, bool(line) * LINES + y))
        for i, x in enumerate(layers):
            tile = x // deep - shift
            jobs.append((take(rows_of(below + 1 + tile)), x, n - 1, edge_wind_y, 2 * (line + i)))
            jobs.append((take(rows_of(above + 1 + tile)), x, 0, edge_wind_y, 2 * (line + i) + 1))
    spread(jobs, parts)

    west_in, east_in = inside("gx")
    south_in, north_in = inside("gy")
    begin, end = LO, n - HI
    one[rows_of((begin + LO) * reach, (end - begin) * reach)] = inner[...]
    for x in [x for x in range(n) if not begin <= x < end]:
        one[rows_of((x + LO) * reach + LO, n)] = mid[rows_of((x + LO) * n, n)]

    @pl.loop(0, LINES)
    def _(i):
        corners = [corner[rows_of(i * LINES + y)] for y in range(LINES)]
        cells = corners[:LO] + [side[rows_of(i * n + y)] for y in range(n)] + corners[LO:]
        winds = [side_wind_y[rows_of(i * n + y)] for y in range(n)]
        winds = [edge_wind_y[rows_of(2 * i)]] + winds + [edge_wind_y[rows_of(2 * i + 1)]]
        keep = jnp.where(i < LO, west_in, east_in)
        line = halo_line(i, n) + LO
        for y, value in enumerate(line_change(cells, winds)):
            one[rows_of(line * reach + LO + y)] = (mid[rows_of(line * n + y)] + value) * keep

    @pl.loop(0, LINES)
    def _(i):
        line = halo_line(i, n) + LO
        near = [corner[rows_of(k * LINES + i)] for k in range(LINES)]
        cells = near[:LO] + [cell[rows_of(x * span + LO + line)] for x in range(n)] + near[LO:]
        winds = [halo_wind_x[rows_of(i * n + x)] for x in range(n)]
        winds = [corner_wind_x[rows_of(i)]] + winds + [corner_wind_x[rows_of(LINES + i)]]
        keep = jnp.where(i < LO, south_in, north_in)
        low = line_fluxes(cells[: LO + begin + 1], winds[: begin + 1]) + [edge[rows_of(line)]]
        high = [edge[rows_of(reach + line)]] + line_fluxes(cells[LO + end - HI :], winds[end + 1 :])
        values = dict(zip(range(begin), changes(low))) | dict(zip(range(end, n), changes(high)))
        for x, value in values.items():
            one[rows_of((x + LO) * reach + line)] = (cells[x + LO] + (value + change[rows_of(x * reach + line)])) * keep

    fall_half(
        n, parts, 0, one, cell, wind_x, far_wind_x, wind_y, far_wind_y, wind_z, inner_second, rate_ref, steps_ref,
        out_refs, second, fallen,
    )


def late_kernel(
    n, parts, one, cell, wind_x, far_wind_x, wind_y, far_wind_y, wind_z, inner_second, rate_ref, steps_ref, *refs
):
    fall_half(
        n, parts, n // 2, one, cell, wind_x, far_wind_x, wind_y, far_wind_y, wind_z, inner_second, rate_ref, steps_ref,
        refs[:2], *refs[2:],
    )


def fall_half(
    n, parts, begin, one, cell, wind_x, far_wind_x, wind_y, far_wind_y, wind_z, inner_second, rate_ref, steps_ref,
    out_refs, second, fallen,
):
    width = groups(parts)[0]
    span, reach, half = n + PAD_LO + PAD_HI, n + LINES, n // 2
    end = begin + half
    ready = [x for x in range(LO, n - HI) if begin <= x < end]
    left = [x for x in range(begin, end) if x not in ready]
    second[rows_of((ready[0] - begin) * n, len(ready) * n)] = inner_second[rows_of((ready[0] - LO) * n, len(ready) * n)]

    @pl.loop(left[0], left[-1] + 1)
    def _(x):
        second_y_z(n, width, x, one, x + LO, wind_y, far_wind_y, wind_z, second, x - begin)

    @pl.loop(0, n)
    def _(y):
        cells = [one[rows_of(x * reach + LO + y)] for x in range(begin, end + LINES)]
        winds = [wind_x[rows_of(x * n + y)] for x in range(max(begin - 1, 0), min(end + 1, n))]
        if begin == 0:
            winds = [far_wind_x[rows_of(LO * n + y)]] + winds
        else:
            winds = winds + [far_wind_x[rows_of((LO + 1) * n + y)]]
        for i, value in enumerate(line_change(cells, winds)):
            value = cells[i + LO] + (value + second[rows_of(i * n + y)])
            fallen[rows_of(i * n + y)] = 0.5 * cell[rows_of((begin + i) * span + PAD_LO + y)] + 0.5 * value

    bins = LANES // 2 // parts
    ids = lax.axis_index("gz") * bins + lane_ids() % bins
    rates, steps = [
        pick(jnp.broadcast_to(jnp.concatenate([ref[...]] * 2, axis=1), (ROWS, LANES)), ids) for ref in (rate_ref, steps_ref)
    ]

    columns = [[fallen[eight(i * n, k)] for k in range(ROWS)] for i in range(half)]
    rain = [jnp.zeros((ROWS, LANES), F32)] * half
    for block in range(SUBS // AHEAD):
        columns = [column + [from_above(v, width) for v in column[:AHEAD]] for column in columns]
        for s in range(AHEAD):
            rate = jnp.where(block * AHEAD + s < steps, rates, 0.0)
            for i, column in enumerate(columns):
                rain[i] = rain[i] + rate * column[0]
                columns[i] = [v + rate * (u - v) for v, u in zip(column, column[1:])]
    for i, column in enumerate(columns):
        for k in range(ROWS):
            fallen[eight(i * n, k)] = column[k]

    if parts == 2:
        send_ref, keep_ref = out_refs
        lower = is_even("gz")
        low = lane_ids() < 64
        count = half * n // 2
        for c in range(count):
            a, b = fallen[rows_of(c)], fallen[rows_of(count + c)]
            at = rows_of(c)
            keep_ref[at], send_ref[at] = order(jnp.where(low, a, turn(b, 64)), jnp.where(low, turn(a, 64), b), lower)
        value = by_quarter([turn(rain[i], 32 * i) for i in range(4)])
        keep_ref[rows_of(count)] = value
        send_ref[rows_of(count)] = value
    else:
        settled_ref, rain_ref = out_refs
        settled_ref[...] = fallen[...]
        for i in range(half):
            rain_ref[rows_of(i)] = rain[i]


def matrix_kernel(bins, gain_ref, loss_ref, pairs_ref, lost_ref, wide, tall):
    zero = jnp.zeros((bins, LANES - bins), F32)
    shifts = bins // 2

    @pl.loop(0, bins)
    def _(i):
        rows = gain_ref[pl.ds(i * bins, bins)].astype(F32)
        rows = jnp.concatenate([rows, zero], axis=1)
        wide[pl.ds(i * 2 * bins, bins)] = rows
        wide[pl.ds(i * 2 * bins + bins, bins)] = rows
        tall[pl.ds(i * bins, bins)] = rows

        @pl.when(i < shifts)
        def _():
            tall[pl.ds((i + bins) * bins, bins)] = rows

    for d in range(shifts + 1):
        rows = wide[pl.ds(d, bins, stride=2 * bins + 1)]
        if 0 < d < shifts:
            rows = rows + tall[pl.ds(d * bins, bins, stride=bins + 1)]
        pairs_ref[pl.ds(d * LANES, bins)] = rows.astype(jnp.bfloat16)
        pairs_ref[pl.ds(d * LANES + bins, bins)] = pltpu.roll(rows, bins, 1).astype(jnp.bfloat16)
    rows = jnp.concatenate([loss_ref[...].astype(F32), zero], axis=1)
    lost_ref[pl.ds(0, bins)] = rows.astype(jnp.bfloat16)
    lost_ref[pl.ds(bins, bins)] = pltpu.roll(rows, bins, 1).astype(jnp.bfloat16)


def breakup_rows(mass, pairs_ref, lost_ref, products):
    bins = LANES // 2
    count = mass.shape[0]
    lanes = lane_ids()
    rounded = mass.astype(jnp.bfloat16)
    wide = rounded.astype(F32)
    gained = None
    shifts = bins // 2 + 1
    for begin in range(0, shifts, 4):
        end = min(begin + 4, shifts)
        for d in range(begin, end):
            ids = lanes // bins * bins + (lanes + d) % bins
            for r in range(0, count, 2 * ROWS):
                halves = [wide[r + ROWS * k : r + ROWS * (k + 1)] for k in range(2)]
                halves = [v * pick(v, ids) if d else v * v for v in halves]
                both = jnp.concatenate(halves, axis=0).astype(jnp.bfloat16)
                products[pl.ds(r, 2 * ROWS), d * LANES : (d + 1) * LANES] = both
        part = jnp.dot(
            products[pl.ds(0, count), begin * LANES : end * LANES],
            pairs_ref[pl.ds(begin * LANES, (end - begin) * LANES)],
            preferred_element_type=F32,
        )
        gained = part if gained is None else gained + part
    loss = jnp.dot(rounded, lost_ref[...], preferred_element_type=F32)
    return mass + gained - mass * loss


def breakup_half(n, keep_ref, got_ref, pairs_ref, lost_ref, columns, products):
    first = is_even("gz")
    count = n * n // 4
    for c in range(count):
        a, b = order(keep_ref[rows_of(c)], got_ref[rows_of(c)], first)
        columns[rows_of(c)] = by_quarter([a, turn(b, 32), turn(a, 32), turn(b, 64)])
        columns[rows_of(count + c)] = by_quarter([turn(a, -64), turn(b, -32), turn(a, -32), b])
    a, b = order(keep_ref[rows_of(count)], got_ref[rows_of(count)], first)
    a, b = [jnp.where(first, v[: n // 2], v[n // 2 :]) for v in (a, b)]
    columns[...] = breakup_rows(columns[...], pairs_ref, lost_ref, products)
    return [jnp.concatenate([a[:, 32 * i : 32 * i + 32], b[:, 32 * i : 32 * i + 32]], axis=1) for i in range(4)]


def lay_out(columns, mass, n, begin):
    for x in range(n // 2):
        for y in range(n):
            value = columns[rows_of(x * n + y)]
            mass[begin + x, y, 0:ROWS] = value[:, :64]
            mass[begin + x, y, ROWS : 2 * ROWS] = value[:, 64:]


def breakup_first_kernel(n, keep_ref, got_ref, pairs_ref, lost_ref, mass_ref, rain_ref, columns, products):
    for i, value in enumerate(breakup_half(n, keep_ref, got_ref, pairs_ref, lost_ref, columns, products)):
        rain_ref[i] = value
    lay_out(columns, mass_ref, n, 0)


def breakup_last_kernel(
    n, keep_ref, got_ref, pairs_ref, lost_ref, early, early_rain, mass_out, rain_out, columns, products, mass, rain, sems
):
    half = n // 2
    early_copy = pltpu.make_async_copy(early, mass_out.at[pl.ds(0, half)], sems.at[0])
    early_copy.start()
    late_rain = breakup_half(n, keep_ref, got_ref, pairs_ref, lost_ref, columns, products)
    for i in range(half):
        rain[i] = early_rain[i]
        rain[half + i] = late_rain[i]
    rain_copy = pltpu.make_async_copy(rain, rain_out, sems.at[2])
    rain_copy.start()
    lay_out(columns, mass, n, 0)
    late_copy = pltpu.make_async_copy(mass, mass_out.at[pl.ds(half, half)], sems.at[1])
    late_copy.start()
    for copy in (early_copy, rain_copy, late_copy):
        copy.wait()


def breakup_plain_kernel(mass_ref, pairs_ref, lost_ref, out_ref, products):
    count = products.shape[0]

    @pl.loop(0, mass_ref.shape[0] // count)
    def _(i):
        start = pl.multiple_of(i * count, count)
        out_ref[pl.ds(start, count)] = breakup_rows(mass_ref[pl.ds(start, count)], pairs_ref, lost_ref, products)


def shape(*dims, dtype=F32):
    return jax.ShapeDtypeStruct(dims, dtype)


def tiles_of(count):
    return shape(count * ROWS, LANES)


def call(kernel, outs, args, scratch=(), micros=1.0, out_place=pltpu.VMEM, copies=0):
    scratch = [pltpu.VMEM(s.shape, s.dtype) for s in scratch]
    if copies:
        scratch.append(pltpu.SemaphoreType.DMA((copies,)))
    return pl.pallas_call(
        kernel,
        out_shape=outs,
        in_specs=[VMEM] * len(args),
        out_specs=jax.tree.map(lambda _: pl.BlockSpec(memory_space=out_place), outs),
        scratch_shapes=scratch,
        compiler_params=pltpu.CompilerParams(vmem_limit_bytes=40 << 20),
        cost_estimate=pl.CostEstimate(
            flops=int(micros * 1.1e9), bytes_accessed=int(micros * 3.6e6), transcendentals=0
        ),
    )(*args)


def swap_neighbours(axis, begin, message):
    axes = ("gx", "gy", "gz")
    sizes = [lax.axis_size(a) for a in axes]
    along, other = (0, 2) if axis == "gx" else (1, 0)

    def partner(place, start, count):
        to = start + ((place - start) ^ 1)
        return to if start <= place and to < count else place

    index = {place: i for i, place in enumerate(itertools.product(*map(range, sizes)))}
    pairs = []
    for place, i in index.items():
        to = list(place)
        to[along] = partner(place[along], begin, sizes[along])
        if to[along] == place[along]:
            to[other] = partner(place[other], 0, sizes[other])
        pairs.append((i, index[tuple(to)]))
    return lax.ppermute(message, axes, pairs)


def per_device(bin_mass, courant, sub_courant, fall_steps, frag_gain, collide):
    nx, ny, nz, bins = bin_mass.shape
    n = nx
    parts = lax.axis_size("gz")
    gz, gy = lax.axis_index("gz"), lax.axis_index("gy")
    width = bins // parts
    tiles = groups(parts)[2]
    winds = 3 * tiles

    pair_rows = (bins // 2 + 1) * LANES
    pairs, lost = call(
        functools.partial(matrix_kernel, bins),
        (shape(pair_rows, LANES, dtype=jnp.bfloat16), shape(LANES, LANES, dtype=jnp.bfloat16)),
        (frag_gain, collide),
        [shape(2 * bins * bins, LANES), shape(3 * bins * bins // 2, LANES)],
        micros=0.02,
    )

    y_message = tiles_of(n * PAD_LO + winds)
    x_message = tiles_of(n * PAD_LO + winds // 2)
    if parts == 2:
        half = tiles_of(n * n // 2)
        send, keep = call(pack_kernel, (half, half), (bin_mass,), micros=0.3)
        got = lax.ppermute(send, "gz", [(0, 1), (1, 0)])
        own_wind = call(wind_kernel, tiles_of(3), (courant, keep), micros=0.1)
        got_wind = lax.ppermute(own_wind, "gz", [(0, 1), (1, 0)])
        block, *messages = call(
            merge_kernel,
            [tiles_of(n * n + winds), y_message, y_message, x_message, x_message],
            (keep, got, own_wind, got_wind, lost),
            micros=0.2,
        )
    else:
        split = bin_mass.reshape(nx, ny, nz // ROWS, ROWS, parts, width).transpose(4, 0, 1, 3, 2, 5)
        split = lax.all_to_all(split, "gz", split_axis=0, concat_axis=0, tiled=True)
        cube = split.transpose(1, 2, 3, 0, 4, 5).reshape(n, n, ROWS, LANES)
        air = courant.reshape(3, nx, ny, nz // ROWS, ROWS).transpose(0, 4, 3, 1, 2) * (1.0 / 12.0)
        air = lax.all_gather(air, "gz").reshape(parts, 3, ROWS, nz // ROWS, tiles, nx // tiles, ny)
        air = air.transpose(1, 4, 2, 0, 3, 5, 6).reshape(3, tiles, ROWS, LANES)
        block = jnp.concatenate([cube.reshape(-1, LANES), air.reshape(-1, LANES)])
        messages = []
        for layers, low_air, high_air, message, even in (
            (cube.transpose(1, 0, 2, 3), air, air, y_message, gy % 2 == 0),
            (cube, air[:, : tiles // 2], air[:, tiles // 2 :], x_message, lax.axis_index("gx") % 2 == 0),
        ):
            up, down = layers[n - PAD_LO :], layers[:PAD_HI]
            if message is y_message:
                up, down = up.transpose(1, 0, 2, 3), down.transpose(1, 0, 2, 3)
            up = jnp.concatenate([up.reshape(-1, LANES), high_air.reshape(-1, LANES)])
            down = jnp.concatenate([down.reshape(-1, LANES), low_air.reshape(-1, LANES)])
            messages += order(up, jnp.pad(down, ((0, up.shape[0] - down.shape[0]), (0, 0))), even)

    from_y = swap_neighbours("gy", 0, messages[0]), swap_neighbours("gy", 1, messages[1])
    from_x = swap_neighbours("gx", 1, messages[3]), swap_neighbours("gx", 0, messages[2])
    wind_x, wind_y, wind_z, own_change, edge_x, edge_y = call(
        functools.partial(own_kernel, n, parts), [tiles_of(n * n)] * 4 + [tiles_of(2 * n)] * 2, (block,), micros=1.6
    )
    message = tiles_of(LO * LINES + 2 + tiles)
    corners = call(functools.partial(corner_kernel, n, parts), (message, message), (*from_y, own_change), micros=0.1)
    corners = swap_neighbours("gx", 1, corners[1]), swap_neighbours("gx", 0, corners[0])
    cell, change, halo_wind_x, far_wind_y = call(
        functools.partial(y_kernel, n, parts),
        [tiles_of(n * (n + PAD_LO + PAD_HI)), tiles_of(n * (n + LINES)), tiles_of(LINES * n), tiles_of(n * (LINES + 2))],
        (block, *from_y, wind_y, own_change, edge_y),
        [tiles_of(LINES * n)] * 2,
        micros=2.0,
    )
    reach, half, inner = n + LINES, n // 2, n - LINES
    near = call(
        functools.partial(inner_kernel, n, parts),
        [tiles_of(inner * reach), tiles_of(2 * reach), tiles_of(inner * n)],
        (cell, change, halo_wind_x, wind_y, far_wind_y, wind_z, edge_x),
        micros=0.9,
    )
    mid, far_wind_x, side, side_wind_y = call(
        functools.partial(x_kernel, n, parts),
        [tiles_of(count) for count in (reach * n, (LINES + 2) * n, LINES * n, LINES * n)],
        (cell, change, wind_x, near[1], *from_x),
        [tiles_of(LINES * n)] * 3,
        micros=1.7,
    )
    fall = sub_courant.reshape(1, bins), fall_steps.reshape(1, bins)
    message = [tiles_of(n * half // 2 + 1)] * 2 if parts == 2 else [tiles_of(n * half), tiles_of(half)]
    one, *early = call(
        functools.partial(main_kernel, n, parts),
        [tiles_of(reach * reach)] + message,
        (
            *(cell, change, wind_x, wind_y, wind_z, halo_wind_x, far_wind_y, *near),
            *(mid, far_wind_x, side, side_wind_y, *corners, *fall),
        ),
        [tiles_of(count) for count in (LINES * LINES, 2 * LINES, 2 * LINES, n * half, n * half)],
        micros=2.0,
    )
    if parts == 2:
        early_got = lax.ppermute(early[0], "gz", [(0, 1), (1, 0)])
    late = call(
        functools.partial(late_kernel, n, parts),
        message,
        (one, cell, wind_x, far_wind_x, wind_y, far_wind_y, wind_z, near[2], *fall),
        [tiles_of(n * half)] * 2,
        micros=1.5,
    )

    products = shape(n * half * ROWS, pair_rows, dtype=jnp.bfloat16)
    if parts == 2:
        late_got = lax.ppermute(late[0], "gz", [(0, 1), (1, 0)])
        early = call(
            functools.partial(breakup_first_kernel, n),
            [shape(half, ny, nz, bins), shape(half, ny // parts, bins)],
            (early[1], early_got, pairs, lost),
            [tiles_of(n * half), products],
            micros=1.5,
        )
        outs = [shape(nx, ny, nz, bins), shape(nx, ny // parts, bins)]
        return tuple(
            call(
                functools.partial(breakup_last_kernel, n),
                outs,
                (late[1], late_got, pairs, lost, *early),
                [tiles_of(n * half), products, shape(half, ny, nz, bins), outs[1]],
                micros=1.5,
                out_place=pl.ANY,
                copies=3,
            )
        )

    settled, rain = [jnp.concatenate(halves) for halves in zip(early, late)]
    rain = rain.reshape(nx, ny, LANES)[:, :, :width]
    rain = lax.all_to_all(rain, "gz", split_axis=1, concat_axis=2, tiled=True)
    settled = settled.reshape(nx, ny, ROWS, parts, nz // ROWS, width).transpose(3, 0, 1, 4, 2, 5)
    settled = lax.all_to_all(settled, "gz", split_axis=0, concat_axis=0, tiled=True)
    settled = settled.transpose(1, 2, 3, 4, 0, 5).reshape(nx * ny, nz // ROWS, ROWS, bins)
    paired = settled.transpose(0, 2, 1, 3).reshape(-1, LANES)
    updated = call(breakup_plain_kernel, tiles_of(n * n), (paired, pairs, lost), [products], micros=3.0)
    updated = updated.reshape(nx, ny, ROWS, nz // ROWS, bins).transpose(0, 1, 3, 2, 4).reshape(nx, ny, nz, bins)
    return updated, rain


def solution(mesh):
    in_specs = (P("gx", "gy", "gz", None), P(None, "gx", "gy", "gz"), P(), P(), P(), P())
    out_specs = (P("gx", "gy", "gz", None), P("gx", ("gy", "gz"), None))
    return jax.shard_map(per_device, mesh=mesh, in_specs=in_specs, out_specs=out_specs, check_vma=False)
```

```python
import functools
import itertools

import jax
import jax.numpy as jnp
from jax import lax
from jax.experimental import pallas as pl
from jax.experimental.pallas import tpu as pltpu
from jax.sharding import PartitionSpec as P

SUBS = 24
EPS = 1e-06
LO, HI = 3, 2
PAD_LO, PAD_HI = 2 * LO, 2 * HI
LINES = LO + HI
ROWS, LANES = 8, 128
AHEAD = 4
EARLY = 6
F32 = jnp.float32
VMEM = pl.BlockSpec(memory_space=pltpu.VMEM)


def lane_ids():
    return lax.broadcasted_iota(jnp.int32, (ROWS, LANES), 1)


def pick(tile, ids):
    return jnp.take_along_axis(tile, ids, axis=1, mode="promise_in_bounds")


def turn(tile, lanes):
    lanes %= LANES
    return pltpu.roll(tile, lanes, 1) if lanes else tile


def rows_of(first, count=1):
    return pl.ds(first * ROWS, count * ROWS)


def eight(first, level, step=1):
    return pl.ds(first * ROWS + level, ROWS, stride=step * ROWS)


def order(a, b, straight):
    return jnp.where(straight, a, b), jnp.where(straight, b, a)


def is_even(axis):
    return lax.axis_index(axis) % 2 == 0


def by_quarter(parts):
    quarter = lane_ids() // (LANES // 4)
    return jnp.where(quarter < 2, jnp.where(quarter == 0, parts[0], parts[1]), jnp.where(quarter == 2, parts[2], parts[3]))


def groups(parts):
    width = LANES // (2 * parts)
    return width, width // ROWS, ROWS * ROWS // width


def spread(jobs, parts):
    width, deep, _ = groups(parts)
    place = lane_ids() % width
    rows = [[], []]
    for tile, x, y, _, _ in jobs:
        top = tile.astype(jnp.bfloat16).astype(F32)
        here = place == x % deep * ROWS + y
        for out, term in zip(rows, (top, tile - top)):
            out.append(jnp.where(here, term, 0.0))
    terms = jnp.concatenate([jnp.concatenate(r, axis=0).astype(jnp.bfloat16) for r in rows], axis=1)
    source, target = [lax.broadcasted_iota(jnp.int32, (2 * LANES, LANES), k) for k in range(2)]
    same = jnp.where(source % LANES // width == target // width, 1.0, 0.0).astype(jnp.bfloat16)
    out = jnp.dot(terms, same, preferred_element_type=F32)
    for k, (_, _, _, ref, at) in enumerate(jobs):
        ref[rows_of(at)] = out[k * ROWS : (k + 1) * ROWS]


def halo_line(i, n):
    return jnp.where(i < LO, i - LO, i - LO + n)


def line_change(cells, winds):
    return changes(line_fluxes(cells, winds))


def changes(fluxes):
    return [a - b for a, b in zip(fluxes, fluxes[1:])]


def long_line(cells, winds, low_edge, high_edge, n):
    begin, end = LO, n - HI
    low = line_fluxes(cells[: PAD_LO + begin + 1], winds[: LO + 1 + begin]) + [low_edge]
    high = [high_edge] + line_fluxes(cells[PAD_LO + end - HI :], winds[LO + 1 + end :])
    return dict(zip(range(-LO, begin), changes(low))) | dict(zip(range(end, n + HI), changes(high)))


def line_fluxes(cells, winds):
    first = [b - a for a, b in zip(cells, cells[1:])]
    twice = [d + d for d in first]
    second = [b - a for a, b in zip(first, first[1:])]
    third = [a - b for a, b in zip(second, second[1:])]
    curved = [(13.0 / 3.0) * (c * c) + 4.0 * EPS for c in second]
    fluxes = []
    for j in range(len(cells) - 4):
        left = twice[j + 1] + second[j]
        mid = first[j + 1] + first[j + 2]
        right = twice[j + 2] - second[j + 2]
        e0 = curved[j] + left * left
        e1 = curved[j + 1] + mid * mid
        e2 = curved[j + 2] + right * right
        e0 = e0 * e0
        e1 = e1 * e1
        e2 = e2 * e2
        e0 = 3.0 * e0
        e2_twice = e2 + e2
        top = e1 * (e2_twice * third[j] + e0 * third[j + 1])
        low = e1 * (e2 + e0) + e0 * e2_twice
        inverse = pl.reciprocal(low, approx=True)
        estimate = 6.0 * cells[j + 2] + (first[j + 1] + twice[j + 2]) + top * inverse
        fluxes.append((winds[j] + winds[j + 1]) * estimate)
    return fluxes


def from_below(value, width):
    return jnp.where(lane_ids() < width, 0.0, turn(value, width))


def from_above(value, width):
    return jnp.where(lane_ids() >= LANES - width, 0.0, turn(value, -width))


def level_change(cells, winds, width):
    long_cells = [from_below(v, width) for v in cells[ROWS - LO :]] + cells + [from_above(v, width) for v in cells[:HI]]
    long_winds = [from_below(winds[-1], width)] + winds + [from_above(winds[0], width)]
    return line_change(long_cells, long_winds)


def pack_kernel(mass_ref, send_ref, keep_ref):
    lower = is_even("gz")
    n = mass_ref.shape[0]
    zero = jnp.zeros((ROWS, LANES // 2), F32)
    for x in range(n // 2):
        for y in range(n):
            tiles = [
                jnp.concatenate([mass_ref[xx, y, z : z + ROWS], zero], axis=1) for xx in (x, x + n // 2) for z in (0, ROWS)
            ]
            low = by_quarter([turn(v, 32 * k) for k, v in enumerate(tiles)])
            high = by_quarter([turn(v, 32 * k - 32) for k, v in enumerate(tiles)])
            at = rows_of(x * n + y)
            keep_ref[at], send_ref[at] = order(low, high, lower)


def wind_kernel(wind_ref, keep_ref, out_ref):
    del keep_ref
    n = wind_ref.shape[1]
    for d in range(3):
        levels = wind_ref[d].reshape(n * n, 2 * ROWS).T * (1.0 / 12.0)
        out_ref[rows_of(d)] = jnp.concatenate([levels[:ROWS], levels[ROWS:]], axis=1)


def sides(axis, first_ref, second_ref):
    even, place = is_even(axis), lax.axis_index(axis)
    inner_low, inner_high = place > 0, place < lax.axis_size(axis) - 1

    def below(at):
        return jnp.where(inner_low, jnp.where(even, second_ref[at], first_ref[at]), 0.0)

    def above(at):
        return jnp.where(inner_high, jnp.where(even, first_ref[at], second_ref[at]), 0.0)

    return below, above


def by_parity(axis, body):
    even = is_even(axis)
    pl.when(even)(lambda: body(0, 1))
    pl.when(jnp.logical_not(even))(lambda: body(1, 0))


def merge_kernel(keep_ref, got_ref, own_wind_ref, got_wind_ref, lost_ref, block_ref, y_first, y_second, x_first, x_second):
    del lost_ref
    n = 8
    lower = is_even("gz")
    low = lane_ids() < 64
    for x in range(n // 2):
        for y in range(n):
            at = rows_of(x * n + y)
            a, b = order(keep_ref[at], got_ref[at], lower)
            block_ref[at] = jnp.where(low, a, turn(b, 64))
            block_ref[rows_of((x + n // 2) * n + y)] = jnp.where(low, turn(a, 64), b)
    for d in range(3):
        a, b = order(own_wind_ref[rows_of(d)], got_wind_ref[rows_of(d)], lower)
        block_ref[rows_of(n * n + 2 * d)] = by_quarter([a, turn(a, -32), turn(b, 64), turn(b, 32)])
        block_ref[rows_of(n * n + 2 * d + 1)] = by_quarter([turn(a, -32), turn(a, -64), turn(b, 32), b])

    def along_y(up, down):
        for ref, start, wide in (((y_first, y_second)[up], n - PAD_LO, PAD_LO), ((y_first, y_second)[down], 0, PAD_HI)):
            for x in range(n):
                ref[rows_of(x * wide, wide)] = block_ref[rows_of(x * n + start, wide)]
            ref[rows_of(n * wide, 6)] = block_ref[rows_of(n * n, 6)]

    def along_x(up, down):
        for ref, start, wide, part in (((x_first, x_second)[up], n - PAD_LO, PAD_LO, 1), ((x_first, x_second)[down], 0, PAD_HI, 0)):
            ref[rows_of(0, wide * n)] = block_ref[rows_of(start * n, wide * n)]
            for d in range(3):
                ref[rows_of(wide * n + d)] = block_ref[rows_of(n * n + 2 * d + part)]

    by_parity("gy", along_y)
    by_parity("gx", along_x)


def corner_kernel(n, parts, first_ref, second_ref, own_change, *messages):
    del own_change
    tiles = groups(parts)[2]
    half = tiles // 2
    below, above = sides("gy", first_ref, second_ref)

    def body(up, down):
        for ref, start, narrow, part in ((messages[up], n - LO, LO, half), (messages[down], 0, HI, 0)):
            at = 0
            for x in range(start, start + narrow):
                ref[rows_of(at, LO)] = below(rows_of(x * PAD_LO + PAD_LO - LO, LO))
                ref[rows_of(at + LO, HI)] = above(rows_of(x * PAD_HI, HI))
                at += LINES
            for side, base in ((below, n * PAD_LO), (above, n * PAD_HI)):
                ref[rows_of(at)] = side(rows_of(base + (tiles - 1 if part else 0)))
                ref[rows_of(at + 1, half)] = side(rows_of(base + tiles + part, half))
                at += 1 + half

    by_parity("gx", body)


def own_kernel(n, parts, block_ref, wind_x, wind_y, wind_z, change, edge_x, edge_y):
    width, deep, tiles = groups(parts)
    for d, out in enumerate((wind_x, wind_y, wind_z)):
        jobs = []
        for x in range(n):
            tile = block_ref[rows_of(n * n + d * tiles + x // deep)]
            jobs += [(tile, x, y, out, x * n + y) for y in range(n)]
        spread(jobs, parts)

    @pl.loop(0, n)
    def _(x):
        cells = [block_ref[eight(x * n, k)] for k in range(ROWS)]
        winds = [wind_z[eight(x * n, k)] for k in range(ROWS)]
        for k, value in enumerate(level_change(cells, winds, width)):
            change[eight(x * n, k)] = value

    begin, end = LO, n - HI
    for wind, edge, place in ((wind_x, edge_x, lambda i, k: k * n + i), (wind_y, edge_y, lambda i, k: i * n + k)):

        @pl.loop(0, n)
        def _(i):
            cells = [block_ref[rows_of(place(i, k))] for k in range(n)]
            fluxes = line_fluxes(cells, [wind[rows_of(place(i, k))] for k in range(begin - 1, end + 1)])
            edge[rows_of(i)] = fluxes[0]
            edge[rows_of(n + i)] = fluxes[-1]
            for k, value in zip(range(begin, end), changes(fluxes)):
                at = rows_of(place(i, k))
                change[at] = change[at] + value


def y_kernel(n, parts, block_ref, first_ref, second_ref, wind_y, own_change, edge_y, *refs):
    width, deep, tiles = groups(parts)
    cell, change, wind_x, far_y, wind_z, halo_change = refs
    below, above = sides("gy", first_ref, second_ref)
    span, reach = n + PAD_LO + PAD_HI, n + LINES

    for x in range(n):
        cell[rows_of(x * span, PAD_LO)] = below(rows_of(x * PAD_LO, PAD_LO))
        cell[rows_of(x * span + PAD_LO, n)] = block_ref[rows_of(x * n, n)]
        cell[rows_of(x * span + PAD_LO + n, PAD_HI)] = above(rows_of(x * PAD_HI, PAD_HI))
    jobs = []
    for d in range(3):
        for t in range(tiles):
            low, high = below(rows_of(n * PAD_LO + d * tiles + t)), above(rows_of(n * PAD_HI + d * tiles + t))
            for x in range(t * deep, (t + 1) * deep):
                if d == 1:
                    jobs += [(low, x, n - LO - 1 + y, far_y, x * (LINES + 2) + y) for y in range(LO + 1)]
                    jobs += [(high, x, y, far_y, x * (LINES + 2) + LO + 1 + y) for y in range(HI + 1)]
                else:
                    out = wind_z if d else wind_x
                    jobs += [(low, x, n - LO + y, out, y * n + x) for y in range(LO)]
                    jobs += [(high, x, y, out, (LO + y) * n + x) for y in range(HI)]
    spread(jobs, parts)

    @pl.loop(0, LINES)
    def _(i):
        first = halo_line(i, n) + PAD_LO
        cells = [cell[eight(first, k, span)] for k in range(ROWS)]
        winds = [wind_z[eight(i * n, k)] for k in range(ROWS)]
        for k, value in enumerate(level_change(cells, winds, width)):
            halo_change[eight(i * n, k)] = value

    @pl.loop(0, n)
    def _(x):
        cells = [cell[rows_of(x * span + y)] for y in range(span)]
        far = [far_y[rows_of(x * (LINES + 2) + y)] for y in range(LINES + 2)]
        winds = far[: LO + 1] + [wind_y[rows_of(x * n + y)] for y in range(n)] + far[LO + 1 :]
        for y, value in long_line(cells, winds, edge_y[rows_of(x)], edge_y[rows_of(n + x)], n).items():
            if 0 <= y < n:
                value = value + own_change[rows_of(x * n + y)]
            else:
                value = value + halo_change[rows_of((y + LO if y < 0 else y + LO - n) * n + x)]
            change[rows_of(x * reach + y + LO)] = value
        for y in range(LO, n - HI):
            change[rows_of(x * reach + y + LO)] = own_change[rows_of(x * n + y)]


def inside(axis):
    place = lax.axis_index(axis)
    return [jnp.where(ok, 1.0, 0.0) for ok in (place > 0, place < lax.axis_size(axis) - 1)]


def inner_kernel(n, parts, cell, change, halo_wind_x, wind_y, far_wind_y, wind_z, edge_x, one, edge, second):
    width = groups(parts)[0]
    span, reach = n + PAD_LO + PAD_HI, n + LINES
    begin, end = LO, n - HI
    south_in, north_in = inside("gy")

    for k in range(2):
        edge[rows_of(k * reach + LO, n)] = edge_x[rows_of(k * n, n)]
    for i in range(end - begin):
        x = begin + i
        one[rows_of(i * reach + LO, n)] = cell[rows_of(x * span + PAD_LO, n)] + change[rows_of(x * reach + LO, n)]

    @pl.loop(0, LINES)
    def _(i):
        at = halo_line(i, n) + LO
        cells = [cell[rows_of(x * span + LO + at)] for x in range(n)]
        fluxes = line_fluxes(cells, [halo_wind_x[rows_of(i * n + x)] for x in range(begin - 1, end + 1)])
        edge[rows_of(at)] = fluxes[0]
        edge[rows_of(reach + at)] = fluxes[-1]
        keep = jnp.where(i < LO, south_in, north_in)
        for k, value in enumerate(changes(fluxes)):
            x = begin + k
            one[rows_of(k * reach + at)] = (cells[x] + (value + change[rows_of(x * reach + at)])) * keep

    @pl.loop(0, end - begin)
    def _(i):
        second_y_z(n, width, begin + i, one, i, wind_y, far_wind_y, wind_z, second, i)


def second_y_z(n, width, x, one, one_x, wind_y, far_wind_y, wind_z, second, second_x):
    reach = n + LINES
    cells = [one[rows_of(one_x * reach + y)] for y in range(reach)]
    winds = [far_wind_y[rows_of(x * (LINES + 2) + LO)]] + [wind_y[rows_of(x * n + y)] for y in range(n)]
    winds += [far_wind_y[rows_of(x * (LINES + 2) + LO + 1)]]
    for y, value in enumerate(line_change(cells, winds)):
        second[rows_of(second_x * n + y)] = value
    cells = [one[eight(one_x * reach + LO, k)] for k in range(ROWS)]
    winds = [wind_z[eight(x * n, k)] for k in range(ROWS)]
    for k, value in enumerate(level_change(cells, winds, width)):
        at = eight(second_x * n, k)
        second[at] = second[at] + value


def x_kernel(n, parts, cell, change, wind_x, edge, second_ref, first_ref, mid, far_wind_x, side, side_wind_y, *scratch):
    far, side_wind_z, side_change = scratch
    width, deep, tiles = groups(parts)
    half = tiles // 2
    west, east = sides("gx", first_ref, second_ref)
    span, reach = n + PAD_LO + PAD_HI, n + LINES

    jobs = []
    for take, wide, near_from, far_from, line in ((west, PAD_LO, LO, 0, 0), (east, PAD_HI, 0, HI, LO)):
        narrow = wide // 2
        side[rows_of(line * n, narrow * n)] = take(rows_of(near_from * n, narrow * n))
        far[rows_of(line * n, narrow * n)] = take(rows_of(far_from * n, narrow * n))
        layers, shift = (range(n - narrow, n), half) if line == 0 else (range(narrow), 0)
        wider = range(n - narrow - 1, n) if line == 0 else range(narrow + 1)

        def winds_of(d, x):
            return take(rows_of(wide * n + d * half + x // deep - shift))

        for i, x in enumerate(wider):
            jobs += [(winds_of(0, x), x, y, far_wind_x, (line + bool(line) + i) * n + y) for y in range(n)]
        for d, out in ((1, side_wind_y), (2, side_wind_z)):
            for i, x in enumerate(layers):
                jobs += [(winds_of(d, x), x, y, out, (line + i) * n + y) for y in range(n)]
    spread(jobs, parts)

    @pl.loop(0, LINES)
    def _(i):
        cells = [side[eight(i * n, k)] for k in range(ROWS)]
        winds = [side_wind_z[eight(i * n, k)] for k in range(ROWS)]
        for k, value in enumerate(level_change(cells, winds, width)):
            side_change[eight(i * n, k)] = value

    @pl.loop(0, n)
    def _(y):
        outer = [far[rows_of(i * n + y)] for i in range(LINES)]
        near = [side[rows_of(i * n + y)] for i in range(LINES)]
        cells = outer[:LO] + near[:LO] + [cell[rows_of(x * span + PAD_LO + y)] for x in range(n)] + near[LO:] + outer[LO:]
        winds = [far_wind_x[rows_of(i * n + y)] for i in range(LINES + 2)]
        winds = winds[: LO + 1] + [wind_x[rows_of(x * n + y)] for x in range(n)] + winds[LO + 1 :]
        for x, value in long_line(cells, winds, edge[rows_of(LO + y)], edge[rows_of(reach + LO + y)], n).items():
            if 0 <= x < n:
                value = value + change[rows_of(x * reach + LO + y)]
            else:
                value = value + side_change[rows_of((x + LO if x < 0 else x + LO - n) * n + y)]
            mid[rows_of((x + LO) * n + y)] = cells[PAD_LO + x] + value


def main_kernel(n, parts, *refs):
    cell, change, wind_x, wind_y, wind_z, halo_wind_x, far_wind_y, inner, edge, inner_second = refs[:10]
    mid, far_wind_x, side, side_wind_y, second_ref, first_ref, rate_ref, steps_ref = refs[10:18]
    one, *out_refs = refs[18:21]
    corner, corner_wind_x, edge_wind_y, second, fallen = refs[21:]
    deep, tiles = groups(parts)[1:]
    half = tiles // 2
    west, east = sides("gx", first_ref, second_ref)
    span, reach = n + PAD_LO + PAD_HI, n + LINES

    jobs = []
    for take, narrow, line in ((west, LO, 0), (east, HI, LO)):
        at = narrow * LINES
        corner[rows_of(line * LINES, at)] = take(rows_of(0, at))
        below, above = at, at + 1 + half
        layers, shift = (range(n - narrow, n), half) if line == 0 else (range(narrow), 0)
        for y in range(LINES):
            tile = take(rows_of(below if y < LO else above))
            x = layers[-1] if line == 0 else layers[0]
            jobs.append((tile, x, n - LO + y if y < LO else y - LO, corner_wind_x, bool(line) * LINES + y))
        for i, x in enumerate(layers):
            tile = x // deep - shift
            jobs.append((take(rows_of(below + 1 + tile)), x, n - 1, edge_wind_y, 2 * (line + i)))
            jobs.append((take(rows_of(above + 1 + tile)), x, 0, edge_wind_y, 2 * (line + i) + 1))
    spread(jobs, parts)

    west_in, east_in = inside("gx")
    south_in, north_in = inside("gy")
    begin, end = LO, n - HI
    one[rows_of((begin + LO) * reach, (end - begin) * reach)] = inner[...]
    for x in [x for x in range(n) if not begin <= x < end]:
        one[rows_of((x + LO) * reach + LO, n)] = mid[rows_of((x + LO) * n, n)]

    @pl.loop(0, LINES)
    def _(i):
        corners = [corner[rows_of(i * LINES + y)] for y in range(LINES)]
        cells = corners[:LO] + [side[rows_of(i * n + y)] for y in range(n)] + corners[LO:]
        winds = [side_wind_y[rows_of(i * n + y)] for y in range(n)]
        winds = [edge_wind_y[rows_of(2 * i)]] + winds + [edge_wind_y[rows_of(2 * i + 1)]]
        keep = jnp.where(i < LO, west_in, east_in)
        line = halo_line(i, n) + LO
        for y, value in enumerate(line_change(cells, winds)):
            one[rows_of(line * reach + LO + y)] = (mid[rows_of(line * n + y)] + value) * keep

    @pl.loop(0, LINES)
    def _(i):
        line = halo_line(i, n) + LO
        near = [corner[rows_of(k * LINES + i)] for k in range(LINES)]
        cells = near[:LO] + [cell[rows_of(x * span + LO + line)] for x in range(n)] + near[LO:]
        winds = [halo_wind_x[rows_of(i * n + x)] for x in range(n)]
        winds = [corner_wind_x[rows_of(i)]] + winds + [corner_wind_x[rows_of(LINES + i)]]
        keep = jnp.where(i < LO, south_in, north_in)
        low = line_fluxes(cells[: LO + begin + 1], winds[: begin + 1]) + [edge[rows_of(line)]]
        high = [edge[rows_of(reach + line)]] + line_fluxes(cells[LO + end - HI :], winds[end + 1 :])
        values = dict(zip(range(begin), changes(low))) | dict(zip(range(end, n), changes(high)))
        for x, value in values.items():
            one[rows_of((x + LO) * reach + line)] = (cells[x + LO] + (value + change[rows_of(x * reach + line)])) * keep

    fall_layers(
        n, parts, 0, EARLY, one, cell, wind_x, far_wind_x, wind_y, far_wind_y, wind_z, inner_second, rate_ref, steps_ref,
        out_refs, second, fallen,
    )


def late_kernel(
    n, parts, one, cell, wind_x, far_wind_x, wind_y, far_wind_y, wind_z, inner_second, rate_ref, steps_ref, *refs
):
    fall_layers(
        n, parts, EARLY, n, one, cell, wind_x, far_wind_x, wind_y, far_wind_y, wind_z, inner_second, rate_ref, steps_ref,
        refs[:2], *refs[2:],
    )


def fall_layers(
    n, parts, begin, end, one, cell, wind_x, far_wind_x, wind_y, far_wind_y, wind_z, inner_second, rate_ref, steps_ref,
    out_refs, second, fallen,
):
    width = groups(parts)[0]
    span, reach, count = n + PAD_LO + PAD_HI, n + LINES, end - begin
    ready = [x for x in range(LO, n - HI) if begin <= x < end]
    left = [x for x in range(begin, end) if x not in ready]
    if ready:
        second[rows_of((ready[0] - begin) * n, len(ready) * n)] = inner_second[rows_of((ready[0] - LO) * n, len(ready) * n)]

    @pl.loop(left[0], left[-1] + 1)
    def _(x):
        second_y_z(n, width, x, one, x + LO, wind_y, far_wind_y, wind_z, second, x - begin)

    @pl.loop(0, n)
    def _(y):
        cells = [one[rows_of(x * reach + LO + y)] for x in range(begin, end + LINES)]
        winds = [wind_x[rows_of(x * n + y)] for x in range(max(begin - 1, 0), min(end + 1, n))]
        if begin == 0:
            winds = [far_wind_x[rows_of(LO * n + y)]] + winds
        if end == n:
            winds = winds + [far_wind_x[rows_of((LO + 1) * n + y)]]
        for i, value in enumerate(line_change(cells, winds)):
            value = cells[i + LO] + (value + second[rows_of(i * n + y)])
            fallen[rows_of(i * n + y)] = 0.5 * cell[rows_of((begin + i) * span + PAD_LO + y)] + 0.5 * value

    bins = LANES // 2 // parts
    ids = lax.axis_index("gz") * bins + lane_ids() % bins
    rates, steps = [
        pick(jnp.broadcast_to(jnp.concatenate([ref[...]] * 2, axis=1), (ROWS, LANES)), ids) for ref in (rate_ref, steps_ref)
    ]

    rain = []
    for some in [range(i, min(i + 3, count)) for i in range(0, count, 3)]:
        columns = [[fallen[eight(i * n, k)] for k in range(ROWS)] for i in some]
        drops = [jnp.zeros((ROWS, LANES), F32) for _ in some]
        for block in range(SUBS // AHEAD):
            columns = [column + [from_above(v, width) for v in column[:AHEAD]] for column in columns]
            for s in range(AHEAD):
                rate = jnp.where(block * AHEAD + s < steps, rates, 0.0)
                for i, column in enumerate(columns):
                    drops[i] = drops[i] + rate * column[0]
                    columns[i] = [v + rate * (u - v) for v, u in zip(column, column[1:])]
        for i, column in zip(some, columns):
            for k in range(ROWS):
                fallen[eight(i * n, k)] = column[k]
        rain += drops

    if parts == 2:
        send_ref, keep_ref = out_refs
        lower = is_even("gz")
        low = lane_ids() < 64
        half = count * n // 2
        for c in range(half):
            a, b = fallen[rows_of(c)], fallen[rows_of(half + c)]
            at = rows_of(c)
            keep_ref[at], send_ref[at] = order(jnp.where(low, a, turn(b, 64)), jnp.where(low, turn(a, 64), b), lower)
        for j in range(0, count, 4):
            four = (rain[j : j + 4] + rain[j:] * 3)[:4]
            value = by_quarter([turn(v, 32 * i) for i, v in enumerate(four)])
            keep_ref[rows_of(half + j // 4)] = value
            send_ref[rows_of(half + j // 4)] = value
    else:
        settled_ref, rain_ref = out_refs
        settled_ref[...] = fallen[...]
        for i in range(count):
            rain_ref[rows_of(i)] = rain[i]


def matrix_kernel(bins, gain_ref, loss_ref, pairs_ref, lost_ref, wide, tall):
    zero = jnp.zeros((bins, LANES - bins), F32)
    shifts = bins // 2

    @pl.loop(0, bins)
    def _(i):
        rows = gain_ref[pl.ds(i * bins, bins)].astype(F32)
        rows = jnp.concatenate([rows, zero], axis=1)
        wide[pl.ds(i * 2 * bins, bins)] = rows
        wide[pl.ds(i * 2 * bins + bins, bins)] = rows
        tall[pl.ds(i * bins, bins)] = rows

        @pl.when(i < shifts)
        def _():
            tall[pl.ds((i + bins) * bins, bins)] = rows

    for d in range(shifts + 1):
        rows = wide[pl.ds(d, bins, stride=2 * bins + 1)]
        if 0 < d < shifts:
            rows = rows + tall[pl.ds(d * bins, bins, stride=bins + 1)]
        pairs_ref[pl.ds(d * LANES, bins)] = rows.astype(jnp.bfloat16)
        pairs_ref[pl.ds(d * LANES + bins, bins)] = pltpu.roll(rows, bins, 1).astype(jnp.bfloat16)
    rows = jnp.concatenate([loss_ref[...].astype(F32), zero], axis=1)
    lost_ref[pl.ds(0, bins)] = rows.astype(jnp.bfloat16)
    lost_ref[pl.ds(bins, bins)] = pltpu.roll(rows, bins, 1).astype(jnp.bfloat16)


def breakup_rows(mass, pairs_ref, lost_ref, products):
    bins = LANES // 2
    count = mass.shape[0]
    lanes = lane_ids()
    rounded = mass.astype(jnp.bfloat16)
    wide = rounded.astype(F32)
    gained = None
    shifts = bins // 2 + 1
    for begin in range(0, shifts, 4):
        end = min(begin + 4, shifts)
        for d in range(begin, end):
            ids = lanes // bins * bins + (lanes + d) % bins
            for r in range(0, count, 2 * ROWS):
                halves = [wide[r + ROWS * k : r + ROWS * (k + 1)] for k in range(2)]
                halves = [v * pick(v, ids) if d else v * v for v in halves]
                both = jnp.concatenate(halves, axis=0).astype(jnp.bfloat16)
                products[pl.ds(r, 2 * ROWS), d * LANES : (d + 1) * LANES] = both
        part = jnp.dot(
            products[pl.ds(0, count), begin * LANES : end * LANES],
            pairs_ref[pl.ds(begin * LANES, (end - begin) * LANES)],
            preferred_element_type=F32,
        )
        gained = part if gained is None else gained + part
    loss = jnp.dot(rounded, lost_ref[...], preferred_element_type=F32)
    return mass + gained - mass * loss


def breakup_layers(n, count, keep_ref, got_ref, pairs_ref, lost_ref, columns, products):
    first = is_even("gz")
    half = count * n // 2
    for c in range(half):
        a, b = order(keep_ref[rows_of(c)], got_ref[rows_of(c)], first)
        columns[rows_of(c)] = by_quarter([a, turn(b, 32), turn(a, 32), turn(b, 64)])
        columns[rows_of(half + c)] = by_quarter([turn(a, -64), turn(b, -32), turn(a, -32), b])
    rain = []
    for i in range(count):
        a, b = order(keep_ref[rows_of(half + i // 4)], got_ref[rows_of(half + i // 4)], first)
        a, b = [jnp.where(first, v[: n // 2], v[n // 2 :])[:, 32 * (i % 4) : 32 * (i % 4) + 32] for v in (a, b)]
        rain.append(jnp.concatenate([a, b], axis=1))
    columns[...] = breakup_rows(columns[...], pairs_ref, lost_ref, products)
    return rain


def lay_out(columns, mass, n, count):
    for x in range(count):
        for y in range(n):
            value = columns[rows_of(x * n + y)]
            mass[x, y, 0:ROWS] = value[:, :64]
            mass[x, y, ROWS : 2 * ROWS] = value[:, 64:]


def breakup_first_kernel(n, keep_ref, got_ref, pairs_ref, lost_ref, mass_ref, rain_ref, columns, products):
    for i, value in enumerate(breakup_layers(n, EARLY, keep_ref, got_ref, pairs_ref, lost_ref, columns, products)):
        rain_ref[i] = value
    lay_out(columns, mass_ref, n, EARLY)


def breakup_last_kernel(
    n, keep_ref, got_ref, pairs_ref, lost_ref, early, early_rain, mass_out, rain_out, columns, products, mass, rain, sems
):
    early_copy = pltpu.make_async_copy(early, mass_out.at[pl.ds(0, EARLY)], sems.at[0])
    early_copy.start()
    late_rain = breakup_layers(n, n - EARLY, keep_ref, got_ref, pairs_ref, lost_ref, columns, products)
    for i in range(EARLY):
        rain[i] = early_rain[i]
    for i, value in enumerate(late_rain):
        rain[EARLY + i] = value
    rain_copy = pltpu.make_async_copy(rain, rain_out, sems.at[2])
    rain_copy.start()
    lay_out(columns, mass, n, n - EARLY)
    late_copy = pltpu.make_async_copy(mass, mass_out.at[pl.ds(EARLY, n - EARLY)], sems.at[1])
    late_copy.start()
    for copy in (early_copy, rain_copy, late_copy):
        copy.wait()


def breakup_plain_kernel(mass_ref, pairs_ref, lost_ref, out_ref, products):
    count = products.shape[0]

    @pl.loop(0, mass_ref.shape[0] // count)
    def _(i):
        start = pl.multiple_of(i * count, count)
        out_ref[pl.ds(start, count)] = breakup_rows(mass_ref[pl.ds(start, count)], pairs_ref, lost_ref, products)


def shape(*dims, dtype=F32):
    return jax.ShapeDtypeStruct(dims, dtype)


def tiles_of(count):
    return shape(count * ROWS, LANES)


def call(kernel, outs, args, scratch=(), micros=1.0, out_place=pltpu.VMEM, copies=0):
    scratch = [pltpu.VMEM(s.shape, s.dtype) for s in scratch]
    if copies:
        scratch.append(pltpu.SemaphoreType.DMA((copies,)))
    return pl.pallas_call(
        kernel,
        out_shape=outs,
        in_specs=[VMEM] * len(args),
        out_specs=jax.tree.map(lambda _: pl.BlockSpec(memory_space=out_place), outs),
        scratch_shapes=scratch,
        compiler_params=pltpu.CompilerParams(vmem_limit_bytes=40 << 20),
        cost_estimate=pl.CostEstimate(
            flops=int(micros * 1.1e9), bytes_accessed=int(micros * 3.6e6), transcendentals=0
        ),
    )(*args)


def swap_neighbours(axis, begin, message):
    axes = ("gx", "gy", "gz")
    sizes = [lax.axis_size(a) for a in axes]
    along, other = (0, 2) if axis == "gx" else (1, 0)

    def partner(place, start, count):
        to = start + ((place - start) ^ 1)
        return to if start <= place and to < count else place

    index = {place: i for i, place in enumerate(itertools.product(*map(range, sizes)))}
    pairs = []
    for place, i in index.items():
        to = list(place)
        to[along] = partner(place[along], begin, sizes[along])
        if to[along] == place[along]:
            to[other] = partner(place[other], 0, sizes[other])
        pairs.append((i, index[tuple(to)]))
    return lax.ppermute(message, axes, pairs)


def per_device(bin_mass, courant, sub_courant, fall_steps, frag_gain, collide):
    nx, ny, nz, bins = bin_mass.shape
    n = nx
    parts = lax.axis_size("gz")
    gz, gy = lax.axis_index("gz"), lax.axis_index("gy")
    width = bins // parts
    tiles = groups(parts)[2]
    winds = 3 * tiles

    pair_rows = (bins // 2 + 1) * LANES
    pairs, lost = call(
        functools.partial(matrix_kernel, bins),
        (shape(pair_rows, LANES, dtype=jnp.bfloat16), shape(LANES, LANES, dtype=jnp.bfloat16)),
        (frag_gain, collide),
        [shape(2 * bins * bins, LANES), shape(3 * bins * bins // 2, LANES)],
        micros=0.02,
    )

    y_message = tiles_of(n * PAD_LO + winds)
    x_message = tiles_of(n * PAD_LO + winds // 2)
    if parts == 2:
        half = tiles_of(n * n // 2)
        send, keep = call(pack_kernel, (half, half), (bin_mass,), micros=0.3)
        got = lax.ppermute(send, "gz", [(0, 1), (1, 0)])
        own_wind = call(wind_kernel, tiles_of(3), (courant, keep), micros=0.1)
        got_wind = lax.ppermute(own_wind, "gz", [(0, 1), (1, 0)])
        block, *messages = call(
            merge_kernel,
            [tiles_of(n * n + winds), y_message, y_message, x_message, x_message],
            (keep, got, own_wind, got_wind, lost),
            micros=0.2,
        )
    else:
        split = bin_mass.reshape(nx, ny, nz // ROWS, ROWS, parts, width).transpose(4, 0, 1, 3, 2, 5)
        split = lax.all_to_all(split, "gz", split_axis=0, concat_axis=0, tiled=True)
        cube = split.transpose(1, 2, 3, 0, 4, 5).reshape(n, n, ROWS, LANES)
        air = courant.reshape(3, nx, ny, nz // ROWS, ROWS).transpose(0, 4, 3, 1, 2) * (1.0 / 12.0)
        air = lax.all_gather(air, "gz").reshape(parts, 3, ROWS, nz // ROWS, tiles, nx // tiles, ny)
        air = air.transpose(1, 4, 2, 0, 3, 5, 6).reshape(3, tiles, ROWS, LANES)
        block = jnp.concatenate([cube.reshape(-1, LANES), air.reshape(-1, LANES)])
        messages = []
        for layers, low_air, high_air, message, even in (
            (cube.transpose(1, 0, 2, 3), air, air, y_message, gy % 2 == 0),
            (cube, air[:, : tiles // 2], air[:, tiles // 2 :], x_message, lax.axis_index("gx") % 2 == 0),
        ):
            up, down = layers[n - PAD_LO :], layers[:PAD_HI]
            if message is y_message:
                up, down = up.transpose(1, 0, 2, 3), down.transpose(1, 0, 2, 3)
            up = jnp.concatenate([up.reshape(-1, LANES), high_air.reshape(-1, LANES)])
            down = jnp.concatenate([down.reshape(-1, LANES), low_air.reshape(-1, LANES)])
            messages += order(up, jnp.pad(down, ((0, up.shape[0] - down.shape[0]), (0, 0))), even)

    from_y = swap_neighbours("gy", 0, messages[0]), swap_neighbours("gy", 1, messages[1])
    from_x = swap_neighbours("gx", 1, messages[3]), swap_neighbours("gx", 0, messages[2])
    wind_x, wind_y, wind_z, own_change, edge_x, edge_y = call(
        functools.partial(own_kernel, n, parts), [tiles_of(n * n)] * 4 + [tiles_of(2 * n)] * 2, (block,), micros=1.6
    )
    message = tiles_of(LO * LINES + 2 + tiles)
    corners = call(functools.partial(corner_kernel, n, parts), (message, message), (*from_y, own_change), micros=0.1)
    corners = swap_neighbours("gx", 1, corners[1]), swap_neighbours("gx", 0, corners[0])
    cell, change, halo_wind_x, far_wind_y = call(
        functools.partial(y_kernel, n, parts),
        [tiles_of(n * (n + PAD_LO + PAD_HI)), tiles_of(n * (n + LINES)), tiles_of(LINES * n), tiles_of(n * (LINES + 2))],
        (block, *from_y, wind_y, own_change, edge_y),
        [tiles_of(LINES * n)] * 2,
        micros=2.0,
    )
    reach, inner = n + LINES, n - LINES
    near = call(
        functools.partial(inner_kernel, n, parts),
        [tiles_of(inner * reach), tiles_of(2 * reach), tiles_of(inner * n)],
        (cell, change, halo_wind_x, wind_y, far_wind_y, wind_z, edge_x),
        micros=0.9,
    )
    mid, far_wind_x, side, side_wind_y = call(
        functools.partial(x_kernel, n, parts),
        [tiles_of(count) for count in (reach * n, (LINES + 2) * n, LINES * n, LINES * n)],
        (cell, change, wind_x, near[1], *from_x),
        [tiles_of(LINES * n)] * 3,
        micros=1.7,
    )
    fall = sub_courant.reshape(1, bins), fall_steps.reshape(1, bins)

    def fallen(count):
        if parts == 2:
            return [tiles_of(n * count // 2 + (count + 3) // 4)] * 2
        return [tiles_of(n * count), tiles_of(count)]

    one, *early = call(
        functools.partial(main_kernel, n, parts),
        [tiles_of(reach * reach)] + fallen(EARLY),
        (
            *(cell, change, wind_x, wind_y, wind_z, halo_wind_x, far_wind_y, *near),
            *(mid, far_wind_x, side, side_wind_y, *corners, *fall),
        ),
        [tiles_of(count) for count in (LINES * LINES, 2 * LINES, 2 * LINES, n * EARLY, n * EARLY)],
        micros=2.6,
    )
    if parts == 2:
        early_got = lax.ppermute(early[0], "gz", [(0, 1), (1, 0)])
    late = call(
        functools.partial(late_kernel, n, parts),
        fallen(n - EARLY),
        (one, cell, wind_x, far_wind_x, wind_y, far_wind_y, wind_z, near[2], *fall),
        [tiles_of(n * (n - EARLY))] * 2,
        micros=0.7,
    )

    def products(count):
        return shape(n * count * ROWS, pair_rows, dtype=jnp.bfloat16)

    if parts == 2:
        late_got = lax.ppermute(late[0], "gz", [(0, 1), (1, 0)])
        early = call(
            functools.partial(breakup_first_kernel, n),
            [shape(EARLY, ny, nz, bins), shape(EARLY, ny // parts, bins)],
            (early[1], early_got, pairs, lost),
            [tiles_of(n * EARLY), products(EARLY)],
            micros=1.8,
        )
        outs = [shape(nx, ny, nz, bins), shape(nx, ny // parts, bins)]
        return tuple(
            call(
                functools.partial(breakup_last_kernel, n),
                outs,
                (late[1], late_got, pairs, lost, *early),
                [tiles_of(n * (n - EARLY)), products(n - EARLY), shape(n - EARLY, ny, nz, bins), outs[1]],
                micros=1.2,
                out_place=pl.ANY,
                copies=3,
            )
        )

    settled, rain = [jnp.concatenate(halves) for halves in zip(early, late)]
    rain = rain.reshape(nx, ny, LANES)[:, :, :width]
    rain = lax.all_to_all(rain, "gz", split_axis=1, concat_axis=2, tiled=True)
    settled = settled.reshape(nx, ny, ROWS, parts, nz // ROWS, width).transpose(3, 0, 1, 4, 2, 5)
    settled = lax.all_to_all(settled, "gz", split_axis=0, concat_axis=0, tiled=True)
    settled = settled.transpose(1, 2, 3, 4, 0, 5).reshape(nx * ny, nz // ROWS, ROWS, bins)
    paired = settled.transpose(0, 2, 1, 3).reshape(-1, LANES)
    updated = call(breakup_plain_kernel, tiles_of(n * n), (paired, pairs, lost), [products(n // 2)], micros=3.0)
    updated = updated.reshape(nx, ny, ROWS, nz // ROWS, bins).transpose(0, 1, 3, 2, 4).reshape(nx, ny, nz, bins)
    return updated, rain


def solution(mesh):
    in_specs = (P("gx", "gy", "gz", None), P(None, "gx", "gy", "gz"), P(), P(), P(), P())
    out_specs = (P("gx", "gy", "gz", None), P("gx", ("gy", "gz"), None))
    return jax.shard_map(per_device, mesh=mesh, in_specs=in_specs, out_specs=out_specs, check_vma=False)
```

```python
import functools
import itertools

import jax
import jax.numpy as jnp
from jax import lax
from jax.experimental import pallas as pl
from jax.experimental.pallas import tpu as pltpu
from jax.sharding import PartitionSpec as P

SUBS = 24
EPS = 1e-06
LO, HI = 3, 2
PAD_LO, PAD_HI = 2 * LO, 2 * HI
LINES = LO + HI
ROWS, LANES = 8, 128
AHEAD = 4
EARLY = 5
F32 = jnp.float32
VMEM = pl.BlockSpec(memory_space=pltpu.VMEM)


def lane_ids():
    return lax.broadcasted_iota(jnp.int32, (ROWS, LANES), 1)


def pick(tile, ids):
    return jnp.take_along_axis(tile, ids, axis=1, mode="promise_in_bounds")


def turn(tile, lanes):
    lanes %= LANES
    return pltpu.roll(tile, lanes, 1) if lanes else tile


def rows_of(first, count=1):
    return pl.ds(first * ROWS, count * ROWS)


def eight(first, level, step=1):
    return pl.ds(first * ROWS + level, ROWS, stride=step * ROWS)


def order(a, b, straight):
    return jnp.where(straight, a, b), jnp.where(straight, b, a)


def is_even(axis):
    return lax.axis_index(axis) % 2 == 0


def by_quarter(parts):
    quarter = lane_ids() // (LANES // 4)
    return jnp.where(quarter < 2, jnp.where(quarter == 0, parts[0], parts[1]), jnp.where(quarter == 2, parts[2], parts[3]))


def groups(parts):
    width = LANES // (2 * parts)
    return width, width // ROWS, ROWS * ROWS // width


def spread(jobs, parts):
    width, deep, _ = groups(parts)
    place = lane_ids() % width
    rows = [[], []]
    for tile, x, y, _, _ in jobs:
        top = tile.astype(jnp.bfloat16).astype(F32)
        here = place == x % deep * ROWS + y
        for out, term in zip(rows, (top, tile - top)):
            out.append(jnp.where(here, term, 0.0))
    terms = jnp.concatenate([jnp.concatenate(r, axis=0).astype(jnp.bfloat16) for r in rows], axis=1)
    source, target = [lax.broadcasted_iota(jnp.int32, (2 * LANES, LANES), k) for k in range(2)]
    same = jnp.where(source % LANES // width == target // width, 1.0, 0.0).astype(jnp.bfloat16)
    out = jnp.dot(terms, same, preferred_element_type=F32)
    for k, (_, _, _, ref, at) in enumerate(jobs):
        ref[rows_of(at)] = out[k * ROWS : (k + 1) * ROWS]


def halo_line(i, n):
    return jnp.where(i < LO, i - LO, i - LO + n)


def line_change(cells, winds):
    return changes(line_fluxes(cells, winds))


def changes(fluxes):
    return [a - b for a, b in zip(fluxes, fluxes[1:])]


def long_line(cells, winds, low_edge, high_edge, n):
    begin, end = LO, n - HI
    low = line_fluxes(cells[: PAD_LO + begin + 1], winds[: LO + 1 + begin]) + [low_edge]
    high = [high_edge] + line_fluxes(cells[PAD_LO + end - HI :], winds[LO + 1 + end :])
    return dict(zip(range(-LO, begin), changes(low))) | dict(zip(range(end, n + HI), changes(high)))


def line_fluxes(cells, winds):
    first = [b - a for a, b in zip(cells, cells[1:])]
    twice = [d + d for d in first]
    second = [b - a for a, b in zip(first, first[1:])]
    third = [a - b for a, b in zip(second, second[1:])]
    third_twice = [t + t for t in third]
    curved = [(13.0 / 3.0) * (c * c) + 4.0 * EPS for c in second]
    fluxes = []
    for j in range(len(cells) - 4):
        left = twice[j + 1] + second[j]
        mid = first[j + 1] + first[j + 2]
        right = twice[j + 2] - second[j + 2]
        w0 = pl.reciprocal(curved[j] + left * left, approx=True)
        w1 = pl.reciprocal(curved[j + 1] + mid * mid, approx=True)
        w2 = pl.reciprocal(curved[j + 2] + right * right, approx=True)
        w0 = w0 * w0
        w1 = 6.0 * (w1 * w1)
        w2 = 3.0 * (w2 * w2)
        top = w0 * third_twice[j] + w2 * third[j + 1]
        inverse = pl.reciprocal(w0 + w1 + w2, approx=True)
        estimate = 6.0 * cells[j + 2] + (first[j + 1] + twice[j + 2]) + top * inverse
        fluxes.append((winds[j] + winds[j + 1]) * estimate)
    return fluxes


def from_below(value, width):
    return jnp.where(lane_ids() < width, 0.0, turn(value, width))


def from_above(value, width):
    return jnp.where(lane_ids() >= LANES - width, 0.0, turn(value, -width))


def level_change(cells, winds, width):
    long_cells = [from_below(v, width) for v in cells[ROWS - LO :]] + cells + [from_above(v, width) for v in cells[:HI]]
    long_winds = [from_below(winds[-1], width)] + winds + [from_above(winds[0], width)]
    return line_change(long_cells, long_winds)


def pack_kernel(mass_ref, send_ref, keep_ref):
    lower = is_even("gz")
    n = mass_ref.shape[0]
    zero = jnp.zeros((ROWS, LANES // 2), F32)
    for x in range(n // 2):
        for y in range(n):
            tiles = [
                jnp.concatenate([mass_ref[xx, y, z : z + ROWS], zero], axis=1) for xx in (x, x + n // 2) for z in (0, ROWS)
            ]
            low = by_quarter([turn(v, 32 * k) for k, v in enumerate(tiles)])
            high = by_quarter([turn(v, 32 * k - 32) for k, v in enumerate(tiles)])
            at = rows_of(x * n + y)
            keep_ref[at], send_ref[at] = order(low, high, lower)


def wind_kernel(wind_ref, keep_ref, out_ref):
    del keep_ref
    n = wind_ref.shape[1]
    for d in range(3):
        levels = wind_ref[d].reshape(n * n, 2 * ROWS).T * (1.0 / 12.0)
        out_ref[rows_of(d)] = jnp.concatenate([levels[:ROWS], levels[ROWS:]], axis=1)


def sides(axis, first_ref, second_ref):
    even, place = is_even(axis), lax.axis_index(axis)
    inner_low, inner_high = place > 0, place < lax.axis_size(axis) - 1

    def below(at):
        return jnp.where(inner_low, jnp.where(even, second_ref[at], first_ref[at]), 0.0)

    def above(at):
        return jnp.where(inner_high, jnp.where(even, first_ref[at], second_ref[at]), 0.0)

    return below, above


def by_parity(axis, body):
    even = is_even(axis)
    pl.when(even)(lambda: body(0, 1))
    pl.when(jnp.logical_not(even))(lambda: body(1, 0))


def merge_kernel(keep_ref, got_ref, own_wind_ref, got_wind_ref, lost_ref, block_ref, y_first, y_second, x_first, x_second):
    del lost_ref
    n = 8
    lower = is_even("gz")
    low = lane_ids() < 64
    for x in range(n // 2):
        for y in range(n):
            at = rows_of(x * n + y)
            a, b = order(keep_ref[at], got_ref[at], lower)
            block_ref[at] = jnp.where(low, a, turn(b, 64))
            block_ref[rows_of((x + n // 2) * n + y)] = jnp.where(low, turn(a, 64), b)
    for d in range(3):
        a, b = order(own_wind_ref[rows_of(d)], got_wind_ref[rows_of(d)], lower)
        block_ref[rows_of(n * n + 2 * d)] = by_quarter([a, turn(a, -32), turn(b, 64), turn(b, 32)])
        block_ref[rows_of(n * n + 2 * d + 1)] = by_quarter([turn(a, -32), turn(a, -64), turn(b, 32), b])

    def along_y(up, down):
        for ref, start, wide in (((y_first, y_second)[up], n - PAD_LO, PAD_LO), ((y_first, y_second)[down], 0, PAD_HI)):
            for x in range(n):
                ref[rows_of(x * wide, wide)] = block_ref[rows_of(x * n + start, wide)]
            ref[rows_of(n * wide, 6)] = block_ref[rows_of(n * n, 6)]

    def along_x(up, down):
        for ref, start, wide, part in (((x_first, x_second)[up], n - PAD_LO, PAD_LO, 1), ((x_first, x_second)[down], 0, PAD_HI, 0)):
            ref[rows_of(0, wide * n)] = block_ref[rows_of(start * n, wide * n)]
            for d in range(3):
                ref[rows_of(wide * n + d)] = block_ref[rows_of(n * n + 2 * d + part)]

    by_parity("gy", along_y)
    by_parity("gx", along_x)


def corner_kernel(n, parts, first_ref, second_ref, own_change, *messages):
    del own_change
    tiles = groups(parts)[2]
    half = tiles // 2
    below, above = sides("gy", first_ref, second_ref)

    def body(up, down):
        for ref, start, narrow, part in ((messages[up], n - LO, LO, half), (messages[down], 0, HI, 0)):
            at = 0
            for x in range(start, start + narrow):
                ref[rows_of(at, LO)] = below(rows_of(x * PAD_LO + PAD_LO - LO, LO))
                ref[rows_of(at + LO, HI)] = above(rows_of(x * PAD_HI, HI))
                at += LINES
            for side, base in ((below, n * PAD_LO), (above, n * PAD_HI)):
                ref[rows_of(at)] = side(rows_of(base + (tiles - 1 if part else 0)))
                ref[rows_of(at + 1, half)] = side(rows_of(base + tiles + part, half))
                at += 1 + half

    by_parity("gx", body)


def own_kernel(n, parts, block_ref, wind_x, wind_y, wind_z, change, edge_x, edge_y):
    width, deep, tiles = groups(parts)
    for d, out in enumerate((wind_x, wind_y, wind_z)):
        jobs = []
        for x in range(n):
            tile = block_ref[rows_of(n * n + d * tiles + x // deep)]
            jobs += [(tile, x, y, out, x * n + y) for y in range(n)]
        spread(jobs, parts)

    @pl.loop(0, n)
    def _(x):
        cells = [block_ref[eight(x * n, k)] for k in range(ROWS)]
        winds = [wind_z[eight(x * n, k)] for k in range(ROWS)]
        for k, value in enumerate(level_change(cells, winds, width)):
            change[eight(x * n, k)] = value

    begin, end = LO, n - HI
    for wind, edge, place in ((wind_x, edge_x, lambda i, k: k * n + i), (wind_y, edge_y, lambda i, k: i * n + k)):

        @pl.loop(0, n)
        def _(i):
            cells = [block_ref[rows_of(place(i, k))] for k in range(n)]
            fluxes = line_fluxes(cells, [wind[rows_of(place(i, k))] for k in range(begin - 1, end + 1)])
            edge[rows_of(i)] = fluxes[0]
            edge[rows_of(n + i)] = fluxes[-1]
            for k, value in zip(range(begin, end), changes(fluxes)):
                at = rows_of(place(i, k))
                change[at] = change[at] + value


def y_kernel(n, parts, block_ref, first_ref, second_ref, wind_y, own_change, edge_y, *refs):
    width, deep, tiles = groups(parts)
    cell, change, wind_x, far_y, wind_z, halo_change = refs
    below, above = sides("gy", first_ref, second_ref)
    span, reach = n + PAD_LO + PAD_HI, n + LINES

    for x in range(n):
        cell[rows_of(x * span, PAD_LO)] = below(rows_of(x * PAD_LO, PAD_LO))
        cell[rows_of(x * span + PAD_LO, n)] = block_ref[rows_of(x * n, n)]
        cell[rows_of(x * span + PAD_LO + n, PAD_HI)] = above(rows_of(x * PAD_HI, PAD_HI))
    jobs = []
    for d in range(3):
        for t in range(tiles):
            low, high = below(rows_of(n * PAD_LO + d * tiles + t)), above(rows_of(n * PAD_HI + d * tiles + t))
            for x in range(t * deep, (t + 1) * deep):
                if d == 1:
                    jobs += [(low, x, n - LO - 1 + y, far_y, x * (LINES + 2) + y) for y in range(LO + 1)]
                    jobs += [(high, x, y, far_y, x * (LINES + 2) + LO + 1 + y) for y in range(HI + 1)]
                else:
                    out = wind_z if d else wind_x
                    jobs += [(low, x, n - LO + y, out, y * n + x) for y in range(LO)]
                    jobs += [(high, x, y, out, (LO + y) * n + x) for y in range(HI)]
    spread(jobs, parts)

    @pl.loop(0, LINES)
    def _(i):
        first = halo_line(i, n) + PAD_LO
        cells = [cell[eight(first, k, span)] for k in range(ROWS)]
        winds = [wind_z[eight(i * n, k)] for k in range(ROWS)]
        for k, value in enumerate(level_change(cells, winds, width)):
            halo_change[eight(i * n, k)] = value

    @pl.loop(0, n)
    def _(x):
        cells = [cell[rows_of(x * span + y)] for y in range(span)]
        far = [far_y[rows_of(x * (LINES + 2) + y)] for y in range(LINES + 2)]
        winds = far[: LO + 1] + [wind_y[rows_of(x * n + y)] for y in range(n)] + far[LO + 1 :]
        for y, value in long_line(cells, winds, edge_y[rows_of(x)], edge_y[rows_of(n + x)], n).items():
            if 0 <= y < n:
                value = value + own_change[rows_of(x * n + y)]
            else:
                value = value + halo_change[rows_of((y + LO if y < 0 else y + LO - n) * n + x)]
            change[rows_of(x * reach + y + LO)] = value
        for y in range(LO, n - HI):
            change[rows_of(x * reach + y + LO)] = own_change[rows_of(x * n + y)]


def inside(axis):
    place = lax.axis_index(axis)
    return [jnp.where(ok, 1.0, 0.0) for ok in (place > 0, place < lax.axis_size(axis) - 1)]


def inner_kernel(n, parts, cell, change, halo_wind_x, wind_y, far_wind_y, wind_z, edge_x, one, edge, second):
    width = groups(parts)[0]
    span, reach = n + PAD_LO + PAD_HI, n + LINES
    begin, end = LO, n - HI
    south_in, north_in = inside("gy")

    for k in range(2):
        edge[rows_of(k * reach + LO, n)] = edge_x[rows_of(k * n, n)]
    for i in range(end - begin):
        x = begin + i
        one[rows_of(i * reach + LO, n)] = cell[rows_of(x * span + PAD_LO, n)] + change[rows_of(x * reach + LO, n)]

    @pl.loop(0, LINES)
    def _(i):
        at = halo_line(i, n) + LO
        cells = [cell[rows_of(x * span + LO + at)] for x in range(n)]
        fluxes = line_fluxes(cells, [halo_wind_x[rows_of(i * n + x)] for x in range(begin - 1, end + 1)])
        edge[rows_of(at)] = fluxes[0]
        edge[rows_of(reach + at)] = fluxes[-1]
        keep = jnp.where(i < LO, south_in, north_in)
        for k, value in enumerate(changes(fluxes)):
            x = begin + k
            one[rows_of(k * reach + at)] = (cells[x] + (value + change[rows_of(x * reach + at)])) * keep

    @pl.loop(0, end - begin)
    def _(i):
        second_y_z(n, width, begin + i, one, i, wind_y, far_wind_y, wind_z, second, i)


def second_y_z(n, width, x, one, one_x, wind_y, far_wind_y, wind_z, second, second_x):
    reach = n + LINES
    cells = [one[rows_of(one_x * reach + y)] for y in range(reach)]
    winds = [far_wind_y[rows_of(x * (LINES + 2) + LO)]] + [wind_y[rows_of(x * n + y)] for y in range(n)]
    winds += [far_wind_y[rows_of(x * (LINES + 2) + LO + 1)]]
    for y, value in enumerate(line_change(cells, winds)):
        second[rows_of(second_x * n + y)] = value
    cells = [one[eight(one_x * reach + LO, k)] for k in range(ROWS)]
    winds = [wind_z[eight(x * n, k)] for k in range(ROWS)]
    for k, value in enumerate(level_change(cells, winds, width)):
        at = eight(second_x * n, k)
        second[at] = second[at] + value


def x_kernel(n, parts, cell, change, wind_x, edge, second_ref, first_ref, mid, far_wind_x, side, side_wind_y, *scratch):
    far, side_wind_z, side_change = scratch
    width, deep, tiles = groups(parts)
    half = tiles // 2
    west, east = sides("gx", first_ref, second_ref)
    span, reach = n + PAD_LO + PAD_HI, n + LINES

    jobs = []
    for take, wide, near_from, far_from, line in ((west, PAD_LO, LO, 0, 0), (east, PAD_HI, 0, HI, LO)):
        narrow = wide // 2
        side[rows_of(line * n, narrow * n)] = take(rows_of(near_from * n, narrow * n))
        far[rows_of(line * n, narrow * n)] = take(rows_of(far_from * n, narrow * n))
        layers, shift = (range(n - narrow, n), half) if line == 0 else (range(narrow), 0)
        wider = range(n - narrow - 1, n) if line == 0 else range(narrow + 1)

        def winds_of(d, x):
            return take(rows_of(wide * n + d * half + x // deep - shift))

        for i, x in enumerate(wider):
            jobs += [(winds_of(0, x), x, y, far_wind_x, (line + bool(line) + i) * n + y) for y in range(n)]
        for d, out in ((1, side_wind_y), (2, side_wind_z)):
            for i, x in enumerate(layers):
                jobs += [(winds_of(d, x), x, y, out, (line + i) * n + y) for y in range(n)]
    spread(jobs, parts)

    @pl.loop(0, LINES)
    def _(i):
        cells = [side[eight(i * n, k)] for k in range(ROWS)]
        winds = [side_wind_z[eight(i * n, k)] for k in range(ROWS)]
        for k, value in enumerate(level_change(cells, winds, width)):
            side_change[eight(i * n, k)] = value

    @pl.loop(0, n)
    def _(y):
        outer = [far[rows_of(i * n + y)] for i in range(LINES)]
        near = [side[rows_of(i * n + y)] for i in range(LINES)]
        cells = outer[:LO] + near[:LO] + [cell[rows_of(x * span + PAD_LO + y)] for x in range(n)] + near[LO:] + outer[LO:]
        winds = [far_wind_x[rows_of(i * n + y)] for i in range(LINES + 2)]
        winds = winds[: LO + 1] + [wind_x[rows_of(x * n + y)] for x in range(n)] + winds[LO + 1 :]
        for x, value in long_line(cells, winds, edge[rows_of(LO + y)], edge[rows_of(reach + LO + y)], n).items():
            if 0 <= x < n:
                value = value + change[rows_of(x * reach + LO + y)]
            else:
                value = value + side_change[rows_of((x + LO if x < 0 else x + LO - n) * n + y)]
            mid[rows_of((x + LO) * n + y)] = cells[PAD_LO + x] + value


def main_kernel(n, parts, *refs):
    cell, change, wind_x, wind_y, wind_z, halo_wind_x, far_wind_y, inner, edge, inner_second = refs[:10]
    mid, far_wind_x, side, side_wind_y, second_ref, first_ref, rate_ref, steps_ref = refs[10:18]
    one, *out_refs = refs[18:21]
    corner, corner_wind_x, edge_wind_y, second, fallen = refs[21:]
    deep, tiles = groups(parts)[1:]
    half = tiles // 2
    west, east = sides("gx", first_ref, second_ref)
    span, reach = n + PAD_LO + PAD_HI, n + LINES

    jobs = []
    for take, narrow, line in ((west, LO, 0), (east, HI, LO)):
        at = narrow * LINES
        corner[rows_of(line * LINES, at)] = take(rows_of(0, at))
        below, above = at, at + 1 + half
        layers, shift = (range(n - narrow, n), half) if line == 0 else (range(narrow), 0)
        for y in range(LINES):
            tile = take(rows_of(below if y < LO else above))
            x = layers[-1] if line == 0 else layers[0]
            jobs.append((tile, x, n - LO + y if y < LO else y - LO, corner_wind_x, bool(line) * LINES + y))
        for i, x in enumerate(layers):
            tile = x // deep - shift
            jobs.append((take(rows_of(below + 1 + tile)), x, n - 1, edge_wind_y, 2 * (line + i)))
            jobs.append((take(rows_of(above + 1 + tile)), x, 0, edge_wind_y, 2 * (line + i) + 1))
    spread(jobs, parts)

    west_in, east_in = inside("gx")
    south_in, north_in = inside("gy")
    begin, end = LO, n - HI
    one[rows_of((begin + LO) * reach, (end - begin) * reach)] = inner[...]
    for x in [x for x in range(n) if not begin <= x < end]:
        one[rows_of((x + LO) * reach + LO, n)] = mid[rows_of((x + LO) * n, n)]

    @pl.loop(0, LINES)
    def _(i):
        corners = [corner[rows_of(i * LINES + y)] for y in range(LINES)]
        cells = corners[:LO] + [side[rows_of(i * n + y)] for y in range(n)] + corners[LO:]
        winds = [side_wind_y[rows_of(i * n + y)] for y in range(n)]
        winds = [edge_wind_y[rows_of(2 * i)]] + winds + [edge_wind_y[rows_of(2 * i + 1)]]
        keep = jnp.where(i < LO, west_in, east_in)
        line = halo_line(i, n) + LO
        for y, value in enumerate(line_change(cells, winds)):
            one[rows_of(line * reach + LO + y)] = (mid[rows_of(line * n + y)] + value) * keep

    @pl.loop(0, LINES)
    def _(i):
        line = halo_line(i, n) + LO
        near = [corner[rows_of(k * LINES + i)] for k in range(LINES)]
        cells = near[:LO] + [cell[rows_of(x * span + LO + line)] for x in range(n)] + near[LO:]
        winds = [halo_wind_x[rows_of(i * n + x)] for x in range(n)]
        winds = [corner_wind_x[rows_of(i)]] + winds + [corner_wind_x[rows_of(LINES + i)]]
        keep = jnp.where(i < LO, south_in, north_in)
        low = line_fluxes(cells[: LO + begin + 1], winds[: begin + 1]) + [edge[rows_of(line)]]
        high = [edge[rows_of(reach + line)]] + line_fluxes(cells[LO + end - HI :], winds[end + 1 :])
        values = dict(zip(range(begin), changes(low))) | dict(zip(range(end, n), changes(high)))
        for x, value in values.items():
            one[rows_of((x + LO) * reach + line)] = (cells[x + LO] + (value + change[rows_of(x * reach + line)])) * keep

    fall_layers(
        n, parts, 0, EARLY, one, cell, wind_x, far_wind_x, wind_y, far_wind_y, wind_z, inner_second, rate_ref, steps_ref,
        out_refs, second, fallen,
    )


def late_kernel(
    n, parts, one, cell, wind_x, far_wind_x, wind_y, far_wind_y, wind_z, inner_second, rate_ref, steps_ref, *refs
):
    fall_layers(
        n, parts, EARLY, n, one, cell, wind_x, far_wind_x, wind_y, far_wind_y, wind_z, inner_second, rate_ref, steps_ref,
        refs[:2], *refs[2:],
    )


def fall_layers(
    n, parts, begin, end, one, cell, wind_x, far_wind_x, wind_y, far_wind_y, wind_z, inner_second, rate_ref, steps_ref,
    out_refs, second, fallen,
):
    width = groups(parts)[0]
    span, reach, count = n + PAD_LO + PAD_HI, n + LINES, end - begin
    ready = [x for x in range(LO, n - HI) if begin <= x < end]
    left = [x for x in range(begin, end) if x not in ready]
    if ready:
        second[rows_of((ready[0] - begin) * n, len(ready) * n)] = inner_second[rows_of((ready[0] - LO) * n, len(ready) * n)]

    @pl.loop(left[0], left[-1] + 1)
    def _(x):
        second_y_z(n, width, x, one, x + LO, wind_y, far_wind_y, wind_z, second, x - begin)

    @pl.loop(0, n)
    def _(y):
        cells = [one[rows_of(x * reach + LO + y)] for x in range(begin, end + LINES)]
        winds = [wind_x[rows_of(x * n + y)] for x in range(max(begin - 1, 0), min(end + 1, n))]
        if begin == 0:
            winds = [far_wind_x[rows_of(LO * n + y)]] + winds
        if end == n:
            winds = winds + [far_wind_x[rows_of((LO + 1) * n + y)]]
        for i, value in enumerate(line_change(cells, winds)):
            value = cells[i + LO] + (value + second[rows_of(i * n + y)])
            fallen[rows_of(i * n + y)] = 0.5 * cell[rows_of((begin + i) * span + PAD_LO + y)] + 0.5 * value

    bins = LANES // 2 // parts
    ids = lax.axis_index("gz") * bins + lane_ids() % bins
    rates, steps = [
        pick(jnp.broadcast_to(jnp.concatenate([ref[...]] * 2, axis=1), (ROWS, LANES)), ids) for ref in (rate_ref, steps_ref)
    ]

    rain = []
    for some in [range(i, min(i + 3, count)) for i in range(0, count, 3)]:
        columns = [[fallen[eight(i * n, k)] for k in range(ROWS)] for i in some]
        drops = [jnp.zeros((ROWS, LANES), F32) for _ in some]
        for block in range(SUBS // AHEAD):
            columns = [column + [from_above(v, width) for v in column[:AHEAD]] for column in columns]
            for s in range(AHEAD):
                rate = jnp.where(block * AHEAD + s < steps, rates, 0.0)
                for i, column in enumerate(columns):
                    drops[i] = drops[i] + rate * column[0]
                    columns[i] = [v + rate * (u - v) for v, u in zip(column, column[1:])]
        for i, column in zip(some, columns):
            for k in range(ROWS):
                fallen[eight(i * n, k)] = column[k]
        rain += drops

    if parts == 2:
        send_ref, keep_ref = out_refs
        lower = is_even("gz")
        low = lane_ids() < 64
        half = count * n // 2
        for c in range(half):
            a, b = fallen[rows_of(c)], fallen[rows_of(half + c)]
            at = rows_of(c)
            keep_ref[at], send_ref[at] = order(jnp.where(low, a, turn(b, 64)), jnp.where(low, turn(a, 64), b), lower)
        for j in range(0, count, 4):
            four = (rain[j : j + 4] + rain[j:] * 3)[:4]
            value = by_quarter([turn(v, 32 * i) for i, v in enumerate(four)])
            keep_ref[rows_of(half + j // 4)] = value
            send_ref[rows_of(half + j // 4)] = value
    else:
        settled_ref, rain_ref = out_refs
        settled_ref[...] = fallen[...]
        for i in range(count):
            rain_ref[rows_of(i)] = rain[i]


def matrix_kernel(bins, gain_ref, loss_ref, pairs_ref, lost_ref, wide, tall):
    zero = jnp.zeros((bins, LANES - bins), F32)
    shifts = bins // 2

    @pl.loop(0, bins)
    def _(i):
        rows = gain_ref[pl.ds(i * bins, bins)].astype(F32)
        rows = jnp.concatenate([rows, zero], axis=1)
        wide[pl.ds(i * 2 * bins, bins)] = rows
        wide[pl.ds(i * 2 * bins + bins, bins)] = rows
        tall[pl.ds(i * bins, bins)] = rows

        @pl.when(i < shifts)
        def _():
            tall[pl.ds((i + bins) * bins, bins)] = rows

    for d in range(shifts + 1):
        rows = wide[pl.ds(d, bins, stride=2 * bins + 1)]
        if 0 < d < shifts:
            rows = rows + tall[pl.ds(d * bins, bins, stride=bins + 1)]
        pairs_ref[pl.ds(d * LANES, bins)] = rows.astype(jnp.bfloat16)
        pairs_ref[pl.ds(d * LANES + bins, bins)] = pltpu.roll(rows, bins, 1).astype(jnp.bfloat16)
    rows = jnp.concatenate([loss_ref[...].astype(F32), zero], axis=1)
    lost_ref[pl.ds(0, bins)] = rows.astype(jnp.bfloat16)
    lost_ref[pl.ds(bins, bins)] = pltpu.roll(rows, bins, 1).astype(jnp.bfloat16)


def breakup_rows(mass, pairs_ref, lost_ref, products):
    bins = LANES // 2
    count = mass.shape[0]
    lanes = lane_ids()
    rounded = mass.astype(jnp.bfloat16)
    wide = rounded.astype(F32)
    gained = None
    shifts = bins // 2 + 1
    for begin in range(0, shifts, 4):
        end = min(begin + 4, shifts)
        for d in range(begin, end):
            ids = lanes // bins * bins + (lanes + d) % bins
            for r in range(0, count, 2 * ROWS):
                halves = [wide[r + ROWS * k : r + ROWS * (k + 1)] for k in range(2)]
                halves = [v * pick(v, ids) if d else v * v for v in halves]
                both = jnp.concatenate(halves, axis=0).astype(jnp.bfloat16)
                products[pl.ds(r, 2 * ROWS), d * LANES : (d + 1) * LANES] = both
        part = jnp.dot(
            products[pl.ds(0, count), begin * LANES : end * LANES],
            pairs_ref[pl.ds(begin * LANES, (end - begin) * LANES)],
            preferred_element_type=F32,
        )
        gained = part if gained is None else gained + part
    loss = jnp.dot(rounded, lost_ref[...], preferred_element_type=F32)
    return mass + gained - mass * loss


def breakup_layers(n, count, keep_ref, got_ref, pairs_ref, lost_ref, columns, products):
    first = is_even("gz")
    half = count * n // 2
    for c in range(half):
        a, b = order(keep_ref[rows_of(c)], got_ref[rows_of(c)], first)
        columns[rows_of(c)] = by_quarter([a, turn(b, 32), turn(a, 32), turn(b, 64)])
        columns[rows_of(half + c)] = by_quarter([turn(a, -64), turn(b, -32), turn(a, -32), b])
    rain = []
    for i in range(count):
        a, b = order(keep_ref[rows_of(half + i // 4)], got_ref[rows_of(half + i // 4)], first)
        a, b = [jnp.where(first, v[: n // 2], v[n // 2 :])[:, 32 * (i % 4) : 32 * (i % 4) + 32] for v in (a, b)]
        rain.append(jnp.concatenate([a, b], axis=1))
    columns[...] = breakup_rows(columns[...], pairs_ref, lost_ref, products)
    return rain


def lay_out(columns, mass, n, count):
    for x in range(count):
        for y in range(n):
            value = columns[rows_of(x * n + y)]
            mass[x, y, 0:ROWS] = value[:, :64]
            mass[x, y, ROWS : 2 * ROWS] = value[:, 64:]


def breakup_first_kernel(n, keep_ref, got_ref, pairs_ref, lost_ref, mass_ref, rain_ref, columns, products):
    for i, value in enumerate(breakup_layers(n, EARLY, keep_ref, got_ref, pairs_ref, lost_ref, columns, products)):
        rain_ref[i] = value
    lay_out(columns, mass_ref, n, EARLY)


def breakup_last_kernel(
    n, keep_ref, got_ref, pairs_ref, lost_ref, early, early_rain, mass_out, rain_out, columns, products, mass, rain, sems
):
    early_copy = pltpu.make_async_copy(early, mass_out.at[pl.ds(0, EARLY)], sems.at[0])
    early_copy.start()
    late_rain = breakup_layers(n, n - EARLY, keep_ref, got_ref, pairs_ref, lost_ref, columns, products)
    for i in range(EARLY):
        rain[i] = early_rain[i]
    for i, value in enumerate(late_rain):
        rain[EARLY + i] = value
    rain_copy = pltpu.make_async_copy(rain, rain_out, sems.at[2])
    rain_copy.start()
    lay_out(columns, mass, n, n - EARLY)
    late_copy = pltpu.make_async_copy(mass, mass_out.at[pl.ds(EARLY, n - EARLY)], sems.at[1])
    late_copy.start()
    for copy in (early_copy, rain_copy, late_copy):
        copy.wait()


def breakup_plain_kernel(mass_ref, pairs_ref, lost_ref, out_ref, products):
    count = products.shape[0]

    @pl.loop(0, mass_ref.shape[0] // count)
    def _(i):
        start = pl.multiple_of(i * count, count)
        out_ref[pl.ds(start, count)] = breakup_rows(mass_ref[pl.ds(start, count)], pairs_ref, lost_ref, products)


def shape(*dims, dtype=F32):
    return jax.ShapeDtypeStruct(dims, dtype)


def tiles_of(count):
    return shape(count * ROWS, LANES)


def call(kernel, outs, args, scratch=(), micros=1.0, out_place=pltpu.VMEM, copies=0):
    scratch = [pltpu.VMEM(s.shape, s.dtype) for s in scratch]
    if copies:
        scratch.append(pltpu.SemaphoreType.DMA((copies,)))
    return pl.pallas_call(
        kernel,
        out_shape=outs,
        in_specs=[VMEM] * len(args),
        out_specs=jax.tree.map(lambda _: pl.BlockSpec(memory_space=out_place), outs),
        scratch_shapes=scratch,
        compiler_params=pltpu.CompilerParams(vmem_limit_bytes=40 << 20),
        cost_estimate=pl.CostEstimate(
            flops=int(micros * 1.1e9), bytes_accessed=int(micros * 3.6e6), transcendentals=0
        ),
    )(*args)


def swap_neighbours(axis, begin, message):
    axes = ("gx", "gy", "gz")
    sizes = [lax.axis_size(a) for a in axes]
    along, other = (0, 2) if axis == "gx" else (1, 0)

    def partner(place, start, count):
        to = start + ((place - start) ^ 1)
        return to if start <= place and to < count else place

    index = {place: i for i, place in enumerate(itertools.product(*map(range, sizes)))}
    pairs = []
    for place, i in index.items():
        to = list(place)
        to[along] = partner(place[along], begin, sizes[along])
        if to[along] == place[along]:
            to[other] = partner(place[other], 0, sizes[other])
        pairs.append((i, index[tuple(to)]))
    return lax.ppermute(message, axes, pairs)


def per_device(bin_mass, courant, sub_courant, fall_steps, frag_gain, collide):
    nx, ny, nz, bins = bin_mass.shape
    n = nx
    parts = lax.axis_size("gz")
    gz, gy = lax.axis_index("gz"), lax.axis_index("gy")
    width = bins // parts
    tiles = groups(parts)[2]
    winds = 3 * tiles

    pair_rows = (bins // 2 + 1) * LANES
    pairs, lost = call(
        functools.partial(matrix_kernel, bins),
        (shape(pair_rows, LANES, dtype=jnp.bfloat16), shape(LANES, LANES, dtype=jnp.bfloat16)),
        (frag_gain, collide),
        [shape(2 * bins * bins, LANES), shape(3 * bins * bins // 2, LANES)],
        micros=0.02,
    )

    y_message = tiles_of(n * PAD_LO + winds)
    x_message = tiles_of(n * PAD_LO + winds // 2)
    if parts == 2:
        half = tiles_of(n * n // 2)
        send, keep = call(pack_kernel, (half, half), (bin_mass,), micros=0.3)
        got = lax.ppermute(send, "gz", [(0, 1), (1, 0)])
        own_wind = call(wind_kernel, tiles_of(3), (courant, keep), micros=0.1)
        got_wind = lax.ppermute(own_wind, "gz", [(0, 1), (1, 0)])
        block, *messages = call(
            merge_kernel,
            [tiles_of(n * n + winds), y_message, y_message, x_message, x_message],
            (keep, got, own_wind, got_wind, lost),
            micros=0.2,
        )
    else:
        split = bin_mass.reshape(nx, ny, nz // ROWS, ROWS, parts, width).transpose(4, 0, 1, 3, 2, 5)
        split = lax.all_to_all(split, "gz", split_axis=0, concat_axis=0, tiled=True)
        cube = split.transpose(1, 2, 3, 0, 4, 5).reshape(n, n, ROWS, LANES)
        air = courant.reshape(3, nx, ny, nz // ROWS, ROWS).transpose(0, 4, 3, 1, 2) * (1.0 / 12.0)
        air = lax.all_gather(air, "gz").reshape(parts, 3, ROWS, nz // ROWS, tiles, nx // tiles, ny)
        air = air.transpose(1, 4, 2, 0, 3, 5, 6).reshape(3, tiles, ROWS, LANES)
        block = jnp.concatenate([cube.reshape(-1, LANES), air.reshape(-1, LANES)])
        messages = []
        for layers, low_air, high_air, message, even in (
            (cube.transpose(1, 0, 2, 3), air, air, y_message, gy % 2 == 0),
            (cube, air[:, : tiles // 2], air[:, tiles // 2 :], x_message, lax.axis_index("gx") % 2 == 0),
        ):
            up, down = layers[n - PAD_LO :], layers[:PAD_HI]
            if message is y_message:
                up, down = up.transpose(1, 0, 2, 3), down.transpose(1, 0, 2, 3)
            up = jnp.concatenate([up.reshape(-1, LANES), high_air.reshape(-1, LANES)])
            down = jnp.concatenate([down.reshape(-1, LANES), low_air.reshape(-1, LANES)])
            messages += order(up, jnp.pad(down, ((0, up.shape[0] - down.shape[0]), (0, 0))), even)

    from_y = swap_neighbours("gy", 0, messages[0]), swap_neighbours("gy", 1, messages[1])
    from_x = swap_neighbours("gx", 1, messages[3]), swap_neighbours("gx", 0, messages[2])
    wind_x, wind_y, wind_z, own_change, edge_x, edge_y = call(
        functools.partial(own_kernel, n, parts), [tiles_of(n * n)] * 4 + [tiles_of(2 * n)] * 2, (block,), micros=1.6
    )
    message = tiles_of(LO * LINES + 2 + tiles)
    corners = call(functools.partial(corner_kernel, n, parts), (message, message), (*from_y, own_change), micros=0.1)
    corners = swap_neighbours("gx", 1, corners[1]), swap_neighbours("gx", 0, corners[0])
    cell, change, halo_wind_x, far_wind_y = call(
        functools.partial(y_kernel, n, parts),
        [tiles_of(n * (n + PAD_LO + PAD_HI)), tiles_of(n * (n + LINES)), tiles_of(LINES * n), tiles_of(n * (LINES + 2))],
        (block, *from_y, wind_y, own_change, edge_y),
        [tiles_of(LINES * n)] * 2,
        micros=2.0,
    )
    reach, inner = n + LINES, n - LINES
    near = call(
        functools.partial(inner_kernel, n, parts),
        [tiles_of(inner * reach), tiles_of(2 * reach), tiles_of(inner * n)],
        (cell, change, halo_wind_x, wind_y, far_wind_y, wind_z, edge_x),
        micros=0.9,
    )
    mid, far_wind_x, side, side_wind_y = call(
        functools.partial(x_kernel, n, parts),
        [tiles_of(count) for count in (reach * n, (LINES + 2) * n, LINES * n, LINES * n)],
        (cell, change, wind_x, near[1], *from_x),
        [tiles_of(LINES * n)] * 3,
        micros=1.7,
    )
    fall = sub_courant.reshape(1, bins), fall_steps.reshape(1, bins)

    def fallen(count):
        if parts == 2:
            return [tiles_of(n * count // 2 + (count + 3) // 4)] * 2
        return [tiles_of(n * count), tiles_of(count)]

    one, *early = call(
        functools.partial(main_kernel, n, parts),
        [tiles_of(reach * reach)] + fallen(EARLY),
        (
            *(cell, change, wind_x, wind_y, wind_z, halo_wind_x, far_wind_y, *near),
            *(mid, far_wind_x, side, side_wind_y, *corners, *fall),
        ),
        [tiles_of(count) for count in (LINES * LINES, 2 * LINES, 2 * LINES, n * EARLY, n * EARLY)],
        micros=2.6,
    )
    if parts == 2:
        early_got = lax.ppermute(early[0], "gz", [(0, 1), (1, 0)])
    late = call(
        functools.partial(late_kernel, n, parts),
        fallen(n - EARLY),
        (one, cell, wind_x, far_wind_x, wind_y, far_wind_y, wind_z, near[2], *fall),
        [tiles_of(n * (n - EARLY))] * 2,
        micros=0.7,
    )

    def products(count):
        return shape(n * count * ROWS, pair_rows, dtype=jnp.bfloat16)

    if parts == 2:
        late_got = lax.ppermute(late[0], "gz", [(0, 1), (1, 0)])
        early = call(
            functools.partial(breakup_first_kernel, n),
            [shape(EARLY, ny, nz, bins), shape(EARLY, ny // parts, bins)],
            (early[1], early_got, pairs, lost),
            [tiles_of(n * EARLY), products(EARLY)],
            micros=1.8,
        )
        outs = [shape(nx, ny, nz, bins), shape(nx, ny // parts, bins)]
        return tuple(
            call(
                functools.partial(breakup_last_kernel, n),
                outs,
                (late[1], late_got, pairs, lost, *early),
                [tiles_of(n * (n - EARLY)), products(n - EARLY), shape(n - EARLY, ny, nz, bins), outs[1]],
                micros=1.2,
                out_place=pl.ANY,
                copies=3,
            )
        )

    settled, rain = [jnp.concatenate(halves) for halves in zip(early, late)]
    rain = rain.reshape(nx, ny, LANES)[:, :, :width]
    rain = lax.all_to_all(rain, "gz", split_axis=1, concat_axis=2, tiled=True)
    settled = settled.reshape(nx, ny, ROWS, parts, nz // ROWS, width).transpose(3, 0, 1, 4, 2, 5)
    settled = lax.all_to_all(settled, "gz", split_axis=0, concat_axis=0, tiled=True)
    settled = settled.transpose(1, 2, 3, 4, 0, 5).reshape(nx * ny, nz // ROWS, ROWS, bins)
    paired = settled.transpose(0, 2, 1, 3).reshape(-1, LANES)
    updated = call(breakup_plain_kernel, tiles_of(n * n), (paired, pairs, lost), [products(n // 2)], micros=3.0)
    updated = updated.reshape(nx, ny, ROWS, nz // ROWS, bins).transpose(0, 1, 3, 2, 4).reshape(nx, ny, nz, bins)
    return updated, rain


def solution(mesh):
    in_specs = (P("gx", "gy", "gz", None), P(None, "gx", "gy", "gz"), P(), P(), P(), P())
    out_specs = (P("gx", "gy", "gz", None), P("gx", ("gy", "gz"), None))
    return jax.shard_map(per_device, mesh=mesh, in_specs=in_specs, out_specs=out_specs, check_vma=False)
```

```python
import functools
import itertools

import jax
import jax.numpy as jnp
from jax import lax
from jax.experimental import pallas as pl
from jax.experimental.pallas import tpu as pltpu
from jax.sharding import PartitionSpec as P

SUBS = 24
EPS = 1e-06
LO, HI = 3, 2
PAD_LO, PAD_HI = 2 * LO, 2 * HI
LINES = LO + HI
ROWS, LANES = 8, 128
AHEAD = 4
EARLY = 5
F32 = jnp.float32
VMEM = pl.BlockSpec(memory_space=pltpu.VMEM)


def lane_ids():
    return lax.broadcasted_iota(jnp.int32, (ROWS, LANES), 1)


def pick(tile, ids):
    return jnp.take_along_axis(tile, ids, axis=1, mode="promise_in_bounds")


def turn(tile, lanes):
    lanes %= LANES
    return pltpu.roll(tile, lanes, 1) if lanes else tile


def rows_of(first, count=1):
    return pl.ds(first * ROWS, count * ROWS)


def eight(first, level, step=1):
    return pl.ds(first * ROWS + level, ROWS, stride=step * ROWS)


def order(a, b, straight):
    return jnp.where(straight, a, b), jnp.where(straight, b, a)


def is_even(axis):
    return lax.axis_index(axis) % 2 == 0


def by_quarter(parts):
    quarter = lane_ids() // (LANES // 4)
    return jnp.where(quarter < 2, jnp.where(quarter == 0, parts[0], parts[1]), jnp.where(quarter == 2, parts[2], parts[3]))


def groups(parts):
    width = LANES // (2 * parts)
    return width, width // ROWS, ROWS * ROWS // width


def spread(jobs, parts):
    width, deep, _ = groups(parts)
    place = lane_ids() % width
    rows = [[], []]
    for tile, x, y, _, _ in jobs:
        top = tile.astype(jnp.bfloat16).astype(F32)
        here = place == x % deep * ROWS + y
        for out, term in zip(rows, (top, tile - top)):
            out.append(jnp.where(here, term, 0.0))
    terms = jnp.concatenate([jnp.concatenate(r, axis=0).astype(jnp.bfloat16) for r in rows], axis=1)
    source, target = [lax.broadcasted_iota(jnp.int32, (2 * LANES, LANES), k) for k in range(2)]
    same = jnp.where(source % LANES // width == target // width, 1.0, 0.0).astype(jnp.bfloat16)
    out = jnp.dot(terms, same, preferred_element_type=F32)
    for k, (_, _, _, ref, at) in enumerate(jobs):
        ref[rows_of(at)] = out[k * ROWS : (k + 1) * ROWS]


def each(count, together, body):
    def some(places):
        stores = [store for i in places for store in body(i)]
        for ref, at, value in stores:
            ref[at] = value

    whole = count // together

    @pl.loop(0, whole)
    def _(i):
        some([i * together + k for k in range(together)])

    if count % together:
        some(range(whole * together, count))


def halo_line(i, n):
    if isinstance(i, int):
        return i - LO + (n if i >= LO else 0)
    return jnp.where(i < LO, i - LO, i - LO + n)


def line_change(cells, winds):
    return changes(line_fluxes(cells, winds))


def changes(fluxes):
    return [a - b for a, b in zip(fluxes, fluxes[1:])]


def long_line(cells, winds, low_edge, high_edge, n):
    begin, end = LO, n - HI
    low = line_fluxes(cells[: PAD_LO + begin + 1], winds[: LO + 1 + begin]) + [low_edge]
    high = [high_edge] + line_fluxes(cells[PAD_LO + end - HI :], winds[LO + 1 + end :])
    return dict(zip(range(-LO, begin), changes(low))) | dict(zip(range(end, n + HI), changes(high)))


def line_fluxes(cells, winds):
    first = [b - a for a, b in zip(cells, cells[1:])]
    twice = [d + d for d in first]
    second = [b - a for a, b in zip(first, first[1:])]
    third = [a - b for a, b in zip(second, second[1:])]
    curved = [(13.0 / 3.0) * (c * c) + 4.0 * EPS for c in second]
    fluxes = []
    for j in range(len(cells) - 4):
        left = twice[j + 1] + second[j]
        mid = first[j + 1] + first[j + 2]
        right = twice[j + 2] - second[j + 2]
        e0 = curved[j] + left * left
        e1 = curved[j + 1] + mid * mid
        e2 = curved[j + 2] + right * right
        e0 = 3.0 * (e0 * e0)
        e1 = e1 * e1
        e2 = e2 * e2
        e2_twice = e2 + e2
        top = e1 * (e2_twice * third[j] + e0 * third[j + 1])
        inverse = pl.reciprocal(e1 * (e2 + e0) + e0 * e2_twice, approx=True)
        estimate = 6.0 * cells[j + 2] + (first[j + 1] + twice[j + 2]) + top * inverse
        fluxes.append((winds[j] + winds[j + 1]) * estimate)
    return fluxes


def from_below(value, width):
    return jnp.where(lane_ids() < width, 0.0, turn(value, width))


def from_above(value, width):
    return jnp.where(lane_ids() >= LANES - width, 0.0, turn(value, -width))


def level_change(cells, winds, width):
    long_cells = [from_below(v, width) for v in cells[ROWS - LO :]] + cells + [from_above(v, width) for v in cells[:HI]]
    long_winds = [from_below(winds[-1], width)] + winds + [from_above(winds[0], width)]
    return line_change(long_cells, long_winds)


def pack_kernel(mass_ref, send_ref, keep_ref):
    lower = is_even("gz")
    n = mass_ref.shape[0]
    zero = jnp.zeros((ROWS, LANES // 2), F32)
    for x in range(n // 2):
        for y in range(n):
            tiles = [
                jnp.concatenate([mass_ref[xx, y, z : z + ROWS], zero], axis=1) for xx in (x, x + n // 2) for z in (0, ROWS)
            ]
            low = by_quarter([turn(v, 32 * k) for k, v in enumerate(tiles)])
            high = by_quarter([turn(v, 32 * k - 32) for k, v in enumerate(tiles)])
            at = rows_of(x * n + y)
            keep_ref[at], send_ref[at] = order(low, high, lower)


def wind_kernel(wind_ref, keep_ref, out_ref):
    del keep_ref
    n = wind_ref.shape[1]
    for d in range(3):
        levels = wind_ref[d].reshape(n * n, 2 * ROWS).T * (1.0 / 12.0)
        out_ref[rows_of(d)] = jnp.concatenate([levels[:ROWS], levels[ROWS:]], axis=1)


def sides(axis, first_ref, second_ref):
    even, place = is_even(axis), lax.axis_index(axis)
    inner_low, inner_high = place > 0, place < lax.axis_size(axis) - 1

    def below(at):
        return jnp.where(inner_low, jnp.where(even, second_ref[at], first_ref[at]), 0.0)

    def above(at):
        return jnp.where(inner_high, jnp.where(even, first_ref[at], second_ref[at]), 0.0)

    return below, above


def by_parity(axis, body):
    even = is_even(axis)
    pl.when(even)(lambda: body(0, 1))
    pl.when(jnp.logical_not(even))(lambda: body(1, 0))


def merge_kernel(keep_ref, got_ref, own_wind_ref, got_wind_ref, lost_ref, block_ref, y_first, y_second, x_first, x_second):
    del lost_ref
    n = 8
    lower = is_even("gz")
    low = lane_ids() < 64
    for x in range(n // 2):
        for y in range(n):
            at = rows_of(x * n + y)
            a, b = order(keep_ref[at], got_ref[at], lower)
            block_ref[at] = jnp.where(low, a, turn(b, 64))
            block_ref[rows_of((x + n // 2) * n + y)] = jnp.where(low, turn(a, 64), b)
    for d in range(3):
        a, b = order(own_wind_ref[rows_of(d)], got_wind_ref[rows_of(d)], lower)
        block_ref[rows_of(n * n + 2 * d)] = by_quarter([a, turn(a, -32), turn(b, 64), turn(b, 32)])
        block_ref[rows_of(n * n + 2 * d + 1)] = by_quarter([turn(a, -32), turn(a, -64), turn(b, 32), b])

    def along_y(up, down):
        for ref, start, wide in (((y_first, y_second)[up], n - PAD_LO, PAD_LO), ((y_first, y_second)[down], 0, PAD_HI)):
            for x in range(n):
                ref[rows_of(x * wide, wide)] = block_ref[rows_of(x * n + start, wide)]
            ref[rows_of(n * wide, 6)] = block_ref[rows_of(n * n, 6)]

    def along_x(up, down):
        for ref, start, wide, part in (((x_first, x_second)[up], n - PAD_LO, PAD_LO, 1), ((x_first, x_second)[down], 0, PAD_HI, 0)):
            ref[rows_of(0, wide * n)] = block_ref[rows_of(start * n, wide * n)]
            for d in range(3):
                ref[rows_of(wide * n + d)] = block_ref[rows_of(n * n + 2 * d + part)]

    by_parity("gy", along_y)
    by_parity("gx", along_x)


def corner_kernel(n, parts, first_ref, second_ref, own_change, *messages):
    del own_change
    tiles = groups(parts)[2]
    half = tiles // 2
    below, above = sides("gy", first_ref, second_ref)

    def body(up, down):
        for ref, start, narrow, part in ((messages[up], n - LO, LO, half), (messages[down], 0, HI, 0)):
            at = 0
            for x in range(start, start + narrow):
                ref[rows_of(at, LO)] = below(rows_of(x * PAD_LO + PAD_LO - LO, LO))
                ref[rows_of(at + LO, HI)] = above(rows_of(x * PAD_HI, HI))
                at += LINES
            for side, base in ((below, n * PAD_LO), (above, n * PAD_HI)):
                ref[rows_of(at)] = side(rows_of(base + (tiles - 1 if part else 0)))
                ref[rows_of(at + 1, half)] = side(rows_of(base + tiles + part, half))
                at += 1 + half

    by_parity("gx", body)


def own_kernel(n, parts, block_ref, wind_x, wind_y, wind_z, change, edge_x, edge_y):
    width, deep, tiles = groups(parts)
    for d, out in enumerate((wind_x, wind_y, wind_z)):
        jobs = []
        for x in range(n):
            tile = block_ref[rows_of(n * n + d * tiles + x // deep)]
            jobs += [(tile, x, y, out, x * n + y) for y in range(n)]
        spread(jobs, parts)

    def along_z(x):
        cells = [block_ref[eight(x * n, k)] for k in range(ROWS)]
        winds = [wind_z[eight(x * n, k)] for k in range(ROWS)]
        return [(change, eight(x * n, k), value) for k, value in enumerate(level_change(cells, winds, width))]

    each(n, 2, along_z)
    begin, end = LO, n - HI
    for wind, edge, place in ((wind_x, edge_x, lambda i, k: k * n + i), (wind_y, edge_y, lambda i, k: i * n + k)):

        def along(i):
            cells = [block_ref[rows_of(place(i, k))] for k in range(n)]
            fluxes = line_fluxes(cells, [wind[rows_of(place(i, k))] for k in range(begin - 1, end + 1)])
            at = [rows_of(place(i, k)) for k in range(begin, end)]
            stores = [(change, here, change[here] + value) for here, value in zip(at, changes(fluxes))]
            return stores + [(edge, rows_of(i), fluxes[0]), (edge, rows_of(n + i), fluxes[-1])]

        each(n, 4, along)


def y_kernel(n, parts, block_ref, first_ref, second_ref, wind_y, own_change, edge_y, *refs):
    width, deep, tiles = groups(parts)
    cell, change, wind_x, far_y, wind_z, halo_change = refs
    below, above = sides("gy", first_ref, second_ref)
    span, reach = n + PAD_LO + PAD_HI, n + LINES

    for x in range(n):
        cell[rows_of(x * span, PAD_LO)] = below(rows_of(x * PAD_LO, PAD_LO))
        cell[rows_of(x * span + PAD_LO, n)] = block_ref[rows_of(x * n, n)]
        cell[rows_of(x * span + PAD_LO + n, PAD_HI)] = above(rows_of(x * PAD_HI, PAD_HI))
    jobs = []
    for d in range(3):
        for t in range(tiles):
            low, high = below(rows_of(n * PAD_LO + d * tiles + t)), above(rows_of(n * PAD_HI + d * tiles + t))
            for x in range(t * deep, (t + 1) * deep):
                if d == 1:
                    jobs += [(low, x, n - LO - 1 + y, far_y, x * (LINES + 2) + y) for y in range(LO + 1)]
                    jobs += [(high, x, y, far_y, x * (LINES + 2) + LO + 1 + y) for y in range(HI + 1)]
                else:
                    out = wind_z if d else wind_x
                    jobs += [(low, x, n - LO + y, out, y * n + x) for y in range(LO)]
                    jobs += [(high, x, y, out, (LO + y) * n + x) for y in range(HI)]
    spread(jobs, parts)

    def along_z(i):
        first = halo_line(i, n) + PAD_LO
        cells = [cell[eight(first, k, span)] for k in range(ROWS)]
        winds = [wind_z[eight(i * n, k)] for k in range(ROWS)]
        return [(halo_change, eight(i * n, k), value) for k, value in enumerate(level_change(cells, winds, width))]

    each(LINES, 2, along_z)

    def along_y(x):
        cells = [cell[rows_of(x * span + y)] for y in range(span)]
        far = [far_y[rows_of(x * (LINES + 2) + y)] for y in range(LINES + 2)]
        winds = far[: LO + 1] + [wind_y[rows_of(x * n + y)] for y in range(n)] + far[LO + 1 :]
        stores = []
        for y, value in long_line(cells, winds, edge_y[rows_of(x)], edge_y[rows_of(n + x)], n).items():
            if 0 <= y < n:
                value = value + own_change[rows_of(x * n + y)]
            else:
                value = value + halo_change[rows_of((y + LO if y < 0 else y + LO - n) * n + x)]
            stores.append((change, rows_of(x * reach + y + LO), value))
        for y in range(LO, n - HI):
            stores.append((change, rows_of(x * reach + y + LO), own_change[rows_of(x * n + y)]))
        return stores

    each(n, 2, along_y)


def which(i, lower, upper):
    if isinstance(i, int):
        return lower if i < LO else upper
    return jnp.where(i < LO, lower, upper)


def inside(axis):
    place = lax.axis_index(axis)
    return [jnp.where(ok, 1.0, 0.0) for ok in (place > 0, place < lax.axis_size(axis) - 1)]


def inner_kernel(n, parts, cell, change, halo_wind_x, wind_y, far_wind_y, wind_z, edge_x, one, edge, second):
    width = groups(parts)[0]
    span, reach = n + PAD_LO + PAD_HI, n + LINES
    begin, end = LO, n - HI
    south_in, north_in = inside("gy")

    for k in range(2):
        edge[rows_of(k * reach + LO, n)] = edge_x[rows_of(k * n, n)]
    for i in range(end - begin):
        x = begin + i
        one[rows_of(i * reach + LO, n)] = cell[rows_of(x * span + PAD_LO, n)] + change[rows_of(x * reach + LO, n)]

    def along_x(i):
        at = halo_line(i, n) + LO
        cells = [cell[rows_of(x * span + LO + at)] for x in range(n)]
        fluxes = line_fluxes(cells, [halo_wind_x[rows_of(i * n + x)] for x in range(begin - 1, end + 1)])
        keep = which(i, south_in, north_in)
        stores = [(edge, rows_of(at), fluxes[0]), (edge, rows_of(reach + at), fluxes[-1])]
        for k, value in enumerate(changes(fluxes)):
            x = begin + k
            value = (cells[x] + (value + change[rows_of(x * reach + at)])) * keep
            stores.append((one, rows_of(k * reach + at), value))
        return stores

    each(LINES, LINES, along_x)
    second_y_z(n, width, range(begin, end), begin, one, begin, wind_y, far_wind_y, wind_z, second)


def second_y_z(n, width, layers, first, one, one_first, wind_y, far_wind_y, wind_z, second):
    reach = n + LINES

    def along_y(i):
        x = layers[0] + i
        cells = [one[rows_of((x - one_first) * reach + y)] for y in range(reach)]
        winds = [far_wind_y[rows_of(x * (LINES + 2) + LO)]] + [wind_y[rows_of(x * n + y)] for y in range(n)]
        winds += [far_wind_y[rows_of(x * (LINES + 2) + LO + 1)]]
        return [(second, rows_of((x - first) * n + y), value) for y, value in enumerate(line_change(cells, winds))]

    def along_z(i):
        x = layers[0] + i
        cells = [one[eight((x - one_first) * reach + LO, k)] for k in range(ROWS)]
        winds = [wind_z[eight(x * n, k)] for k in range(ROWS)]
        at = [eight((x - first) * n, k) for k in range(ROWS)]
        return [(second, here, second[here] + value) for here, value in zip(at, level_change(cells, winds, width))]

    each(len(layers), len(layers), along_y)
    each(len(layers), len(layers), along_z)


def x_kernel(n, parts, cell, change, wind_x, edge, second_ref, first_ref, mid, far_wind_x, side, side_wind_y, *scratch):
    far, side_wind_z, side_change = scratch
    width, deep, tiles = groups(parts)
    half = tiles // 2
    west, east = sides("gx", first_ref, second_ref)
    span, reach = n + PAD_LO + PAD_HI, n + LINES

    jobs = []
    for take, wide, near_from, far_from, line in ((west, PAD_LO, LO, 0, 0), (east, PAD_HI, 0, HI, LO)):
        narrow = wide // 2
        side[rows_of(line * n, narrow * n)] = take(rows_of(near_from * n, narrow * n))
        far[rows_of(line * n, narrow * n)] = take(rows_of(far_from * n, narrow * n))
        layers, shift = (range(n - narrow, n), half) if line == 0 else (range(narrow), 0)
        wider = range(n - narrow - 1, n) if line == 0 else range(narrow + 1)

        def winds_of(d, x):
            return take(rows_of(wide * n + d * half + x // deep - shift))

        for i, x in enumerate(wider):
            jobs += [(winds_of(0, x), x, y, far_wind_x, (line + bool(line) + i) * n + y) for y in range(n)]
        for d, out in ((1, side_wind_y), (2, side_wind_z)):
            for i, x in enumerate(layers):
                jobs += [(winds_of(d, x), x, y, out, (line + i) * n + y) for y in range(n)]
    spread(jobs, parts)

    def along_z(i):
        cells = [side[eight(i * n, k)] for k in range(ROWS)]
        winds = [side_wind_z[eight(i * n, k)] for k in range(ROWS)]
        return [(side_change, eight(i * n, k), value) for k, value in enumerate(level_change(cells, winds, width))]

    each(LINES, 2, along_z)

    def along_x(y):
        outer = [far[rows_of(i * n + y)] for i in range(LINES)]
        near = [side[rows_of(i * n + y)] for i in range(LINES)]
        cells = outer[:LO] + near[:LO] + [cell[rows_of(x * span + PAD_LO + y)] for x in range(n)] + near[LO:] + outer[LO:]
        winds = [far_wind_x[rows_of(i * n + y)] for i in range(LINES + 2)]
        winds = winds[: LO + 1] + [wind_x[rows_of(x * n + y)] for x in range(n)] + winds[LO + 1 :]
        stores = []
        for x, value in long_line(cells, winds, edge[rows_of(LO + y)], edge[rows_of(reach + LO + y)], n).items():
            if 0 <= x < n:
                value = value + change[rows_of(x * reach + LO + y)]
            else:
                value = value + side_change[rows_of((x + LO if x < 0 else x + LO - n) * n + y)]
            stores.append((mid, rows_of((x + LO) * n + y), cells[PAD_LO + x] + value))
        return stores

    each(n, 2, along_x)


def main_kernel(n, parts, *refs):
    cell, change, wind_x, wind_y, wind_z, halo_wind_x, far_wind_y, inner, edge, inner_second = refs[:10]
    mid, far_wind_x, side, side_wind_y, second_ref, first_ref, rate_ref, steps_ref = refs[10:18]
    one, *out_refs = refs[18:21]
    corner, corner_wind_x, edge_wind_y, second, fallen = refs[21:]
    deep, tiles = groups(parts)[1:]
    half = tiles // 2
    west, east = sides("gx", first_ref, second_ref)
    span, reach = n + PAD_LO + PAD_HI, n + LINES

    jobs = []
    for take, narrow, line in ((west, LO, 0), (east, HI, LO)):
        at = narrow * LINES
        corner[rows_of(line * LINES, at)] = take(rows_of(0, at))
        below, above = at, at + 1 + half
        layers, shift = (range(n - narrow, n), half) if line == 0 else (range(narrow), 0)
        for y in range(LINES):
            tile = take(rows_of(below if y < LO else above))
            x = layers[-1] if line == 0 else layers[0]
            jobs.append((tile, x, n - LO + y if y < LO else y - LO, corner_wind_x, bool(line) * LINES + y))
        for i, x in enumerate(layers):
            tile = x // deep - shift
            jobs.append((take(rows_of(below + 1 + tile)), x, n - 1, edge_wind_y, 2 * (line + i)))
            jobs.append((take(rows_of(above + 1 + tile)), x, 0, edge_wind_y, 2 * (line + i) + 1))
    spread(jobs, parts)

    west_in, east_in = inside("gx")
    south_in, north_in = inside("gy")
    begin, end = LO, n - HI
    one[rows_of((begin + LO) * reach, (end - begin) * reach)] = inner[...]
    for x in [x for x in range(n) if not begin <= x < end]:
        one[rows_of((x + LO) * reach + LO, n)] = mid[rows_of((x + LO) * n, n)]

    def along_y(i):
        corners = [corner[rows_of(i * LINES + y)] for y in range(LINES)]
        cells = corners[:LO] + [side[rows_of(i * n + y)] for y in range(n)] + corners[LO:]
        winds = [side_wind_y[rows_of(i * n + y)] for y in range(n)]
        winds = [edge_wind_y[rows_of(2 * i)]] + winds + [edge_wind_y[rows_of(2 * i + 1)]]
        line = halo_line(i, n) + LO
        return [
            (one, rows_of(line * reach + LO + y), (mid[rows_of(line * n + y)] + value) * which(i, west_in, east_in))
            for y, value in enumerate(line_change(cells, winds))
        ]

    def along_x(i):
        line = halo_line(i, n) + LO
        near = [corner[rows_of(k * LINES + i)] for k in range(LINES)]
        cells = near[:LO] + [cell[rows_of(x * span + LO + line)] for x in range(n)] + near[LO:]
        winds = [halo_wind_x[rows_of(i * n + x)] for x in range(n)]
        winds = [corner_wind_x[rows_of(i)]] + winds + [corner_wind_x[rows_of(LINES + i)]]
        low = line_fluxes(cells[: LO + begin + 1], winds[: begin + 1]) + [edge[rows_of(line)]]
        high = [edge[rows_of(reach + line)]] + line_fluxes(cells[LO + end - HI :], winds[end + 1 :])
        values = dict(zip(range(begin), changes(low))) | dict(zip(range(end, n), changes(high)))
        stores = []
        for x, value in values.items():
            value = (cells[x + LO] + (value + change[rows_of(x * reach + line)])) * which(i, south_in, north_in)
            stores.append((one, rows_of((x + LO) * reach + line), value))
        return stores

    each(LINES, 2, along_y)
    each(LINES, LINES, along_x)
    fall_layers(
        n, parts, 0, EARLY, one, cell, wind_x, far_wind_x, wind_y, far_wind_y, wind_z, inner_second, rate_ref, steps_ref,
        out_refs, second, fallen,
    )


def late_kernel(
    n, parts, one, cell, wind_x, far_wind_x, wind_y, far_wind_y, wind_z, inner_second, rate_ref, steps_ref, *refs
):
    fall_layers(
        n, parts, EARLY, n, one, cell, wind_x, far_wind_x, wind_y, far_wind_y, wind_z, inner_second, rate_ref, steps_ref,
        refs[:2], *refs[2:],
    )


def fall_layers(
    n, parts, begin, end, one, cell, wind_x, far_wind_x, wind_y, far_wind_y, wind_z, inner_second, rate_ref, steps_ref,
    out_refs, second, fallen,
):
    width = groups(parts)[0]
    span, reach, count = n + PAD_LO + PAD_HI, n + LINES, end - begin
    ready = [x for x in range(LO, n - HI) if begin <= x < end]
    left = [x for x in range(begin, end) if x not in ready]
    if ready:
        second[rows_of((ready[0] - begin) * n, len(ready) * n)] = inner_second[rows_of((ready[0] - LO) * n, len(ready) * n)]

    second_y_z(n, width, left, begin, one, -LO, wind_y, far_wind_y, wind_z, second)

    def along_x(y):
        cells = [one[rows_of(x * reach + LO + y)] for x in range(begin, end + LINES)]
        winds = [wind_x[rows_of(x * n + y)] for x in range(max(begin - 1, 0), min(end + 1, n))]
        if begin == 0:
            winds = [far_wind_x[rows_of(LO * n + y)]] + winds
        if end == n:
            winds = winds + [far_wind_x[rows_of((LO + 1) * n + y)]]
        stores = []
        for i, value in enumerate(line_change(cells, winds)):
            value = cells[i + LO] + (value + second[rows_of(i * n + y)])
            value = 0.5 * cell[rows_of((begin + i) * span + PAD_LO + y)] + 0.5 * value
            stores.append((fallen, rows_of(i * n + y), value))
        return stores

    each(n, 4, along_x)

    bins = LANES // 2 // parts
    ids = lax.axis_index("gz") * bins + lane_ids() % bins
    rates, steps = [
        pick(jnp.broadcast_to(jnp.concatenate([ref[...]] * 2, axis=1), (ROWS, LANES)), ids) for ref in (rate_ref, steps_ref)
    ]

    rain = []
    for some in [range(i, min(i + 3, count)) for i in range(0, count, 3)]:
        columns = [[fallen[eight(i * n, k)] for k in range(ROWS)] for i in some]
        drops = [jnp.zeros((ROWS, LANES), F32) for _ in some]
        for block in range(SUBS // AHEAD):
            columns = [column + [from_above(v, width) for v in column[:AHEAD]] for column in columns]
            for s in range(AHEAD):
                rate = jnp.where(block * AHEAD + s < steps, rates, 0.0)
                for i, column in enumerate(columns):
                    drops[i] = drops[i] + rate * column[0]
                    columns[i] = [v + rate * (u - v) for v, u in zip(column, column[1:])]
        for i, column in zip(some, columns):
            for k in range(ROWS):
                fallen[eight(i * n, k)] = column[k]
        rain += drops

    if parts == 2:
        send_ref, keep_ref = out_refs
        lower = is_even("gz")
        low = lane_ids() < 64
        half = count * n // 2
        for c in range(half):
            a, b = fallen[rows_of(c)], fallen[rows_of(half + c)]
            at = rows_of(c)
            keep_ref[at], send_ref[at] = order(jnp.where(low, a, turn(b, 64)), jnp.where(low, turn(a, 64), b), lower)
        for j in range(0, count, 4):
            four = (rain[j : j + 4] + rain[j:] * 3)[:4]
            value = by_quarter([turn(v, 32 * i) for i, v in enumerate(four)])
            keep_ref[rows_of(half + j // 4)] = value
            send_ref[rows_of(half + j // 4)] = value
    else:
        settled_ref, rain_ref = out_refs
        settled_ref[...] = fallen[...]
        for i in range(count):
            rain_ref[rows_of(i)] = rain[i]


def matrix_kernel(bins, gain_ref, loss_ref, pairs_ref, lost_ref, wide, tall):
    zero = jnp.zeros((bins, LANES - bins), F32)
    shifts = bins // 2

    @pl.loop(0, bins)
    def _(i):
        rows = gain_ref[pl.ds(i * bins, bins)].astype(F32)
        rows = jnp.concatenate([rows, zero], axis=1)
        wide[pl.ds(i * 2 * bins, bins)] = rows
        wide[pl.ds(i * 2 * bins + bins, bins)] = rows
        tall[pl.ds(i * bins, bins)] = rows

        @pl.when(i < shifts)
        def _():
            tall[pl.ds((i + bins) * bins, bins)] = rows

    for d in range(shifts + 1):
        rows = wide[pl.ds(d, bins, stride=2 * bins + 1)]
        if 0 < d < shifts:
            rows = rows + tall[pl.ds(d * bins, bins, stride=bins + 1)]
        pairs_ref[pl.ds(d * LANES, bins)] = rows.astype(jnp.bfloat16)
        pairs_ref[pl.ds(d * LANES + bins, bins)] = pltpu.roll(rows, bins, 1).astype(jnp.bfloat16)
    rows = jnp.concatenate([loss_ref[...].astype(F32), zero], axis=1)
    lost_ref[pl.ds(0, bins)] = rows.astype(jnp.bfloat16)
    lost_ref[pl.ds(bins, bins)] = pltpu.roll(rows, bins, 1).astype(jnp.bfloat16)


def breakup_rows(mass, pairs_ref, lost_ref, products):
    bins = LANES // 2
    count = mass.shape[0]
    lanes = lane_ids()
    rounded = mass.astype(jnp.bfloat16)
    wide = rounded.astype(F32)
    gained = None
    shifts = bins // 2 + 1
    for begin in range(0, shifts, 4):
        end = min(begin + 4, shifts)
        for d in range(begin, end):
            ids = lanes // bins * bins + (lanes + d) % bins
            for r in range(0, count, 2 * ROWS):
                halves = [wide[r + ROWS * k : r + ROWS * (k + 1)] for k in range(2)]
                halves = [v * pick(v, ids) if d else v * v for v in halves]
                both = jnp.concatenate(halves, axis=0).astype(jnp.bfloat16)
                products[pl.ds(r, 2 * ROWS), d * LANES : (d + 1) * LANES] = both
        part = jnp.dot(
            products[pl.ds(0, count), begin * LANES : end * LANES],
            pairs_ref[pl.ds(begin * LANES, (end - begin) * LANES)],
            preferred_element_type=F32,
        )
        gained = part if gained is None else gained + part
    loss = jnp.dot(rounded, lost_ref[...], preferred_element_type=F32)
    return mass + gained - mass * loss


def breakup_layers(n, count, keep_ref, got_ref, pairs_ref, lost_ref, columns, products):
    first = is_even("gz")
    half = count * n // 2
    for c in range(half):
        a, b = order(keep_ref[rows_of(c)], got_ref[rows_of(c)], first)
        columns[rows_of(c)] = by_quarter([a, turn(b, 32), turn(a, 32), turn(b, 64)])
        columns[rows_of(half + c)] = by_quarter([turn(a, -64), turn(b, -32), turn(a, -32), b])
    rain = []
    for i in range(count):
        a, b = order(keep_ref[rows_of(half + i // 4)], got_ref[rows_of(half + i // 4)], first)
        a, b = [jnp.where(first, v[: n // 2], v[n // 2 :])[:, 32 * (i % 4) : 32 * (i % 4) + 32] for v in (a, b)]
        rain.append(jnp.concatenate([a, b], axis=1))
    columns[...] = breakup_rows(columns[...], pairs_ref, lost_ref, products)
    return rain


def lay_out(columns, mass, n, count):
    for x in range(count):
        for y in range(n):
            value = columns[rows_of(x * n + y)]
            mass[x, y, 0:ROWS] = value[:, :64]
            mass[x, y, ROWS : 2 * ROWS] = value[:, 64:]


def breakup_first_kernel(n, keep_ref, got_ref, pairs_ref, lost_ref, mass_ref, rain_ref, columns, products):
    for i, value in enumerate(breakup_layers(n, EARLY, keep_ref, got_ref, pairs_ref, lost_ref, columns, products)):
        rain_ref[i] = value
    lay_out(columns, mass_ref, n, EARLY)


def breakup_last_kernel(
    n, keep_ref, got_ref, pairs_ref, lost_ref, early, early_rain, mass_out, rain_out, columns, products, mass, rain, sems
):
    early_copy = pltpu.make_async_copy(early, mass_out.at[pl.ds(0, EARLY)], sems.at[0])
    early_copy.start()
    late_rain = breakup_layers(n, n - EARLY, keep_ref, got_ref, pairs_ref, lost_ref, columns, products)
    for i in range(EARLY):
        rain[i] = early_rain[i]
    for i, value in enumerate(late_rain):
        rain[EARLY + i] = value
    rain_copy = pltpu.make_async_copy(rain, rain_out, sems.at[2])
    rain_copy.start()
    lay_out(columns, mass, n, n - EARLY)
    late_copy = pltpu.make_async_copy(mass, mass_out.at[pl.ds(EARLY, n - EARLY)], sems.at[1])
    late_copy.start()
    for copy in (early_copy, rain_copy, late_copy):
        copy.wait()


def breakup_plain_kernel(mass_ref, pairs_ref, lost_ref, out_ref, products):
    count = products.shape[0]

    @pl.loop(0, mass_ref.shape[0] // count)
    def _(i):
        start = pl.multiple_of(i * count, count)
        out_ref[pl.ds(start, count)] = breakup_rows(mass_ref[pl.ds(start, count)], pairs_ref, lost_ref, products)


def shape(*dims, dtype=F32):
    return jax.ShapeDtypeStruct(dims, dtype)


def tiles_of(count):
    return shape(count * ROWS, LANES)


def call(kernel, outs, args, scratch=(), micros=1.0, out_place=pltpu.VMEM, copies=0):
    scratch = [pltpu.VMEM(s.shape, s.dtype) for s in scratch]
    if copies:
        scratch.append(pltpu.SemaphoreType.DMA((copies,)))
    return pl.pallas_call(
        kernel,
        out_shape=outs,
        in_specs=[VMEM] * len(args),
        out_specs=jax.tree.map(lambda _: pl.BlockSpec(memory_space=out_place), outs),
        scratch_shapes=scratch,
        compiler_params=pltpu.CompilerParams(vmem_limit_bytes=40 << 20),
        cost_estimate=pl.CostEstimate(
            flops=int(micros * 1.1e9), bytes_accessed=int(micros * 3.6e6), transcendentals=0
        ),
    )(*args)


def swap_neighbours(axis, begin, message):
    axes = ("gx", "gy", "gz")
    sizes = [lax.axis_size(a) for a in axes]
    along, other = (0, 2) if axis == "gx" else (1, 0)

    def partner(place, start, count):
        to = start + ((place - start) ^ 1)
        return to if start <= place and to < count else place

    index = {place: i for i, place in enumerate(itertools.product(*map(range, sizes)))}
    pairs = []
    for place, i in index.items():
        to = list(place)
        to[along] = partner(place[along], begin, sizes[along])
        if to[along] == place[along]:
            to[other] = partner(place[other], 0, sizes[other])
        pairs.append((i, index[tuple(to)]))
    return lax.ppermute(message, axes, pairs)


def per_device(bin_mass, courant, sub_courant, fall_steps, frag_gain, collide):
    nx, ny, nz, bins = bin_mass.shape
    n = nx
    parts = lax.axis_size("gz")
    gz, gy = lax.axis_index("gz"), lax.axis_index("gy")
    width = bins // parts
    tiles = groups(parts)[2]
    winds = 3 * tiles

    pair_rows = (bins // 2 + 1) * LANES
    pairs, lost = call(
        functools.partial(matrix_kernel, bins),
        (shape(pair_rows, LANES, dtype=jnp.bfloat16), shape(LANES, LANES, dtype=jnp.bfloat16)),
        (frag_gain, collide),
        [shape(2 * bins * bins, LANES), shape(3 * bins * bins // 2, LANES)],
        micros=0.02,
    )

    y_message = tiles_of(n * PAD_LO + winds)
    x_message = tiles_of(n * PAD_LO + winds // 2)
    if parts == 2:
        half = tiles_of(n * n // 2)
        send, keep = call(pack_kernel, (half, half), (bin_mass,), micros=0.3)
        got = lax.ppermute(send, "gz", [(0, 1), (1, 0)])
        own_wind = call(wind_kernel, tiles_of(3), (courant, keep), micros=0.1)
        got_wind = lax.ppermute(own_wind, "gz", [(0, 1), (1, 0)])
        block, *messages = call(
            merge_kernel,
            [tiles_of(n * n + winds), y_message, y_message, x_message, x_message],
            (keep, got, own_wind, got_wind, lost),
            micros=0.2,
        )
    else:
        split = bin_mass.reshape(nx, ny, nz // ROWS, ROWS, parts, width).transpose(4, 0, 1, 3, 2, 5)
        split = lax.all_to_all(split, "gz", split_axis=0, concat_axis=0, tiled=True)
        cube = split.transpose(1, 2, 3, 0, 4, 5).reshape(n, n, ROWS, LANES)
        air = courant.reshape(3, nx, ny, nz // ROWS, ROWS).transpose(0, 4, 3, 1, 2) * (1.0 / 12.0)
        air = lax.all_gather(air, "gz").reshape(parts, 3, ROWS, nz // ROWS, tiles, nx // tiles, ny)
        air = air.transpose(1, 4, 2, 0, 3, 5, 6).reshape(3, tiles, ROWS, LANES)
        block = jnp.concatenate([cube.reshape(-1, LANES), air.reshape(-1, LANES)])
        messages = []
        for layers, low_air, high_air, message, even in (
            (cube.transpose(1, 0, 2, 3), air, air, y_message, gy % 2 == 0),
            (cube, air[:, : tiles // 2], air[:, tiles // 2 :], x_message, lax.axis_index("gx") % 2 == 0),
        ):
            up, down = layers[n - PAD_LO :], layers[:PAD_HI]
            if message is y_message:
                up, down = up.transpose(1, 0, 2, 3), down.transpose(1, 0, 2, 3)
            up = jnp.concatenate([up.reshape(-1, LANES), high_air.reshape(-1, LANES)])
            down = jnp.concatenate([down.reshape(-1, LANES), low_air.reshape(-1, LANES)])
            messages += order(up, jnp.pad(down, ((0, up.shape[0] - down.shape[0]), (0, 0))), even)

    from_y = swap_neighbours("gy", 0, messages[0]), swap_neighbours("gy", 1, messages[1])
    from_x = swap_neighbours("gx", 1, messages[3]), swap_neighbours("gx", 0, messages[2])
    wind_x, wind_y, wind_z, own_change, edge_x, edge_y = call(
        functools.partial(own_kernel, n, parts), [tiles_of(n * n)] * 4 + [tiles_of(2 * n)] * 2, (block,), micros=1.6
    )
    message = tiles_of(LO * LINES + 2 + tiles)
    corners = call(functools.partial(corner_kernel, n, parts), (message, message), (*from_y, own_change), micros=0.1)
    corners = swap_neighbours("gx", 1, corners[1]), swap_neighbours("gx", 0, corners[0])
    cell, change, halo_wind_x, far_wind_y = call(
        functools.partial(y_kernel, n, parts),
        [tiles_of(n * (n + PAD_LO + PAD_HI)), tiles_of(n * (n + LINES)), tiles_of(LINES * n), tiles_of(n * (LINES + 2))],
        (block, *from_y, wind_y, own_change, edge_y),
        [tiles_of(LINES * n)] * 2,
        micros=2.0,
    )
    reach, inner = n + LINES, n - LINES
    near = call(
        functools.partial(inner_kernel, n, parts),
        [tiles_of(inner * reach), tiles_of(2 * reach), tiles_of(inner * n)],
        (cell, change, halo_wind_x, wind_y, far_wind_y, wind_z, edge_x),
        micros=0.9,
    )
    mid, far_wind_x, side, side_wind_y = call(
        functools.partial(x_kernel, n, parts),
        [tiles_of(count) for count in (reach * n, (LINES + 2) * n, LINES * n, LINES * n)],
        (cell, change, wind_x, near[1], *from_x),
        [tiles_of(LINES * n)] * 3,
        micros=1.7,
    )
    fall = sub_courant.reshape(1, bins), fall_steps.reshape(1, bins)

    def fallen(count):
        if parts == 2:
            return [tiles_of(n * count // 2 + (count + 3) // 4)] * 2
        return [tiles_of(n * count), tiles_of(count)]

    one, *early = call(
        functools.partial(main_kernel, n, parts),
        [tiles_of(reach * reach)] + fallen(EARLY),
        (
            *(cell, change, wind_x, wind_y, wind_z, halo_wind_x, far_wind_y, *near),
            *(mid, far_wind_x, side, side_wind_y, *corners, *fall),
        ),
        [tiles_of(count) for count in (LINES * LINES, 2 * LINES, 2 * LINES, n * EARLY, n * EARLY)],
        micros=2.6,
    )
    if parts == 2:
        early_got = lax.ppermute(early[0], "gz", [(0, 1), (1, 0)])
    late = call(
        functools.partial(late_kernel, n, parts),
        fallen(n - EARLY),
        (one, cell, wind_x, far_wind_x, wind_y, far_wind_y, wind_z, near[2], *fall),
        [tiles_of(n * (n - EARLY))] * 2,
        micros=0.7,
    )

    def products(count):
        return shape(n * count * ROWS, pair_rows, dtype=jnp.bfloat16)

    if parts == 2:
        late_got = lax.ppermute(late[0], "gz", [(0, 1), (1, 0)])
        early = call(
            functools.partial(breakup_first_kernel, n),
            [shape(EARLY, ny, nz, bins), shape(EARLY, ny // parts, bins)],
            (early[1], early_got, pairs, lost),
            [tiles_of(n * EARLY), products(EARLY)],
            micros=1.8,
        )
        outs = [shape(nx, ny, nz, bins), shape(nx, ny // parts, bins)]
        return tuple(
            call(
                functools.partial(breakup_last_kernel, n),
                outs,
                (late[1], late_got, pairs, lost, *early),
                [tiles_of(n * (n - EARLY)), products(n - EARLY), shape(n - EARLY, ny, nz, bins), outs[1]],
                micros=1.2,
                out_place=pl.ANY,
                copies=3,
            )
        )

    settled, rain = [jnp.concatenate(halves) for halves in zip(early, late)]
    rain = rain.reshape(nx, ny, LANES)[:, :, :width]
    rain = lax.all_to_all(rain, "gz", split_axis=1, concat_axis=2, tiled=True)
    settled = settled.reshape(nx, ny, ROWS, parts, nz // ROWS, width).transpose(3, 0, 1, 4, 2, 5)
    settled = lax.all_to_all(settled, "gz", split_axis=0, concat_axis=0, tiled=True)
    settled = settled.transpose(1, 2, 3, 4, 0, 5).reshape(nx * ny, nz // ROWS, ROWS, bins)
    paired = settled.transpose(0, 2, 1, 3).reshape(-1, LANES)
    updated = call(breakup_plain_kernel, tiles_of(n * n), (paired, pairs, lost), [products(n // 2)], micros=3.0)
    updated = updated.reshape(nx, ny, ROWS, nz // ROWS, bins).transpose(0, 1, 3, 2, 4).reshape(nx, ny, nz, bins)
    return updated, rain


def solution(mesh):
    in_specs = (P("gx", "gy", "gz", None), P(None, "gx", "gy", "gz"), P(), P(), P(), P())
    out_specs = (P("gx", "gy", "gz", None), P("gx", ("gy", "gz"), None))
    return jax.shard_map(per_device, mesh=mesh, in_specs=in_specs, out_specs=out_specs, check_vma=False)
```

```python
import functools
import itertools

import jax
import jax.numpy as jnp
from jax import lax
from jax.experimental import pallas as pl
from jax.experimental.pallas import tpu as pltpu
from jax.sharding import PartitionSpec as P

SUBS = 24
EPS = 1e-06
LO, HI = 3, 2
PAD_LO, PAD_HI = 2 * LO, 2 * HI
LINES = LO + HI
ROWS, LANES = 8, 128
AHEAD = 4
EARLY = 5
F32 = jnp.float32
VMEM = pl.BlockSpec(memory_space=pltpu.VMEM)


def lane_ids():
    return lax.broadcasted_iota(jnp.int32, (ROWS, LANES), 1)


def pick(tile, ids):
    return jnp.take_along_axis(tile, ids, axis=1, mode="promise_in_bounds")


def turn(tile, lanes):
    lanes %= LANES
    return pltpu.roll(tile, lanes, 1) if lanes else tile


def rows_of(first, count=1):
    return pl.ds(first * ROWS, count * ROWS)


def eight(first, level, step=1):
    return pl.ds(first * ROWS + level, ROWS, stride=step * ROWS)


def order(a, b, straight):
    return jnp.where(straight, a, b), jnp.where(straight, b, a)


def is_even(axis):
    return lax.axis_index(axis) % 2 == 0


def by_quarter(parts):
    quarter = lane_ids() // (LANES // 4)
    return jnp.where(quarter < 2, jnp.where(quarter == 0, parts[0], parts[1]), jnp.where(quarter == 2, parts[2], parts[3]))


def groups(parts):
    width = LANES // (2 * parts)
    return width, width // ROWS, ROWS * ROWS // width


def spread(jobs, parts):
    width, deep, _ = groups(parts)
    place = lane_ids() % width
    rows = [[], []]
    for tile, x, y, _, _ in jobs:
        top = tile.astype(jnp.bfloat16).astype(F32)
        here = place == x % deep * ROWS + y
        for out, term in zip(rows, (top, tile - top)):
            out.append(jnp.where(here, term, 0.0))
    terms = jnp.concatenate([jnp.concatenate(r, axis=0).astype(jnp.bfloat16) for r in rows], axis=1)
    source, target = [lax.broadcasted_iota(jnp.int32, (2 * LANES, LANES), k) for k in range(2)]
    same = jnp.where(source % LANES // width == target // width, 1.0, 0.0).astype(jnp.bfloat16)
    out = jnp.dot(terms, same, preferred_element_type=F32)
    for k, (_, _, _, ref, at) in enumerate(jobs):
        ref[rows_of(at)] = out[k * ROWS : (k + 1) * ROWS]


def each(count, together, body):
    def some(places):
        stores = [store for i in places for store in body(i)]
        for ref, at, value in stores:
            ref[at] = value

    whole = count // together

    @pl.loop(0, whole)
    def _(i):
        some([i * together + k for k in range(together)])

    if count % together:
        some(range(whole * together, count))


def halo_line(i, n):
    if isinstance(i, int):
        return i - LO + (n if i >= LO else 0)
    return jnp.where(i < LO, i - LO, i - LO + n)


def line_change(cells, winds):
    return changes(line_fluxes(cells, winds))


def changes(fluxes):
    return [a - b for a, b in zip(fluxes, fluxes[1:])]


def long_line(cells, winds, low_edge, high_edge, n):
    begin, end = LO, n - HI
    low = line_fluxes(cells[: PAD_LO + begin + 1], winds[: LO + 1 + begin]) + [low_edge]
    high = [high_edge] + line_fluxes(cells[PAD_LO + end - HI :], winds[LO + 1 + end :])
    return dict(zip(range(-LO, begin), changes(low))) | dict(zip(range(end, n + HI), changes(high)))


def line_fluxes(cells, winds):
    first = [b - a for a, b in zip(cells, cells[1:])]
    twice = [d + d for d in first]
    second = [b - a for a, b in zip(first, first[1:])]
    third = [a - b for a, b in zip(second, second[1:])]
    third_twice = [t + t for t in third]
    curved = [(13.0 / 3.0) * (c * c) + 4.0 * EPS for c in second]
    fluxes = []
    for j in range(len(cells) - 4):
        left = twice[j + 1] + second[j]
        mid = first[j + 1] + first[j + 2]
        right = twice[j + 2] - second[j + 2]
        w0 = pl.reciprocal(curved[j] + left * left, approx=True)
        w1 = pl.reciprocal(curved[j + 1] + mid * mid, approx=True)
        w2 = pl.reciprocal(curved[j + 2] + right * right, approx=True)
        w0 = w0 * w0
        w1 = 6.0 * (w1 * w1)
        w2 = 3.0 * (w2 * w2)
        top = w0 * third_twice[j] + w2 * third[j + 1]
        inverse = pl.reciprocal(w0 + w1 + w2, approx=True)
        estimate = 6.0 * cells[j + 2] + (first[j + 1] + twice[j + 2]) + top * inverse
        fluxes.append((winds[j] + winds[j + 1]) * estimate)
    return fluxes


def from_below(value, width):
    return jnp.where(lane_ids() < width, 0.0, turn(value, width))


def from_above(value, width):
    return jnp.where(lane_ids() >= LANES - width, 0.0, turn(value, -width))


def level_change(cells, winds, width):
    long_cells = [from_below(v, width) for v in cells[ROWS - LO :]] + cells + [from_above(v, width) for v in cells[:HI]]
    long_winds = [from_below(winds[-1], width)] + winds + [from_above(winds[0], width)]
    return line_change(long_cells, long_winds)


def pack_kernel(mass_ref, send_ref, keep_ref):
    lower = is_even("gz")
    n = mass_ref.shape[0]
    zero = jnp.zeros((ROWS, LANES // 2), F32)
    for x in range(n // 2):
        for y in range(n):
            tiles = [
                jnp.concatenate([mass_ref[xx, y, z : z + ROWS], zero], axis=1) for xx in (x, x + n // 2) for z in (0, ROWS)
            ]
            low = by_quarter([turn(v, 32 * k) for k, v in enumerate(tiles)])
            high = by_quarter([turn(v, 32 * k - 32) for k, v in enumerate(tiles)])
            at = rows_of(x * n + y)
            keep_ref[at], send_ref[at] = order(low, high, lower)


def wind_kernel(wind_ref, keep_ref, out_ref):
    del keep_ref
    n = wind_ref.shape[1]
    for d in range(3):
        levels = wind_ref[d].reshape(n * n, 2 * ROWS).T * (1.0 / 12.0)
        out_ref[rows_of(d)] = jnp.concatenate([levels[:ROWS], levels[ROWS:]], axis=1)


def sides(axis, first_ref, second_ref):
    even, place = is_even(axis), lax.axis_index(axis)
    inner_low, inner_high = place > 0, place < lax.axis_size(axis) - 1

    def below(at):
        return jnp.where(inner_low, jnp.where(even, second_ref[at], first_ref[at]), 0.0)

    def above(at):
        return jnp.where(inner_high, jnp.where(even, first_ref[at], second_ref[at]), 0.0)

    return below, above


def by_parity(axis, body):
    even = is_even(axis)
    pl.when(even)(lambda: body(0, 1))
    pl.when(jnp.logical_not(even))(lambda: body(1, 0))


def merge_kernel(keep_ref, got_ref, own_wind_ref, got_wind_ref, lost_ref, block_ref, y_first, y_second, x_first, x_second):
    del lost_ref
    n = 8
    lower = is_even("gz")
    low = lane_ids() < 64
    for x in range(n // 2):
        for y in range(n):
            at = rows_of(x * n + y)
            a, b = order(keep_ref[at], got_ref[at], lower)
            block_ref[at] = jnp.where(low, a, turn(b, 64))
            block_ref[rows_of((x + n // 2) * n + y)] = jnp.where(low, turn(a, 64), b)
    for d in range(3):
        a, b = order(own_wind_ref[rows_of(d)], got_wind_ref[rows_of(d)], lower)
        block_ref[rows_of(n * n + 2 * d)] = by_quarter([a, turn(a, -32), turn(b, 64), turn(b, 32)])
        block_ref[rows_of(n * n + 2 * d + 1)] = by_quarter([turn(a, -32), turn(a, -64), turn(b, 32), b])

    def along_y(up, down):
        for ref, start, wide in (((y_first, y_second)[up], n - PAD_LO, PAD_LO), ((y_first, y_second)[down], 0, PAD_HI)):
            for x in range(n):
                ref[rows_of(x * wide, wide)] = block_ref[rows_of(x * n + start, wide)]
            ref[rows_of(n * wide, 6)] = block_ref[rows_of(n * n, 6)]

    def along_x(up, down):
        for ref, start, wide, part in (((x_first, x_second)[up], n - PAD_LO, PAD_LO, 1), ((x_first, x_second)[down], 0, PAD_HI, 0)):
            ref[rows_of(0, wide * n)] = block_ref[rows_of(start * n, wide * n)]
            for d in range(3):
                ref[rows_of(wide * n + d)] = block_ref[rows_of(n * n + 2 * d + part)]

    by_parity("gy", along_y)
    by_parity("gx", along_x)


def corner_kernel(n, parts, first_ref, second_ref, own_change, *messages):
    del own_change
    tiles = groups(parts)[2]
    half = tiles // 2
    below, above = sides("gy", first_ref, second_ref)

    def body(up, down):
        for ref, start, narrow, part in ((messages[up], n - LO, LO, half), (messages[down], 0, HI, 0)):
            at = 0
            for x in range(start, start + narrow):
                ref[rows_of(at, LO)] = below(rows_of(x * PAD_LO + PAD_LO - LO, LO))
                ref[rows_of(at + LO, HI)] = above(rows_of(x * PAD_HI, HI))
                at += LINES
            for side, base in ((below, n * PAD_LO), (above, n * PAD_HI)):
                ref[rows_of(at)] = side(rows_of(base + (tiles - 1 if part else 0)))
                ref[rows_of(at + 1, half)] = side(rows_of(base + tiles + part, half))
                at += 1 + half

    by_parity("gx", body)


def own_kernel(n, parts, block_ref, wind_x, wind_y, wind_z, change, edge_x, edge_y):
    width, deep, tiles = groups(parts)
    for d, out in enumerate((wind_x, wind_y, wind_z)):
        jobs = []
        for x in range(n):
            tile = block_ref[rows_of(n * n + d * tiles + x // deep)]
            jobs += [(tile, x, y, out, x * n + y) for y in range(n)]
        spread(jobs, parts)

    def along_z(x):
        cells = [block_ref[eight(x * n, k)] for k in range(ROWS)]
        winds = [wind_z[eight(x * n, k)] for k in range(ROWS)]
        return [(change, eight(x * n, k), value) for k, value in enumerate(level_change(cells, winds, width))]

    each(n, 2, along_z)
    begin, end = LO, n - HI
    for wind, edge, place in ((wind_x, edge_x, lambda i, k: k * n + i), (wind_y, edge_y, lambda i, k: i * n + k)):

        def along(i):
            cells = [block_ref[rows_of(place(i, k))] for k in range(n)]
            fluxes = line_fluxes(cells, [wind[rows_of(place(i, k))] for k in range(begin - 1, end + 1)])
            at = [rows_of(place(i, k)) for k in range(begin, end)]
            stores = [(change, here, change[here] + value) for here, value in zip(at, changes(fluxes))]
            return stores + [(edge, rows_of(i), fluxes[0]), (edge, rows_of(n + i), fluxes[-1])]

        each(n, 4, along)


def y_kernel(n, parts, block_ref, first_ref, second_ref, wind_y, own_change, edge_y, *refs):
    width, deep, tiles = groups(parts)
    cell, change, wind_x, far_y, wind_z, halo_change = refs
    below, above = sides("gy", first_ref, second_ref)
    span, reach = n + PAD_LO + PAD_HI, n + LINES

    for x in range(n):
        cell[rows_of(x * span, PAD_LO)] = below(rows_of(x * PAD_LO, PAD_LO))
        cell[rows_of(x * span + PAD_LO, n)] = block_ref[rows_of(x * n, n)]
        cell[rows_of(x * span + PAD_LO + n, PAD_HI)] = above(rows_of(x * PAD_HI, PAD_HI))
    jobs = []
    for d in range(3):
        for t in range(tiles):
            low, high = below(rows_of(n * PAD_LO + d * tiles + t)), above(rows_of(n * PAD_HI + d * tiles + t))
            for x in range(t * deep, (t + 1) * deep):
                if d == 1:
                    jobs += [(low, x, n - LO - 1 + y, far_y, x * (LINES + 2) + y) for y in range(LO + 1)]
                    jobs += [(high, x, y, far_y, x * (LINES + 2) + LO + 1 + y) for y in range(HI + 1)]
                else:
                    out = wind_z if d else wind_x
                    jobs += [(low, x, n - LO + y, out, y * n + x) for y in range(LO)]
                    jobs += [(high, x, y, out, (LO + y) * n + x) for y in range(HI)]
    spread(jobs, parts)

    def along_z(i):
        first = halo_line(i, n) + PAD_LO
        cells = [cell[eight(first, k, span)] for k in range(ROWS)]
        winds = [wind_z[eight(i * n, k)] for k in range(ROWS)]
        return [(halo_change, eight(i * n, k), value) for k, value in enumerate(level_change(cells, winds, width))]

    each(LINES, 2, along_z)

    def along_y(x):
        cells = [cell[rows_of(x * span + y)] for y in range(span)]
        far = [far_y[rows_of(x * (LINES + 2) + y)] for y in range(LINES + 2)]
        winds = far[: LO + 1] + [wind_y[rows_of(x * n + y)] for y in range(n)] + far[LO + 1 :]
        stores = []
        for y, value in long_line(cells, winds, edge_y[rows_of(x)], edge_y[rows_of(n + x)], n).items():
            if 0 <= y < n:
                value = value + own_change[rows_of(x * n + y)]
            else:
                value = value + halo_change[rows_of((y + LO if y < 0 else y + LO - n) * n + x)]
            stores.append((change, rows_of(x * reach + y + LO), value))
        for y in range(LO, n - HI):
            stores.append((change, rows_of(x * reach + y + LO), own_change[rows_of(x * n + y)]))
        return stores

    each(n, 2, along_y)


def which(i, lower, upper):
    if isinstance(i, int):
        return lower if i < LO else upper
    return jnp.where(i < LO, lower, upper)


def inside(axis):
    place = lax.axis_index(axis)
    return [jnp.where(ok, 1.0, 0.0) for ok in (place > 0, place < lax.axis_size(axis) - 1)]


def inner_kernel(n, parts, cell, change, halo_wind_x, wind_y, far_wind_y, wind_z, edge_x, one, edge, second):
    width = groups(parts)[0]
    span, reach = n + PAD_LO + PAD_HI, n + LINES
    begin, end = LO, n - HI
    south_in, north_in = inside("gy")

    for k in range(2):
        edge[rows_of(k * reach + LO, n)] = edge_x[rows_of(k * n, n)]
    for i in range(end - begin):
        x = begin + i
        one[rows_of(i * reach + LO, n)] = cell[rows_of(x * span + PAD_LO, n)] + change[rows_of(x * reach + LO, n)]

    def along_x(i):
        at = halo_line(i, n) + LO
        cells = [cell[rows_of(x * span + LO + at)] for x in range(n)]
        fluxes = line_fluxes(cells, [halo_wind_x[rows_of(i * n + x)] for x in range(begin - 1, end + 1)])
        keep = which(i, south_in, north_in)
        stores = [(edge, rows_of(at), fluxes[0]), (edge, rows_of(reach + at), fluxes[-1])]
        for k, value in enumerate(changes(fluxes)):
            x = begin + k
            value = (cells[x] + (value + change[rows_of(x * reach + at)])) * keep
            stores.append((one, rows_of(k * reach + at), value))
        return stores

    each(LINES, LINES, along_x)
    second_y_z(n, width, range(begin, end), begin, one, begin, wind_y, far_wind_y, wind_z, second)


def second_y_z(n, width, layers, first, one, one_first, wind_y, far_wind_y, wind_z, second):
    reach = n + LINES

    def along_y(i):
        x = layers[0] + i
        cells = [one[rows_of((x - one_first) * reach + y)] for y in range(reach)]
        winds = [far_wind_y[rows_of(x * (LINES + 2) + LO)]] + [wind_y[rows_of(x * n + y)] for y in range(n)]
        winds += [far_wind_y[rows_of(x * (LINES + 2) + LO + 1)]]
        return [(second, rows_of((x - first) * n + y), value) for y, value in enumerate(line_change(cells, winds))]

    def along_z(i):
        x = layers[0] + i
        cells = [one[eight((x - one_first) * reach + LO, k)] for k in range(ROWS)]
        winds = [wind_z[eight(x * n, k)] for k in range(ROWS)]
        at = [eight((x - first) * n, k) for k in range(ROWS)]
        return [(second, here, second[here] + value) for here, value in zip(at, level_change(cells, winds, width))]

    each(len(layers), len(layers), along_y)
    each(len(layers), len(layers), along_z)


def x_kernel(n, parts, cell, change, wind_x, edge, second_ref, first_ref, mid, far_wind_x, side, side_wind_y, *scratch):
    far, side_wind_z, side_change = scratch
    width, deep, tiles = groups(parts)
    half = tiles // 2
    west, east = sides("gx", first_ref, second_ref)
    span, reach = n + PAD_LO + PAD_HI, n + LINES

    jobs = []
    for take, wide, near_from, far_from, line in ((west, PAD_LO, LO, 0, 0), (east, PAD_HI, 0, HI, LO)):
        narrow = wide // 2
        side[rows_of(line * n, narrow * n)] = take(rows_of(near_from * n, narrow * n))
        far[rows_of(line * n, narrow * n)] = take(rows_of(far_from * n, narrow * n))
        layers, shift = (range(n - narrow, n), half) if line == 0 else (range(narrow), 0)
        wider = range(n - narrow - 1, n) if line == 0 else range(narrow + 1)

        def winds_of(d, x):
            return take(rows_of(wide * n + d * half + x // deep - shift))

        for i, x in enumerate(wider):
            jobs += [(winds_of(0, x), x, y, far_wind_x, (line + bool(line) + i) * n + y) for y in range(n)]
        for d, out in ((1, side_wind_y), (2, side_wind_z)):
            for i, x in enumerate(layers):
                jobs += [(winds_of(d, x), x, y, out, (line + i) * n + y) for y in range(n)]
    spread(jobs, parts)

    def along_z(i):
        cells = [side[eight(i * n, k)] for k in range(ROWS)]
        winds = [side_wind_z[eight(i * n, k)] for k in range(ROWS)]
        return [(side_change, eight(i * n, k), value) for k, value in enumerate(level_change(cells, winds, width))]

    each(LINES, 2, along_z)

    def along_x(y):
        outer = [far[rows_of(i * n + y)] for i in range(LINES)]
        near = [side[rows_of(i * n + y)] for i in range(LINES)]
        cells = outer[:LO] + near[:LO] + [cell[rows_of(x * span + PAD_LO + y)] for x in range(n)] + near[LO:] + outer[LO:]
        winds = [far_wind_x[rows_of(i * n + y)] for i in range(LINES + 2)]
        winds = winds[: LO + 1] + [wind_x[rows_of(x * n + y)] for x in range(n)] + winds[LO + 1 :]
        stores = []
        for x, value in long_line(cells, winds, edge[rows_of(LO + y)], edge[rows_of(reach + LO + y)], n).items():
            if 0 <= x < n:
                value = value + change[rows_of(x * reach + LO + y)]
            else:
                value = value + side_change[rows_of((x + LO if x < 0 else x + LO - n) * n + y)]
            stores.append((mid, rows_of((x + LO) * n + y), cells[PAD_LO + x] + value))
        return stores

    each(n, 2, along_x)


def main_kernel(n, parts, *refs):
    cell, change, wind_x, wind_y, wind_z, halo_wind_x, far_wind_y, inner, edge, inner_second = refs[:10]
    mid, far_wind_x, side, side_wind_y, second_ref, first_ref, rate_ref, steps_ref = refs[10:18]
    one, *out_refs = refs[18:21]
    corner, corner_wind_x, edge_wind_y, second, fallen = refs[21:]
    deep, tiles = groups(parts)[1:]
    half = tiles // 2
    west, east = sides("gx", first_ref, second_ref)
    span, reach = n + PAD_LO + PAD_HI, n + LINES

    jobs = []
    for take, narrow, line in ((west, LO, 0), (east, HI, LO)):
        at = narrow * LINES
        corner[rows_of(line * LINES, at)] = take(rows_of(0, at))
        below, above = at, at + 1 + half
        layers, shift = (range(n - narrow, n), half) if line == 0 else (range(narrow), 0)
        for y in range(LINES):
            tile = take(rows_of(below if y < LO else above))
            x = layers[-1] if line == 0 else layers[0]
            jobs.append((tile, x, n - LO + y if y < LO else y - LO, corner_wind_x, bool(line) * LINES + y))
        for i, x in enumerate(layers):
            tile = x // deep - shift
            jobs.append((take(rows_of(below + 1 + tile)), x, n - 1, edge_wind_y, 2 * (line + i)))
            jobs.append((take(rows_of(above + 1 + tile)), x, 0, edge_wind_y, 2 * (line + i) + 1))
    spread(jobs, parts)

    west_in, east_in = inside("gx")
    south_in, north_in = inside("gy")
    begin, end = LO, n - HI
    one[rows_of((begin + LO) * reach, (end - begin) * reach)] = inner[...]
    for x in [x for x in range(n) if not begin <= x < end]:
        one[rows_of((x + LO) * reach + LO, n)] = mid[rows_of((x + LO) * n, n)]

    def along_y(i):
        corners = [corner[rows_of(i * LINES + y)] for y in range(LINES)]
        cells = corners[:LO] + [side[rows_of(i * n + y)] for y in range(n)] + corners[LO:]
        winds = [side_wind_y[rows_of(i * n + y)] for y in range(n)]
        winds = [edge_wind_y[rows_of(2 * i)]] + winds + [edge_wind_y[rows_of(2 * i + 1)]]
        line = halo_line(i, n) + LO
        return [
            (one, rows_of(line * reach + LO + y), (mid[rows_of(line * n + y)] + value) * which(i, west_in, east_in))
            for y, value in enumerate(line_change(cells, winds))
        ]

    def along_x(i):
        line = halo_line(i, n) + LO
        near = [corner[rows_of(k * LINES + i)] for k in range(LINES)]
        cells = near[:LO] + [cell[rows_of(x * span + LO + line)] for x in range(n)] + near[LO:]
        winds = [halo_wind_x[rows_of(i * n + x)] for x in range(n)]
        winds = [corner_wind_x[rows_of(i)]] + winds + [corner_wind_x[rows_of(LINES + i)]]
        low = line_fluxes(cells[: LO + begin + 1], winds[: begin + 1]) + [edge[rows_of(line)]]
        high = [edge[rows_of(reach + line)]] + line_fluxes(cells[LO + end - HI :], winds[end + 1 :])
        values = dict(zip(range(begin), changes(low))) | dict(zip(range(end, n), changes(high)))
        stores = []
        for x, value in values.items():
            value = (cells[x + LO] + (value + change[rows_of(x * reach + line)])) * which(i, south_in, north_in)
            stores.append((one, rows_of((x + LO) * reach + line), value))
        return stores

    each(LINES, 2, along_y)
    each(LINES, LINES, along_x)
    fall_layers(
        n, parts, 0, EARLY, one, cell, wind_x, far_wind_x, wind_y, far_wind_y, wind_z, inner_second, rate_ref, steps_ref,
        out_refs, second, fallen,
    )


def late_kernel(
    n, parts, one, cell, wind_x, far_wind_x, wind_y, far_wind_y, wind_z, inner_second, rate_ref, steps_ref, *refs
):
    fall_layers(
        n, parts, EARLY, n, one, cell, wind_x, far_wind_x, wind_y, far_wind_y, wind_z, inner_second, rate_ref, steps_ref,
        refs[:2], *refs[2:],
    )


def fall_layers(
    n, parts, begin, end, one, cell, wind_x, far_wind_x, wind_y, far_wind_y, wind_z, inner_second, rate_ref, steps_ref,
    out_refs, second, fallen,
):
    width = groups(parts)[0]
    span, reach, count = n + PAD_LO + PAD_HI, n + LINES, end - begin
    ready = [x for x in range(LO, n - HI) if begin <= x < end]
    left = [x for x in range(begin, end) if x not in ready]
    if ready:
        second[rows_of((ready[0] - begin) * n, len(ready) * n)] = inner_second[rows_of((ready[0] - LO) * n, len(ready) * n)]

    second_y_z(n, width, left, begin, one, -LO, wind_y, far_wind_y, wind_z, second)

    def along_x(y):
        cells = [one[rows_of(x * reach + LO + y)] for x in range(begin, end + LINES)]
        winds = [wind_x[rows_of(x * n + y)] for x in range(max(begin - 1, 0), min(end + 1, n))]
        if begin == 0:
            winds = [far_wind_x[rows_of(LO * n + y)]] + winds
        if end == n:
            winds = winds + [far_wind_x[rows_of((LO + 1) * n + y)]]
        stores = []
        for i, value in enumerate(line_change(cells, winds)):
            value = cells[i + LO] + (value + second[rows_of(i * n + y)])
            value = 0.5 * cell[rows_of((begin + i) * span + PAD_LO + y)] + 0.5 * value
            stores.append((fallen, rows_of(i * n + y), value))
        return stores

    each(n, 4, along_x)

    bins = LANES // 2 // parts
    ids = lax.axis_index("gz") * bins + lane_ids() % bins
    rates, steps = [
        pick(jnp.broadcast_to(jnp.concatenate([ref[...]] * 2, axis=1), (ROWS, LANES)), ids) for ref in (rate_ref, steps_ref)
    ]

    rain = []
    for some in [range(i, min(i + 3, count)) for i in range(0, count, 3)]:
        columns = [[fallen[eight(i * n, k)] for k in range(ROWS)] for i in some]
        drops = [jnp.zeros((ROWS, LANES), F32) for _ in some]
        for block in range(SUBS // AHEAD):
            columns = [column + [from_above(v, width) for v in column[:AHEAD]] for column in columns]
            for s in range(AHEAD):
                rate = jnp.where(block * AHEAD + s < steps, rates, 0.0)
                for i, column in enumerate(columns):
                    drops[i] = drops[i] + rate * column[0]
                    columns[i] = [v + rate * (u - v) for v, u in zip(column, column[1:])]
        for i, column in zip(some, columns):
            for k in range(ROWS):
                fallen[eight(i * n, k)] = column[k]
        rain += drops

    if parts == 2:
        send_ref, keep_ref = out_refs
        lower = is_even("gz")
        low = lane_ids() < 64
        half = count * n // 2
        for c in range(half):
            a, b = fallen[rows_of(c)], fallen[rows_of(half + c)]
            at = rows_of(c)
            keep_ref[at], send_ref[at] = order(jnp.where(low, a, turn(b, 64)), jnp.where(low, turn(a, 64), b), lower)
        for j in range(0, count, 4):
            four = (rain[j : j + 4] + rain[j:] * 3)[:4]
            value = by_quarter([turn(v, 32 * i) for i, v in enumerate(four)])
            keep_ref[rows_of(half + j // 4)] = value
            send_ref[rows_of(half + j // 4)] = value
    else:
        settled_ref, rain_ref = out_refs
        settled_ref[...] = fallen[...]
        for i in range(count):
            rain_ref[rows_of(i)] = rain[i]


def matrix_kernel(bins, gain_ref, loss_ref, pairs_ref, lost_ref, wide, tall):
    zero = jnp.zeros((bins, LANES - bins), F32)
    shifts = bins // 2

    @pl.loop(0, bins)
    def _(i):
        rows = gain_ref[pl.ds(i * bins, bins)].astype(F32)
        rows = jnp.concatenate([rows, zero], axis=1)
        wide[pl.ds(i * 2 * bins, bins)] = rows
        wide[pl.ds(i * 2 * bins + bins, bins)] = rows
        tall[pl.ds(i * bins, bins)] = rows

        @pl.when(i < shifts)
        def _():
            tall[pl.ds((i + bins) * bins, bins)] = rows

    for d in range(shifts + 1):
        rows = wide[pl.ds(d, bins, stride=2 * bins + 1)]
        if 0 < d < shifts:
            rows = rows + tall[pl.ds(d * bins, bins, stride=bins + 1)]
        pairs_ref[pl.ds(d * LANES, bins)] = rows.astype(jnp.bfloat16)
        pairs_ref[pl.ds(d * LANES + bins, bins)] = pltpu.roll(rows, bins, 1).astype(jnp.bfloat16)
    rows = jnp.concatenate([loss_ref[...].astype(F32), zero], axis=1)
    lost_ref[pl.ds(0, bins)] = rows.astype(jnp.bfloat16)
    lost_ref[pl.ds(bins, bins)] = pltpu.roll(rows, bins, 1).astype(jnp.bfloat16)


def breakup_rows(mass, pairs_ref, lost_ref, products):
    bins = LANES // 2
    count = mass.shape[0]
    rounded = mass.astype(jnp.bfloat16)
    tiles = [rounded[r : r + 2 * ROWS] for r in range(0, count, 2 * ROWS)]
    place = lax.broadcasted_iota(jnp.int32, (2 * ROWS, LANES), 1) % bins
    gained = None
    shifts = bins // 2 + 1
    for begin in range(0, shifts, 4):
        end = min(begin + 4, shifts)
        for d in range(begin, end):
            near = jnp.where(place < bins - d, 1.0, 0.0).astype(jnp.bfloat16) > 0
            for k, tile in enumerate(tiles):
                other = tile
                if d:
                    other = jnp.where(near, pltpu.roll(tile, LANES - d, 1), pltpu.roll(tile, bins - d, 1))
                products[pl.ds(2 * ROWS * k, 2 * ROWS), d * LANES : (d + 1) * LANES] = tile * other
        part = jnp.dot(
            products[pl.ds(0, count), begin * LANES : end * LANES],
            pairs_ref[pl.ds(begin * LANES, (end - begin) * LANES)],
            preferred_element_type=F32,
        )
        gained = part if gained is None else gained + part
    loss = jnp.dot(rounded, lost_ref[...], preferred_element_type=F32)
    return mass + gained - mass * loss


def breakup_layers(n, count, keep_ref, got_ref, pairs_ref, lost_ref, columns, products):
    first = is_even("gz")
    half = count * n // 2
    for c in range(half):
        a, b = order(keep_ref[rows_of(c)], got_ref[rows_of(c)], first)
        columns[rows_of(c)] = by_quarter([a, turn(b, 32), turn(a, 32), turn(b, 64)])
        columns[rows_of(half + c)] = by_quarter([turn(a, -64), turn(b, -32), turn(a, -32), b])
    rain = []
    for i in range(count):
        a, b = order(keep_ref[rows_of(half + i // 4)], got_ref[rows_of(half + i // 4)], first)
        a, b = [jnp.where(first, v[: n // 2], v[n // 2 :])[:, 32 * (i % 4) : 32 * (i % 4) + 32] for v in (a, b)]
        rain.append(jnp.concatenate([a, b], axis=1))
    columns[...] = breakup_rows(columns[...], pairs_ref, lost_ref, products)
    return rain


def lay_out(columns, mass, n, count):
    for x in range(count):
        for y in range(n):
            value = columns[rows_of(x * n + y)]
            mass[x, y, 0:ROWS] = value[:, :64]
            mass[x, y, ROWS : 2 * ROWS] = value[:, 64:]


def breakup_first_kernel(n, keep_ref, got_ref, pairs_ref, lost_ref, mass_ref, rain_ref, columns, products):
    for i, value in enumerate(breakup_layers(n, EARLY, keep_ref, got_ref, pairs_ref, lost_ref, columns, products)):
        rain_ref[i] = value
    lay_out(columns, mass_ref, n, EARLY)


def breakup_last_kernel(
    n, keep_ref, got_ref, pairs_ref, lost_ref, early, early_rain, mass_out, rain_out, columns, products, mass, rain, sems
):
    early_copy = pltpu.make_async_copy(early, mass_out.at[pl.ds(0, EARLY)], sems.at[0])
    early_copy.start()
    late_rain = breakup_layers(n, n - EARLY, keep_ref, got_ref, pairs_ref, lost_ref, columns, products)
    for i in range(EARLY):
        rain[i] = early_rain[i]
    for i, value in enumerate(late_rain):
        rain[EARLY + i] = value
    rain_copy = pltpu.make_async_copy(rain, rain_out, sems.at[2])
    rain_copy.start()
    lay_out(columns, mass, n, n - EARLY)
    late_copy = pltpu.make_async_copy(mass, mass_out.at[pl.ds(EARLY, n - EARLY)], sems.at[1])
    late_copy.start()
    for copy in (early_copy, rain_copy, late_copy):
        copy.wait()


def breakup_plain_kernel(mass_ref, pairs_ref, lost_ref, out_ref, products):
    count = products.shape[0]

    @pl.loop(0, mass_ref.shape[0] // count)
    def _(i):
        start = pl.multiple_of(i * count, count)
        out_ref[pl.ds(start, count)] = breakup_rows(mass_ref[pl.ds(start, count)], pairs_ref, lost_ref, products)


def shape(*dims, dtype=F32):
    return jax.ShapeDtypeStruct(dims, dtype)


def tiles_of(count):
    return shape(count * ROWS, LANES)


def call(kernel, outs, args, scratch=(), micros=1.0, out_place=pltpu.VMEM, copies=0):
    scratch = [pltpu.VMEM(s.shape, s.dtype) for s in scratch]
    if copies:
        scratch.append(pltpu.SemaphoreType.DMA((copies,)))
    return pl.pallas_call(
        kernel,
        out_shape=outs,
        in_specs=[VMEM] * len(args),
        out_specs=jax.tree.map(lambda _: pl.BlockSpec(memory_space=out_place), outs),
        scratch_shapes=scratch,
        compiler_params=pltpu.CompilerParams(vmem_limit_bytes=40 << 20),
        cost_estimate=pl.CostEstimate(
            flops=int(micros * 1.1e9), bytes_accessed=int(micros * 3.6e6), transcendentals=0
        ),
    )(*args)


def swap_neighbours(axis, begin, message):
    axes = ("gx", "gy", "gz")
    sizes = [lax.axis_size(a) for a in axes]
    along, other = (0, 2) if axis == "gx" else (1, 0)

    def partner(place, start, count):
        to = start + ((place - start) ^ 1)
        return to if start <= place and to < count else place

    index = {place: i for i, place in enumerate(itertools.product(*map(range, sizes)))}
    pairs = []
    for place, i in index.items():
        to = list(place)
        to[along] = partner(place[along], begin, sizes[along])
        if to[along] == place[along]:
            to[other] = partner(place[other], 0, sizes[other])
        pairs.append((i, index[tuple(to)]))
    return lax.ppermute(message, axes, pairs)


def per_device(bin_mass, courant, sub_courant, fall_steps, frag_gain, collide):
    nx, ny, nz, bins = bin_mass.shape
    n = nx
    parts = lax.axis_size("gz")
    gz, gy = lax.axis_index("gz"), lax.axis_index("gy")
    width = bins // parts
    tiles = groups(parts)[2]
    winds = 3 * tiles

    pair_rows = (bins // 2 + 1) * LANES
    pairs, lost = call(
        functools.partial(matrix_kernel, bins),
        (shape(pair_rows, LANES, dtype=jnp.bfloat16), shape(LANES, LANES, dtype=jnp.bfloat16)),
        (frag_gain, collide),
        [shape(2 * bins * bins, LANES), shape(3 * bins * bins // 2, LANES)],
        micros=0.02,
    )

    y_message = tiles_of(n * PAD_LO + winds)
    x_message = tiles_of(n * PAD_LO + winds // 2)
    if parts == 2:
        half = tiles_of(n * n // 2)
        send, keep = call(pack_kernel, (half, half), (bin_mass,), micros=0.3)
        got = lax.ppermute(send, "gz", [(0, 1), (1, 0)])
        own_wind = call(wind_kernel, tiles_of(3), (courant, keep), micros=0.1)
        got_wind = lax.ppermute(own_wind, "gz", [(0, 1), (1, 0)])
        block, *messages = call(
            merge_kernel,
            [tiles_of(n * n + winds), y_message, y_message, x_message, x_message],
            (keep, got, own_wind, got_wind, lost),
            micros=0.2,
        )
    else:
        split = bin_mass.reshape(nx, ny, nz // ROWS, ROWS, parts, width).transpose(4, 0, 1, 3, 2, 5)
        split = lax.all_to_all(split, "gz", split_axis=0, concat_axis=0, tiled=True)
        cube = split.transpose(1, 2, 3, 0, 4, 5).reshape(n, n, ROWS, LANES)
        air = courant.reshape(3, nx, ny, nz // ROWS, ROWS).transpose(0, 4, 3, 1, 2) * (1.0 / 12.0)
        air = lax.all_gather(air, "gz").reshape(parts, 3, ROWS, nz // ROWS, tiles, nx // tiles, ny)
        air = air.transpose(1, 4, 2, 0, 3, 5, 6).reshape(3, tiles, ROWS, LANES)
        block = jnp.concatenate([cube.reshape(-1, LANES), air.reshape(-1, LANES)])
        messages = []
        for layers, low_air, high_air, message, even in (
            (cube.transpose(1, 0, 2, 3), air, air, y_message, gy % 2 == 0),
            (cube, air[:, : tiles // 2], air[:, tiles // 2 :], x_message, lax.axis_index("gx") % 2 == 0),
        ):
            up, down = layers[n - PAD_LO :], layers[:PAD_HI]
            if message is y_message:
                up, down = up.transpose(1, 0, 2, 3), down.transpose(1, 0, 2, 3)
            up = jnp.concatenate([up.reshape(-1, LANES), high_air.reshape(-1, LANES)])
            down = jnp.concatenate([down.reshape(-1, LANES), low_air.reshape(-1, LANES)])
            messages += order(up, jnp.pad(down, ((0, up.shape[0] - down.shape[0]), (0, 0))), even)

    from_y = swap_neighbours("gy", 0, messages[0]), swap_neighbours("gy", 1, messages[1])
    from_x = swap_neighbours("gx", 1, messages[3]), swap_neighbours("gx", 0, messages[2])
    wind_x, wind_y, wind_z, own_change, edge_x, edge_y = call(
        functools.partial(own_kernel, n, parts), [tiles_of(n * n)] * 4 + [tiles_of(2 * n)] * 2, (block,), micros=1.6
    )
    message = tiles_of(LO * LINES + 2 + tiles)
    corners = call(functools.partial(corner_kernel, n, parts), (message, message), (*from_y, own_change), micros=0.1)
    corners = swap_neighbours("gx", 1, corners[1]), swap_neighbours("gx", 0, corners[0])
    cell, change, halo_wind_x, far_wind_y = call(
        functools.partial(y_kernel, n, parts),
        [tiles_of(n * (n + PAD_LO + PAD_HI)), tiles_of(n * (n + LINES)), tiles_of(LINES * n), tiles_of(n * (LINES + 2))],
        (block, *from_y, wind_y, own_change, edge_y),
        [tiles_of(LINES * n)] * 2,
        micros=2.0,
    )
    reach, inner = n + LINES, n - LINES
    near = call(
        functools.partial(inner_kernel, n, parts),
        [tiles_of(inner * reach), tiles_of(2 * reach), tiles_of(inner * n)],
        (cell, change, halo_wind_x, wind_y, far_wind_y, wind_z, edge_x),
        micros=0.9,
    )
    mid, far_wind_x, side, side_wind_y = call(
        functools.partial(x_kernel, n, parts),
        [tiles_of(count) for count in (reach * n, (LINES + 2) * n, LINES * n, LINES * n)],
        (cell, change, wind_x, near[1], *from_x),
        [tiles_of(LINES * n)] * 3,
        micros=1.7,
    )
    fall = sub_courant.reshape(1, bins), fall_steps.reshape(1, bins)

    def fallen(count):
        if parts == 2:
            return [tiles_of(n * count // 2 + (count + 3) // 4)] * 2
        return [tiles_of(n * count), tiles_of(count)]

    one, *early = call(
        functools.partial(main_kernel, n, parts),
        [tiles_of(reach * reach)] + fallen(EARLY),
        (
            *(cell, change, wind_x, wind_y, wind_z, halo_wind_x, far_wind_y, *near),
            *(mid, far_wind_x, side, side_wind_y, *corners, *fall),
        ),
        [tiles_of(count) for count in (LINES * LINES, 2 * LINES, 2 * LINES, n * EARLY, n * EARLY)],
        micros=2.6,
    )
    if parts == 2:
        early_got = lax.ppermute(early[0], "gz", [(0, 1), (1, 0)])
    late = call(
        functools.partial(late_kernel, n, parts),
        fallen(n - EARLY),
        (one, cell, wind_x, far_wind_x, wind_y, far_wind_y, wind_z, near[2], *fall),
        [tiles_of(n * (n - EARLY))] * 2,
        micros=0.7,
    )

    def products(count):
        return shape(n * count * ROWS, pair_rows, dtype=jnp.bfloat16)

    if parts == 2:
        late_got = lax.ppermute(late[0], "gz", [(0, 1), (1, 0)])
        early = call(
            functools.partial(breakup_first_kernel, n),
            [shape(EARLY, ny, nz, bins), shape(EARLY, ny // parts, bins)],
            (early[1], early_got, pairs, lost),
            [tiles_of(n * EARLY), products(EARLY)],
            micros=1.8,
        )
        outs = [shape(nx, ny, nz, bins), shape(nx, ny // parts, bins)]
        return tuple(
            call(
                functools.partial(breakup_last_kernel, n),
                outs,
                (late[1], late_got, pairs, lost, *early),
                [tiles_of(n * (n - EARLY)), products(n - EARLY), shape(n - EARLY, ny, nz, bins), outs[1]],
                micros=1.2,
                out_place=pl.ANY,
                copies=3,
            )
        )

    settled, rain = [jnp.concatenate(halves) for halves in zip(early, late)]
    rain = rain.reshape(nx, ny, LANES)[:, :, :width]
    rain = lax.all_to_all(rain, "gz", split_axis=1, concat_axis=2, tiled=True)
    settled = settled.reshape(nx, ny, ROWS, parts, nz // ROWS, width).transpose(3, 0, 1, 4, 2, 5)
    settled = lax.all_to_all(settled, "gz", split_axis=0, concat_axis=0, tiled=True)
    settled = settled.transpose(1, 2, 3, 4, 0, 5).reshape(nx * ny, nz // ROWS, ROWS, bins)
    paired = settled.transpose(0, 2, 1, 3).reshape(-1, LANES)
    updated = call(breakup_plain_kernel, tiles_of(n * n), (paired, pairs, lost), [products(n // 2)], micros=3.0)
    updated = updated.reshape(nx, ny, ROWS, nz // ROWS, bins).transpose(0, 1, 3, 2, 4).reshape(nx, ny, nz, bins)
    return updated, rain


def solution(mesh):
    in_specs = (P("gx", "gy", "gz", None), P(None, "gx", "gy", "gz"), P(), P(), P(), P())
    out_specs = (P("gx", "gy", "gz", None), P("gx", ("gy", "gz"), None))
    return jax.shard_map(per_device, mesh=mesh, in_specs=in_specs, out_specs=out_specs, check_vma=False)
```

```python
import functools
import itertools

import jax
import jax.numpy as jnp
from jax import lax
from jax.experimental import pallas as pl
from jax.experimental.pallas import tpu as pltpu
from jax.sharding import PartitionSpec as P

SUBS = 24
EPS = 1e-06
LO, HI = 3, 2
PAD_LO, PAD_HI = 2 * LO, 2 * HI
LINES = LO + HI
ROWS, LANES = 8, 128
AHEAD = 4
EARLY = 5
F32 = jnp.float32
VMEM = pl.BlockSpec(memory_space=pltpu.VMEM)


def lane_ids():
    return lax.broadcasted_iota(jnp.int32, (ROWS, LANES), 1)


def pick(tile, ids):
    return jnp.take_along_axis(tile, ids, axis=1, mode="promise_in_bounds")


def turn(tile, lanes):
    lanes %= LANES
    return pltpu.roll(tile, lanes, 1) if lanes else tile


def rows_of(first, count=1):
    return pl.ds(first * ROWS, count * ROWS)


def eight(first, level, step=1):
    return pl.ds(first * ROWS + level, ROWS, stride=step * ROWS)


def order(a, b, straight):
    return jnp.where(straight, a, b), jnp.where(straight, b, a)


def is_even(axis):
    return lax.axis_index(axis) % 2 == 0


def by_quarter(parts):
    quarter = lane_ids() // (LANES // 4)
    return jnp.where(quarter < 2, jnp.where(quarter == 0, parts[0], parts[1]), jnp.where(quarter == 2, parts[2], parts[3]))


def groups(parts):
    width = LANES // (2 * parts)
    return width, width // ROWS, ROWS * ROWS // width


def spread(jobs, parts):
    width = groups(parts)[0]
    place = lane_ids() % width
    rows = [[], []]
    for tile, lane, _, _ in jobs:
        top = tile.astype(jnp.bfloat16).astype(F32)
        here = place == lane
        for out, term in zip(rows, (top, tile - top)):
            out.append(jnp.where(here, term, 0.0))
    terms = jnp.concatenate([jnp.concatenate(r, axis=0).astype(jnp.bfloat16) for r in rows], axis=1)
    source, target = [lax.broadcasted_iota(jnp.int32, (2 * LANES, LANES), k) for k in range(2)]
    same = jnp.where(source % LANES // width == target // width, 1.0, 0.0).astype(jnp.bfloat16)
    out = jnp.dot(terms, same, preferred_element_type=F32)
    for k, (_, _, ref, at) in enumerate(jobs):
        ref[rows_of(at)] = out[k * ROWS : (k + 1) * ROWS]


def lane_of(x, y, parts):
    return x % groups(parts)[1] * ROWS + y


def half_lane_of(x, y, parts):
    _, deep, tiles = groups(parts)
    return x % deep * ROWS + x // deep // (tiles // 2) * (ROWS // 2) + y % (ROWS // 2)


def half_tiles(low, high, upper):
    near = lane_ids() % ROWS < ROWS // 2
    if upper:
        return jnp.where(near, turn(low, -(ROWS // 2)), high)
    return jnp.where(near, low, turn(high, ROWS // 2))


def each(count, together, body):
    def some(places):
        stores = [store for i in places for store in body(i)]
        for ref, at, value in stores:
            ref[at] = value

    whole = count // together

    @pl.loop(0, whole)
    def _(i):
        some([i * together + k for k in range(together)])

    if count % together:
        some(range(whole * together, count))


def halo_line(i, n):
    if isinstance(i, int):
        return i - LO + (n if i >= LO else 0)
    return jnp.where(i < LO, i - LO, i - LO + n)


def line_change(cells, winds):
    return changes(line_fluxes(cells, winds))


def changes(fluxes):
    return [a - b for a, b in zip(fluxes, fluxes[1:])]


def long_line(cells, winds, low_edge, high_edge, n):
    begin, end = LO, n - HI
    low = line_fluxes(cells[: PAD_LO + begin + 1], winds[: LO + 1 + begin]) + [low_edge]
    high = [high_edge] + line_fluxes(cells[PAD_LO + end - HI :], winds[LO + 1 + end :])
    return dict(zip(range(-LO, begin), changes(low))) | dict(zip(range(end, n + HI), changes(high)))


def line_fluxes(cells, winds):
    first = [b - a for a, b in zip(cells, cells[1:])]
    twice = [d + d for d in first]
    second = [b - a for a, b in zip(first, first[1:])]
    third = [a - b for a, b in zip(second, second[1:])]
    curved = [(13.0 / 3.0) * (c * c) + 4.0 * EPS for c in second]
    fluxes = []
    for j in range(len(cells) - 4):
        left = twice[j + 1] + second[j]
        mid = first[j + 1] + first[j + 2]
        right = twice[j + 2] - second[j + 2]
        e0 = curved[j] + left * left
        e1 = curved[j + 1] + mid * mid
        e2 = curved[j + 2] + right * right
        e0 = 3.0 * (e0 * e0)
        e1 = e1 * e1
        e2 = e2 * e2
        e2_twice = e2 + e2
        top = e1 * (e2_twice * third[j] + e0 * third[j + 1])
        inverse = pl.reciprocal(e1 * (e2 + e0) + e0 * e2_twice, approx=True)
        estimate = 6.0 * cells[j + 2] + (first[j + 1] + twice[j + 2]) + top * inverse
        fluxes.append((winds[j] + winds[j + 1]) * estimate)
    return fluxes


def from_below(value, width):
    return jnp.where(lane_ids() < width, 0.0, turn(value, width))


def from_above(value, width):
    return jnp.where(lane_ids() >= LANES - width, 0.0, turn(value, -width))


def level_change(cells, winds, width):
    long_cells = [from_below(v, width) for v in cells[ROWS - LO :]] + cells + [from_above(v, width) for v in cells[:HI]]
    long_winds = [from_below(winds[-1], width)] + winds + [from_above(winds[0], width)]
    return line_change(long_cells, long_winds)


def pack_kernel(mass_ref, send_ref, keep_ref):
    lower = is_even("gz")
    n = mass_ref.shape[0]
    zero = jnp.zeros((ROWS, LANES // 2), F32)
    for x in range(n // 2):
        for y in range(n):
            tiles = [
                jnp.concatenate([mass_ref[xx, y, z : z + ROWS], zero], axis=1) for xx in (x, x + n // 2) for z in (0, ROWS)
            ]
            low = by_quarter([turn(v, 32 * k) for k, v in enumerate(tiles)])
            high = by_quarter([turn(v, 32 * k - 32) for k, v in enumerate(tiles)])
            at = rows_of(x * n + y)
            keep_ref[at], send_ref[at] = order(low, high, lower)


def wind_kernel(wind_ref, keep_ref, out_ref):
    del keep_ref
    n = wind_ref.shape[1]
    for d in range(3):
        levels = wind_ref[d].reshape(n * n, 2 * ROWS).T * (1.0 / 12.0)
        out_ref[rows_of(d)] = jnp.concatenate([levels[:ROWS], levels[ROWS:]], axis=1)


def sides(axis, first_ref, second_ref):
    even, place = is_even(axis), lax.axis_index(axis)
    inner_low, inner_high = place > 0, place < lax.axis_size(axis) - 1

    def below(at):
        return jnp.where(inner_low, jnp.where(even, second_ref[at], first_ref[at]), 0.0)

    def above(at):
        return jnp.where(inner_high, jnp.where(even, first_ref[at], second_ref[at]), 0.0)

    return below, above


def by_parity(axis, body):
    even = is_even(axis)
    pl.when(even)(lambda: body(0, 1))
    pl.when(jnp.logical_not(even))(lambda: body(1, 0))


def merge_kernel(keep_ref, got_ref, own_wind_ref, got_wind_ref, lost_ref, block_ref, y_first, y_second, x_first, x_second):
    del lost_ref
    n = 8
    lower = is_even("gz")
    low = lane_ids() < 64
    for x in range(n // 2):
        for y in range(n):
            at = rows_of(x * n + y)
            a, b = order(keep_ref[at], got_ref[at], lower)
            block_ref[at] = jnp.where(low, a, turn(b, 64))
            block_ref[rows_of((x + n // 2) * n + y)] = jnp.where(low, turn(a, 64), b)
    for d in range(3):
        a, b = order(own_wind_ref[rows_of(d)], got_wind_ref[rows_of(d)], lower)
        block_ref[rows_of(n * n + 2 * d)] = by_quarter([a, turn(a, -32), turn(b, 64), turn(b, 32)])
        block_ref[rows_of(n * n + 2 * d + 1)] = by_quarter([turn(a, -32), turn(a, -64), turn(b, 32), b])

    def along_y(up, down):
        for ref, start, wide in (((y_first, y_second)[up], n - PAD_LO, PAD_LO), ((y_first, y_second)[down], 0, PAD_HI)):
            for x in range(n):
                ref[rows_of(x * wide, wide)] = block_ref[rows_of(x * n + start, wide)]
            for d in range(3):
                low, high = [block_ref[rows_of(n * n + 2 * d + k)] for k in range(2)]
                ref[rows_of(n * wide + d)] = half_tiles(low, high, wide == PAD_LO)

    def along_x(up, down):
        for ref, start, wide, part in (((x_first, x_second)[up], n - PAD_LO, PAD_LO, 1), ((x_first, x_second)[down], 0, PAD_HI, 0)):
            ref[rows_of(0, wide * n)] = block_ref[rows_of(start * n, wide * n)]
            for d in range(3):
                ref[rows_of(wide * n + d)] = block_ref[rows_of(n * n + 2 * d + part)]

    by_parity("gy", along_y)
    by_parity("gx", along_x)


def corner_kernel(n, parts, first_ref, second_ref, own_change, *messages):
    del own_change
    tiles = groups(parts)[2]
    half = tiles // 2
    below, above = sides("gy", first_ref, second_ref)

    def body(up, down):
        for ref, start, narrow, part in ((messages[up], n - LO, LO, half), (messages[down], 0, HI, 0)):
            at = 0
            for x in range(start, start + narrow):
                ref[rows_of(at, LO)] = below(rows_of(x * PAD_LO + PAD_LO - LO, LO))
                ref[rows_of(at + LO, HI)] = above(rows_of(x * PAD_HI, HI))
                at += LINES
            for side, base in ((below, n * PAD_LO), (above, n * PAD_HI)):
                ref[rows_of(at)] = side(rows_of(base + (half - 1 if part else 0)))
                ref[rows_of(at + 1, half)] = side(rows_of(base + half, half))
                at += 1 + half

    by_parity("gx", body)


def own_kernel(n, parts, block_ref, wind_x, wind_y, wind_z, change, edge_x, edge_y):
    width, deep, tiles = groups(parts)
    for d, out in enumerate((wind_x, wind_y, wind_z)):
        jobs = []
        for x in range(n):
            tile = block_ref[rows_of(n * n + d * tiles + x // deep)]
            jobs += [(tile, lane_of(x, y, parts), out, x * n + y) for y in range(n)]
        spread(jobs, parts)

    def along_z(x):
        cells = [block_ref[eight(x * n, k)] for k in range(ROWS)]
        winds = [wind_z[eight(x * n, k)] for k in range(ROWS)]
        return [(change, eight(x * n, k), value) for k, value in enumerate(level_change(cells, winds, width))]

    each(n, 2, along_z)
    begin, end = LO, n - HI
    for wind, edge, place in ((wind_x, edge_x, lambda i, k: k * n + i), (wind_y, edge_y, lambda i, k: i * n + k)):

        def along(i):
            cells = [block_ref[rows_of(place(i, k))] for k in range(n)]
            fluxes = line_fluxes(cells, [wind[rows_of(place(i, k))] for k in range(begin - 1, end + 1)])
            at = [rows_of(place(i, k)) for k in range(begin, end)]
            stores = [(change, here, change[here] + value) for here, value in zip(at, changes(fluxes))]
            return stores + [(edge, rows_of(i), fluxes[0]), (edge, rows_of(n + i), fluxes[-1])]

        each(n, 4, along)


def y_kernel(n, parts, block_ref, first_ref, second_ref, wind_y, own_change, edge_y, *refs):
    width, deep, tiles = groups(parts)
    cell, change, wind_x, far_y, wind_z, halo_change = refs
    below, above = sides("gy", first_ref, second_ref)
    span, reach = n + PAD_LO + PAD_HI, n + LINES

    for x in range(n):
        cell[rows_of(x * span, PAD_LO)] = below(rows_of(x * PAD_LO, PAD_LO))
        cell[rows_of(x * span + PAD_LO, n)] = block_ref[rows_of(x * n, n)]
        cell[rows_of(x * span + PAD_LO + n, PAD_HI)] = above(rows_of(x * PAD_HI, PAD_HI))
    jobs = []
    half = tiles // 2
    for d in range(3):
        for t in range(half):
            low, high = below(rows_of(n * PAD_LO + d * half + t)), above(rows_of(n * PAD_HI + d * half + t))
            for x in [x for x in range(n) if x // deep % half == t]:
                lanes = [half_lane_of(x, y, parts) for y in range(n)]
                if d == 1:
                    jobs += [(low, lanes[n - LO - 1 + y], far_y, x * (LINES + 2) + y) for y in range(LO + 1)]
                    jobs += [(high, lanes[y], far_y, x * (LINES + 2) + LO + 1 + y) for y in range(HI + 1)]
                else:
                    out = wind_z if d else wind_x
                    jobs += [(low, lanes[n - LO + y], out, y * n + x) for y in range(LO)]
                    jobs += [(high, lanes[y], out, (LO + y) * n + x) for y in range(HI)]
    spread(jobs, parts)

    def along_z(i):
        first = halo_line(i, n) + PAD_LO
        cells = [cell[eight(first, k, span)] for k in range(ROWS)]
        winds = [wind_z[eight(i * n, k)] for k in range(ROWS)]
        return [(halo_change, eight(i * n, k), value) for k, value in enumerate(level_change(cells, winds, width))]

    each(LINES, 2, along_z)

    def along_y(x):
        cells = [cell[rows_of(x * span + y)] for y in range(span)]
        far = [far_y[rows_of(x * (LINES + 2) + y)] for y in range(LINES + 2)]
        winds = far[: LO + 1] + [wind_y[rows_of(x * n + y)] for y in range(n)] + far[LO + 1 :]
        stores = []
        for y, value in long_line(cells, winds, edge_y[rows_of(x)], edge_y[rows_of(n + x)], n).items():
            if 0 <= y < n:
                value = value + own_change[rows_of(x * n + y)]
            else:
                value = value + halo_change[rows_of((y + LO if y < 0 else y + LO - n) * n + x)]
            stores.append((change, rows_of(x * reach + y + LO), value))
        for y in range(LO, n - HI):
            stores.append((change, rows_of(x * reach + y + LO), own_change[rows_of(x * n + y)]))
        return stores

    each(n, 2, along_y)


def which(i, lower, upper):
    if isinstance(i, int):
        return lower if i < LO else upper
    return jnp.where(i < LO, lower, upper)


def inside(axis):
    place = lax.axis_index(axis)
    return [jnp.where(ok, 1.0, 0.0) for ok in (place > 0, place < lax.axis_size(axis) - 1)]


def inner_kernel(n, parts, cell, change, halo_wind_x, wind_y, far_wind_y, wind_z, edge_x, one, edge, second):
    width = groups(parts)[0]
    span, reach = n + PAD_LO + PAD_HI, n + LINES
    begin, end = LO, n - HI
    south_in, north_in = inside("gy")

    for k in range(2):
        edge[rows_of(k * reach + LO, n)] = edge_x[rows_of(k * n, n)]
    for i in range(end - begin):
        x = begin + i
        one[rows_of(i * reach + LO, n)] = cell[rows_of(x * span + PAD_LO, n)] + change[rows_of(x * reach + LO, n)]

    def along_x(i):
        at = halo_line(i, n) + LO
        cells = [cell[rows_of(x * span + LO + at)] for x in range(n)]
        fluxes = line_fluxes(cells, [halo_wind_x[rows_of(i * n + x)] for x in range(begin - 1, end + 1)])
        keep = which(i, south_in, north_in)
        stores = [(edge, rows_of(at), fluxes[0]), (edge, rows_of(reach + at), fluxes[-1])]
        for k, value in enumerate(changes(fluxes)):
            x = begin + k
            value = (cells[x] + (value + change[rows_of(x * reach + at)])) * keep
            stores.append((one, rows_of(k * reach + at), value))
        return stores

    each(LINES, LINES, along_x)
    second_y_z(n, width, range(begin, end), begin, one, begin, wind_y, far_wind_y, wind_z, second)


def second_y_z(n, width, layers, first, one, one_first, wind_y, far_wind_y, wind_z, second):
    reach = n + LINES

    def along_y(i):
        x = layers[0] + i
        cells = [one[rows_of((x - one_first) * reach + y)] for y in range(reach)]
        winds = [far_wind_y[rows_of(x * (LINES + 2) + LO)]] + [wind_y[rows_of(x * n + y)] for y in range(n)]
        winds += [far_wind_y[rows_of(x * (LINES + 2) + LO + 1)]]
        return [(second, rows_of((x - first) * n + y), value) for y, value in enumerate(line_change(cells, winds))]

    def along_z(i):
        x = layers[0] + i
        cells = [one[eight((x - one_first) * reach + LO, k)] for k in range(ROWS)]
        winds = [wind_z[eight(x * n, k)] for k in range(ROWS)]
        at = [eight((x - first) * n, k) for k in range(ROWS)]
        return [(second, here, second[here] + value) for here, value in zip(at, level_change(cells, winds, width))]

    each(len(layers), len(layers), along_y)
    each(len(layers), len(layers), along_z)


def x_kernel(n, parts, cell, change, wind_x, edge, second_ref, first_ref, mid, far_wind_x, side, side_wind_y, *scratch):
    far, side_wind_z, side_change = scratch
    width, deep, tiles = groups(parts)
    half = tiles // 2
    west, east = sides("gx", first_ref, second_ref)
    span, reach = n + PAD_LO + PAD_HI, n + LINES

    jobs = []
    for take, wide, near_from, far_from, line in ((west, PAD_LO, LO, 0, 0), (east, PAD_HI, 0, HI, LO)):
        narrow = wide // 2
        side[rows_of(line * n, narrow * n)] = take(rows_of(near_from * n, narrow * n))
        far[rows_of(line * n, narrow * n)] = take(rows_of(far_from * n, narrow * n))
        layers, shift = (range(n - narrow, n), half) if line == 0 else (range(narrow), 0)
        wider = range(n - narrow - 1, n) if line == 0 else range(narrow + 1)

        def winds_of(d, x):
            return take(rows_of(wide * n + d * half + x // deep - shift))

        for i, x in enumerate(wider):
            jobs += [(winds_of(0, x), lane_of(x, y, parts), far_wind_x, (line + bool(line) + i) * n + y) for y in range(n)]
        for d, out in ((1, side_wind_y), (2, side_wind_z)):
            for i, x in enumerate(layers):
                jobs += [(winds_of(d, x), lane_of(x, y, parts), out, (line + i) * n + y) for y in range(n)]
    spread(jobs, parts)

    def along_z(i):
        cells = [side[eight(i * n, k)] for k in range(ROWS)]
        winds = [side_wind_z[eight(i * n, k)] for k in range(ROWS)]
        return [(side_change, eight(i * n, k), value) for k, value in enumerate(level_change(cells, winds, width))]

    each(LINES, 2, along_z)

    def along_x(y):
        outer = [far[rows_of(i * n + y)] for i in range(LINES)]
        near = [side[rows_of(i * n + y)] for i in range(LINES)]
        cells = outer[:LO] + near[:LO] + [cell[rows_of(x * span + PAD_LO + y)] for x in range(n)] + near[LO:] + outer[LO:]
        winds = [far_wind_x[rows_of(i * n + y)] for i in range(LINES + 2)]
        winds = winds[: LO + 1] + [wind_x[rows_of(x * n + y)] for x in range(n)] + winds[LO + 1 :]
        stores = []
        for x, value in long_line(cells, winds, edge[rows_of(LO + y)], edge[rows_of(reach + LO + y)], n).items():
            if 0 <= x < n:
                value = value + change[rows_of(x * reach + LO + y)]
            else:
                value = value + side_change[rows_of((x + LO if x < 0 else x + LO - n) * n + y)]
            stores.append((mid, rows_of((x + LO) * n + y), cells[PAD_LO + x] + value))
        return stores

    each(n, 2, along_x)


def main_kernel(n, parts, *refs):
    cell, change, wind_x, wind_y, wind_z, halo_wind_x, far_wind_y, inner, edge, inner_second = refs[:10]
    mid, far_wind_x, side, side_wind_y, second_ref, first_ref, rate_ref, steps_ref = refs[10:18]
    one, *out_refs = refs[18:21]
    corner, corner_wind_x, edge_wind_y, second, fallen = refs[21:]
    deep, tiles = groups(parts)[1:]
    half = tiles // 2
    west, east = sides("gx", first_ref, second_ref)
    span, reach = n + PAD_LO + PAD_HI, n + LINES

    jobs = []
    for take, narrow, line in ((west, LO, 0), (east, HI, LO)):
        at = narrow * LINES
        corner[rows_of(line * LINES, at)] = take(rows_of(0, at))
        below, above = at, at + 1 + half
        layers = range(n - narrow, n) if line == 0 else range(narrow)
        for y in range(LINES):
            tile = take(rows_of(below if y < LO else above))
            x = layers[-1] if line == 0 else layers[0]
            lane = half_lane_of(x, n - LO + y if y < LO else y - LO, parts)
            jobs.append((tile, lane, corner_wind_x, bool(line) * LINES + y))
        for i, x in enumerate(layers):
            tile = x // deep % half
            for k, (base, y) in enumerate(((below, n - 1), (above, 0))):
                lane = half_lane_of(x, y, parts)
                jobs.append((take(rows_of(base + 1 + tile)), lane, edge_wind_y, 2 * (line + i) + k))
    spread(jobs, parts)

    west_in, east_in = inside("gx")
    south_in, north_in = inside("gy")
    begin, end = LO, n - HI
    one[rows_of((begin + LO) * reach, (end - begin) * reach)] = inner[...]
    for x in [x for x in range(n) if not begin <= x < end]:
        one[rows_of((x + LO) * reach + LO, n)] = mid[rows_of((x + LO) * n, n)]

    def along_y(i):
        corners = [corner[rows_of(i * LINES + y)] for y in range(LINES)]
        cells = corners[:LO] + [side[rows_of(i * n + y)] for y in range(n)] + corners[LO:]
        winds = [side_wind_y[rows_of(i * n + y)] for y in range(n)]
        winds = [edge_wind_y[rows_of(2 * i)]] + winds + [edge_wind_y[rows_of(2 * i + 1)]]
        line = halo_line(i, n) + LO
        return [
            (one, rows_of(line * reach + LO + y), (mid[rows_of(line * n + y)] + value) * which(i, west_in, east_in))
            for y, value in enumerate(line_change(cells, winds))
        ]

    def along_x(i):
        line = halo_line(i, n) + LO
        near = [corner[rows_of(k * LINES + i)] for k in range(LINES)]
        cells = near[:LO] + [cell[rows_of(x * span + LO + line)] for x in range(n)] + near[LO:]
        winds = [halo_wind_x[rows_of(i * n + x)] for x in range(n)]
        winds = [corner_wind_x[rows_of(i)]] + winds + [corner_wind_x[rows_of(LINES + i)]]
        low = line_fluxes(cells[: LO + begin + 1], winds[: begin + 1]) + [edge[rows_of(line)]]
        high = [edge[rows_of(reach + line)]] + line_fluxes(cells[LO + end - HI :], winds[end + 1 :])
        values = dict(zip(range(begin), changes(low))) | dict(zip(range(end, n), changes(high)))
        stores = []
        for x, value in values.items():
            value = (cells[x + LO] + (value + change[rows_of(x * reach + line)])) * which(i, south_in, north_in)
            stores.append((one, rows_of((x + LO) * reach + line), value))
        return stores

    each(LINES, 2, along_y)
    each(LINES, LINES, along_x)
    fall_layers(
        n, parts, 0, EARLY, one, cell, wind_x, far_wind_x, wind_y, far_wind_y, wind_z, inner_second, rate_ref, steps_ref,
        out_refs, second, fallen,
    )


def late_kernel(
    n, parts, one, cell, wind_x, far_wind_x, wind_y, far_wind_y, wind_z, inner_second, rate_ref, steps_ref, *refs
):
    fall_layers(
        n, parts, EARLY, n, one, cell, wind_x, far_wind_x, wind_y, far_wind_y, wind_z, inner_second, rate_ref, steps_ref,
        refs[:2], *refs[2:],
    )


def fall_layers(
    n, parts, begin, end, one, cell, wind_x, far_wind_x, wind_y, far_wind_y, wind_z, inner_second, rate_ref, steps_ref,
    out_refs, second, fallen,
):
    width = groups(parts)[0]
    span, reach, count = n + PAD_LO + PAD_HI, n + LINES, end - begin
    ready = [x for x in range(LO, n - HI) if begin <= x < end]
    left = [x for x in range(begin, end) if x not in ready]
    if ready:
        second[rows_of((ready[0] - begin) * n, len(ready) * n)] = inner_second[rows_of((ready[0] - LO) * n, len(ready) * n)]

    second_y_z(n, width, left, begin, one, -LO, wind_y, far_wind_y, wind_z, second)

    def along_x(y):
        cells = [one[rows_of(x * reach + LO + y)] for x in range(begin, end + LINES)]
        winds = [wind_x[rows_of(x * n + y)] for x in range(max(begin - 1, 0), min(end + 1, n))]
        if begin == 0:
            winds = [far_wind_x[rows_of(LO * n + y)]] + winds
        if end == n:
            winds = winds + [far_wind_x[rows_of((LO + 1) * n + y)]]
        stores = []
        for i, value in enumerate(line_change(cells, winds)):
            value = cells[i + LO] + (value + second[rows_of(i * n + y)])
            value = 0.5 * cell[rows_of((begin + i) * span + PAD_LO + y)] + 0.5 * value
            stores.append((fallen, rows_of(i * n + y), value))
        return stores

    each(n, 4, along_x)

    bins = LANES // 2 // parts
    ids = lax.axis_index("gz") * bins + lane_ids() % bins
    rates, steps = [
        pick(jnp.broadcast_to(jnp.concatenate([ref[...]] * 2, axis=1), (ROWS, LANES)), ids) for ref in (rate_ref, steps_ref)
    ]

    rain = []
    for some in [range(count)]:
        columns = [[fallen[eight(i * n, k)] for k in range(ROWS)] for i in some]
        drops = [jnp.zeros((ROWS, LANES), F32) for _ in some]
        for block in range(SUBS // AHEAD):
            columns = [column + [from_above(v, width) for v in column[:AHEAD]] for column in columns]
            for s in range(AHEAD):
                rate = jnp.where(block * AHEAD + s < steps, rates, 0.0)
                for i, column in enumerate(columns):
                    drops[i] = drops[i] + rate * column[0]
                    columns[i] = [v + rate * (u - v) for v, u in zip(column, column[1:])]
        for i, column in zip(some, columns):
            for k in range(ROWS):
                fallen[eight(i * n, k)] = column[k]
        rain += drops

    if parts == 2:
        send_ref, keep_ref = out_refs
        lower = is_even("gz")
        low = lane_ids() < 64
        half = count * n // 2
        for c in range(half):
            a, b = fallen[rows_of(c)], fallen[rows_of(half + c)]
            at = rows_of(c)
            keep_ref[at], send_ref[at] = order(jnp.where(low, a, turn(b, 64)), jnp.where(low, turn(a, 64), b), lower)
        for j in range(0, count, 4):
            four = (rain[j : j + 4] + rain[j:] * 3)[:4]
            value = by_quarter([turn(v, 32 * i) for i, v in enumerate(four)])
            keep_ref[rows_of(half + j // 4)] = value
            send_ref[rows_of(half + j // 4)] = value
    else:
        settled_ref, rain_ref = out_refs
        settled_ref[...] = fallen[...]
        for i in range(count):
            rain_ref[rows_of(i)] = rain[i]


def matrix_kernel(bins, gain_ref, loss_ref, pairs_ref, lost_ref, wide, tall):
    zero = jnp.zeros((bins, LANES - bins), F32)
    shifts = bins // 2

    @pl.loop(0, bins)
    def _(i):
        rows = gain_ref[pl.ds(i * bins, bins)].astype(F32)
        rows = jnp.concatenate([rows, zero], axis=1)
        wide[pl.ds(i * 2 * bins, bins)] = rows
        wide[pl.ds(i * 2 * bins + bins, bins)] = rows
        tall[pl.ds(i * bins, bins)] = rows

        @pl.when(i < shifts)
        def _():
            tall[pl.ds((i + bins) * bins, bins)] = rows

    for d in range(shifts + 1):
        rows = wide[pl.ds(d, bins, stride=2 * bins + 1)]
        if 0 < d < shifts:
            rows = rows + tall[pl.ds(d * bins, bins, stride=bins + 1)]
        pairs_ref[pl.ds(d * LANES, bins)] = rows.astype(jnp.bfloat16)
        pairs_ref[pl.ds(d * LANES + bins, bins)] = pltpu.roll(rows, bins, 1).astype(jnp.bfloat16)
    rows = jnp.concatenate([loss_ref[...].astype(F32), zero], axis=1)
    lost_ref[pl.ds(0, bins)] = rows.astype(jnp.bfloat16)
    lost_ref[pl.ds(bins, bins)] = pltpu.roll(rows, bins, 1).astype(jnp.bfloat16)


def breakup_rows(mass, pairs_ref, lost_ref, products):
    bins = LANES // 2
    count = mass.shape[0]
    lanes = lane_ids()
    rounded = mass.astype(jnp.bfloat16)
    wide = rounded.astype(F32)
    gained = None
    shifts = bins // 2 + 1
    for begin in range(0, shifts, 4):
        end = min(begin + 4, shifts)
        for d in range(begin, end):
            ids = lanes // bins * bins + (lanes + d) % bins
            for r in range(0, count, 2 * ROWS):
                halves = [wide[r + ROWS * k : r + ROWS * (k + 1)] for k in range(2)]
                halves = [v * pick(v, ids) if d else v * v for v in halves]
                both = jnp.concatenate(halves, axis=0).astype(jnp.bfloat16)
                products[pl.ds(r, 2 * ROWS), d * LANES : (d + 1) * LANES] = both
        part = jnp.dot(
            products[pl.ds(0, count), begin * LANES : end * LANES],
            pairs_ref[pl.ds(begin * LANES, (end - begin) * LANES)],
            preferred_element_type=F32,
        )
        gained = part if gained is None else gained + part
    loss = jnp.dot(rounded, lost_ref[...], preferred_element_type=F32)
    return mass + gained - mass * loss


def breakup_layers(n, count, keep_ref, got_ref, pairs_ref, lost_ref, columns, products):
    first = is_even("gz")
    half = count * n // 2
    for c in range(half):
        a, b = order(keep_ref[rows_of(c)], got_ref[rows_of(c)], first)
        columns[rows_of(c)] = by_quarter([a, turn(b, 32), turn(a, 32), turn(b, 64)])
        columns[rows_of(half + c)] = by_quarter([turn(a, -64), turn(b, -32), turn(a, -32), b])
    rain = []
    for i in range(count):
        a, b = order(keep_ref[rows_of(half + i // 4)], got_ref[rows_of(half + i // 4)], first)
        a, b = [jnp.where(first, v[: n // 2], v[n // 2 :])[:, 32 * (i % 4) : 32 * (i % 4) + 32] for v in (a, b)]
        rain.append(jnp.concatenate([a, b], axis=1))
    columns[...] = breakup_rows(columns[...], pairs_ref, lost_ref, products)
    return rain


def lay_out(columns, mass, n, count):
    for x in range(count):
        for y in range(n):
            value = columns[rows_of(x * n + y)]
            mass[x, y, 0:ROWS] = value[:, :64]
            mass[x, y, ROWS : 2 * ROWS] = value[:, 64:]


def breakup_first_kernel(n, keep_ref, got_ref, pairs_ref, lost_ref, mass_ref, rain_ref, columns, products):
    for i, value in enumerate(breakup_layers(n, EARLY, keep_ref, got_ref, pairs_ref, lost_ref, columns, products)):
        rain_ref[i] = value
    lay_out(columns, mass_ref, n, EARLY)


def breakup_last_kernel(
    n, keep_ref, got_ref, pairs_ref, lost_ref, early, early_rain, mass_out, rain_out, columns, products, mass, rain, sems
):
    early_copy = pltpu.make_async_copy(early, mass_out.at[pl.ds(0, EARLY)], sems.at[0])
    early_copy.start()
    late_rain = breakup_layers(n, n - EARLY, keep_ref, got_ref, pairs_ref, lost_ref, columns, products)
    for i in range(EARLY):
        rain[i] = early_rain[i]
    for i, value in enumerate(late_rain):
        rain[EARLY + i] = value
    rain_copy = pltpu.make_async_copy(rain, rain_out, sems.at[2])
    rain_copy.start()
    lay_out(columns, mass, n, n - EARLY)
    late_copy = pltpu.make_async_copy(mass, mass_out.at[pl.ds(EARLY, n - EARLY)], sems.at[1])
    late_copy.start()
    for copy in (early_copy, rain_copy, late_copy):
        copy.wait()


def breakup_plain_kernel(mass_ref, pairs_ref, lost_ref, out_ref, products):
    count = products.shape[0]

    @pl.loop(0, mass_ref.shape[0] // count)
    def _(i):
        start = pl.multiple_of(i * count, count)
        out_ref[pl.ds(start, count)] = breakup_rows(mass_ref[pl.ds(start, count)], pairs_ref, lost_ref, products)


def shape(*dims, dtype=F32):
    return jax.ShapeDtypeStruct(dims, dtype)


def tiles_of(count):
    return shape(count * ROWS, LANES)


def call(kernel, outs, args, scratch=(), micros=1.0, out_place=pltpu.VMEM, copies=0):
    scratch = [pltpu.VMEM(s.shape, s.dtype) for s in scratch]
    if copies:
        scratch.append(pltpu.SemaphoreType.DMA((copies,)))
    return pl.pallas_call(
        kernel,
        out_shape=outs,
        in_specs=[VMEM] * len(args),
        out_specs=jax.tree.map(lambda _: pl.BlockSpec(memory_space=out_place), outs),
        scratch_shapes=scratch,
        compiler_params=pltpu.CompilerParams(vmem_limit_bytes=40 << 20),
        cost_estimate=pl.CostEstimate(
            flops=int(micros * 1.1e9), bytes_accessed=int(micros * 3.6e6), transcendentals=0
        ),
    )(*args)


def swap_neighbours(axis, begin, message):
    axes = ("gx", "gy", "gz")
    sizes = [lax.axis_size(a) for a in axes]
    along, other = (0, 2) if axis == "gx" else (1, 0)

    def partner(place, start, count):
        to = start + ((place - start) ^ 1)
        return to if start <= place and to < count else place

    index = {place: i for i, place in enumerate(itertools.product(*map(range, sizes)))}
    pairs = []
    for place, i in index.items():
        to = list(place)
        to[along] = partner(place[along], begin, sizes[along])
        if to[along] == place[along]:
            to[other] = partner(place[other], 0, sizes[other])
        pairs.append((i, index[tuple(to)]))
    return lax.ppermute(message, axes, pairs)


def per_device(bin_mass, courant, sub_courant, fall_steps, frag_gain, collide):
    nx, ny, nz, bins = bin_mass.shape
    n = nx
    parts = lax.axis_size("gz")
    gz, gy = lax.axis_index("gz"), lax.axis_index("gy")
    width = bins // parts
    tiles = groups(parts)[2]
    winds = 3 * tiles

    pair_rows = (bins // 2 + 1) * LANES
    pairs, lost = call(
        functools.partial(matrix_kernel, bins),
        (shape(pair_rows, LANES, dtype=jnp.bfloat16), shape(LANES, LANES, dtype=jnp.bfloat16)),
        (frag_gain, collide),
        [shape(2 * bins * bins, LANES), shape(3 * bins * bins // 2, LANES)],
        micros=0.02,
    )

    y_message = tiles_of(n * PAD_LO + winds // 2)
    x_message = tiles_of(n * PAD_LO + winds // 2)
    if parts == 2:
        half = tiles_of(n * n // 2)
        send, keep = call(pack_kernel, (half, half), (bin_mass,), micros=0.3)
        got = lax.ppermute(send, "gz", [(0, 1), (1, 0)])
        own_wind = call(wind_kernel, tiles_of(3), (courant, keep), micros=0.1)
        got_wind = lax.ppermute(own_wind, "gz", [(0, 1), (1, 0)])
        block, *messages = call(
            merge_kernel,
            [tiles_of(n * n + winds), y_message, y_message, x_message, x_message],
            (keep, got, own_wind, got_wind, lost),
            micros=0.2,
        )
    else:
        split = bin_mass.reshape(nx, ny, nz // ROWS, ROWS, parts, width).transpose(4, 0, 1, 3, 2, 5)
        split = lax.all_to_all(split, "gz", split_axis=0, concat_axis=0, tiled=True)
        cube = split.transpose(1, 2, 3, 0, 4, 5).reshape(n, n, ROWS, LANES)
        air = courant.reshape(3, nx, ny, nz // ROWS, ROWS).transpose(0, 4, 3, 1, 2) * (1.0 / 12.0)
        air = lax.all_gather(air, "gz").reshape(parts, 3, ROWS, nz // ROWS, tiles, nx // tiles, ny)
        air = air.transpose(1, 4, 2, 0, 3, 5, 6).reshape(3, tiles, ROWS, LANES)
        block = jnp.concatenate([cube.reshape(-1, LANES), air.reshape(-1, LANES)])
        halves = [air[:, : tiles // 2], air[:, tiles // 2 :]]
        near = jnp.arange(LANES) % ROWS < ROWS // 2
        low_y = jnp.where(near, halves[0], jnp.roll(halves[1], ROWS // 2, axis=-1))
        high_y = jnp.where(near, jnp.roll(halves[0], -(ROWS // 2), axis=-1), halves[1])
        messages = []
        for layers, low_air, high_air, message, even in (
            (cube.transpose(1, 0, 2, 3), low_y, high_y, y_message, gy % 2 == 0),
            (cube, *halves, x_message, lax.axis_index("gx") % 2 == 0),
        ):
            up, down = layers[n - PAD_LO :], layers[:PAD_HI]
            if message is y_message:
                up, down = up.transpose(1, 0, 2, 3), down.transpose(1, 0, 2, 3)
            up = jnp.concatenate([up.reshape(-1, LANES), high_air.reshape(-1, LANES)])
            down = jnp.concatenate([down.reshape(-1, LANES), low_air.reshape(-1, LANES)])
            messages += order(up, jnp.pad(down, ((0, up.shape[0] - down.shape[0]), (0, 0))), even)

    from_y = swap_neighbours("gy", 0, messages[0]), swap_neighbours("gy", 1, messages[1])
    from_x = swap_neighbours("gx", 1, messages[3]), swap_neighbours("gx", 0, messages[2])
    wind_x, wind_y, wind_z, own_change, edge_x, edge_y = call(
        functools.partial(own_kernel, n, parts), [tiles_of(n * n)] * 4 + [tiles_of(2 * n)] * 2, (block,), micros=1.6
    )
    message = tiles_of(LO * LINES + 2 + tiles)
    corners = call(functools.partial(corner_kernel, n, parts), (message, message), (*from_y, own_change), micros=0.1)
    corners = swap_neighbours("gx", 1, corners[1]), swap_neighbours("gx", 0, corners[0])
    cell, change, halo_wind_x, far_wind_y = call(
        functools.partial(y_kernel, n, parts),
        [tiles_of(n * (n + PAD_LO + PAD_HI)), tiles_of(n * (n + LINES)), tiles_of(LINES * n), tiles_of(n * (LINES + 2))],
        (block, *from_y, wind_y, own_change, edge_y),
        [tiles_of(LINES * n)] * 2,
        micros=2.0,
    )
    reach, inner = n + LINES, n - LINES
    near = call(
        functools.partial(inner_kernel, n, parts),
        [tiles_of(inner * reach), tiles_of(2 * reach), tiles_of(inner * n)],
        (cell, change, halo_wind_x, wind_y, far_wind_y, wind_z, edge_x),
        micros=0.9,
    )
    mid, far_wind_x, side, side_wind_y = call(
        functools.partial(x_kernel, n, parts),
        [tiles_of(count) for count in (reach * n, (LINES + 2) * n, LINES * n, LINES * n)],
        (cell, change, wind_x, near[1], *from_x),
        [tiles_of(LINES * n)] * 3,
        micros=1.7,
    )
    fall = sub_courant.reshape(1, bins), fall_steps.reshape(1, bins)

    def fallen(count):
        if parts == 2:
            return [tiles_of(n * count // 2 + (count + 3) // 4)] * 2
        return [tiles_of(n * count), tiles_of(count)]

    one, *early = call(
        functools.partial(main_kernel, n, parts),
        [tiles_of(reach * reach)] + fallen(EARLY),
        (
            *(cell, change, wind_x, wind_y, wind_z, halo_wind_x, far_wind_y, *near),
            *(mid, far_wind_x, side, side_wind_y, *corners, *fall),
        ),
        [tiles_of(count) for count in (LINES * LINES, 2 * LINES, 2 * LINES, n * EARLY, n * EARLY)],
        micros=2.6,
    )
    if parts == 2:
        early_got = lax.ppermute(early[0], "gz", [(0, 1), (1, 0)])
    late = call(
        functools.partial(late_kernel, n, parts),
        fallen(n - EARLY),
        (one, cell, wind_x, far_wind_x, wind_y, far_wind_y, wind_z, near[2], *fall),
        [tiles_of(n * (n - EARLY))] * 2,
        micros=0.7,
    )

    def products(count):
        return shape(n * count * ROWS, pair_rows, dtype=jnp.bfloat16)

    if parts == 2:
        late_got = lax.ppermute(late[0], "gz", [(0, 1), (1, 0)])
        early = call(
            functools.partial(breakup_first_kernel, n),
            [shape(EARLY, ny, nz, bins), shape(EARLY, ny // parts, bins)],
            (early[1], early_got, pairs, lost),
            [tiles_of(n * EARLY), products(EARLY)],
            micros=1.8,
        )
        outs = [shape(nx, ny, nz, bins), shape(nx, ny // parts, bins)]
        return tuple(
            call(
                functools.partial(breakup_last_kernel, n),
                outs,
                (late[1], late_got, pairs, lost, *early),
                [tiles_of(n * (n - EARLY)), products(n - EARLY), shape(n - EARLY, ny, nz, bins), outs[1]],
                micros=1.2,
                out_place=pl.ANY,
                copies=3,
            )
        )

    settled, rain = [jnp.concatenate(halves) for halves in zip(early, late)]
    rain = rain.reshape(nx, ny, LANES)[:, :, :width]
    rain = lax.all_to_all(rain, "gz", split_axis=1, concat_axis=2, tiled=True)
    settled = settled.reshape(nx, ny, ROWS, parts, nz // ROWS, width).transpose(3, 0, 1, 4, 2, 5)
    settled = lax.all_to_all(settled, "gz", split_axis=0, concat_axis=0, tiled=True)
    settled = settled.transpose(1, 2, 3, 4, 0, 5).reshape(nx * ny, nz // ROWS, ROWS, bins)
    paired = settled.transpose(0, 2, 1, 3).reshape(-1, LANES)
    updated = call(breakup_plain_kernel, tiles_of(n * n), (paired, pairs, lost), [products(n // 2)], micros=3.0)
    updated = updated.reshape(nx, ny, ROWS, nz // ROWS, bins).transpose(0, 1, 3, 2, 4).reshape(nx, ny, nz, bins)
    return updated, rain


def solution(mesh):
    in_specs = (P("gx", "gy", "gz", None), P(None, "gx", "gy", "gz"), P(), P(), P(), P())
    out_specs = (P("gx", "gy", "gz", None), P("gx", ("gy", "gz"), None))
    return jax.shard_map(per_device, mesh=mesh, in_specs=in_specs, out_specs=out_specs, check_vma=False)
```

```python
import functools
import itertools

import jax
import jax.numpy as jnp
from jax import lax
from jax.experimental import pallas as pl
from jax.experimental.pallas import tpu as pltpu
from jax.sharding import PartitionSpec as P

SUBS = 24
EPS = 1e-06
LO, HI = 3, 2
PAD_LO, PAD_HI = 2 * LO, 2 * HI
LINES = LO + HI
ROWS, LANES = 8, 128
AHEAD = 4
EARLY = 5
F32 = jnp.float32
VMEM = pl.BlockSpec(memory_space=pltpu.VMEM)


def lane_ids():
    return lax.broadcasted_iota(jnp.int32, (ROWS, LANES), 1)


def pick(tile, ids):
    return jnp.take_along_axis(tile, ids, axis=1, mode="promise_in_bounds")


def turn(tile, lanes):
    lanes %= LANES
    return pltpu.roll(tile, lanes, 1) if lanes else tile


def rows_of(first, count=1):
    return pl.ds(first * ROWS, count * ROWS)


def eight(first, level, step=1):
    return pl.ds(first * ROWS + level, ROWS, stride=step * ROWS)


def order(a, b, straight):
    return jnp.where(straight, a, b), jnp.where(straight, b, a)


def is_even(axis):
    return lax.axis_index(axis) % 2 == 0


def by_quarter(parts):
    quarter = lane_ids() // (LANES // 4)
    return jnp.where(quarter < 2, jnp.where(quarter == 0, parts[0], parts[1]), jnp.where(quarter == 2, parts[2], parts[3]))


def groups(parts):
    width = LANES // (2 * parts)
    return width, width // ROWS, ROWS * ROWS // width


def spread(jobs, parts):
    width = groups(parts)[0]
    place = lane_ids() % width
    rows = [[], []]
    for tile, lane, _, _ in jobs:
        top = tile.astype(jnp.bfloat16).astype(F32)
        here = place == lane
        for out, term in zip(rows, (top, tile - top)):
            out.append(jnp.where(here, term, 0.0))
    terms = jnp.concatenate([jnp.concatenate(r, axis=0).astype(jnp.bfloat16) for r in rows], axis=1)
    source, target = [lax.broadcasted_iota(jnp.int32, (2 * LANES, LANES), k) for k in range(2)]
    same = jnp.where(source % LANES // width == target // width, 1.0, 0.0).astype(jnp.bfloat16)
    out = jnp.dot(terms, same, preferred_element_type=F32)
    for k, (_, _, ref, at) in enumerate(jobs):
        ref[rows_of(at)] = out[k * ROWS : (k + 1) * ROWS]


def lane_of(x, y, parts):
    return x % groups(parts)[1] * ROWS + y


def half_lane_of(x, y, parts):
    _, deep, tiles = groups(parts)
    return x % deep * ROWS + x // deep // (tiles // 2) * (ROWS // 2) + y % (ROWS // 2)


def half_tiles(low, high, upper):
    near = lane_ids() % ROWS < ROWS // 2
    if upper:
        return jnp.where(near, turn(low, -(ROWS // 2)), high)
    return jnp.where(near, low, turn(high, ROWS // 2))


def each(count, together, body):
    def some(places):
        stores = [store for i in places for store in body(i)]
        for ref, at, value in stores:
            ref[at] = value

    whole = count // together

    @pl.loop(0, whole)
    def _(i):
        some([i * together + k for k in range(together)])

    if count % together:
        some(range(whole * together, count))


def halo_line(i, n):
    if isinstance(i, int):
        return i - LO + (n if i >= LO else 0)
    return jnp.where(i < LO, i - LO, i - LO + n)


def line_change(cells, winds):
    return changes(line_fluxes(cells, winds))


def changes(fluxes):
    return [a - b for a, b in zip(fluxes, fluxes[1:])]


def long_line(cells, winds, low_edge, high_edge, n):
    begin, end = LO, n - HI
    low = line_fluxes(cells[: PAD_LO + begin + 1], winds[: LO + 1 + begin]) + [low_edge]
    high = [high_edge] + line_fluxes(cells[PAD_LO + end - HI :], winds[LO + 1 + end :])
    return dict(zip(range(-LO, begin), changes(low))) | dict(zip(range(end, n + HI), changes(high)))


def line_fluxes(cells, winds):
    first = [b - a for a, b in zip(cells, cells[1:])]
    twice = [d + d for d in first]
    second = [b - a for a, b in zip(first, first[1:])]
    third = [a - b for a, b in zip(second, second[1:])]
    curved = [(13.0 / 3.0) * (c * c) + 4.0 * EPS for c in second]
    fluxes = []
    for j in range(len(cells) - 4):
        left = twice[j + 1] + second[j]
        mid = first[j + 1] + first[j + 2]
        right = twice[j + 2] - second[j + 2]
        e0 = curved[j] + left * left
        e1 = curved[j + 1] + mid * mid
        e2 = curved[j + 2] + right * right
        e0 = 3.0 * (e0 * e0)
        e1 = e1 * e1
        e2 = e2 * e2
        e2_twice = e2 + e2
        top = e1 * (e2_twice * third[j] + e0 * third[j + 1])
        inverse = pl.reciprocal(e1 * (e2 + e0) + e0 * e2_twice, approx=True)
        estimate = 6.0 * cells[j + 2] + (first[j + 1] + twice[j + 2]) + top * inverse
        fluxes.append((winds[j] + winds[j + 1]) * estimate)
    return fluxes


def from_below(value, width):
    return jnp.where(lane_ids() < width, 0.0, turn(value, width))


def from_above(value, width):
    return jnp.where(lane_ids() >= LANES - width, 0.0, turn(value, -width))


def level_change(cells, winds, width):
    long_cells = [from_below(v, width) for v in cells[ROWS - LO :]] + cells + [from_above(v, width) for v in cells[:HI]]
    long_winds = [from_below(winds[-1], width)] + winds + [from_above(winds[0], width)]
    return line_change(long_cells, long_winds)


def pack_kernel(mass_ref, send_ref, keep_ref):
    lower = is_even("gz")
    n = mass_ref.shape[0]
    zero = jnp.zeros((ROWS, LANES // 2), F32)
    for x in range(n // 2):
        for y in range(n):
            tiles = [
                jnp.concatenate([mass_ref[xx, y, z : z + ROWS], zero], axis=1) for xx in (x, x + n // 2) for z in (0, ROWS)
            ]
            low = by_quarter([turn(v, 32 * k) for k, v in enumerate(tiles)])
            high = by_quarter([turn(v, 32 * k - 32) for k, v in enumerate(tiles)])
            at = rows_of(x * n + y)
            keep_ref[at], send_ref[at] = order(low, high, lower)


def wind_kernel(wind_ref, keep_ref, out_ref):
    del keep_ref
    n = wind_ref.shape[1]
    for d in range(3):
        levels = wind_ref[d].reshape(n * n, 2 * ROWS).T * (1.0 / 12.0)
        out_ref[rows_of(d)] = jnp.concatenate([levels[:ROWS], levels[ROWS:]], axis=1)


def sides(axis, first_ref, second_ref):
    even, place = is_even(axis), lax.axis_index(axis)
    inner_low, inner_high = place > 0, place < lax.axis_size(axis) - 1

    def below(at):
        return jnp.where(inner_low, jnp.where(even, second_ref[at], first_ref[at]), 0.0)

    def above(at):
        return jnp.where(inner_high, jnp.where(even, first_ref[at], second_ref[at]), 0.0)

    return below, above


def by_parity(axis, body):
    even = is_even(axis)
    pl.when(even)(lambda: body(0, 1))
    pl.when(jnp.logical_not(even))(lambda: body(1, 0))


def merge_kernel(keep_ref, got_ref, own_wind_ref, got_wind_ref, lost_ref, block_ref, y_first, y_second, x_first, x_second):
    del lost_ref
    n = 8
    lower = is_even("gz")
    low = lane_ids() < 64
    for x in range(n // 2):
        for y in range(n):
            at = rows_of(x * n + y)
            a, b = order(keep_ref[at], got_ref[at], lower)
            block_ref[at] = jnp.where(low, a, turn(b, 64))
            block_ref[rows_of((x + n // 2) * n + y)] = jnp.where(low, turn(a, 64), b)
    for d in range(3):
        a, b = order(own_wind_ref[rows_of(d)], got_wind_ref[rows_of(d)], lower)
        block_ref[rows_of(n * n + 2 * d)] = by_quarter([a, turn(a, -32), turn(b, 64), turn(b, 32)])
        block_ref[rows_of(n * n + 2 * d + 1)] = by_quarter([turn(a, -32), turn(a, -64), turn(b, 32), b])

    def along_y(up, down):
        for ref, start, wide in (((y_first, y_second)[up], n - PAD_LO, PAD_LO), ((y_first, y_second)[down], 0, PAD_HI)):
            for x in range(n):
                ref[rows_of(x * wide, wide)] = block_ref[rows_of(x * n + start, wide)]
            for d in range(3):
                low, high = [block_ref[rows_of(n * n + 2 * d + k)] for k in range(2)]
                ref[rows_of(n * wide + d)] = half_tiles(low, high, wide == PAD_LO)

    def along_x(up, down):
        for ref, start, wide, part in (((x_first, x_second)[up], n - PAD_LO, PAD_LO, 1), ((x_first, x_second)[down], 0, PAD_HI, 0)):
            ref[rows_of(0, wide * n)] = block_ref[rows_of(start * n, wide * n)]
            for d in range(3):
                ref[rows_of(wide * n + d)] = block_ref[rows_of(n * n + 2 * d + part)]

    by_parity("gy", along_y)
    by_parity("gx", along_x)


def corner_kernel(n, parts, first_ref, second_ref, own_change, *messages):
    del own_change
    tiles = groups(parts)[2]
    half = tiles // 2
    below, above = sides("gy", first_ref, second_ref)

    def body(up, down):
        for ref, start, narrow, part in ((messages[up], n - LO, LO, half), (messages[down], 0, HI, 0)):
            at = 0
            for x in range(start, start + narrow):
                ref[rows_of(at, LO)] = below(rows_of(x * PAD_LO + PAD_LO - LO, LO))
                ref[rows_of(at + LO, HI)] = above(rows_of(x * PAD_HI, HI))
                at += LINES
            for side, base in ((below, n * PAD_LO), (above, n * PAD_HI)):
                ref[rows_of(at)] = side(rows_of(base + (half - 1 if part else 0)))
                ref[rows_of(at + 1, half)] = side(rows_of(base + half, half))
                at += 1 + half

    by_parity("gx", body)


def own_kernel(n, parts, block_ref, wind_x, wind_y, wind_z, change, edge_x, edge_y):
    width, deep, tiles = groups(parts)
    for d, out in enumerate((wind_x, wind_y, wind_z)):
        jobs = []
        for x in range(n):
            tile = block_ref[rows_of(n * n + d * tiles + x // deep)]
            jobs += [(tile, lane_of(x, y, parts), out, x * n + y) for y in range(n)]
        spread(jobs, parts)

    def along_z(x):
        cells = [block_ref[eight(x * n, k)] for k in range(ROWS)]
        winds = [wind_z[eight(x * n, k)] for k in range(ROWS)]
        return [(change, eight(x * n, k), value) for k, value in enumerate(level_change(cells, winds, width))]

    each(n, 4, along_z)
    begin, end = LO, n - HI
    for wind, edge, place in ((wind_x, edge_x, lambda i, k: k * n + i), (wind_y, edge_y, lambda i, k: i * n + k)):

        def along(i):
            cells = [block_ref[rows_of(place(i, k))] for k in range(n)]
            fluxes = line_fluxes(cells, [wind[rows_of(place(i, k))] for k in range(begin - 1, end + 1)])
            at = [rows_of(place(i, k)) for k in range(begin, end)]
            stores = [(change, here, change[here] + value) for here, value in zip(at, changes(fluxes))]
            return stores + [(edge, rows_of(i), fluxes[0]), (edge, rows_of(n + i), fluxes[-1])]

        each(n, 4, along)


def y_kernel(n, parts, block_ref, first_ref, second_ref, wind_y, own_change, edge_y, *refs):
    width, deep, tiles = groups(parts)
    cell, change, wind_x, far_y, wind_z, halo_change = refs
    below, above = sides("gy", first_ref, second_ref)
    span, reach = n + PAD_LO + PAD_HI, n + LINES

    for x in range(n):
        cell[rows_of(x * span, PAD_LO)] = below(rows_of(x * PAD_LO, PAD_LO))
        cell[rows_of(x * span + PAD_LO, n)] = block_ref[rows_of(x * n, n)]
        cell[rows_of(x * span + PAD_LO + n, PAD_HI)] = above(rows_of(x * PAD_HI, PAD_HI))
    jobs = []
    half = tiles // 2
    for d in range(3):
        for t in range(half):
            low, high = below(rows_of(n * PAD_LO + d * half + t)), above(rows_of(n * PAD_HI + d * half + t))
            for x in [x for x in range(n) if x // deep % half == t]:
                lanes = [half_lane_of(x, y, parts) for y in range(n)]
                if d == 1:
                    jobs += [(low, lanes[n - LO - 1 + y], far_y, x * (LINES + 2) + y) for y in range(LO + 1)]
                    jobs += [(high, lanes[y], far_y, x * (LINES + 2) + LO + 1 + y) for y in range(HI + 1)]
                else:
                    out = wind_z if d else wind_x
                    jobs += [(low, lanes[n - LO + y], out, y * n + x) for y in range(LO)]
                    jobs += [(high, lanes[y], out, (LO + y) * n + x) for y in range(HI)]
    spread(jobs, parts)

    def along_z(i):
        first = halo_line(i, n) + PAD_LO
        cells = [cell[eight(first, k, span)] for k in range(ROWS)]
        winds = [wind_z[eight(i * n, k)] for k in range(ROWS)]
        return [(halo_change, eight(i * n, k), value) for k, value in enumerate(level_change(cells, winds, width))]

    each(LINES, LINES, along_z)

    def along_y(x):
        cells = [cell[rows_of(x * span + y)] for y in range(span)]
        far = [far_y[rows_of(x * (LINES + 2) + y)] for y in range(LINES + 2)]
        winds = far[: LO + 1] + [wind_y[rows_of(x * n + y)] for y in range(n)] + far[LO + 1 :]
        stores = []
        for y, value in long_line(cells, winds, edge_y[rows_of(x)], edge_y[rows_of(n + x)], n).items():
            if 0 <= y < n:
                value = value + own_change[rows_of(x * n + y)]
            else:
                value = value + halo_change[rows_of((y + LO if y < 0 else y + LO - n) * n + x)]
            stores.append((change, rows_of(x * reach + y + LO), value))
        for y in range(LO, n - HI):
            stores.append((change, rows_of(x * reach + y + LO), own_change[rows_of(x * n + y)]))
        return stores

    each(n, 4, along_y)


def which(i, lower, upper):
    if isinstance(i, int):
        return lower if i < LO else upper
    return jnp.where(i < LO, lower, upper)


def inside(axis):
    place = lax.axis_index(axis)
    return [jnp.where(ok, 1.0, 0.0) for ok in (place > 0, place < lax.axis_size(axis) - 1)]


def inner_kernel(n, parts, cell, change, halo_wind_x, wind_y, far_wind_y, wind_z, edge_x, one, edge, second):
    width = groups(parts)[0]
    span, reach = n + PAD_LO + PAD_HI, n + LINES
    begin, end = LO, n - HI
    south_in, north_in = inside("gy")

    for k in range(2):
        edge[rows_of(k * reach + LO, n)] = edge_x[rows_of(k * n, n)]
    for i in range(end - begin):
        x = begin + i
        one[rows_of(i * reach + LO, n)] = cell[rows_of(x * span + PAD_LO, n)] + change[rows_of(x * reach + LO, n)]

    def along_x(i):
        at = halo_line(i, n) + LO
        cells = [cell[rows_of(x * span + LO + at)] for x in range(n)]
        fluxes = line_fluxes(cells, [halo_wind_x[rows_of(i * n + x)] for x in range(begin - 1, end + 1)])
        keep = which(i, south_in, north_in)
        stores = [(edge, rows_of(at), fluxes[0]), (edge, rows_of(reach + at), fluxes[-1])]
        for k, value in enumerate(changes(fluxes)):
            x = begin + k
            value = (cells[x] + (value + change[rows_of(x * reach + at)])) * keep
            stores.append((one, rows_of(k * reach + at), value))
        return stores

    each(LINES, LINES, along_x)
    second_y_z(n, width, range(begin, end), begin, one, begin, wind_y, far_wind_y, wind_z, second)


def second_y_z(n, width, layers, first, one, one_first, wind_y, far_wind_y, wind_z, second):
    reach = n + LINES

    def along_y(i):
        x = layers[0] + i
        cells = [one[rows_of((x - one_first) * reach + y)] for y in range(reach)]
        winds = [far_wind_y[rows_of(x * (LINES + 2) + LO)]] + [wind_y[rows_of(x * n + y)] for y in range(n)]
        winds += [far_wind_y[rows_of(x * (LINES + 2) + LO + 1)]]
        return [(second, rows_of((x - first) * n + y), value) for y, value in enumerate(line_change(cells, winds))]

    def along_z(i):
        x = layers[0] + i
        cells = [one[eight((x - one_first) * reach + LO, k)] for k in range(ROWS)]
        winds = [wind_z[eight(x * n, k)] for k in range(ROWS)]
        at = [eight((x - first) * n, k) for k in range(ROWS)]
        return [(second, here, second[here] + value) for here, value in zip(at, level_change(cells, winds, width))]

    each(len(layers), len(layers), along_y)
    each(len(layers), len(layers), along_z)


def x_kernel(n, parts, cell, change, wind_x, edge, second_ref, first_ref, mid, far_wind_x, side, side_wind_y, *scratch):
    far, side_wind_z, side_change = scratch
    width, deep, tiles = groups(parts)
    half = tiles // 2
    west, east = sides("gx", first_ref, second_ref)
    span, reach = n + PAD_LO + PAD_HI, n + LINES

    jobs = []
    for take, wide, near_from, far_from, line in ((west, PAD_LO, LO, 0, 0), (east, PAD_HI, 0, HI, LO)):
        narrow = wide // 2
        side[rows_of(line * n, narrow * n)] = take(rows_of(near_from * n, narrow * n))
        far[rows_of(line * n, narrow * n)] = take(rows_of(far_from * n, narrow * n))
        layers, shift = (range(n - narrow, n), half) if line == 0 else (range(narrow), 0)
        wider = range(n - narrow - 1, n) if line == 0 else range(narrow + 1)

        def winds_of(d, x):
            return take(rows_of(wide * n + d * half + x // deep - shift))

        for i, x in enumerate(wider):
            jobs += [(winds_of(0, x), lane_of(x, y, parts), far_wind_x, (line + bool(line) + i) * n + y) for y in range(n)]
        for d, out in ((1, side_wind_y), (2, side_wind_z)):
            for i, x in enumerate(layers):
                jobs += [(winds_of(d, x), lane_of(x, y, parts), out, (line + i) * n + y) for y in range(n)]
    spread(jobs, parts)

    def along_z(i):
        cells = [side[eight(i * n, k)] for k in range(ROWS)]
        winds = [side_wind_z[eight(i * n, k)] for k in range(ROWS)]
        return [(side_change, eight(i * n, k), value) for k, value in enumerate(level_change(cells, winds, width))]

    each(LINES, LINES, along_z)

    def along_x(y):
        outer = [far[rows_of(i * n + y)] for i in range(LINES)]
        near = [side[rows_of(i * n + y)] for i in range(LINES)]
        cells = outer[:LO] + near[:LO] + [cell[rows_of(x * span + PAD_LO + y)] for x in range(n)] + near[LO:] + outer[LO:]
        winds = [far_wind_x[rows_of(i * n + y)] for i in range(LINES + 2)]
        winds = winds[: LO + 1] + [wind_x[rows_of(x * n + y)] for x in range(n)] + winds[LO + 1 :]
        stores = []
        for x, value in long_line(cells, winds, edge[rows_of(LO + y)], edge[rows_of(reach + LO + y)], n).items():
            if 0 <= x < n:
                value = value + change[rows_of(x * reach + LO + y)]
            else:
                value = value + side_change[rows_of((x + LO if x < 0 else x + LO - n) * n + y)]
            stores.append((mid, rows_of((x + LO) * n + y), cells[PAD_LO + x] + value))
        return stores

    each(n, 4, along_x)


def main_kernel(n, parts, *refs):
    cell, change, wind_x, wind_y, wind_z, halo_wind_x, far_wind_y, inner, edge, inner_second = refs[:10]
    mid, far_wind_x, side, side_wind_y, second_ref, first_ref, rate_ref, steps_ref = refs[10:18]
    one, *out_refs = refs[18:21]
    corner, corner_wind_x, edge_wind_y, second, fallen = refs[21:]
    deep, tiles = groups(parts)[1:]
    half = tiles // 2
    west, east = sides("gx", first_ref, second_ref)
    span, reach = n + PAD_LO + PAD_HI, n + LINES

    jobs = []
    for take, narrow, line in ((west, LO, 0), (east, HI, LO)):
        at = narrow * LINES
        corner[rows_of(line * LINES, at)] = take(rows_of(0, at))
        below, above = at, at + 1 + half
        layers = range(n - narrow, n) if line == 0 else range(narrow)
        for y in range(LINES):
            tile = take(rows_of(below if y < LO else above))
            x = layers[-1] if line == 0 else layers[0]
            lane = half_lane_of(x, n - LO + y if y < LO else y - LO, parts)
            jobs.append((tile, lane, corner_wind_x, bool(line) * LINES + y))
        for i, x in enumerate(layers):
            tile = x // deep % half
            for k, (base, y) in enumerate(((below, n - 1), (above, 0))):
                lane = half_lane_of(x, y, parts)
                jobs.append((take(rows_of(base + 1 + tile)), lane, edge_wind_y, 2 * (line + i) + k))
    spread(jobs, parts)

    west_in, east_in = inside("gx")
    south_in, north_in = inside("gy")
    begin, end = LO, n - HI
    one[rows_of((begin + LO) * reach, (end - begin) * reach)] = inner[...]
    for x in [x for x in range(n) if not begin <= x < end]:
        one[rows_of((x + LO) * reach + LO, n)] = mid[rows_of((x + LO) * n, n)]

    def along_y(i):
        corners = [corner[rows_of(i * LINES + y)] for y in range(LINES)]
        cells = corners[:LO] + [side[rows_of(i * n + y)] for y in range(n)] + corners[LO:]
        winds = [side_wind_y[rows_of(i * n + y)] for y in range(n)]
        winds = [edge_wind_y[rows_of(2 * i)]] + winds + [edge_wind_y[rows_of(2 * i + 1)]]
        line = halo_line(i, n) + LO
        return [
            (one, rows_of(line * reach + LO + y), (mid[rows_of(line * n + y)] + value) * which(i, west_in, east_in))
            for y, value in enumerate(line_change(cells, winds))
        ]

    def along_x(i):
        line = halo_line(i, n) + LO
        near = [corner[rows_of(k * LINES + i)] for k in range(LINES)]
        cells = near[:LO] + [cell[rows_of(x * span + LO + line)] for x in range(n)] + near[LO:]
        winds = [halo_wind_x[rows_of(i * n + x)] for x in range(n)]
        winds = [corner_wind_x[rows_of(i)]] + winds + [corner_wind_x[rows_of(LINES + i)]]
        low = line_fluxes(cells[: LO + begin + 1], winds[: begin + 1]) + [edge[rows_of(line)]]
        high = [edge[rows_of(reach + line)]] + line_fluxes(cells[LO + end - HI :], winds[end + 1 :])
        values = dict(zip(range(begin), changes(low))) | dict(zip(range(end, n), changes(high)))
        stores = []
        for x, value in values.items():
            value = (cells[x + LO] + (value + change[rows_of(x * reach + line)])) * which(i, south_in, north_in)
            stores.append((one, rows_of((x + LO) * reach + line), value))
        return stores

    each(LINES, LINES, along_y)
    each(LINES, LINES, along_x)
    fall_layers(
        n, parts, 0, EARLY, one, cell, wind_x, far_wind_x, wind_y, far_wind_y, wind_z, inner_second, rate_ref, steps_ref,
        out_refs, second, fallen,
    )


def late_kernel(
    n, parts, one, cell, wind_x, far_wind_x, wind_y, far_wind_y, wind_z, inner_second, rate_ref, steps_ref, *refs
):
    fall_layers(
        n, parts, EARLY, n, one, cell, wind_x, far_wind_x, wind_y, far_wind_y, wind_z, inner_second, rate_ref, steps_ref,
        refs[:2], *refs[2:],
    )


def fall_layers(
    n, parts, begin, end, one, cell, wind_x, far_wind_x, wind_y, far_wind_y, wind_z, inner_second, rate_ref, steps_ref,
    out_refs, second, fallen,
):
    width = groups(parts)[0]
    span, reach, count = n + PAD_LO + PAD_HI, n + LINES, end - begin
    ready = [x for x in range(LO, n - HI) if begin <= x < end]
    left = [x for x in range(begin, end) if x not in ready]
    if ready:
        second[rows_of((ready[0] - begin) * n, len(ready) * n)] = inner_second[rows_of((ready[0] - LO) * n, len(ready) * n)]

    second_y_z(n, width, left, begin, one, -LO, wind_y, far_wind_y, wind_z, second)

    def along_x(y):
        cells = [one[rows_of(x * reach + LO + y)] for x in range(begin, end + LINES)]
        winds = [wind_x[rows_of(x * n + y)] for x in range(max(begin - 1, 0), min(end + 1, n))]
        if begin == 0:
            winds = [far_wind_x[rows_of(LO * n + y)]] + winds
        if end == n:
            winds = winds + [far_wind_x[rows_of((LO + 1) * n + y)]]
        stores = []
        for i, value in enumerate(line_change(cells, winds)):
            value = cells[i + LO] + (value + second[rows_of(i * n + y)])
            value = 0.5 * cell[rows_of((begin + i) * span + PAD_LO + y)] + 0.5 * value
            stores.append((fallen, rows_of(i * n + y), value))
        return stores

    each(n, 4, along_x)

    bins = LANES // 2 // parts
    ids = lax.axis_index("gz") * bins + lane_ids() % bins
    rates, steps = [
        pick(jnp.broadcast_to(jnp.concatenate([ref[...]] * 2, axis=1), (ROWS, LANES)), ids) for ref in (rate_ref, steps_ref)
    ]

    rain = []
    for some in [range(count)]:
        columns = [[fallen[eight(i * n, k)] for k in range(ROWS)] for i in some]
        drops = [jnp.zeros((ROWS, LANES), F32) for _ in some]
        for block in range(SUBS // AHEAD):
            columns = [column + [from_above(v, width) for v in column[:AHEAD]] for column in columns]
            for s in range(AHEAD):
                rate = jnp.where(block * AHEAD + s < steps, rates, 0.0)
                for i, column in enumerate(columns):
                    drops[i] = drops[i] + rate * column[0]
                    columns[i] = [v + rate * (u - v) for v, u in zip(column, column[1:])]
        for i, column in zip(some, columns):
            for k in range(ROWS):
                fallen[eight(i * n, k)] = column[k]
        rain += drops

    if parts == 2:
        send_ref, keep_ref = out_refs
        lower = is_even("gz")
        low = lane_ids() < 64
        half = count * n // 2
        for c in range(half):
            a, b = fallen[rows_of(c)], fallen[rows_of(half + c)]
            at = rows_of(c)
            keep_ref[at], send_ref[at] = order(jnp.where(low, a, turn(b, 64)), jnp.where(low, turn(a, 64), b), lower)
        for j in range(0, count, 4):
            four = (rain[j : j + 4] + rain[j:] * 3)[:4]
            value = by_quarter([turn(v, 32 * i) for i, v in enumerate(four)])
            keep_ref[rows_of(half + j // 4)] = value
            send_ref[rows_of(half + j // 4)] = value
    else:
        settled_ref, rain_ref = out_refs
        settled_ref[...] = fallen[...]
        for i in range(count):
            rain_ref[rows_of(i)] = rain[i]


def by_matrix(bins):
    return [d for d in range(bins // 2) if d % 4 > 1]


def matrix_kernel(bins, gain_ref, loss_ref, pairs_ref, lost_ref, shifts_ref, wide, tall):
    zero = jnp.zeros((bins, LANES - bins), F32)
    shifts = bins // 2

    @pl.loop(0, bins)
    def _(i):
        rows = gain_ref[pl.ds(i * bins, bins)].astype(F32)
        rows = jnp.concatenate([rows, zero], axis=1)
        wide[pl.ds(i * 2 * bins, bins)] = rows
        wide[pl.ds(i * 2 * bins + bins, bins)] = rows
        tall[pl.ds(i * bins, bins)] = rows

        @pl.when(i < shifts)
        def _():
            tall[pl.ds((i + bins) * bins, bins)] = rows

    for d in range(shifts + 1):
        rows = wide[pl.ds(d, bins, stride=2 * bins + 1)]
        if 0 < d < shifts:
            rows = rows + tall[pl.ds(d * bins, bins, stride=bins + 1)]
        pairs_ref[pl.ds(d * LANES, bins)] = rows.astype(jnp.bfloat16)
        pairs_ref[pl.ds(d * LANES + bins, bins)] = pltpu.roll(rows, bins, 1).astype(jnp.bfloat16)
    source, target = [lax.broadcasted_iota(jnp.int32, (LANES, LANES), k) for k in range(2)]
    for k, d in enumerate(by_matrix(bins)):
        here = source == target // bins * bins + (target + d) % bins
        shifts_ref[:, k * LANES : (k + 1) * LANES] = jnp.where(here, 1.0, 0.0).astype(jnp.bfloat16)
    rows = jnp.concatenate([loss_ref[...].astype(F32), zero], axis=1)
    lost_ref[pl.ds(0, bins)] = rows.astype(jnp.bfloat16)
    lost_ref[pl.ds(bins, bins)] = pltpu.roll(rows, bins, 1).astype(jnp.bfloat16)


def breakup_rows(mass, pairs_ref, lost_ref, shifts_ref, products):
    bins = LANES // 2
    count = mass.shape[0]
    lanes = lane_ids()
    rounded = mass.astype(jnp.bfloat16)
    wide = rounded.astype(F32)
    gained = None
    shifts = bins // 2 + 1
    for begin in range(0, shifts, 4):
        end = min(begin + 4, shifts)
        matrix = begin // 2 * LANES
        if end == begin + 4:
            shifted = jnp.dot(rounded, shifts_ref[:, matrix : matrix + 2 * LANES], preferred_element_type=F32)
        for d in range(begin, end):
            ids = lanes // bins * bins + (lanes + d) % bins
            for r in range(0, count, 2 * ROWS):
                halves = []
                for at in (r, r + ROWS):
                    value = other = wide[at : at + ROWS]
                    if d % 4 > 1:
                        other = shifted[at : at + ROWS, (d % 4 - 2) * LANES : (d % 4 - 1) * LANES]
                    elif d:
                        other = pick(value, ids)
                    halves.append(value * other)
                both = jnp.concatenate(halves, axis=0).astype(jnp.bfloat16)
                products[pl.ds(r, 2 * ROWS), d * LANES : (d + 1) * LANES] = both
        part = jnp.dot(
            products[pl.ds(0, count), begin * LANES : end * LANES],
            pairs_ref[pl.ds(begin * LANES, (end - begin) * LANES)],
            preferred_element_type=F32,
        )
        gained = part if gained is None else gained + part
    loss = jnp.dot(rounded, lost_ref[...], preferred_element_type=F32)
    return mass + gained - mass * loss


def breakup_layers(n, count, keep_ref, got_ref, pairs_ref, lost_ref, shifts_ref, columns, products):
    first = is_even("gz")
    half = count * n // 2
    for c in range(half):
        a, b = order(keep_ref[rows_of(c)], got_ref[rows_of(c)], first)
        columns[rows_of(c)] = by_quarter([a, turn(b, 32), turn(a, 32), turn(b, 64)])
        columns[rows_of(half + c)] = by_quarter([turn(a, -64), turn(b, -32), turn(a, -32), b])
    rain = []
    for i in range(count):
        a, b = order(keep_ref[rows_of(half + i // 4)], got_ref[rows_of(half + i // 4)], first)
        a, b = [jnp.where(first, v[: n // 2], v[n // 2 :])[:, 32 * (i % 4) : 32 * (i % 4) + 32] for v in (a, b)]
        rain.append(jnp.concatenate([a, b], axis=1))
    columns[...] = breakup_rows(columns[...], pairs_ref, lost_ref, shifts_ref, products)
    return rain


def lay_out(columns, mass, n, count):
    for x in range(count):
        for y in range(n):
            value = columns[rows_of(x * n + y)]
            mass[x, y, 0:ROWS] = value[:, :64]
            mass[x, y, ROWS : 2 * ROWS] = value[:, 64:]


def breakup_first_kernel(n, keep_ref, got_ref, pairs_ref, lost_ref, shifts_ref, mass_ref, rain_ref, columns, products):
    for i, value in enumerate(breakup_layers(n, EARLY, keep_ref, got_ref, pairs_ref, lost_ref, shifts_ref, columns, products)):
        rain_ref[i] = value
    lay_out(columns, mass_ref, n, EARLY)


def breakup_last_kernel(
    n, keep_ref, got_ref, pairs_ref, lost_ref, shifts_ref, early, early_rain, mass_out, rain_out, columns, products, mass, rain, sems
):
    early_copy = pltpu.make_async_copy(early, mass_out.at[pl.ds(0, EARLY)], sems.at[0])
    early_copy.start()
    late_rain = breakup_layers(n, n - EARLY, keep_ref, got_ref, pairs_ref, lost_ref, shifts_ref, columns, products)
    for i in range(EARLY):
        rain[i] = early_rain[i]
    for i, value in enumerate(late_rain):
        rain[EARLY + i] = value
    rain_copy = pltpu.make_async_copy(rain, rain_out, sems.at[2])
    rain_copy.start()
    lay_out(columns, mass, n, n - EARLY)
    late_copy = pltpu.make_async_copy(mass, mass_out.at[pl.ds(EARLY, n - EARLY)], sems.at[1])
    late_copy.start()
    for copy in (early_copy, rain_copy, late_copy):
        copy.wait()


def breakup_plain_kernel(mass_ref, pairs_ref, lost_ref, shifts_ref, out_ref, products):
    count = products.shape[0]

    @pl.loop(0, mass_ref.shape[0] // count)
    def _(i):
        start = pl.multiple_of(i * count, count)
        out_ref[pl.ds(start, count)] = breakup_rows(mass_ref[pl.ds(start, count)], pairs_ref, lost_ref, shifts_ref, products)


def shape(*dims, dtype=F32):
    return jax.ShapeDtypeStruct(dims, dtype)


def tiles_of(count):
    return shape(count * ROWS, LANES)


def call(kernel, outs, args, scratch=(), micros=1.0, out_place=pltpu.VMEM, copies=0):
    scratch = [pltpu.VMEM(s.shape, s.dtype) for s in scratch]
    if copies:
        scratch.append(pltpu.SemaphoreType.DMA((copies,)))
    return pl.pallas_call(
        kernel,
        out_shape=outs,
        in_specs=[VMEM] * len(args),
        out_specs=jax.tree.map(lambda _: pl.BlockSpec(memory_space=out_place), outs),
        scratch_shapes=scratch,
        compiler_params=pltpu.CompilerParams(vmem_limit_bytes=40 << 20),
        cost_estimate=pl.CostEstimate(
            flops=int(micros * 1.1e9), bytes_accessed=int(micros * 3.6e6), transcendentals=0
        ),
    )(*args)


def swap_neighbours(axis, begin, message):
    axes = ("gx", "gy", "gz")
    sizes = [lax.axis_size(a) for a in axes]
    along, other = (0, 2) if axis == "gx" else (1, 0)

    def partner(place, start, count):
        to = start + ((place - start) ^ 1)
        return to if start <= place and to < count else place

    index = {place: i for i, place in enumerate(itertools.product(*map(range, sizes)))}
    pairs = []
    for place, i in index.items():
        to = list(place)
        to[along] = partner(place[along], begin, sizes[along])
        if to[along] == place[along]:
            to[other] = partner(place[other], 0, sizes[other])
        pairs.append((i, index[tuple(to)]))
    return lax.ppermute(message, axes, pairs)


def per_device(bin_mass, courant, sub_courant, fall_steps, frag_gain, collide):
    nx, ny, nz, bins = bin_mass.shape
    n = nx
    parts = lax.axis_size("gz")
    gz, gy = lax.axis_index("gz"), lax.axis_index("gy")
    width = bins // parts
    tiles = groups(parts)[2]
    winds = 3 * tiles

    pair_rows = (bins // 2 + 1) * LANES
    matrices = pairs, lost, _ = call(
        functools.partial(matrix_kernel, bins),
        [
            shape(pair_rows, LANES, dtype=jnp.bfloat16),
            shape(LANES, LANES, dtype=jnp.bfloat16),
            shape(LANES, len(by_matrix(bins)) * LANES, dtype=jnp.bfloat16),
        ],
        (frag_gain, collide),
        [shape(2 * bins * bins, LANES), shape(3 * bins * bins // 2, LANES)],
        micros=0.02,
    )

    y_message = tiles_of(n * PAD_LO + winds // 2)
    x_message = tiles_of(n * PAD_LO + winds // 2)
    if parts == 2:
        half = tiles_of(n * n // 2)
        send, keep = call(pack_kernel, (half, half), (bin_mass,), micros=0.3)
        got = lax.ppermute(send, "gz", [(0, 1), (1, 0)])
        own_wind = call(wind_kernel, tiles_of(3), (courant, keep), micros=0.1)
        got_wind = lax.ppermute(own_wind, "gz", [(0, 1), (1, 0)])
        block, *messages = call(
            merge_kernel,
            [tiles_of(n * n + winds), y_message, y_message, x_message, x_message],
            (keep, got, own_wind, got_wind, lost),
            micros=0.2,
        )
    else:
        split = bin_mass.reshape(nx, ny, nz // ROWS, ROWS, parts, width).transpose(4, 0, 1, 3, 2, 5)
        split = lax.all_to_all(split, "gz", split_axis=0, concat_axis=0, tiled=True)
        cube = split.transpose(1, 2, 3, 0, 4, 5).reshape(n, n, ROWS, LANES)
        air = courant.reshape(3, nx, ny, nz // ROWS, ROWS).transpose(0, 4, 3, 1, 2) * (1.0 / 12.0)
        air = lax.all_gather(air, "gz").reshape(parts, 3, ROWS, nz // ROWS, tiles, nx // tiles, ny)
        air = air.transpose(1, 4, 2, 0, 3, 5, 6).reshape(3, tiles, ROWS, LANES)
        block = jnp.concatenate([cube.reshape(-1, LANES), air.reshape(-1, LANES)])
        halves = [air[:, : tiles // 2], air[:, tiles // 2 :]]
        near = jnp.arange(LANES) % ROWS < ROWS // 2
        low_y = jnp.where(near, halves[0], jnp.roll(halves[1], ROWS // 2, axis=-1))
        high_y = jnp.where(near, jnp.roll(halves[0], -(ROWS // 2), axis=-1), halves[1])
        messages = []
        for layers, low_air, high_air, message, even in (
            (cube.transpose(1, 0, 2, 3), low_y, high_y, y_message, gy % 2 == 0),
            (cube, *halves, x_message, lax.axis_index("gx") % 2 == 0),
        ):
            up, down = layers[n - PAD_LO :], layers[:PAD_HI]
            if message is y_message:
                up, down = up.transpose(1, 0, 2, 3), down.transpose(1, 0, 2, 3)
            up = jnp.concatenate([up.reshape(-1, LANES), high_air.reshape(-1, LANES)])
            down = jnp.concatenate([down.reshape(-1, LANES), low_air.reshape(-1, LANES)])
            messages += order(up, jnp.pad(down, ((0, up.shape[0] - down.shape[0]), (0, 0))), even)

    from_y = swap_neighbours("gy", 0, messages[0]), swap_neighbours("gy", 1, messages[1])
    from_x = swap_neighbours("gx", 1, messages[3]), swap_neighbours("gx", 0, messages[2])
    wind_x, wind_y, wind_z, own_change, edge_x, edge_y = call(
        functools.partial(own_kernel, n, parts), [tiles_of(n * n)] * 4 + [tiles_of(2 * n)] * 2, (block,), micros=1.6
    )
    message = tiles_of(LO * LINES + 2 + tiles)
    corners = call(functools.partial(corner_kernel, n, parts), (message, message), (*from_y, own_change), micros=0.1)
    corners = swap_neighbours("gx", 1, corners[1]), swap_neighbours("gx", 0, corners[0])
    cell, change, halo_wind_x, far_wind_y = call(
        functools.partial(y_kernel, n, parts),
        [tiles_of(n * (n + PAD_LO + PAD_HI)), tiles_of(n * (n + LINES)), tiles_of(LINES * n), tiles_of(n * (LINES + 2))],
        (block, *from_y, wind_y, own_change, edge_y),
        [tiles_of(LINES * n)] * 2,
        micros=2.0,
    )
    reach, inner = n + LINES, n - LINES
    near = call(
        functools.partial(inner_kernel, n, parts),
        [tiles_of(inner * reach), tiles_of(2 * reach), tiles_of(inner * n)],
        (cell, change, halo_wind_x, wind_y, far_wind_y, wind_z, edge_x),
        micros=0.9,
    )
    mid, far_wind_x, side, side_wind_y = call(
        functools.partial(x_kernel, n, parts),
        [tiles_of(count) for count in (reach * n, (LINES + 2) * n, LINES * n, LINES * n)],
        (cell, change, wind_x, near[1], *from_x),
        [tiles_of(LINES * n)] * 3,
        micros=1.7,
    )
    fall = sub_courant.reshape(1, bins), fall_steps.reshape(1, bins)

    def fallen(count):
        if parts == 2:
            return [tiles_of(n * count // 2 + (count + 3) // 4)] * 2
        return [tiles_of(n * count), tiles_of(count)]

    one, *early = call(
        functools.partial(main_kernel, n, parts),
        [tiles_of(reach * reach)] + fallen(EARLY),
        (
            *(cell, change, wind_x, wind_y, wind_z, halo_wind_x, far_wind_y, *near),
            *(mid, far_wind_x, side, side_wind_y, *corners, *fall),
        ),
        [tiles_of(count) for count in (LINES * LINES, 2 * LINES, 2 * LINES, n * EARLY, n * EARLY)],
        micros=2.6,
    )
    if parts == 2:
        early_got = lax.ppermute(early[0], "gz", [(0, 1), (1, 0)])
    late = call(
        functools.partial(late_kernel, n, parts),
        fallen(n - EARLY),
        (one, cell, wind_x, far_wind_x, wind_y, far_wind_y, wind_z, near[2], *fall),
        [tiles_of(n * (n - EARLY))] * 2,
        micros=0.7,
    )

    def products(count):
        return shape(n * count * ROWS, pair_rows, dtype=jnp.bfloat16)

    if parts == 2:
        late_got = lax.ppermute(late[0], "gz", [(0, 1), (1, 0)])
        early = call(
            functools.partial(breakup_first_kernel, n),
            [shape(EARLY, ny, nz, bins), shape(EARLY, ny // parts, bins)],
            (early[1], early_got, *matrices),
            [tiles_of(n * EARLY), products(EARLY)],
            micros=1.8,
        )
        outs = [shape(nx, ny, nz, bins), shape(nx, ny // parts, bins)]
        return tuple(
            call(
                functools.partial(breakup_last_kernel, n),
                outs,
                (late[1], late_got, *matrices, *early),
                [tiles_of(n * (n - EARLY)), products(n - EARLY), shape(n - EARLY, ny, nz, bins), outs[1]],
                micros=1.2,
                out_place=pl.ANY,
                copies=3,
            )
        )

    settled, rain = [jnp.concatenate(halves) for halves in zip(early, late)]
    rain = rain.reshape(nx, ny, LANES)[:, :, :width]
    rain = lax.all_to_all(rain, "gz", split_axis=1, concat_axis=2, tiled=True)
    settled = settled.reshape(nx, ny, ROWS, parts, nz // ROWS, width).transpose(3, 0, 1, 4, 2, 5)
    settled = lax.all_to_all(settled, "gz", split_axis=0, concat_axis=0, tiled=True)
    settled = settled.transpose(1, 2, 3, 4, 0, 5).reshape(nx * ny, nz // ROWS, ROWS, bins)
    paired = settled.transpose(0, 2, 1, 3).reshape(-1, LANES)
    updated = call(breakup_plain_kernel, tiles_of(n * n), (paired, *matrices), [products(n // 2)], micros=3.0)
    updated = updated.reshape(nx, ny, ROWS, nz // ROWS, bins).transpose(0, 1, 3, 2, 4).reshape(nx, ny, nz, bins)
    return updated, rain


def solution(mesh):
    in_specs = (P("gx", "gy", "gz", None), P(None, "gx", "gy", "gz"), P(), P(), P(), P())
    out_specs = (P("gx", "gy", "gz", None), P("gx", ("gy", "gz"), None))
    return jax.shard_map(per_device, mesh=mesh, in_specs=in_specs, out_specs=out_specs, check_vma=False)
```

```python
import functools
import itertools

import jax
import jax.numpy as jnp
from jax import lax
from jax.experimental import pallas as pl
from jax.experimental.pallas import tpu as pltpu
from jax.sharding import PartitionSpec as P

SUBS = 24
EPS = 1e-06
LO, HI = 3, 2
PAD_LO, PAD_HI = 2 * LO, 2 * HI
LINES = LO + HI
ROWS, LANES = 8, 128
AHEAD = 4
EARLY = 5
F32 = jnp.float32
VMEM = pl.BlockSpec(memory_space=pltpu.VMEM)


def lane_ids():
    return lax.broadcasted_iota(jnp.int32, (ROWS, LANES), 1)


def pick(tile, ids):
    return jnp.take_along_axis(tile, ids, axis=1, mode="promise_in_bounds")


def turn(tile, lanes):
    lanes %= LANES
    return pltpu.roll(tile, lanes, 1) if lanes else tile


def rows_of(first, count=1):
    return pl.ds(first * ROWS, count * ROWS)


def eight(first, level, step=1):
    return pl.ds(first * ROWS + level, ROWS, stride=step * ROWS)


def order(a, b, straight):
    return jnp.where(straight, a, b), jnp.where(straight, b, a)


def is_even(axis):
    return lax.axis_index(axis) % 2 == 0


def by_quarter(parts):
    quarter = lane_ids() // (LANES // 4)
    return jnp.where(quarter < 2, jnp.where(quarter == 0, parts[0], parts[1]), jnp.where(quarter == 2, parts[2], parts[3]))


def groups(parts):
    width = LANES // (2 * parts)
    return width, width // ROWS, ROWS * ROWS // width


def spread(jobs, parts):
    width = groups(parts)[0]
    place = lane_ids() % width
    rows = [[], []]
    for tile, lane, _, _ in jobs:
        top = tile.astype(jnp.bfloat16).astype(F32)
        here = place == lane
        for out, term in zip(rows, (top, tile - top)):
            out.append(jnp.where(here, term, 0.0))
    terms = jnp.concatenate([jnp.concatenate(r, axis=0).astype(jnp.bfloat16) for r in rows], axis=1)
    source, target = [lax.broadcasted_iota(jnp.int32, (2 * LANES, LANES), k) for k in range(2)]
    same = jnp.where(source % LANES // width == target // width, 1.0, 0.0).astype(jnp.bfloat16)
    out = jnp.dot(terms, same, preferred_element_type=F32)
    for k, (_, _, ref, at) in enumerate(jobs):
        ref[rows_of(at)] = out[k * ROWS : (k + 1) * ROWS]


def lane_of(x, y, parts):
    return x % groups(parts)[1] * ROWS + y


def half_lane_of(x, y, parts):
    _, deep, tiles = groups(parts)
    return x % deep * ROWS + x // deep // (tiles // 2) * (ROWS // 2) + y % (ROWS // 2)


def half_tiles(low, high, upper):
    near = lane_ids() % ROWS < ROWS // 2
    if upper:
        return jnp.where(near, turn(low, -(ROWS // 2)), high)
    return jnp.where(near, low, turn(high, ROWS // 2))


def each(count, together, body):
    def some(places):
        stores = [store for i in places for store in body(i)]
        for ref, at, value in stores:
            ref[at] = value

    whole = count // together

    @pl.loop(0, whole)
    def _(i):
        some([i * together + k for k in range(together)])

    if count % together:
        some(range(whole * together, count))


def halo_line(i, n):
    if isinstance(i, int):
        return i - LO + (n if i >= LO else 0)
    return jnp.where(i < LO, i - LO, i - LO + n)


def line_change(cells, winds):
    return changes(line_fluxes(cells, winds))


def changes(fluxes):
    return [a - b for a, b in zip(fluxes, fluxes[1:])]


def long_line(cells, winds, low_edge, high_edge, n):
    begin, end = LO, n - HI
    low = line_fluxes(cells[: PAD_LO + begin + 1], winds[: LO + 1 + begin]) + [low_edge]
    high = [high_edge] + line_fluxes(cells[PAD_LO + end - HI :], winds[LO + 1 + end :])
    return dict(zip(range(-LO, begin), changes(low))) | dict(zip(range(end, n + HI), changes(high)))


def line_fluxes(cells, winds):
    first = [b - a for a, b in zip(cells, cells[1:])]
    twice = [d + d for d in first]
    second = [b - a for a, b in zip(first, first[1:])]
    third = [a - b for a, b in zip(second, second[1:])]
    curved = [(13.0 / 3.0) * (c * c) + 4.0 * EPS for c in second]
    fluxes = []
    for j in range(len(cells) - 4):
        left = twice[j + 1] + second[j]
        mid = first[j + 1] + first[j + 2]
        right = twice[j + 2] - second[j + 2]
        e0 = curved[j] + left * left
        e1 = curved[j + 1] + mid * mid
        e2 = curved[j + 2] + right * right
        e0 = 3.0 * (e0 * e0)
        e1 = e1 * e1
        e2 = e2 * e2
        e2_twice = e2 + e2
        top = e1 * (e2_twice * third[j] + e0 * third[j + 1])
        inverse = pl.reciprocal(e1 * (e2 + e0) + e0 * e2_twice, approx=True)
        estimate = 6.0 * cells[j + 2] + (first[j + 1] + twice[j + 2]) + top * inverse
        fluxes.append((winds[j] + winds[j + 1]) * estimate)
    return fluxes


def from_below(value, width):
    return jnp.where(lane_ids() < width, 0.0, turn(value, width))


def from_above(value, width):
    return jnp.where(lane_ids() >= LANES - width, 0.0, turn(value, -width))


def level_change(cells, winds, width):
    long_cells = [from_below(v, width) for v in cells[ROWS - LO :]] + cells + [from_above(v, width) for v in cells[:HI]]
    long_winds = [from_below(winds[-1], width)] + winds + [from_above(winds[0], width)]
    return line_change(long_cells, long_winds)


def pack_kernel(mass_ref, send_ref, keep_ref):
    lower = is_even("gz")
    n = mass_ref.shape[0]
    zero = jnp.zeros((ROWS, LANES // 2), F32)
    for x in range(n // 2):
        for y in range(n):
            tiles = [
                jnp.concatenate([mass_ref[xx, y, z : z + ROWS], zero], axis=1) for xx in (x, x + n // 2) for z in (0, ROWS)
            ]
            low = by_quarter([turn(v, 32 * k) for k, v in enumerate(tiles)])
            high = by_quarter([turn(v, 32 * k - 32) for k, v in enumerate(tiles)])
            at = rows_of(x * n + y)
            keep_ref[at], send_ref[at] = order(low, high, lower)


def wind_kernel(wind_ref, keep_ref, out_ref):
    del keep_ref
    n = wind_ref.shape[1]
    for d in range(3):
        levels = wind_ref[d].reshape(n * n, 2 * ROWS).T * (1.0 / 12.0)
        out_ref[rows_of(d)] = jnp.concatenate([levels[:ROWS], levels[ROWS:]], axis=1)


def sides(axis, first_ref, second_ref):
    even, place = is_even(axis), lax.axis_index(axis)
    inner_low, inner_high = place > 0, place < lax.axis_size(axis) - 1

    def below(at):
        return jnp.where(inner_low, jnp.where(even, second_ref[at], first_ref[at]), 0.0)

    def above(at):
        return jnp.where(inner_high, jnp.where(even, first_ref[at], second_ref[at]), 0.0)

    return below, above


def by_parity(axis, body):
    even = is_even(axis)
    pl.when(even)(lambda: body(0, 1))
    pl.when(jnp.logical_not(even))(lambda: body(1, 0))


def merge_kernel(keep_ref, got_ref, own_wind_ref, got_wind_ref, lost_ref, block_ref, y_first, y_second, x_first, x_second):
    del lost_ref
    n = 8
    lower = is_even("gz")
    low = lane_ids() < 64
    for x in range(n // 2):
        for y in range(n):
            at = rows_of(x * n + y)
            a, b = order(keep_ref[at], got_ref[at], lower)
            block_ref[at] = jnp.where(low, a, turn(b, 64))
            block_ref[rows_of((x + n // 2) * n + y)] = jnp.where(low, turn(a, 64), b)
    for d in range(3):
        a, b = order(own_wind_ref[rows_of(d)], got_wind_ref[rows_of(d)], lower)
        block_ref[rows_of(n * n + 2 * d)] = by_quarter([a, turn(a, -32), turn(b, 64), turn(b, 32)])
        block_ref[rows_of(n * n + 2 * d + 1)] = by_quarter([turn(a, -32), turn(a, -64), turn(b, 32), b])

    def along_y(up, down):
        for ref, start, wide in (((y_first, y_second)[up], n - PAD_LO, PAD_LO), ((y_first, y_second)[down], 0, PAD_HI)):
            for x in range(n):
                ref[rows_of(x * wide, wide)] = block_ref[rows_of(x * n + start, wide)]
            for d in range(3):
                low, high = [block_ref[rows_of(n * n + 2 * d + k)] for k in range(2)]
                ref[rows_of(n * wide + d)] = half_tiles(low, high, wide == PAD_LO)

    def along_x(up, down):
        for ref, start, wide, part in (((x_first, x_second)[up], n - PAD_LO, PAD_LO, 1), ((x_first, x_second)[down], 0, PAD_HI, 0)):
            ref[rows_of(0, wide * n)] = block_ref[rows_of(start * n, wide * n)]
            for d in range(3):
                ref[rows_of(wide * n + d)] = block_ref[rows_of(n * n + 2 * d + part)]

    by_parity("gy", along_y)
    by_parity("gx", along_x)


def corner_kernel(n, parts, first_ref, second_ref, own_change, *messages):
    del own_change
    tiles = groups(parts)[2]
    half = tiles // 2
    below, above = sides("gy", first_ref, second_ref)

    def body(up, down):
        for ref, start, narrow, part in ((messages[up], n - LO, LO, half), (messages[down], 0, HI, 0)):
            at = 0
            for x in range(start, start + narrow):
                ref[rows_of(at, LO)] = below(rows_of(x * PAD_LO + PAD_LO - LO, LO))
                ref[rows_of(at + LO, HI)] = above(rows_of(x * PAD_HI, HI))
                at += LINES
            for side, base in ((below, n * PAD_LO), (above, n * PAD_HI)):
                ref[rows_of(at)] = side(rows_of(base + (half - 1 if part else 0)))
                ref[rows_of(at + 1, half)] = side(rows_of(base + half, half))
                at += 1 + half

    by_parity("gx", body)


def own_kernel(n, parts, block_ref, wind_x, wind_y, wind_z, change, edge_x, edge_y):
    width, deep, tiles = groups(parts)
    for d, out in enumerate((wind_x, wind_y, wind_z)):
        jobs = []
        for x in range(n):
            tile = block_ref[rows_of(n * n + d * tiles + x // deep)]
            jobs += [(tile, lane_of(x, y, parts), out, x * n + y) for y in range(n)]
        spread(jobs, parts)

    def along_z(x):
        cells = [block_ref[eight(x * n, k)] for k in range(ROWS)]
        winds = [wind_z[eight(x * n, k)] for k in range(ROWS)]
        return [(change, eight(x * n, k), value) for k, value in enumerate(level_change(cells, winds, width))]

    each(n, 4, along_z)
    begin, end = LO, n - HI
    for wind, edge, place in ((wind_x, edge_x, lambda i, k: k * n + i), (wind_y, edge_y, lambda i, k: i * n + k)):

        def along(i):
            cells = [block_ref[rows_of(place(i, k))] for k in range(n)]
            fluxes = line_fluxes(cells, [wind[rows_of(place(i, k))] for k in range(begin - 1, end + 1)])
            at = [rows_of(place(i, k)) for k in range(begin, end)]
            stores = [(change, here, change[here] + value) for here, value in zip(at, changes(fluxes))]
            return stores + [(edge, rows_of(i), fluxes[0]), (edge, rows_of(n + i), fluxes[-1])]

        each(n, 4, along)


def y_kernel(n, parts, block_ref, first_ref, second_ref, wind_y, own_change, edge_y, *refs):
    width, deep, tiles = groups(parts)
    cell, change, wind_x, far_y, wind_z, halo_change = refs
    below, above = sides("gy", first_ref, second_ref)
    span, reach = n + PAD_LO + PAD_HI, n + LINES

    for x in range(n):
        cell[rows_of(x * span, PAD_LO)] = below(rows_of(x * PAD_LO, PAD_LO))
        cell[rows_of(x * span + PAD_LO, n)] = block_ref[rows_of(x * n, n)]
        cell[rows_of(x * span + PAD_LO + n, PAD_HI)] = above(rows_of(x * PAD_HI, PAD_HI))
    jobs = []
    half = tiles // 2
    for d in range(3):
        for t in range(half):
            low, high = below(rows_of(n * PAD_LO + d * half + t)), above(rows_of(n * PAD_HI + d * half + t))
            for x in [x for x in range(n) if x // deep % half == t]:
                lanes = [half_lane_of(x, y, parts) for y in range(n)]
                if d == 1:
                    jobs += [(low, lanes[n - LO - 1 + y], far_y, x * (LINES + 2) + y) for y in range(LO + 1)]
                    jobs += [(high, lanes[y], far_y, x * (LINES + 2) + LO + 1 + y) for y in range(HI + 1)]
                else:
                    out = wind_z if d else wind_x
                    jobs += [(low, lanes[n - LO + y], out, y * n + x) for y in range(LO)]
                    jobs += [(high, lanes[y], out, (LO + y) * n + x) for y in range(HI)]
    spread(jobs, parts)

    def along_z(i):
        first = halo_line(i, n) + PAD_LO
        cells = [cell[eight(first, k, span)] for k in range(ROWS)]
        winds = [wind_z[eight(i * n, k)] for k in range(ROWS)]
        return [(halo_change, eight(i * n, k), value) for k, value in enumerate(level_change(cells, winds, width))]

    each(LINES, LINES, along_z)

    def along_y(x):
        cells = [cell[rows_of(x * span + y)] for y in range(span)]
        far = [far_y[rows_of(x * (LINES + 2) + y)] for y in range(LINES + 2)]
        winds = far[: LO + 1] + [wind_y[rows_of(x * n + y)] for y in range(n)] + far[LO + 1 :]
        stores = []
        for y, value in long_line(cells, winds, edge_y[rows_of(x)], edge_y[rows_of(n + x)], n).items():
            if 0 <= y < n:
                value = value + own_change[rows_of(x * n + y)]
            else:
                value = value + halo_change[rows_of((y + LO if y < 0 else y + LO - n) * n + x)]
            stores.append((change, rows_of(x * reach + y + LO), value))
        for y in range(LO, n - HI):
            stores.append((change, rows_of(x * reach + y + LO), own_change[rows_of(x * n + y)]))
        return stores

    each(n, 4, along_y)


def which(i, lower, upper):
    if isinstance(i, int):
        return lower if i < LO else upper
    return jnp.where(i < LO, lower, upper)


def inside(axis):
    place = lax.axis_index(axis)
    return [jnp.where(ok, 1.0, 0.0) for ok in (place > 0, place < lax.axis_size(axis) - 1)]


def inner_kernel(n, parts, cell, change, halo_wind_x, wind_y, far_wind_y, wind_z, edge_x, one, edge, second):
    width = groups(parts)[0]
    span, reach = n + PAD_LO + PAD_HI, n + LINES
    begin, end = LO, n - HI
    south_in, north_in = inside("gy")

    for k in range(2):
        edge[rows_of(k * reach + LO, n)] = edge_x[rows_of(k * n, n)]
    for i in range(end - begin):
        x = begin + i
        one[rows_of(i * reach + LO, n)] = cell[rows_of(x * span + PAD_LO, n)] + change[rows_of(x * reach + LO, n)]

    def along_x(i):
        at = halo_line(i, n) + LO
        cells = [cell[rows_of(x * span + LO + at)] for x in range(n)]
        fluxes = line_fluxes(cells, [halo_wind_x[rows_of(i * n + x)] for x in range(begin - 1, end + 1)])
        keep = which(i, south_in, north_in)
        stores = [(edge, rows_of(at), fluxes[0]), (edge, rows_of(reach + at), fluxes[-1])]
        for k, value in enumerate(changes(fluxes)):
            x = begin + k
            value = (cells[x] + (value + change[rows_of(x * reach + at)])) * keep
            stores.append((one, rows_of(k * reach + at), value))
        return stores

    each(LINES, LINES, along_x)
    second_y_z(n, width, range(begin, end), begin, one, begin, wind_y, far_wind_y, wind_z, second)


def second_y_z(n, width, layers, first, one, one_first, wind_y, far_wind_y, wind_z, second):
    reach = n + LINES

    def along_y(i):
        x = layers[0] + i
        cells = [one[rows_of((x - one_first) * reach + y)] for y in range(reach)]
        winds = [far_wind_y[rows_of(x * (LINES + 2) + LO)]] + [wind_y[rows_of(x * n + y)] for y in range(n)]
        winds += [far_wind_y[rows_of(x * (LINES + 2) + LO + 1)]]
        return [(second, rows_of((x - first) * n + y), value) for y, value in enumerate(line_change(cells, winds))]

    def along_z(i):
        x = layers[0] + i
        cells = [one[eight((x - one_first) * reach + LO, k)] for k in range(ROWS)]
        winds = [wind_z[eight(x * n, k)] for k in range(ROWS)]
        at = [eight((x - first) * n, k) for k in range(ROWS)]
        return [(second, here, second[here] + value) for here, value in zip(at, level_change(cells, winds, width))]

    each(len(layers), len(layers), along_y)
    each(len(layers), len(layers), along_z)


def x_kernel(
    n, parts, cell, change, wind_x, edge, second_ref, first_ref, mid, far_wind_x, side, side_wind_y, side_edge, *scratch
):
    far, side_wind_z, side_change = scratch
    width, deep, tiles = groups(parts)
    half = tiles // 2
    west, east = sides("gx", first_ref, second_ref)
    span, reach = n + PAD_LO + PAD_HI, n + LINES

    jobs = []
    for take, wide, near_from, far_from, line in ((west, PAD_LO, LO, 0, 0), (east, PAD_HI, 0, HI, LO)):
        narrow = wide // 2
        side[rows_of(line * n, narrow * n)] = take(rows_of(near_from * n, narrow * n))
        far[rows_of(line * n, narrow * n)] = take(rows_of(far_from * n, narrow * n))
        layers, shift = (range(n - narrow, n), half) if line == 0 else (range(narrow), 0)
        wider = range(n - narrow - 1, n) if line == 0 else range(narrow + 1)

        def winds_of(d, x):
            return take(rows_of(wide * n + d * half + x // deep - shift))

        for i, x in enumerate(wider):
            jobs += [(winds_of(0, x), lane_of(x, y, parts), far_wind_x, (line + bool(line) + i) * n + y) for y in range(n)]
        for d, out in ((1, side_wind_y), (2, side_wind_z)):
            for i, x in enumerate(layers):
                jobs += [(winds_of(d, x), lane_of(x, y, parts), out, (line + i) * n + y) for y in range(n)]
    spread(jobs, parts)

    def along_z(i):
        cells = [side[eight(i * n, k)] for k in range(ROWS)]
        winds = [side_wind_z[eight(i * n, k)] for k in range(ROWS)]
        return [(side_change, eight(i * n, k), value) for k, value in enumerate(level_change(cells, winds, width))]

    each(LINES, LINES, along_z)
    begin, end = LO, n - HI

    def along_y(i):
        cells = [side[rows_of(i * n + y)] for y in range(n)]
        fluxes = line_fluxes(cells, [side_wind_y[rows_of(i * n + y)] for y in range(begin - 1, end + 1)])
        at = [rows_of(i * n + y) for y in range(begin, end)]
        stores = [(side_change, here, side_change[here] + value) for here, value in zip(at, changes(fluxes))]
        return stores + [(side_edge, rows_of(i), fluxes[0]), (side_edge, rows_of(LINES + i), fluxes[-1])]

    each(LINES, LINES, along_y)

    def along_x(y):
        outer = [far[rows_of(i * n + y)] for i in range(LINES)]
        near = [side[rows_of(i * n + y)] for i in range(LINES)]
        cells = outer[:LO] + near[:LO] + [cell[rows_of(x * span + PAD_LO + y)] for x in range(n)] + near[LO:] + outer[LO:]
        winds = [far_wind_x[rows_of(i * n + y)] for i in range(LINES + 2)]
        winds = winds[: LO + 1] + [wind_x[rows_of(x * n + y)] for x in range(n)] + winds[LO + 1 :]
        stores = []
        for x, value in long_line(cells, winds, edge[rows_of(LO + y)], edge[rows_of(reach + LO + y)], n).items():
            if 0 <= x < n:
                value = value + change[rows_of(x * reach + LO + y)]
            else:
                value = value + side_change[rows_of((x + LO if x < 0 else x + LO - n) * n + y)]
            stores.append((mid, rows_of((x + LO) * n + y), cells[PAD_LO + x] + value))
        return stores

    each(n, 4, along_x)


def main_kernel(n, parts, *refs):
    cell, change, wind_x, wind_y, wind_z, halo_wind_x, far_wind_y, inner, edge, inner_second = refs[:10]
    mid, far_wind_x, side, side_wind_y, side_edge, second_ref, first_ref, rate_ref, steps_ref = refs[10:19]
    one, *out_refs = refs[19:22]
    corner, corner_wind_x, edge_wind_y, second, fallen = refs[22:]
    deep, tiles = groups(parts)[1:]
    half = tiles // 2
    west, east = sides("gx", first_ref, second_ref)
    span, reach = n + PAD_LO + PAD_HI, n + LINES

    jobs = []
    for take, narrow, line in ((west, LO, 0), (east, HI, LO)):
        at = narrow * LINES
        corner[rows_of(line * LINES, at)] = take(rows_of(0, at))
        below, above = at, at + 1 + half
        layers = range(n - narrow, n) if line == 0 else range(narrow)
        for y in range(LINES):
            tile = take(rows_of(below if y < LO else above))
            x = layers[-1] if line == 0 else layers[0]
            lane = half_lane_of(x, n - LO + y if y < LO else y - LO, parts)
            jobs.append((tile, lane, corner_wind_x, bool(line) * LINES + y))
        for i, x in enumerate(layers):
            tile = x // deep % half
            for k, (base, y) in enumerate(((below, n - 1), (above, 0))):
                lane = half_lane_of(x, y, parts)
                jobs.append((take(rows_of(base + 1 + tile)), lane, edge_wind_y, 2 * (line + i) + k))
    spread(jobs, parts)

    west_in, east_in = inside("gx")
    south_in, north_in = inside("gy")
    begin, end = LO, n - HI
    one[rows_of((begin + LO) * reach, (end - begin) * reach)] = inner[...]
    for x in [x for x in range(n) if not begin <= x < end]:
        one[rows_of((x + LO) * reach + LO, n)] = mid[rows_of((x + LO) * n, n)]

    def along_y(i):
        corners = [corner[rows_of(i * LINES + y)] for y in range(LINES)]
        cells = corners[:LO] + [side[rows_of(i * n + y)] for y in range(n)] + corners[LO:]
        winds = [side_wind_y[rows_of(i * n + y)] for y in range(n)]
        winds = [edge_wind_y[rows_of(2 * i)]] + winds + [edge_wind_y[rows_of(2 * i + 1)]]
        low = line_fluxes(cells[: LO + begin + 1], winds[: begin + 1]) + [side_edge[rows_of(i)]]
        high = [side_edge[rows_of(LINES + i)]] + line_fluxes(cells[LO + end - HI :], winds[end + 1 :])
        values = dict(zip(range(begin), changes(low))) | dict(zip(range(end, n), changes(high)))
        line, keep = halo_line(i, n) + LO, which(i, west_in, east_in)
        stores = []
        for y in range(n):
            value = mid[rows_of(line * n + y)]
            value = value + values[y] if y in values else value
            stores.append((one, rows_of(line * reach + LO + y), value * keep))
        return stores

    def along_x(i):
        line = halo_line(i, n) + LO
        near = [corner[rows_of(k * LINES + i)] for k in range(LINES)]
        cells = near[:LO] + [cell[rows_of(x * span + LO + line)] for x in range(n)] + near[LO:]
        winds = [halo_wind_x[rows_of(i * n + x)] for x in range(n)]
        winds = [corner_wind_x[rows_of(i)]] + winds + [corner_wind_x[rows_of(LINES + i)]]
        low = line_fluxes(cells[: LO + begin + 1], winds[: begin + 1]) + [edge[rows_of(line)]]
        high = [edge[rows_of(reach + line)]] + line_fluxes(cells[LO + end - HI :], winds[end + 1 :])
        values = dict(zip(range(begin), changes(low))) | dict(zip(range(end, n), changes(high)))
        stores = []
        for x, value in values.items():
            value = (cells[x + LO] + (value + change[rows_of(x * reach + line)])) * which(i, south_in, north_in)
            stores.append((one, rows_of((x + LO) * reach + line), value))
        return stores

    each(LINES, LINES, along_y)
    each(LINES, LINES, along_x)
    fall_layers(
        n, parts, 0, EARLY, one, cell, wind_x, far_wind_x, wind_y, far_wind_y, wind_z, inner_second, rate_ref, steps_ref,
        out_refs, second, fallen,
    )


def late_kernel(
    n, parts, one, cell, wind_x, far_wind_x, wind_y, far_wind_y, wind_z, inner_second, rate_ref, steps_ref, *refs
):
    fall_layers(
        n, parts, EARLY, n, one, cell, wind_x, far_wind_x, wind_y, far_wind_y, wind_z, inner_second, rate_ref, steps_ref,
        refs[:2], *refs[2:],
    )


def fall_layers(
    n, parts, begin, end, one, cell, wind_x, far_wind_x, wind_y, far_wind_y, wind_z, inner_second, rate_ref, steps_ref,
    out_refs, second, fallen,
):
    width = groups(parts)[0]
    span, reach, count = n + PAD_LO + PAD_HI, n + LINES, end - begin
    ready = [x for x in range(LO, n - HI) if begin <= x < end]
    left = [x for x in range(begin, end) if x not in ready]
    if ready:
        second[rows_of((ready[0] - begin) * n, len(ready) * n)] = inner_second[rows_of((ready[0] - LO) * n, len(ready) * n)]

    second_y_z(n, width, left, begin, one, -LO, wind_y, far_wind_y, wind_z, second)

    def along_x(y):
        cells = [one[rows_of(x * reach + LO + y)] for x in range(begin, end + LINES)]
        winds = [wind_x[rows_of(x * n + y)] for x in range(max(begin - 1, 0), min(end + 1, n))]
        if begin == 0:
            winds = [far_wind_x[rows_of(LO * n + y)]] + winds
        if end == n:
            winds = winds + [far_wind_x[rows_of((LO + 1) * n + y)]]
        stores = []
        for i, value in enumerate(line_change(cells, winds)):
            value = cells[i + LO] + (value + second[rows_of(i * n + y)])
            value = 0.5 * cell[rows_of((begin + i) * span + PAD_LO + y)] + 0.5 * value
            stores.append((fallen, rows_of(i * n + y), value))
        return stores

    each(n, 4, along_x)

    bins = LANES // 2 // parts
    ids = lax.axis_index("gz") * bins + lane_ids() % bins
    rates, steps = [
        pick(jnp.broadcast_to(jnp.concatenate([ref[...]] * 2, axis=1), (ROWS, LANES)), ids) for ref in (rate_ref, steps_ref)
    ]

    rain = []
    for some in [range(count)]:
        columns = [[fallen[eight(i * n, k)] for k in range(ROWS)] for i in some]
        drops = [jnp.zeros((ROWS, LANES), F32) for _ in some]
        for block in range(SUBS // AHEAD):
            columns = [column + [from_above(v, width) for v in column[:AHEAD]] for column in columns]
            for s in range(AHEAD):
                rate = jnp.where(block * AHEAD + s < steps, rates, 0.0)
                for i, column in enumerate(columns):
                    drops[i] = drops[i] + rate * column[0]
                    columns[i] = [v + rate * (u - v) for v, u in zip(column, column[1:])]
        for i, column in zip(some, columns):
            for k in range(ROWS):
                fallen[eight(i * n, k)] = column[k]
        rain += drops

    if parts == 2:
        send_ref, keep_ref = out_refs
        lower = is_even("gz")
        low = lane_ids() < 64
        half = count * n // 2
        for c in range(half):
            a, b = fallen[rows_of(c)], fallen[rows_of(half + c)]
            at = rows_of(c)
            keep_ref[at], send_ref[at] = order(jnp.where(low, a, turn(b, 64)), jnp.where(low, turn(a, 64), b), lower)
        for j in range(0, count, 4):
            four = (rain[j : j + 4] + rain[j:] * 3)[:4]
            value = by_quarter([turn(v, 32 * i) for i, v in enumerate(four)])
            keep_ref[rows_of(half + j // 4)] = value
            send_ref[rows_of(half + j // 4)] = value
    else:
        settled_ref, rain_ref = out_refs
        settled_ref[...] = fallen[...]
        for i in range(count):
            rain_ref[rows_of(i)] = rain[i]


def matrix_kernel(bins, gain_ref, loss_ref, pairs_ref, lost_ref, wide, tall):
    zero = jnp.zeros((bins, LANES - bins), F32)
    shifts = bins // 2

    @pl.loop(0, bins)
    def _(i):
        rows = gain_ref[pl.ds(i * bins, bins)].astype(F32)
        rows = jnp.concatenate([rows, zero], axis=1)
        wide[pl.ds(i * 2 * bins, bins)] = rows
        wide[pl.ds(i * 2 * bins + bins, bins)] = rows
        tall[pl.ds(i * bins, bins)] = rows

        @pl.when(i < shifts)
        def _():
            tall[pl.ds((i + bins) * bins, bins)] = rows

    for d in range(shifts + 1):
        rows = wide[pl.ds(d, bins, stride=2 * bins + 1)]
        if 0 < d < shifts:
            rows = rows + tall[pl.ds(d * bins, bins, stride=bins + 1)]
        pairs_ref[pl.ds(d * LANES, bins)] = rows.astype(jnp.bfloat16)
        pairs_ref[pl.ds(d * LANES + bins, bins)] = pltpu.roll(rows, bins, 1).astype(jnp.bfloat16)
    rows = jnp.concatenate([loss_ref[...].astype(F32), zero], axis=1)
    lost_ref[pl.ds(0, bins)] = rows.astype(jnp.bfloat16)
    lost_ref[pl.ds(bins, bins)] = pltpu.roll(rows, bins, 1).astype(jnp.bfloat16)


def breakup_rows(mass, pairs_ref, lost_ref, products):
    bins = LANES // 2
    count = mass.shape[0]
    lanes = lane_ids()
    rounded = mass.astype(jnp.bfloat16)
    wide = rounded.astype(F32)
    gained = None
    shifts = bins // 2 + 1
    for begin in range(0, shifts, 4):
        end = min(begin + 4, shifts)
        for d in range(begin, end):
            ids = lanes // bins * bins + (lanes + d) % bins
            for r in range(0, count, 2 * ROWS):
                halves = [wide[r + ROWS * k : r + ROWS * (k + 1)] for k in range(2)]
                halves = [v * pick(v, ids) if d else v * v for v in halves]
                both = jnp.concatenate(halves, axis=0).astype(jnp.bfloat16)
                products[pl.ds(r, 2 * ROWS), d * LANES : (d + 1) * LANES] = both
        part = jnp.dot(
            products[pl.ds(0, count), begin * LANES : end * LANES],
            pairs_ref[pl.ds(begin * LANES, (end - begin) * LANES)],
            preferred_element_type=F32,
        )
        gained = part if gained is None else gained + part
    loss = jnp.dot(rounded, lost_ref[...], preferred_element_type=F32)
    return mass + gained - mass * loss


def breakup_layers(n, count, keep_ref, got_ref, pairs_ref, lost_ref, columns, products):
    first = is_even("gz")
    half = count * n // 2
    for c in range(half):
        a, b = order(keep_ref[rows_of(c)], got_ref[rows_of(c)], first)
        columns[rows_of(c)] = by_quarter([a, turn(b, 32), turn(a, 32), turn(b, 64)])
        columns[rows_of(half + c)] = by_quarter([turn(a, -64), turn(b, -32), turn(a, -32), b])
    rain = []
    for i in range(count):
        a, b = order(keep_ref[rows_of(half + i // 4)], got_ref[rows_of(half + i // 4)], first)
        a, b = [jnp.where(first, v[: n // 2], v[n // 2 :])[:, 32 * (i % 4) : 32 * (i % 4) + 32] for v in (a, b)]
        rain.append(jnp.concatenate([a, b], axis=1))
    columns[...] = breakup_rows(columns[...], pairs_ref, lost_ref, products)
    return rain


def lay_out(columns, mass, n, count):
    for x in range(count):
        for y in range(n):
            value = columns[rows_of(x * n + y)]
            mass[x, y, 0:ROWS] = value[:, :64]
            mass[x, y, ROWS : 2 * ROWS] = value[:, 64:]


def breakup_first_kernel(n, keep_ref, got_ref, pairs_ref, lost_ref, mass_ref, rain_ref, columns, products):
    for i, value in enumerate(breakup_layers(n, EARLY, keep_ref, got_ref, pairs_ref, lost_ref, columns, products)):
        rain_ref[i] = value
    lay_out(columns, mass_ref, n, EARLY)


def breakup_last_kernel(
    n, keep_ref, got_ref, pairs_ref, lost_ref, early, early_rain, mass_out, rain_out, columns, products, mass, rain, sems
):
    early_copy = pltpu.make_async_copy(early, mass_out.at[pl.ds(0, EARLY)], sems.at[0])
    early_copy.start()
    late_rain = breakup_layers(n, n - EARLY, keep_ref, got_ref, pairs_ref, lost_ref, columns, products)
    for i in range(EARLY):
        rain[i] = early_rain[i]
    for i, value in enumerate(late_rain):
        rain[EARLY + i] = value
    rain_copy = pltpu.make_async_copy(rain, rain_out, sems.at[2])
    rain_copy.start()
    lay_out(columns, mass, n, n - EARLY)
    late_copy = pltpu.make_async_copy(mass, mass_out.at[pl.ds(EARLY, n - EARLY)], sems.at[1])
    late_copy.start()
    for copy in (early_copy, rain_copy, late_copy):
        copy.wait()


def breakup_plain_kernel(mass_ref, pairs_ref, lost_ref, out_ref, products):
    count = products.shape[0]

    @pl.loop(0, mass_ref.shape[0] // count)
    def _(i):
        start = pl.multiple_of(i * count, count)
        out_ref[pl.ds(start, count)] = breakup_rows(mass_ref[pl.ds(start, count)], pairs_ref, lost_ref, products)


def shape(*dims, dtype=F32):
    return jax.ShapeDtypeStruct(dims, dtype)


def tiles_of(count):
    return shape(count * ROWS, LANES)


def call(kernel, outs, args, scratch=(), micros=1.0, out_place=pltpu.VMEM, copies=0):
    scratch = [pltpu.VMEM(s.shape, s.dtype) for s in scratch]
    if copies:
        scratch.append(pltpu.SemaphoreType.DMA((copies,)))
    return pl.pallas_call(
        kernel,
        out_shape=outs,
        in_specs=[VMEM] * len(args),
        out_specs=jax.tree.map(lambda _: pl.BlockSpec(memory_space=out_place), outs),
        scratch_shapes=scratch,
        compiler_params=pltpu.CompilerParams(vmem_limit_bytes=40 << 20),
        cost_estimate=pl.CostEstimate(
            flops=int(micros * 1.1e9), bytes_accessed=int(micros * 3.6e6), transcendentals=0
        ),
    )(*args)


def swap_neighbours(axis, begin, message):
    axes = ("gx", "gy", "gz")
    sizes = [lax.axis_size(a) for a in axes]
    along, other = (0, 2) if axis == "gx" else (1, 0)

    def partner(place, start, count):
        to = start + ((place - start) ^ 1)
        return to if start <= place and to < count else place

    index = {place: i for i, place in enumerate(itertools.product(*map(range, sizes)))}
    pairs = []
    for place, i in index.items():
        to = list(place)
        to[along] = partner(place[along], begin, sizes[along])
        if to[along] == place[along]:
            to[other] = partner(place[other], 0, sizes[other])
        pairs.append((i, index[tuple(to)]))
    return lax.ppermute(message, axes, pairs)


def per_device(bin_mass, courant, sub_courant, fall_steps, frag_gain, collide):
    nx, ny, nz, bins = bin_mass.shape
    n = nx
    parts = lax.axis_size("gz")
    gz, gy = lax.axis_index("gz"), lax.axis_index("gy")
    width = bins // parts
    tiles = groups(parts)[2]
    winds = 3 * tiles

    pair_rows = (bins // 2 + 1) * LANES
    pairs, lost = call(
        functools.partial(matrix_kernel, bins),
        (shape(pair_rows, LANES, dtype=jnp.bfloat16), shape(LANES, LANES, dtype=jnp.bfloat16)),
        (frag_gain, collide),
        [shape(2 * bins * bins, LANES), shape(3 * bins * bins // 2, LANES)],
        micros=0.02,
    )

    y_message = tiles_of(n * PAD_LO + winds // 2)
    x_message = tiles_of(n * PAD_LO + winds // 2)
    if parts == 2:
        half = tiles_of(n * n // 2)
        send, keep = call(pack_kernel, (half, half), (bin_mass,), micros=0.3)
        got = lax.ppermute(send, "gz", [(0, 1), (1, 0)])
        own_wind = call(wind_kernel, tiles_of(3), (courant, keep), micros=0.1)
        got_wind = lax.ppermute(own_wind, "gz", [(0, 1), (1, 0)])
        block, *messages = call(
            merge_kernel,
            [tiles_of(n * n + winds), y_message, y_message, x_message, x_message],
            (keep, got, own_wind, got_wind, lost),
            micros=0.2,
        )
    else:
        split = bin_mass.reshape(nx, ny, nz // ROWS, ROWS, parts, width).transpose(4, 0, 1, 3, 2, 5)
        split = lax.all_to_all(split, "gz", split_axis=0, concat_axis=0, tiled=True)
        cube = split.transpose(1, 2, 3, 0, 4, 5).reshape(n, n, ROWS, LANES)
        air = courant.reshape(3, nx, ny, nz // ROWS, ROWS).transpose(0, 4, 3, 1, 2) * (1.0 / 12.0)
        air = lax.all_gather(air, "gz").reshape(parts, 3, ROWS, nz // ROWS, tiles, nx // tiles, ny)
        air = air.transpose(1, 4, 2, 0, 3, 5, 6).reshape(3, tiles, ROWS, LANES)
        block = jnp.concatenate([cube.reshape(-1, LANES), air.reshape(-1, LANES)])
        halves = [air[:, : tiles // 2], air[:, tiles // 2 :]]
        near = jnp.arange(LANES) % ROWS < ROWS // 2
        low_y = jnp.where(near, halves[0], jnp.roll(halves[1], ROWS // 2, axis=-1))
        high_y = jnp.where(near, jnp.roll(halves[0], -(ROWS // 2), axis=-1), halves[1])
        messages = []
        for layers, low_air, high_air, message, even in (
            (cube.transpose(1, 0, 2, 3), low_y, high_y, y_message, gy % 2 == 0),
            (cube, *halves, x_message, lax.axis_index("gx") % 2 == 0),
        ):
            up, down = layers[n - PAD_LO :], layers[:PAD_HI]
            if message is y_message:
                up, down = up.transpose(1, 0, 2, 3), down.transpose(1, 0, 2, 3)
            up = jnp.concatenate([up.reshape(-1, LANES), high_air.reshape(-1, LANES)])
            down = jnp.concatenate([down.reshape(-1, LANES), low_air.reshape(-1, LANES)])
            messages += order(up, jnp.pad(down, ((0, up.shape[0] - down.shape[0]), (0, 0))), even)

    from_y = swap_neighbours("gy", 0, messages[0]), swap_neighbours("gy", 1, messages[1])
    from_x = swap_neighbours("gx", 1, messages[3]), swap_neighbours("gx", 0, messages[2])
    wind_x, wind_y, wind_z, own_change, edge_x, edge_y = call(
        functools.partial(own_kernel, n, parts), [tiles_of(n * n)] * 4 + [tiles_of(2 * n)] * 2, (block,), micros=1.6
    )
    message = tiles_of(LO * LINES + 2 + tiles)
    corners = call(functools.partial(corner_kernel, n, parts), (message, message), (*from_y, own_change), micros=0.1)
    corners = swap_neighbours("gx", 1, corners[1]), swap_neighbours("gx", 0, corners[0])
    cell, change, halo_wind_x, far_wind_y = call(
        functools.partial(y_kernel, n, parts),
        [tiles_of(n * (n + PAD_LO + PAD_HI)), tiles_of(n * (n + LINES)), tiles_of(LINES * n), tiles_of(n * (LINES + 2))],
        (block, *from_y, wind_y, own_change, edge_y),
        [tiles_of(LINES * n)] * 2,
        micros=2.0,
    )
    reach, inner = n + LINES, n - LINES
    near = call(
        functools.partial(inner_kernel, n, parts),
        [tiles_of(inner * reach), tiles_of(2 * reach), tiles_of(inner * n)],
        (cell, change, halo_wind_x, wind_y, far_wind_y, wind_z, edge_x),
        micros=0.9,
    )
    mid, far_wind_x, side, side_wind_y, side_edge = call(
        functools.partial(x_kernel, n, parts),
        [tiles_of(count) for count in (reach * n, (LINES + 2) * n, LINES * n, LINES * n, 2 * LINES)],
        (cell, change, wind_x, near[1], *from_x),
        [tiles_of(LINES * n)] * 3,
        micros=1.7,
    )
    fall = sub_courant.reshape(1, bins), fall_steps.reshape(1, bins)

    def fallen(count):
        if parts == 2:
            return [tiles_of(n * count // 2 + (count + 3) // 4)] * 2
        return [tiles_of(n * count), tiles_of(count)]

    one, *early = call(
        functools.partial(main_kernel, n, parts),
        [tiles_of(reach * reach)] + fallen(EARLY),
        (
            *(cell, change, wind_x, wind_y, wind_z, halo_wind_x, far_wind_y, *near),
            *(mid, far_wind_x, side, side_wind_y, side_edge, *corners, *fall),
        ),
        [tiles_of(count) for count in (LINES * LINES, 2 * LINES, 2 * LINES, n * EARLY, n * EARLY)],
        micros=2.6,
    )
    if parts == 2:
        early_got = lax.ppermute(early[0], "gz", [(0, 1), (1, 0)])
    late = call(
        functools.partial(late_kernel, n, parts),
        fallen(n - EARLY),
        (one, cell, wind_x, far_wind_x, wind_y, far_wind_y, wind_z, near[2], *fall),
        [tiles_of(n * (n - EARLY))] * 2,
        micros=0.7,
    )

    def products(count):
        return shape(n * count * ROWS, pair_rows, dtype=jnp.bfloat16)

    if parts == 2:
        late_got = lax.ppermute(late[0], "gz", [(0, 1), (1, 0)])
        early = call(
            functools.partial(breakup_first_kernel, n),
            [shape(EARLY, ny, nz, bins), shape(EARLY, ny // parts, bins)],
            (early[1], early_got, pairs, lost),
            [tiles_of(n * EARLY), products(EARLY)],
            micros=1.8,
        )
        outs = [shape(nx, ny, nz, bins), shape(nx, ny // parts, bins)]
        return tuple(
            call(
                functools.partial(breakup_last_kernel, n),
                outs,
                (late[1], late_got, pairs, lost, *early),
                [tiles_of(n * (n - EARLY)), products(n - EARLY), shape(n - EARLY, ny, nz, bins), outs[1]],
                micros=1.2,
                out_place=pl.ANY,
                copies=3,
            )
        )

    settled, rain = [jnp.concatenate(halves) for halves in zip(early, late)]
    rain = rain.reshape(nx, ny, LANES)[:, :, :width]
    rain = lax.all_to_all(rain, "gz", split_axis=1, concat_axis=2, tiled=True)
    settled = settled.reshape(nx, ny, ROWS, parts, nz // ROWS, width).transpose(3, 0, 1, 4, 2, 5)
    settled = lax.all_to_all(settled, "gz", split_axis=0, concat_axis=0, tiled=True)
    settled = settled.transpose(1, 2, 3, 4, 0, 5).reshape(nx * ny, nz // ROWS, ROWS, bins)
    paired = settled.transpose(0, 2, 1, 3).reshape(-1, LANES)
    updated = call(breakup_plain_kernel, tiles_of(n * n), (paired, pairs, lost), [products(n // 2)], micros=3.0)
    updated = updated.reshape(nx, ny, ROWS, nz // ROWS, bins).transpose(0, 1, 3, 2, 4).reshape(nx, ny, nz, bins)
    return updated, rain


def solution(mesh):
    in_specs = (P("gx", "gy", "gz", None), P(None, "gx", "gy", "gz"), P(), P(), P(), P())
    out_specs = (P("gx", "gy", "gz", None), P("gx", ("gy", "gz"), None))
    return jax.shard_map(per_device, mesh=mesh, in_specs=in_specs, out_specs=out_specs, check_vma=False)
```

```python
import functools
import itertools

import jax
import jax.numpy as jnp
from jax import lax
from jax.experimental import pallas as pl
from jax.experimental.pallas import tpu as pltpu
from jax.sharding import PartitionSpec as P

SUBS = 24
EPS = 1e-06
LO, HI = 3, 2
PAD_LO, PAD_HI = 2 * LO, 2 * HI
LINES = LO + HI
ROWS, LANES = 8, 128
AHEAD = 4
EARLY = 5
F32 = jnp.float32
VMEM = pl.BlockSpec(memory_space=pltpu.VMEM)


def lane_ids():
    return lax.broadcasted_iota(jnp.int32, (ROWS, LANES), 1)


def pick(tile, ids):
    return jnp.take_along_axis(tile, ids, axis=1, mode="promise_in_bounds")


def turn(tile, lanes):
    lanes %= LANES
    return pltpu.roll(tile, lanes, 1) if lanes else tile


def rows_of(first, count=1):
    return pl.ds(first * ROWS, count * ROWS)


def eight(first, level, step=1):
    return pl.ds(first * ROWS + level, ROWS, stride=step * ROWS)


def order(a, b, straight):
    return jnp.where(straight, a, b), jnp.where(straight, b, a)


def is_even(axis):
    return lax.axis_index(axis) % 2 == 0


def by_quarter(parts):
    quarter = lane_ids() // (LANES // 4)
    return jnp.where(quarter < 2, jnp.where(quarter == 0, parts[0], parts[1]), jnp.where(quarter == 2, parts[2], parts[3]))


def groups(parts):
    width = LANES // (2 * parts)
    return width, width // ROWS, ROWS * ROWS // width


def spread(jobs, parts):
    width = groups(parts)[0]
    place = lane_ids() % width
    rows = [[], []]
    for tile, lane, _, _ in jobs:
        top = tile.astype(jnp.bfloat16).astype(F32)
        here = place == lane
        for out, term in zip(rows, (top, tile - top)):
            out.append(jnp.where(here, term, 0.0))
    terms = jnp.concatenate([jnp.concatenate(r, axis=0).astype(jnp.bfloat16) for r in rows], axis=1)
    source, target = [lax.broadcasted_iota(jnp.int32, (2 * LANES, LANES), k) for k in range(2)]
    same = jnp.where(source % LANES // width == target // width, 1.0, 0.0).astype(jnp.bfloat16)
    out = jnp.dot(terms, same, preferred_element_type=F32)
    for k, (_, _, ref, at) in enumerate(jobs):
        ref[rows_of(at)] = out[k * ROWS : (k + 1) * ROWS]


def lane_of(x, y, parts):
    return x % groups(parts)[1] * ROWS + y


def half_lane_of(x, y, parts):
    _, deep, tiles = groups(parts)
    return x % deep * ROWS + x // deep // (tiles // 2) * (ROWS // 2) + y % (ROWS // 2)


def half_tiles(low, high, upper):
    near = lane_ids() % ROWS < ROWS // 2
    if upper:
        return jnp.where(near, turn(low, -(ROWS // 2)), high)
    return jnp.where(near, low, turn(high, ROWS // 2))


def each(count, together, body):
    def some(places):
        stores = [store for i in places for store in body(i)]
        for ref, at, value in stores:
            ref[at] = value

    whole = count // together

    @pl.loop(0, whole)
    def _(i):
        some([i * together + k for k in range(together)])

    if count % together:
        some(range(whole * together, count))


def halo_line(i, n):
    if isinstance(i, int):
        return i - LO + (n if i >= LO else 0)
    return jnp.where(i < LO, i - LO, i - LO + n)


def line_change(cells, winds):
    return changes(line_fluxes(cells, winds))


def changes(fluxes):
    return [a - b for a, b in zip(fluxes, fluxes[1:])]


def long_line(cells, winds, low_edge, high_edge, n):
    begin, end = LO, n - HI
    low = line_fluxes(cells[: PAD_LO + begin + 1], winds[: LO + 1 + begin]) + [low_edge]
    high = [high_edge] + line_fluxes(cells[PAD_LO + end - HI :], winds[LO + 1 + end :])
    return dict(zip(range(-LO, begin), changes(low))) | dict(zip(range(end, n + HI), changes(high)))


def line_fluxes(cells, winds):
    first = [b - a for a, b in zip(cells, cells[1:])]
    twice = [d + d for d in first]
    second = [b - a for a, b in zip(first, first[1:])]
    third = [a - b for a, b in zip(second, second[1:])]
    curved = [(13.0 / 3.0) * (c * c) + 4.0 * EPS for c in second]
    fluxes = []
    for j in range(len(cells) - 4):
        left = twice[j + 1] + second[j]
        mid = first[j + 1] + first[j + 2]
        right = twice[j + 2] - second[j + 2]
        e0 = curved[j] + left * left
        e1 = curved[j + 1] + mid * mid
        e2 = curved[j + 2] + right * right
        e0 = 3.0 * (e0 * e0)
        e1 = e1 * e1
        e2 = e2 * e2
        e2_twice = e2 + e2
        top = e1 * (e2_twice * third[j] + e0 * third[j + 1])
        inverse = pl.reciprocal(e1 * (e2 + e0) + e0 * e2_twice, approx=True)
        estimate = 6.0 * cells[j + 2] + (first[j + 1] + twice[j + 2]) + top * inverse
        fluxes.append((winds[j] + winds[j + 1]) * estimate)
    return fluxes


def from_below(value, width):
    return jnp.where(lane_ids() < width, 0.0, turn(value, width))


def from_above(value, width):
    return jnp.where(lane_ids() >= LANES - width, 0.0, turn(value, -width))


def level_change(cells, winds, width):
    long_cells = [from_below(v, width) for v in cells[ROWS - LO :]] + cells + [from_above(v, width) for v in cells[:HI]]
    long_winds = [from_below(winds[-1], width)] + winds + [from_above(winds[0], width)]
    return line_change(long_cells, long_winds)


def pack_kernel(mass_ref, send_ref, keep_ref):
    lower = is_even("gz")
    n = mass_ref.shape[0]
    zero = jnp.zeros((ROWS, LANES // 2), F32)
    for x in range(n // 2):
        for y in range(n):
            tiles = [
                jnp.concatenate([mass_ref[xx, y, z : z + ROWS], zero], axis=1) for xx in (x, x + n // 2) for z in (0, ROWS)
            ]
            low = by_quarter([turn(v, 32 * k) for k, v in enumerate(tiles)])
            high = by_quarter([turn(v, 32 * k - 32) for k, v in enumerate(tiles)])
            at = rows_of(x * n + y)
            keep_ref[at], send_ref[at] = order(low, high, lower)


def wind_kernel(wind_ref, keep_ref, out_ref):
    del keep_ref
    n = wind_ref.shape[1]
    for d in range(3):
        levels = wind_ref[d].reshape(n * n, 2 * ROWS).T * (1.0 / 12.0)
        out_ref[rows_of(d)] = jnp.concatenate([levels[:ROWS], levels[ROWS:]], axis=1)


def sides(axis, first_ref, second_ref):
    even, place = is_even(axis), lax.axis_index(axis)
    inner_low, inner_high = place > 0, place < lax.axis_size(axis) - 1

    def below(at):
        return jnp.where(inner_low, jnp.where(even, second_ref[at], first_ref[at]), 0.0)

    def above(at):
        return jnp.where(inner_high, jnp.where(even, first_ref[at], second_ref[at]), 0.0)

    return below, above


def by_parity(axis, body):
    even = is_even(axis)
    pl.when(even)(lambda: body(0, 1))
    pl.when(jnp.logical_not(even))(lambda: body(1, 0))


def merge_kernel(keep_ref, got_ref, own_wind_ref, got_wind_ref, lost_ref, block_ref, y_first, y_second, x_first, x_second):
    del lost_ref
    n = 8
    lower = is_even("gz")
    low = lane_ids() < 64
    for x in range(n // 2):
        for y in range(n):
            at = rows_of(x * n + y)
            a, b = order(keep_ref[at], got_ref[at], lower)
            block_ref[at] = jnp.where(low, a, turn(b, 64))
            block_ref[rows_of((x + n // 2) * n + y)] = jnp.where(low, turn(a, 64), b)
    for d in range(3):
        a, b = order(own_wind_ref[rows_of(d)], got_wind_ref[rows_of(d)], lower)
        block_ref[rows_of(n * n + 2 * d)] = by_quarter([a, turn(a, -32), turn(b, 64), turn(b, 32)])
        block_ref[rows_of(n * n + 2 * d + 1)] = by_quarter([turn(a, -32), turn(a, -64), turn(b, 32), b])

    def along_y(up, down):
        for ref, start, wide in (((y_first, y_second)[up], n - PAD_LO, PAD_LO), ((y_first, y_second)[down], 0, PAD_HI)):
            for x in range(n):
                ref[rows_of(x * wide, wide)] = block_ref[rows_of(x * n + start, wide)]
            for d in range(3):
                low, high = [block_ref[rows_of(n * n + 2 * d + k)] for k in range(2)]
                ref[rows_of(n * wide + d)] = half_tiles(low, high, wide == PAD_LO)

    def along_x(up, down):
        for ref, start, wide, part in (((x_first, x_second)[up], n - PAD_LO, PAD_LO, 1), ((x_first, x_second)[down], 0, PAD_HI, 0)):
            ref[rows_of(0, wide * n)] = block_ref[rows_of(start * n, wide * n)]
            for d in range(3):
                ref[rows_of(wide * n + d)] = block_ref[rows_of(n * n + 2 * d + part)]

    by_parity("gy", along_y)
    by_parity("gx", along_x)


def corner_kernel(n, parts, first_ref, second_ref, own_change, *messages):
    del own_change
    tiles = groups(parts)[2]
    half = tiles // 2
    below, above = sides("gy", first_ref, second_ref)

    def body(up, down):
        for ref, start, narrow, part in ((messages[up], n - LO, LO, half), (messages[down], 0, HI, 0)):
            at = 0
            for x in range(start, start + narrow):
                ref[rows_of(at, LO)] = below(rows_of(x * PAD_LO + PAD_LO - LO, LO))
                ref[rows_of(at + LO, HI)] = above(rows_of(x * PAD_HI, HI))
                at += LINES
            for side, base in ((below, n * PAD_LO), (above, n * PAD_HI)):
                ref[rows_of(at)] = side(rows_of(base + (half - 1 if part else 0)))
                ref[rows_of(at + 1, half)] = side(rows_of(base + half, half))
                at += 1 + half

    by_parity("gx", body)


def own_kernel(n, parts, block_ref, wind_x, wind_y, wind_z, change, edge_x, edge_y):
    width, deep, tiles = groups(parts)
    for d, out in enumerate((wind_x, wind_y, wind_z)):
        jobs = []
        for x in range(n):
            tile = block_ref[rows_of(n * n + d * tiles + x // deep)]
            jobs += [(tile, lane_of(x, y, parts), out, x * n + y) for y in range(n)]
        spread(jobs, parts)

    def along_z(x):
        cells = [block_ref[eight(x * n, k)] for k in range(ROWS)]
        winds = [wind_z[eight(x * n, k)] for k in range(ROWS)]
        return [(change, eight(x * n, k), value) for k, value in enumerate(level_change(cells, winds, width))]

    each(n, 4, along_z)
    begin, end = LO, n - HI
    for wind, edge, place in ((wind_x, edge_x, lambda i, k: k * n + i), (wind_y, edge_y, lambda i, k: i * n + k)):

        def along(i):
            cells = [block_ref[rows_of(place(i, k))] for k in range(n)]
            fluxes = line_fluxes(cells, [wind[rows_of(place(i, k))] for k in range(begin - 1, end + 1)])
            at = [rows_of(place(i, k)) for k in range(begin, end)]
            stores = [(change, here, change[here] + value) for here, value in zip(at, changes(fluxes))]
            return stores + [(edge, rows_of(i), fluxes[0]), (edge, rows_of(n + i), fluxes[-1])]

        each(n, 4, along)


def y_kernel(n, parts, block_ref, first_ref, second_ref, wind_y, own_change, edge_y, *refs):
    width, deep, tiles = groups(parts)
    cell, change, wind_x, far_y, wind_z, halo_change = refs
    below, above = sides("gy", first_ref, second_ref)
    span, reach = n + PAD_LO + PAD_HI, n + LINES

    for x in range(n):
        cell[rows_of(x * span, PAD_LO)] = below(rows_of(x * PAD_LO, PAD_LO))
        cell[rows_of(x * span + PAD_LO, n)] = block_ref[rows_of(x * n, n)]
        cell[rows_of(x * span + PAD_LO + n, PAD_HI)] = above(rows_of(x * PAD_HI, PAD_HI))
    jobs = []
    half = tiles // 2
    for d in range(3):
        for t in range(half):
            low, high = below(rows_of(n * PAD_LO + d * half + t)), above(rows_of(n * PAD_HI + d * half + t))
            for x in [x for x in range(n) if x // deep % half == t]:
                lanes = [half_lane_of(x, y, parts) for y in range(n)]
                if d == 1:
                    jobs += [(low, lanes[n - LO - 1 + y], far_y, x * (LINES + 2) + y) for y in range(LO + 1)]
                    jobs += [(high, lanes[y], far_y, x * (LINES + 2) + LO + 1 + y) for y in range(HI + 1)]
                else:
                    out = wind_z if d else wind_x
                    jobs += [(low, lanes[n - LO + y], out, y * n + x) for y in range(LO)]
                    jobs += [(high, lanes[y], out, (LO + y) * n + x) for y in range(HI)]
    spread(jobs, parts)

    def along_z(i):
        first = halo_line(i, n) + PAD_LO
        cells = [cell[eight(first, k, span)] for k in range(ROWS)]
        winds = [wind_z[eight(i * n, k)] for k in range(ROWS)]
        return [(halo_change, eight(i * n, k), value) for k, value in enumerate(level_change(cells, winds, width))]

    each(LINES, LINES, along_z)

    def along_y(x):
        cells = [cell[rows_of(x * span + y)] for y in range(span)]
        far = [far_y[rows_of(x * (LINES + 2) + y)] for y in range(LINES + 2)]
        winds = far[: LO + 1] + [wind_y[rows_of(x * n + y)] for y in range(n)] + far[LO + 1 :]
        stores = []
        for y, value in long_line(cells, winds, edge_y[rows_of(x)], edge_y[rows_of(n + x)], n).items():
            if 0 <= y < n:
                value = value + own_change[rows_of(x * n + y)]
            else:
                value = value + halo_change[rows_of((y + LO if y < 0 else y + LO - n) * n + x)]
            stores.append((change, rows_of(x * reach + y + LO), value))
        for y in range(LO, n - HI):
            stores.append((change, rows_of(x * reach + y + LO), own_change[rows_of(x * n + y)]))
        return stores

    each(n, 4, along_y)


def which(i, lower, upper):
    if isinstance(i, int):
        return lower if i < LO else upper
    return jnp.where(i < LO, lower, upper)


def inside(axis):
    place = lax.axis_index(axis)
    return [jnp.where(ok, 1.0, 0.0) for ok in (place > 0, place < lax.axis_size(axis) - 1)]


def inner_kernel(n, parts, cell, change, halo_wind_x, wind_y, far_wind_y, wind_z, edge_x, one, edge, second):
    width = groups(parts)[0]
    span, reach = n + PAD_LO + PAD_HI, n + LINES
    begin, end = LO, n - HI
    south_in, north_in = inside("gy")

    for k in range(2):
        edge[rows_of(k * reach + LO, n)] = edge_x[rows_of(k * n, n)]
    for i in range(end - begin):
        x = begin + i
        one[rows_of(i * reach + LO, n)] = cell[rows_of(x * span + PAD_LO, n)] + change[rows_of(x * reach + LO, n)]

    def along_x(i):
        at = halo_line(i, n) + LO
        cells = [cell[rows_of(x * span + LO + at)] for x in range(n)]
        fluxes = line_fluxes(cells, [halo_wind_x[rows_of(i * n + x)] for x in range(begin - 1, end + 1)])
        keep = which(i, south_in, north_in)
        stores = [(edge, rows_of(at), fluxes[0]), (edge, rows_of(reach + at), fluxes[-1])]
        for k, value in enumerate(changes(fluxes)):
            x = begin + k
            value = (cells[x] + (value + change[rows_of(x * reach + at)])) * keep
            stores.append((one, rows_of(k * reach + at), value))
        return stores

    each(LINES, LINES, along_x)
    second_y_z(n, width, range(begin, end), begin, one, begin, wind_y, far_wind_y, wind_z, second)


def second_y_z(n, width, layers, first, one, one_first, wind_y, far_wind_y, wind_z, second):
    reach = n + LINES

    def along_y(i):
        x = layers[0] + i
        cells = [one[rows_of((x - one_first) * reach + y)] for y in range(reach)]
        winds = [far_wind_y[rows_of(x * (LINES + 2) + LO)]] + [wind_y[rows_of(x * n + y)] for y in range(n)]
        winds += [far_wind_y[rows_of(x * (LINES + 2) + LO + 1)]]
        return [(second, rows_of((x - first) * n + y), value) for y, value in enumerate(line_change(cells, winds))]

    def along_z(i):
        x = layers[0] + i
        cells = [one[eight((x - one_first) * reach + LO, k)] for k in range(ROWS)]
        winds = [wind_z[eight(x * n, k)] for k in range(ROWS)]
        at = [eight((x - first) * n, k) for k in range(ROWS)]
        return [(second, here, second[here] + value) for here, value in zip(at, level_change(cells, winds, width))]

    each(len(layers), len(layers), along_y)
    each(len(layers), len(layers), along_z)


def x_kernel(
    n, parts, cell, change, wind_x, inner, edge, inner_second, second_ref, first_ref,
    mid, far_wind_x, side, side_wind_y, side_edge, ready_second, second_edge, *scratch
):
    far, side_wind_z, side_change = scratch
    width, deep, tiles = groups(parts)
    half = tiles // 2
    west, east = sides("gx", first_ref, second_ref)
    span, reach = n + PAD_LO + PAD_HI, n + LINES

    jobs = []
    for take, wide, near_from, far_from, line in ((west, PAD_LO, LO, 0, 0), (east, PAD_HI, 0, HI, LO)):
        narrow = wide // 2
        side[rows_of(line * n, narrow * n)] = take(rows_of(near_from * n, narrow * n))
        far[rows_of(line * n, narrow * n)] = take(rows_of(far_from * n, narrow * n))
        layers, shift = (range(n - narrow, n), half) if line == 0 else (range(narrow), 0)
        wider = range(n - narrow - 1, n) if line == 0 else range(narrow + 1)

        def winds_of(d, x):
            return take(rows_of(wide * n + d * half + x // deep - shift))

        for i, x in enumerate(wider):
            jobs += [(winds_of(0, x), lane_of(x, y, parts), far_wind_x, (line + bool(line) + i) * n + y) for y in range(n)]
        for d, out in ((1, side_wind_y), (2, side_wind_z)):
            for i, x in enumerate(layers):
                jobs += [(winds_of(d, x), lane_of(x, y, parts), out, (line + i) * n + y) for y in range(n)]
    spread(jobs, parts)

    def along_z(i):
        cells = [side[eight(i * n, k)] for k in range(ROWS)]
        winds = [side_wind_z[eight(i * n, k)] for k in range(ROWS)]
        return [(side_change, eight(i * n, k), value) for k, value in enumerate(level_change(cells, winds, width))]

    each(LINES, LINES, along_z)
    begin, end = LO, n - HI

    def along_y(i):
        cells = [side[rows_of(i * n + y)] for y in range(n)]
        fluxes = line_fluxes(cells, [side_wind_y[rows_of(i * n + y)] for y in range(begin - 1, end + 1)])
        at = [rows_of(i * n + y) for y in range(begin, end)]
        stores = [(side_change, here, side_change[here] + value) for here, value in zip(at, changes(fluxes))]
        return stores + [(side_edge, rows_of(i), fluxes[0]), (side_edge, rows_of(LINES + i), fluxes[-1])]

    each(LINES, LINES, along_y)

    def along_x(y):
        outer = [far[rows_of(i * n + y)] for i in range(LINES)]
        near = [side[rows_of(i * n + y)] for i in range(LINES)]
        cells = outer[:LO] + near[:LO] + [cell[rows_of(x * span + PAD_LO + y)] for x in range(n)] + near[LO:] + outer[LO:]
        winds = [far_wind_x[rows_of(i * n + y)] for i in range(LINES + 2)]
        winds = winds[: LO + 1] + [wind_x[rows_of(x * n + y)] for x in range(n)] + winds[LO + 1 :]
        stores = []
        for x, value in long_line(cells, winds, edge[rows_of(LO + y)], edge[rows_of(reach + LO + y)], n).items():
            if 0 <= x < n:
                value = value + change[rows_of(x * reach + LO + y)]
            else:
                value = value + side_change[rows_of((x + LO if x < 0 else x + LO - n) * n + y)]
            stores.append((mid, rows_of((x + LO) * n + y), cells[PAD_LO + x] + value))
        return stores

    each(n, 4, along_x)

    def second_x(y):
        cells = [mid[rows_of((x + LO) * n + y)] for x in range(begin)]
        cells += [inner[rows_of(i * reach + LO + y)] for i in range(end - begin)]
        cells += [mid[rows_of((x + LO) * n + y)] for x in range(end, n)]
        fluxes = line_fluxes(cells, [wind_x[rows_of(x * n + y)] for x in range(begin - 1, end + 1)])
        at = [rows_of(i * n + y) for i in range(end - begin)]
        stores = [(ready_second, here, inner_second[here] + value) for here, value in zip(at, changes(fluxes))]
        return stores + [(second_edge, rows_of(y), fluxes[0]), (second_edge, rows_of(n + y), fluxes[-1])]

    each(n, 4, second_x)


def main_kernel(n, parts, *refs):
    cell, change, wind_x, wind_y, wind_z, halo_wind_x, far_wind_y, inner, edge = refs[:9]
    mid, far_wind_x, side, side_wind_y, side_edge, inner_second, second_edge = refs[9:16]
    second_ref, first_ref, rate_ref, steps_ref, one, *out_refs = refs[16:23]
    corner, corner_wind_x, edge_wind_y, second, fallen = refs[23:]
    deep, tiles = groups(parts)[1:]
    half = tiles // 2
    west, east = sides("gx", first_ref, second_ref)
    span, reach = n + PAD_LO + PAD_HI, n + LINES

    jobs = []
    for take, narrow, line in ((west, LO, 0), (east, HI, LO)):
        at = narrow * LINES
        corner[rows_of(line * LINES, at)] = take(rows_of(0, at))
        below, above = at, at + 1 + half
        layers = range(n - narrow, n) if line == 0 else range(narrow)
        for y in range(LINES):
            tile = take(rows_of(below if y < LO else above))
            x = layers[-1] if line == 0 else layers[0]
            lane = half_lane_of(x, n - LO + y if y < LO else y - LO, parts)
            jobs.append((tile, lane, corner_wind_x, bool(line) * LINES + y))
        for i, x in enumerate(layers):
            tile = x // deep % half
            for k, (base, y) in enumerate(((below, n - 1), (above, 0))):
                lane = half_lane_of(x, y, parts)
                jobs.append((take(rows_of(base + 1 + tile)), lane, edge_wind_y, 2 * (line + i) + k))
    spread(jobs, parts)

    west_in, east_in = inside("gx")
    south_in, north_in = inside("gy")
    begin, end = LO, n - HI
    one[rows_of((begin + LO) * reach, (end - begin) * reach)] = inner[...]
    for x in [x for x in range(n) if not begin <= x < end]:
        one[rows_of((x + LO) * reach + LO, n)] = mid[rows_of((x + LO) * n, n)]

    def along_y(i):
        corners = [corner[rows_of(i * LINES + y)] for y in range(LINES)]
        cells = corners[:LO] + [side[rows_of(i * n + y)] for y in range(n)] + corners[LO:]
        winds = [side_wind_y[rows_of(i * n + y)] for y in range(n)]
        winds = [edge_wind_y[rows_of(2 * i)]] + winds + [edge_wind_y[rows_of(2 * i + 1)]]
        low = line_fluxes(cells[: LO + begin + 1], winds[: begin + 1]) + [side_edge[rows_of(i)]]
        high = [side_edge[rows_of(LINES + i)]] + line_fluxes(cells[LO + end - HI :], winds[end + 1 :])
        values = dict(zip(range(begin), changes(low))) | dict(zip(range(end, n), changes(high)))
        line, keep = halo_line(i, n) + LO, which(i, west_in, east_in)
        stores = []
        for y in range(n):
            value = mid[rows_of(line * n + y)]
            value = value + values[y] if y in values else value
            stores.append((one, rows_of(line * reach + LO + y), value * keep))
        return stores

    def along_x(i):
        line = halo_line(i, n) + LO
        near = [corner[rows_of(k * LINES + i)] for k in range(LINES)]
        cells = near[:LO] + [cell[rows_of(x * span + LO + line)] for x in range(n)] + near[LO:]
        winds = [halo_wind_x[rows_of(i * n + x)] for x in range(n)]
        winds = [corner_wind_x[rows_of(i)]] + winds + [corner_wind_x[rows_of(LINES + i)]]
        low = line_fluxes(cells[: LO + begin + 1], winds[: begin + 1]) + [edge[rows_of(line)]]
        high = [edge[rows_of(reach + line)]] + line_fluxes(cells[LO + end - HI :], winds[end + 1 :])
        values = dict(zip(range(begin), changes(low))) | dict(zip(range(end, n), changes(high)))
        stores = []
        for x, value in values.items():
            value = (cells[x + LO] + (value + change[rows_of(x * reach + line)])) * which(i, south_in, north_in)
            stores.append((one, rows_of((x + LO) * reach + line), value))
        return stores

    each(LINES, LINES, along_y)
    each(LINES, LINES, along_x)
    fall_layers(
        n, parts, 0, EARLY, one, cell, wind_x, far_wind_x, wind_y, far_wind_y, wind_z, inner_second, second_edge, rate_ref, steps_ref,
        out_refs, second, fallen,
    )


def late_kernel(
    n, parts, one, cell, wind_x, far_wind_x, wind_y, far_wind_y, wind_z, inner_second, second_edge, rate_ref, steps_ref, *refs
):
    fall_layers(
        n, parts, EARLY, n, one, cell, wind_x, far_wind_x, wind_y, far_wind_y, wind_z, inner_second, second_edge, rate_ref, steps_ref,
        refs[:2], *refs[2:],
    )


def fall_layers(
    n, parts, begin, end, one, cell, wind_x, far_wind_x, wind_y, far_wind_y, wind_z, inner_second, second_edge, rate_ref, steps_ref,
    out_refs, second, fallen,
):
    width = groups(parts)[0]
    span, reach, count = n + PAD_LO + PAD_HI, n + LINES, end - begin
    ready = [x for x in range(LO, n - HI) if begin <= x < end]
    left = [x for x in range(begin, end) if x not in ready]
    if ready:
        second[rows_of((ready[0] - begin) * n, len(ready) * n)] = inner_second[rows_of((ready[0] - LO) * n, len(ready) * n)]

    second_y_z(n, width, left, begin, one, -LO, wind_y, far_wind_y, wind_z, second)

    def along_x(y):
        values = {}
        if begin == 0:
            cells = [one[rows_of((x + LO) * reach + LO + y)] for x in range(-LO, LO + 1)]
            winds = [far_wind_x[rows_of(LO * n + y)]] + [wind_x[rows_of(x * n + y)] for x in range(LO)]
            fluxes = line_fluxes(cells, winds) + [second_edge[rows_of(y)]]
            values |= zip(range(LO), changes(fluxes))
        if end == n:
            cells = [one[rows_of((x + LO) * reach + LO + y)] for x in range(n - 2 * HI, n + HI)]
            winds = [wind_x[rows_of(x * n + y)] for x in range(n - HI, n)] + [far_wind_x[rows_of((LO + 1) * n + y)]]
            fluxes = [second_edge[rows_of(n + y)]] + line_fluxes(cells, winds)
            values |= zip(range(n - HI, n), changes(fluxes))
        stores = []
        for x in range(begin, end):
            at = rows_of((x - begin) * n + y)
            value = second[at] + values[x] if x in values else second[at]
            value = one[rows_of((x + LO) * reach + LO + y)] + value
            value = 0.5 * cell[rows_of(x * span + PAD_LO + y)] + 0.5 * value
            stores.append((fallen, at, value))
        return stores

    each(n, 4, along_x)

    bins = LANES // 2 // parts
    ids = lax.axis_index("gz") * bins + lane_ids() % bins
    rates, steps = [
        pick(jnp.broadcast_to(jnp.concatenate([ref[...]] * 2, axis=1), (ROWS, LANES)), ids) for ref in (rate_ref, steps_ref)
    ]

    rain = []
    for some in [range(count)]:
        columns = [[fallen[eight(i * n, k)] for k in range(ROWS)] for i in some]
        drops = [jnp.zeros((ROWS, LANES), F32) for _ in some]
        for block in range(SUBS // AHEAD):
            columns = [column + [from_above(v, width) for v in column[:AHEAD]] for column in columns]
            for s in range(AHEAD):
                rate = jnp.where(block * AHEAD + s < steps, rates, 0.0)
                for i, column in enumerate(columns):
                    drops[i] = drops[i] + rate * column[0]
                    columns[i] = [v + rate * (u - v) for v, u in zip(column, column[1:])]
        for i, column in zip(some, columns):
            for k in range(ROWS):
                fallen[eight(i * n, k)] = column[k]
        rain += drops

    if parts == 2:
        send_ref, keep_ref = out_refs
        lower = is_even("gz")
        low = lane_ids() < 64
        half = count * n // 2
        for c in range(half):
            a, b = fallen[rows_of(c)], fallen[rows_of(half + c)]
            at = rows_of(c)
            keep_ref[at], send_ref[at] = order(jnp.where(low, a, turn(b, 64)), jnp.where(low, turn(a, 64), b), lower)
        for j in range(0, count, 4):
            four = (rain[j : j + 4] + rain[j:] * 3)[:4]
            value = by_quarter([turn(v, 32 * i) for i, v in enumerate(four)])
            keep_ref[rows_of(half + j // 4)] = value
            send_ref[rows_of(half + j // 4)] = value
    else:
        settled_ref, rain_ref = out_refs
        settled_ref[...] = fallen[...]
        for i in range(count):
            rain_ref[rows_of(i)] = rain[i]


def matrix_kernel(bins, gain_ref, loss_ref, pairs_ref, lost_ref, wide, tall):
    zero = jnp.zeros((bins, LANES - bins), F32)
    shifts = bins // 2

    @pl.loop(0, bins)
    def _(i):
        rows = gain_ref[pl.ds(i * bins, bins)].astype(F32)
        rows = jnp.concatenate([rows, zero], axis=1)
        wide[pl.ds(i * 2 * bins, bins)] = rows
        wide[pl.ds(i * 2 * bins + bins, bins)] = rows
        tall[pl.ds(i * bins, bins)] = rows

        @pl.when(i < shifts)
        def _():
            tall[pl.ds((i + bins) * bins, bins)] = rows

    for d in range(shifts + 1):
        rows = wide[pl.ds(d, bins, stride=2 * bins + 1)]
        if 0 < d < shifts:
            rows = rows + tall[pl.ds(d * bins, bins, stride=bins + 1)]
        pairs_ref[pl.ds(d * LANES, bins)] = rows.astype(jnp.bfloat16)
        pairs_ref[pl.ds(d * LANES + bins, bins)] = pltpu.roll(rows, bins, 1).astype(jnp.bfloat16)
    rows = jnp.concatenate([loss_ref[...].astype(F32), zero], axis=1)
    lost_ref[pl.ds(0, bins)] = rows.astype(jnp.bfloat16)
    lost_ref[pl.ds(bins, bins)] = pltpu.roll(rows, bins, 1).astype(jnp.bfloat16)


def breakup_rows(mass, pairs_ref, lost_ref, products):
    bins = LANES // 2
    count = mass.shape[0]
    lanes = lane_ids()
    rounded = mass.astype(jnp.bfloat16)
    wide = rounded.astype(F32)
    gained = None
    shifts = bins // 2 + 1
    for begin in range(0, shifts, 4):
        end = min(begin + 4, shifts)
        for d in range(begin, end):
            ids = lanes // bins * bins + (lanes + d) % bins
            for r in range(0, count, 2 * ROWS):
                halves = [wide[r + ROWS * k : r + ROWS * (k + 1)] for k in range(2)]
                halves = [v * pick(v, ids) if d else v * v for v in halves]
                both = jnp.concatenate(halves, axis=0).astype(jnp.bfloat16)
                products[pl.ds(r, 2 * ROWS), d * LANES : (d + 1) * LANES] = both
        part = jnp.dot(
            products[pl.ds(0, count), begin * LANES : end * LANES],
            pairs_ref[pl.ds(begin * LANES, (end - begin) * LANES)],
            preferred_element_type=F32,
        )
        gained = part if gained is None else gained + part
    loss = jnp.dot(rounded, lost_ref[...], preferred_element_type=F32)
    return mass + gained - mass * loss


def breakup_layers(n, count, keep_ref, got_ref, pairs_ref, lost_ref, columns, products):
    first = is_even("gz")
    half = count * n // 2
    for c in range(half):
        a, b = order(keep_ref[rows_of(c)], got_ref[rows_of(c)], first)
        columns[rows_of(c)] = by_quarter([a, turn(b, 32), turn(a, 32), turn(b, 64)])
        columns[rows_of(half + c)] = by_quarter([turn(a, -64), turn(b, -32), turn(a, -32), b])
    rain = []
    for i in range(count):
        a, b = order(keep_ref[rows_of(half + i // 4)], got_ref[rows_of(half + i // 4)], first)
        a, b = [jnp.where(first, v[: n // 2], v[n // 2 :])[:, 32 * (i % 4) : 32 * (i % 4) + 32] for v in (a, b)]
        rain.append(jnp.concatenate([a, b], axis=1))
    columns[...] = breakup_rows(columns[...], pairs_ref, lost_ref, products)
    return rain


def lay_out(columns, mass, n, count):
    for x in range(count):
        for y in range(n):
            value = columns[rows_of(x * n + y)]
            mass[x, y, 0:ROWS] = value[:, :64]
            mass[x, y, ROWS : 2 * ROWS] = value[:, 64:]


def breakup_first_kernel(n, keep_ref, got_ref, pairs_ref, lost_ref, mass_ref, rain_ref, columns, products):
    for i, value in enumerate(breakup_layers(n, EARLY, keep_ref, got_ref, pairs_ref, lost_ref, columns, products)):
        rain_ref[i] = value
    lay_out(columns, mass_ref, n, EARLY)


def breakup_last_kernel(
    n, keep_ref, got_ref, pairs_ref, lost_ref, early, early_rain, mass_out, rain_out, columns, products, mass, rain, sems
):
    early_copy = pltpu.make_async_copy(early, mass_out.at[pl.ds(0, EARLY)], sems.at[0])
    early_copy.start()
    late_rain = breakup_layers(n, n - EARLY, keep_ref, got_ref, pairs_ref, lost_ref, columns, products)
    for i in range(EARLY):
        rain[i] = early_rain[i]
    for i, value in enumerate(late_rain):
        rain[EARLY + i] = value
    rain_copy = pltpu.make_async_copy(rain, rain_out, sems.at[2])
    rain_copy.start()
    lay_out(columns, mass, n, n - EARLY)
    late_copy = pltpu.make_async_copy(mass, mass_out.at[pl.ds(EARLY, n - EARLY)], sems.at[1])
    late_copy.start()
    for copy in (early_copy, rain_copy, late_copy):
        copy.wait()


def breakup_plain_kernel(mass_ref, pairs_ref, lost_ref, out_ref, products):
    count = products.shape[0]

    @pl.loop(0, mass_ref.shape[0] // count)
    def _(i):
        start = pl.multiple_of(i * count, count)
        out_ref[pl.ds(start, count)] = breakup_rows(mass_ref[pl.ds(start, count)], pairs_ref, lost_ref, products)


def shape(*dims, dtype=F32):
    return jax.ShapeDtypeStruct(dims, dtype)


def tiles_of(count):
    return shape(count * ROWS, LANES)


def call(kernel, outs, args, scratch=(), micros=1.0, out_place=pltpu.VMEM, copies=0):
    scratch = [pltpu.VMEM(s.shape, s.dtype) for s in scratch]
    if copies:
        scratch.append(pltpu.SemaphoreType.DMA((copies,)))
    return pl.pallas_call(
        kernel,
        out_shape=outs,
        in_specs=[VMEM] * len(args),
        out_specs=jax.tree.map(lambda _: pl.BlockSpec(memory_space=out_place), outs),
        scratch_shapes=scratch,
        compiler_params=pltpu.CompilerParams(vmem_limit_bytes=40 << 20),
        cost_estimate=pl.CostEstimate(
            flops=int(micros * 1.1e9), bytes_accessed=int(micros * 3.6e6), transcendentals=0
        ),
    )(*args)


def swap_neighbours(axis, begin, message):
    axes = ("gx", "gy", "gz")
    sizes = [lax.axis_size(a) for a in axes]
    along, other = (0, 2) if axis == "gx" else (1, 0)

    def partner(place, start, count):
        to = start + ((place - start) ^ 1)
        return to if start <= place and to < count else place

    index = {place: i for i, place in enumerate(itertools.product(*map(range, sizes)))}
    pairs = []
    for place, i in index.items():
        to = list(place)
        to[along] = partner(place[along], begin, sizes[along])
        if to[along] == place[along]:
            to[other] = partner(place[other], 0, sizes[other])
        pairs.append((i, index[tuple(to)]))
    return lax.ppermute(message, axes, pairs)


def per_device(bin_mass, courant, sub_courant, fall_steps, frag_gain, collide):
    nx, ny, nz, bins = bin_mass.shape
    n = nx
    parts = lax.axis_size("gz")
    gz, gy = lax.axis_index("gz"), lax.axis_index("gy")
    width = bins // parts
    tiles = groups(parts)[2]
    winds = 3 * tiles

    pair_rows = (bins // 2 + 1) * LANES
    pairs, lost = call(
        functools.partial(matrix_kernel, bins),
        (shape(pair_rows, LANES, dtype=jnp.bfloat16), shape(LANES, LANES, dtype=jnp.bfloat16)),
        (frag_gain, collide),
        [shape(2 * bins * bins, LANES), shape(3 * bins * bins // 2, LANES)],
        micros=0.02,
    )

    y_message = tiles_of(n * PAD_LO + winds // 2)
    x_message = tiles_of(n * PAD_LO + winds // 2)
    if parts == 2:
        half = tiles_of(n * n // 2)
        send, keep = call(pack_kernel, (half, half), (bin_mass,), micros=0.3)
        got = lax.ppermute(send, "gz", [(0, 1), (1, 0)])
        own_wind = call(wind_kernel, tiles_of(3), (courant, keep), micros=0.1)
        got_wind = lax.ppermute(own_wind, "gz", [(0, 1), (1, 0)])
        block, *messages = call(
            merge_kernel,
            [tiles_of(n * n + winds), y_message, y_message, x_message, x_message],
            (keep, got, own_wind, got_wind, lost),
            micros=0.2,
        )
    else:
        split = bin_mass.reshape(nx, ny, nz // ROWS, ROWS, parts, width).transpose(4, 0, 1, 3, 2, 5)
        split = lax.all_to_all(split, "gz", split_axis=0, concat_axis=0, tiled=True)
        cube = split.transpose(1, 2, 3, 0, 4, 5).reshape(n, n, ROWS, LANES)
        air = courant.reshape(3, nx, ny, nz // ROWS, ROWS).transpose(0, 4, 3, 1, 2) * (1.0 / 12.0)
        air = lax.all_gather(air, "gz").reshape(parts, 3, ROWS, nz // ROWS, tiles, nx // tiles, ny)
        air = air.transpose(1, 4, 2, 0, 3, 5, 6).reshape(3, tiles, ROWS, LANES)
        block = jnp.concatenate([cube.reshape(-1, LANES), air.reshape(-1, LANES)])
        halves = [air[:, : tiles // 2], air[:, tiles // 2 :]]
        near = jnp.arange(LANES) % ROWS < ROWS // 2
        low_y = jnp.where(near, halves[0], jnp.roll(halves[1], ROWS // 2, axis=-1))
        high_y = jnp.where(near, jnp.roll(halves[0], -(ROWS // 2), axis=-1), halves[1])
        messages = []
        for layers, low_air, high_air, message, even in (
            (cube.transpose(1, 0, 2, 3), low_y, high_y, y_message, gy % 2 == 0),
            (cube, *halves, x_message, lax.axis_index("gx") % 2 == 0),
        ):
            up, down = layers[n - PAD_LO :], layers[:PAD_HI]
            if message is y_message:
                up, down = up.transpose(1, 0, 2, 3), down.transpose(1, 0, 2, 3)
            up = jnp.concatenate([up.reshape(-1, LANES), high_air.reshape(-1, LANES)])
            down = jnp.concatenate([down.reshape(-1, LANES), low_air.reshape(-1, LANES)])
            messages += order(up, jnp.pad(down, ((0, up.shape[0] - down.shape[0]), (0, 0))), even)

    from_y = swap_neighbours("gy", 0, messages[0]), swap_neighbours("gy", 1, messages[1])
    from_x = swap_neighbours("gx", 1, messages[3]), swap_neighbours("gx", 0, messages[2])
    wind_x, wind_y, wind_z, own_change, edge_x, edge_y = call(
        functools.partial(own_kernel, n, parts), [tiles_of(n * n)] * 4 + [tiles_of(2 * n)] * 2, (block,), micros=1.6
    )
    message = tiles_of(LO * LINES + 2 + tiles)
    corners = call(functools.partial(corner_kernel, n, parts), (message, message), (*from_y, own_change), micros=0.1)
    corners = swap_neighbours("gx", 1, corners[1]), swap_neighbours("gx", 0, corners[0])
    cell, change, halo_wind_x, far_wind_y = call(
        functools.partial(y_kernel, n, parts),
        [tiles_of(n * (n + PAD_LO + PAD_HI)), tiles_of(n * (n + LINES)), tiles_of(LINES * n), tiles_of(n * (LINES + 2))],
        (block, *from_y, wind_y, own_change, edge_y),
        [tiles_of(LINES * n)] * 2,
        micros=2.0,
    )
    reach, inner = n + LINES, n - LINES
    near = call(
        functools.partial(inner_kernel, n, parts),
        [tiles_of(inner * reach), tiles_of(2 * reach), tiles_of(inner * n)],
        (cell, change, halo_wind_x, wind_y, far_wind_y, wind_z, edge_x),
        micros=0.9,
    )
    mid, far_wind_x, side, side_wind_y, side_edge, ready_second, second_edge = call(
        functools.partial(x_kernel, n, parts),
        [tiles_of(count) for count in (reach * n, (LINES + 2) * n, LINES * n, LINES * n, 2 * LINES, inner * n, 2 * n)],
        (cell, change, wind_x, *near, *from_x),
        [tiles_of(LINES * n)] * 3,
        micros=1.7,
    )
    fall = sub_courant.reshape(1, bins), fall_steps.reshape(1, bins)

    def fallen(count):
        if parts == 2:
            return [tiles_of(n * count // 2 + (count + 3) // 4)] * 2
        return [tiles_of(n * count), tiles_of(count)]

    one, *early = call(
        functools.partial(main_kernel, n, parts),
        [tiles_of(reach * reach)] + fallen(EARLY),
        (
            *(cell, change, wind_x, wind_y, wind_z, halo_wind_x, far_wind_y, *near[:2]),
            *(mid, far_wind_x, side, side_wind_y, side_edge, ready_second, second_edge, *corners, *fall),
        ),
        [tiles_of(count) for count in (LINES * LINES, 2 * LINES, 2 * LINES, n * EARLY, n * EARLY)],
        micros=2.6,
    )
    if parts == 2:
        early_got = lax.ppermute(early[0], "gz", [(0, 1), (1, 0)])
    late = call(
        functools.partial(late_kernel, n, parts),
        fallen(n - EARLY),
        (one, cell, wind_x, far_wind_x, wind_y, far_wind_y, wind_z, ready_second, second_edge, *fall),
        [tiles_of(n * (n - EARLY))] * 2,
        micros=0.7,
    )

    def products(count):
        return shape(n * count * ROWS, pair_rows, dtype=jnp.bfloat16)

    if parts == 2:
        late_got = lax.ppermute(late[0], "gz", [(0, 1), (1, 0)])
        early = call(
            functools.partial(breakup_first_kernel, n),
            [shape(EARLY, ny, nz, bins), shape(EARLY, ny // parts, bins)],
            (early[1], early_got, pairs, lost),
            [tiles_of(n * EARLY), products(EARLY)],
            micros=1.8,
        )
        outs = [shape(nx, ny, nz, bins), shape(nx, ny // parts, bins)]
        return tuple(
            call(
                functools.partial(breakup_last_kernel, n),
                outs,
                (late[1], late_got, pairs, lost, *early),
                [tiles_of(n * (n - EARLY)), products(n - EARLY), shape(n - EARLY, ny, nz, bins), outs[1]],
                micros=1.2,
                out_place=pl.ANY,
                copies=3,
            )
        )

    settled, rain = [jnp.concatenate(halves) for halves in zip(early, late)]
    rain = rain.reshape(nx, ny, LANES)[:, :, :width]
    rain = lax.all_to_all(rain, "gz", split_axis=1, concat_axis=2, tiled=True)
    settled = settled.reshape(nx, ny, ROWS, parts, nz // ROWS, width).transpose(3, 0, 1, 4, 2, 5)
    settled = lax.all_to_all(settled, "gz", split_axis=0, concat_axis=0, tiled=True)
    settled = settled.transpose(1, 2, 3, 4, 0, 5).reshape(nx * ny, nz // ROWS, ROWS, bins)
    paired = settled.transpose(0, 2, 1, 3).reshape(-1, LANES)
    updated = call(breakup_plain_kernel, tiles_of(n * n), (paired, pairs, lost), [products(n // 2)], micros=3.0)
    updated = updated.reshape(nx, ny, ROWS, nz // ROWS, bins).transpose(0, 1, 3, 2, 4).reshape(nx, ny, nz, bins)
    return updated, rain


def solution(mesh):
    in_specs = (P("gx", "gy", "gz", None), P(None, "gx", "gy", "gz"), P(), P(), P(), P())
    out_specs = (P("gx", "gy", "gz", None), P("gx", ("gy", "gz"), None))
    return jax.shard_map(per_device, mesh=mesh, in_specs=in_specs, out_specs=out_specs, check_vma=False)
```

```python
import functools
import itertools

import jax
import jax.numpy as jnp
from jax import lax
from jax.experimental import pallas as pl
from jax.experimental.pallas import tpu as pltpu
from jax.sharding import PartitionSpec as P

SUBS = 24
EPS = 1e-06
LO, HI = 3, 2
PAD_LO, PAD_HI = 2 * LO, 2 * HI
LINES = LO + HI
ROWS, LANES = 8, 128
AHEAD = {3: 6, 5: 4}
EARLY = 5
F32 = jnp.float32
VMEM = pl.BlockSpec(memory_space=pltpu.VMEM)


def lane_ids():
    return lax.broadcasted_iota(jnp.int32, (ROWS, LANES), 1)


def pick(tile, ids):
    return jnp.take_along_axis(tile, ids, axis=1, mode="promise_in_bounds")


def turn(tile, lanes):
    lanes %= LANES
    return pltpu.roll(tile, lanes, 1) if lanes else tile


def rows_of(first, count=1):
    return pl.ds(first * ROWS, count * ROWS)


def eight(first, level, step=1):
    return pl.ds(first * ROWS + level, ROWS, stride=step * ROWS)


def order(a, b, straight):
    return jnp.where(straight, a, b), jnp.where(straight, b, a)


def is_even(axis):
    return lax.axis_index(axis) % 2 == 0


def by_quarter(parts):
    quarter = lane_ids() // (LANES // 4)
    return jnp.where(quarter < 2, jnp.where(quarter == 0, parts[0], parts[1]), jnp.where(quarter == 2, parts[2], parts[3]))


def groups(parts):
    width = LANES // (2 * parts)
    return width, width // ROWS, ROWS * ROWS // width


def spread(jobs, parts):
    width = groups(parts)[0]
    place = lane_ids() % width
    rows = [[], []]
    for tile, lane, _, _ in jobs:
        top = tile.astype(jnp.bfloat16).astype(F32)
        here = place == lane
        for out, term in zip(rows, (top, tile - top)):
            out.append(jnp.where(here, term, 0.0))
    terms = jnp.concatenate([jnp.concatenate(r, axis=0).astype(jnp.bfloat16) for r in rows], axis=1)
    source, target = [lax.broadcasted_iota(jnp.int32, (2 * LANES, LANES), k) for k in range(2)]
    same = jnp.where(source % LANES // width == target // width, 1.0, 0.0).astype(jnp.bfloat16)
    out = jnp.dot(terms, same, preferred_element_type=F32)
    for k, (_, _, ref, at) in enumerate(jobs):
        ref[rows_of(at)] = out[k * ROWS : (k + 1) * ROWS]


def lane_of(x, y, parts):
    return x % groups(parts)[1] * ROWS + y


def half_lane_of(x, y, parts):
    _, deep, tiles = groups(parts)
    return x % deep * ROWS + x // deep // (tiles // 2) * (ROWS // 2) + y % (ROWS // 2)


def half_tiles(low, high, upper):
    near = lane_ids() % ROWS < ROWS // 2
    if upper:
        return jnp.where(near, turn(low, -(ROWS // 2)), high)
    return jnp.where(near, low, turn(high, ROWS // 2))


def each(count, together, body):
    def some(places):
        stores = [store for i in places for store in body(i)]
        for ref, at, value in stores:
            ref[at] = value

    whole = count // together

    @pl.loop(0, whole)
    def _(i):
        some([i * together + k for k in range(together)])

    if count % together:
        some(range(whole * together, count))


def halo_line(i, n):
    if isinstance(i, int):
        return i - LO + (n if i >= LO else 0)
    return jnp.where(i < LO, i - LO, i - LO + n)


def line_change(cells, winds):
    return changes(line_fluxes(cells, winds))


def changes(fluxes):
    return [a - b for a, b in zip(fluxes, fluxes[1:])]


def long_line(cells, winds, low_edge, high_edge, n):
    begin, end = LO, n - HI
    low = line_fluxes(cells[: PAD_LO + begin + 1], winds[: LO + 1 + begin]) + [low_edge]
    high = [high_edge] + line_fluxes(cells[PAD_LO + end - HI :], winds[LO + 1 + end :])
    return dict(zip(range(-LO, begin), changes(low))) | dict(zip(range(end, n + HI), changes(high)))


def line_fluxes(cells, winds):
    first = [b - a for a, b in zip(cells, cells[1:])]
    twice = [d + d for d in first]
    second = [b - a for a, b in zip(first, first[1:])]
    third = [a - b for a, b in zip(second, second[1:])]
    curved = [(13.0 / 3.0) * (c * c) + 4.0 * EPS for c in second]
    fluxes = []
    for j in range(len(cells) - 4):
        left = twice[j + 1] + second[j]
        mid = first[j + 1] + first[j + 2]
        right = twice[j + 2] - second[j + 2]
        e0 = curved[j] + left * left
        e1 = curved[j + 1] + mid * mid
        e2 = curved[j + 2] + right * right
        e0 = 3.0 * (e0 * e0)
        e1 = e1 * e1
        e2 = e2 * e2
        e2_twice = e2 + e2
        top = e1 * (e2_twice * third[j] + e0 * third[j + 1])
        inverse = pl.reciprocal(e1 * (e2 + e0) + e0 * e2_twice, approx=True)
        estimate = 6.0 * cells[j + 2] + (first[j + 1] + twice[j + 2]) + top * inverse
        fluxes.append((winds[j] + winds[j + 1]) * estimate)
    return fluxes


def from_below(value, width):
    return jnp.where(lane_ids() < width, 0.0, turn(value, width))


def from_above(value, width):
    return jnp.where(lane_ids() >= LANES - width, 0.0, turn(value, -width))


def level_change(cells, winds, width):
    long_cells = [from_below(v, width) for v in cells[ROWS - LO :]] + cells + [from_above(v, width) for v in cells[:HI]]
    long_winds = [from_below(winds[-1], width)] + winds + [from_above(winds[0], width)]
    return line_change(long_cells, long_winds)


def pack_kernel(mass_ref, send_ref, keep_ref):
    lower = is_even("gz")
    n = mass_ref.shape[0]
    zero = jnp.zeros((ROWS, LANES // 2), F32)
    for x in range(n // 2):
        for y in range(n):
            tiles = [
                jnp.concatenate([mass_ref[xx, y, z : z + ROWS], zero], axis=1) for xx in (x, x + n // 2) for z in (0, ROWS)
            ]
            low = by_quarter([turn(v, 32 * k) for k, v in enumerate(tiles)])
            high = by_quarter([turn(v, 32 * k - 32) for k, v in enumerate(tiles)])
            at = rows_of(x * n + y)
            keep_ref[at], send_ref[at] = order(low, high, lower)


def wind_kernel(wind_ref, keep_ref, out_ref):
    del keep_ref
    n = wind_ref.shape[1]
    for d in range(3):
        levels = wind_ref[d].reshape(n * n, 2 * ROWS).T * (1.0 / 12.0)
        out_ref[rows_of(d)] = jnp.concatenate([levels[:ROWS], levels[ROWS:]], axis=1)


def sides(axis, first_ref, second_ref):
    even, place = is_even(axis), lax.axis_index(axis)
    inner_low, inner_high = place > 0, place < lax.axis_size(axis) - 1

    def below(at):
        return jnp.where(inner_low, jnp.where(even, second_ref[at], first_ref[at]), 0.0)

    def above(at):
        return jnp.where(inner_high, jnp.where(even, first_ref[at], second_ref[at]), 0.0)

    return below, above


def by_parity(axis, body):
    even = is_even(axis)
    pl.when(even)(lambda: body(0, 1))
    pl.when(jnp.logical_not(even))(lambda: body(1, 0))


def merge_kernel(keep_ref, got_ref, own_wind_ref, got_wind_ref, lost_ref, block_ref, y_first, y_second, x_first, x_second):
    del lost_ref
    n = 8
    lower = is_even("gz")
    low = lane_ids() < 64
    for x in range(n // 2):
        for y in range(n):
            at = rows_of(x * n + y)
            a, b = order(keep_ref[at], got_ref[at], lower)
            block_ref[at] = jnp.where(low, a, turn(b, 64))
            block_ref[rows_of((x + n // 2) * n + y)] = jnp.where(low, turn(a, 64), b)
    for d in range(3):
        a, b = order(own_wind_ref[rows_of(d)], got_wind_ref[rows_of(d)], lower)
        block_ref[rows_of(n * n + 2 * d)] = by_quarter([a, turn(a, -32), turn(b, 64), turn(b, 32)])
        block_ref[rows_of(n * n + 2 * d + 1)] = by_quarter([turn(a, -32), turn(a, -64), turn(b, 32), b])

    def along_y(up, down):
        for ref, start, wide in (((y_first, y_second)[up], n - PAD_LO, PAD_LO), ((y_first, y_second)[down], 0, PAD_HI)):
            for x in range(n):
                ref[rows_of(x * wide, wide)] = block_ref[rows_of(x * n + start, wide)]
            for d in range(3):
                low, high = [block_ref[rows_of(n * n + 2 * d + k)] for k in range(2)]
                ref[rows_of(n * wide + d)] = half_tiles(low, high, wide == PAD_LO)

    def along_x(up, down):
        for ref, start, wide, part in (((x_first, x_second)[up], n - PAD_LO, PAD_LO, 1), ((x_first, x_second)[down], 0, PAD_HI, 0)):
            ref[rows_of(0, wide * n)] = block_ref[rows_of(start * n, wide * n)]
            for d in range(3):
                ref[rows_of(wide * n + d)] = block_ref[rows_of(n * n + 2 * d + part)]

    by_parity("gy", along_y)
    by_parity("gx", along_x)


def corner_kernel(n, parts, first_ref, second_ref, own_change, *messages):
    del own_change
    tiles = groups(parts)[2]
    half = tiles // 2
    below, above = sides("gy", first_ref, second_ref)

    def body(up, down):
        for ref, start, narrow, part in ((messages[up], n - LO, LO, half), (messages[down], 0, HI, 0)):
            at = 0
            for x in range(start, start + narrow):
                ref[rows_of(at, LO)] = below(rows_of(x * PAD_LO + PAD_LO - LO, LO))
                ref[rows_of(at + LO, HI)] = above(rows_of(x * PAD_HI, HI))
                at += LINES
            for side, base in ((below, n * PAD_LO), (above, n * PAD_HI)):
                ref[rows_of(at)] = side(rows_of(base + (half - 1 if part else 0)))
                ref[rows_of(at + 1, half)] = side(rows_of(base + half, half))
                at += 1 + half

    by_parity("gx", body)


def own_kernel(n, parts, block_ref, wind_x, wind_y, wind_z, change, edge_x, edge_y):
    width, deep, tiles = groups(parts)
    for d, out in enumerate((wind_x, wind_y, wind_z)):
        jobs = []
        for x in range(n):
            tile = block_ref[rows_of(n * n + d * tiles + x // deep)]
            jobs += [(tile, lane_of(x, y, parts), out, x * n + y) for y in range(n)]
        spread(jobs, parts)

    def along_z(x):
        cells = [block_ref[eight(x * n, k)] for k in range(ROWS)]
        winds = [wind_z[eight(x * n, k)] for k in range(ROWS)]
        return [(change, eight(x * n, k), value) for k, value in enumerate(level_change(cells, winds, width))]

    each(n, 4, along_z)
    begin, end = LO, n - HI
    for wind, edge, place in ((wind_x, edge_x, lambda i, k: k * n + i), (wind_y, edge_y, lambda i, k: i * n + k)):

        def along(i):
            cells = [block_ref[rows_of(place(i, k))] for k in range(n)]
            fluxes = line_fluxes(cells, [wind[rows_of(place(i, k))] for k in range(begin - 1, end + 1)])
            at = [rows_of(place(i, k)) for k in range(begin, end)]
            stores = [(change, here, change[here] + value) for here, value in zip(at, changes(fluxes))]
            return stores + [(edge, rows_of(i), fluxes[0]), (edge, rows_of(n + i), fluxes[-1])]

        each(n, 4, along)


def y_kernel(n, parts, block_ref, first_ref, second_ref, wind_y, own_change, edge_y, *refs):
    width, deep, tiles = groups(parts)
    cell, change, wind_x, far_y, wind_z, halo_change = refs
    below, above = sides("gy", first_ref, second_ref)
    span, reach = n + PAD_LO + PAD_HI, n + LINES

    for x in range(n):
        cell[rows_of(x * span, PAD_LO)] = below(rows_of(x * PAD_LO, PAD_LO))
        cell[rows_of(x * span + PAD_LO, n)] = block_ref[rows_of(x * n, n)]
        cell[rows_of(x * span + PAD_LO + n, PAD_HI)] = above(rows_of(x * PAD_HI, PAD_HI))
    jobs = []
    half = tiles // 2
    for d in range(3):
        for t in range(half):
            low, high = below(rows_of(n * PAD_LO + d * half + t)), above(rows_of(n * PAD_HI + d * half + t))
            for x in [x for x in range(n) if x // deep % half == t]:
                lanes = [half_lane_of(x, y, parts) for y in range(n)]
                if d == 1:
                    jobs += [(low, lanes[n - LO - 1 + y], far_y, x * (LINES + 2) + y) for y in range(LO + 1)]
                    jobs += [(high, lanes[y], far_y, x * (LINES + 2) + LO + 1 + y) for y in range(HI + 1)]
                else:
                    out = wind_z if d else wind_x
                    jobs += [(low, lanes[n - LO + y], out, y * n + x) for y in range(LO)]
                    jobs += [(high, lanes[y], out, (LO + y) * n + x) for y in range(HI)]
    spread(jobs, parts)

    def along_z(i):
        first = halo_line(i, n) + PAD_LO
        cells = [cell[eight(first, k, span)] for k in range(ROWS)]
        winds = [wind_z[eight(i * n, k)] for k in range(ROWS)]
        return [(halo_change, eight(i * n, k), value) for k, value in enumerate(level_change(cells, winds, width))]

    each(LINES, LINES, along_z)

    def along_y(x):
        cells = [cell[rows_of(x * span + y)] for y in range(span)]
        far = [far_y[rows_of(x * (LINES + 2) + y)] for y in range(LINES + 2)]
        winds = far[: LO + 1] + [wind_y[rows_of(x * n + y)] for y in range(n)] + far[LO + 1 :]
        stores = []
        for y, value in long_line(cells, winds, edge_y[rows_of(x)], edge_y[rows_of(n + x)], n).items():
            if 0 <= y < n:
                value = value + own_change[rows_of(x * n + y)]
            else:
                value = value + halo_change[rows_of((y + LO if y < 0 else y + LO - n) * n + x)]
            stores.append((change, rows_of(x * reach + y + LO), value))
        for y in range(LO, n - HI):
            stores.append((change, rows_of(x * reach + y + LO), own_change[rows_of(x * n + y)]))
        return stores

    each(n, 4, along_y)


def which(i, lower, upper):
    if isinstance(i, int):
        return lower if i < LO else upper
    return jnp.where(i < LO, lower, upper)


def inside(axis):
    place = lax.axis_index(axis)
    return [jnp.where(ok, 1.0, 0.0) for ok in (place > 0, place < lax.axis_size(axis) - 1)]


def inner_kernel(n, parts, cell, change, halo_wind_x, wind_y, far_wind_y, wind_z, edge_x, one, edge, second):
    width = groups(parts)[0]
    span, reach = n + PAD_LO + PAD_HI, n + LINES
    begin, end = LO, n - HI
    south_in, north_in = inside("gy")

    for k in range(2):
        edge[rows_of(k * reach + LO, n)] = edge_x[rows_of(k * n, n)]
    for i in range(end - begin):
        x = begin + i
        one[rows_of(i * reach + LO, n)] = cell[rows_of(x * span + PAD_LO, n)] + change[rows_of(x * reach + LO, n)]

    def along_x(i):
        at = halo_line(i, n) + LO
        cells = [cell[rows_of(x * span + LO + at)] for x in range(n)]
        fluxes = line_fluxes(cells, [halo_wind_x[rows_of(i * n + x)] for x in range(begin - 1, end + 1)])
        keep = which(i, south_in, north_in)
        stores = [(edge, rows_of(at), fluxes[0]), (edge, rows_of(reach + at), fluxes[-1])]
        for k, value in enumerate(changes(fluxes)):
            x = begin + k
            value = (cells[x] + (value + change[rows_of(x * reach + at)])) * keep
            stores.append((one, rows_of(k * reach + at), value))
        return stores

    each(LINES, LINES, along_x)
    second_y_z(n, width, range(begin, end), begin, one, begin, wind_y, far_wind_y, wind_z, second)


def second_y_z(n, width, layers, first, one, one_first, wind_y, far_wind_y, wind_z, second):
    reach = n + LINES

    def along_y(i):
        x = layers[0] + i
        cells = [one[rows_of((x - one_first) * reach + y)] for y in range(reach)]
        winds = [far_wind_y[rows_of(x * (LINES + 2) + LO)]] + [wind_y[rows_of(x * n + y)] for y in range(n)]
        winds += [far_wind_y[rows_of(x * (LINES + 2) + LO + 1)]]
        return [(second, rows_of((x - first) * n + y), value) for y, value in enumerate(line_change(cells, winds))]

    def along_z(i):
        x = layers[0] + i
        cells = [one[eight((x - one_first) * reach + LO, k)] for k in range(ROWS)]
        winds = [wind_z[eight(x * n, k)] for k in range(ROWS)]
        at = [eight((x - first) * n, k) for k in range(ROWS)]
        return [(second, here, second[here] + value) for here, value in zip(at, level_change(cells, winds, width))]

    each(len(layers), len(layers), along_y)
    each(len(layers), len(layers), along_z)


def x_kernel(
    n, parts, cell, change, wind_x, inner, edge, inner_second, second_ref, first_ref,
    mid, far_wind_x, side, side_wind_y, side_edge, ready_second, second_edge, *scratch
):
    far, side_wind_z, side_change = scratch
    width, deep, tiles = groups(parts)
    half = tiles // 2
    west, east = sides("gx", first_ref, second_ref)
    span, reach = n + PAD_LO + PAD_HI, n + LINES

    jobs = []
    for take, wide, near_from, far_from, line in ((west, PAD_LO, LO, 0, 0), (east, PAD_HI, 0, HI, LO)):
        narrow = wide // 2
        side[rows_of(line * n, narrow * n)] = take(rows_of(near_from * n, narrow * n))
        far[rows_of(line * n, narrow * n)] = take(rows_of(far_from * n, narrow * n))
        layers, shift = (range(n - narrow, n), half) if line == 0 else (range(narrow), 0)
        wider = range(n - narrow - 1, n) if line == 0 else range(narrow + 1)

        def winds_of(d, x):
            return take(rows_of(wide * n + d * half + x // deep - shift))

        for i, x in enumerate(wider):
            jobs += [(winds_of(0, x), lane_of(x, y, parts), far_wind_x, (line + bool(line) + i) * n + y) for y in range(n)]
        for d, out in ((1, side_wind_y), (2, side_wind_z)):
            for i, x in enumerate(layers):
                jobs += [(winds_of(d, x), lane_of(x, y, parts), out, (line + i) * n + y) for y in range(n)]
    spread(jobs, parts)

    def along_z(i):
        cells = [side[eight(i * n, k)] for k in range(ROWS)]
        winds = [side_wind_z[eight(i * n, k)] for k in range(ROWS)]
        return [(side_change, eight(i * n, k), value) for k, value in enumerate(level_change(cells, winds, width))]

    each(LINES, LINES, along_z)
    begin, end = LO, n - HI

    def along_y(i):
        cells = [side[rows_of(i * n + y)] for y in range(n)]
        fluxes = line_fluxes(cells, [side_wind_y[rows_of(i * n + y)] for y in range(begin - 1, end + 1)])
        at = [rows_of(i * n + y) for y in range(begin, end)]
        stores = [(side_change, here, side_change[here] + value) for here, value in zip(at, changes(fluxes))]
        return stores + [(side_edge, rows_of(i), fluxes[0]), (side_edge, rows_of(LINES + i), fluxes[-1])]

    each(LINES, LINES, along_y)

    def along_x(y):
        outer = [far[rows_of(i * n + y)] for i in range(LINES)]
        near = [side[rows_of(i * n + y)] for i in range(LINES)]
        cells = outer[:LO] + near[:LO] + [cell[rows_of(x * span + PAD_LO + y)] for x in range(n)] + near[LO:] + outer[LO:]
        winds = [far_wind_x[rows_of(i * n + y)] for i in range(LINES + 2)]
        winds = winds[: LO + 1] + [wind_x[rows_of(x * n + y)] for x in range(n)] + winds[LO + 1 :]
        stores = []
        for x, value in long_line(cells, winds, edge[rows_of(LO + y)], edge[rows_of(reach + LO + y)], n).items():
            if 0 <= x < n:
                value = value + change[rows_of(x * reach + LO + y)]
            else:
                value = value + side_change[rows_of((x + LO if x < 0 else x + LO - n) * n + y)]
            stores.append((mid, rows_of((x + LO) * n + y), cells[PAD_LO + x] + value))
        return stores

    each(n, 4, along_x)

    def second_x(y):
        cells = [mid[rows_of((x + LO) * n + y)] for x in range(begin)]
        cells += [inner[rows_of(i * reach + LO + y)] for i in range(end - begin)]
        cells += [mid[rows_of((x + LO) * n + y)] for x in range(end, n)]
        fluxes = line_fluxes(cells, [wind_x[rows_of(x * n + y)] for x in range(begin - 1, end + 1)])
        at = [rows_of(i * n + y) for i in range(end - begin)]
        stores = [(ready_second, here, inner_second[here] + value) for here, value in zip(at, changes(fluxes))]
        return stores + [(second_edge, rows_of(y), fluxes[0]), (second_edge, rows_of(n + y), fluxes[-1])]

    each(n, 4, second_x)


def main_kernel(n, parts, *refs):
    cell, change, wind_x, wind_y, wind_z, halo_wind_x, far_wind_y, inner, edge = refs[:9]
    mid, far_wind_x, side, side_wind_y, side_edge, inner_second, second_edge = refs[9:16]
    second_ref, first_ref, rate_ref, steps_ref, one, *out_refs = refs[16:23]
    corner, corner_wind_x, edge_wind_y, second, fallen = refs[23:]
    deep, tiles = groups(parts)[1:]
    half = tiles // 2
    west, east = sides("gx", first_ref, second_ref)
    span, reach = n + PAD_LO + PAD_HI, n + LINES

    jobs = []
    for take, narrow, line in ((west, LO, 0), (east, HI, LO)):
        at = narrow * LINES
        corner[rows_of(line * LINES, at)] = take(rows_of(0, at))
        below, above = at, at + 1 + half
        layers = range(n - narrow, n) if line == 0 else range(narrow)
        for y in range(LINES):
            tile = take(rows_of(below if y < LO else above))
            x = layers[-1] if line == 0 else layers[0]
            lane = half_lane_of(x, n - LO + y if y < LO else y - LO, parts)
            jobs.append((tile, lane, corner_wind_x, bool(line) * LINES + y))
        for i, x in enumerate(layers):
            tile = x // deep % half
            for k, (base, y) in enumerate(((below, n - 1), (above, 0))):
                lane = half_lane_of(x, y, parts)
                jobs.append((take(rows_of(base + 1 + tile)), lane, edge_wind_y, 2 * (line + i) + k))
    spread(jobs, parts)

    west_in, east_in = inside("gx")
    south_in, north_in = inside("gy")
    begin, end = LO, n - HI
    one[rows_of((begin + LO) * reach, (end - begin) * reach)] = inner[...]
    for x in [x for x in range(n) if not begin <= x < end]:
        one[rows_of((x + LO) * reach + LO, n)] = mid[rows_of((x + LO) * n, n)]

    def along_y(i):
        corners = [corner[rows_of(i * LINES + y)] for y in range(LINES)]
        cells = corners[:LO] + [side[rows_of(i * n + y)] for y in range(n)] + corners[LO:]
        winds = [side_wind_y[rows_of(i * n + y)] for y in range(n)]
        winds = [edge_wind_y[rows_of(2 * i)]] + winds + [edge_wind_y[rows_of(2 * i + 1)]]
        low = line_fluxes(cells[: LO + begin + 1], winds[: begin + 1]) + [side_edge[rows_of(i)]]
        high = [side_edge[rows_of(LINES + i)]] + line_fluxes(cells[LO + end - HI :], winds[end + 1 :])
        values = dict(zip(range(begin), changes(low))) | dict(zip(range(end, n), changes(high)))
        line, keep = halo_line(i, n) + LO, which(i, west_in, east_in)
        stores = []
        for y in range(n):
            value = mid[rows_of(line * n + y)]
            value = value + values[y] if y in values else value
            stores.append((one, rows_of(line * reach + LO + y), value * keep))
        return stores

    def along_x(i):
        line = halo_line(i, n) + LO
        near = [corner[rows_of(k * LINES + i)] for k in range(LINES)]
        cells = near[:LO] + [cell[rows_of(x * span + LO + line)] for x in range(n)] + near[LO:]
        winds = [halo_wind_x[rows_of(i * n + x)] for x in range(n)]
        winds = [corner_wind_x[rows_of(i)]] + winds + [corner_wind_x[rows_of(LINES + i)]]
        low = line_fluxes(cells[: LO + begin + 1], winds[: begin + 1]) + [edge[rows_of(line)]]
        high = [edge[rows_of(reach + line)]] + line_fluxes(cells[LO + end - HI :], winds[end + 1 :])
        values = dict(zip(range(begin), changes(low))) | dict(zip(range(end, n), changes(high)))
        stores = []
        for x, value in values.items():
            value = (cells[x + LO] + (value + change[rows_of(x * reach + line)])) * which(i, south_in, north_in)
            stores.append((one, rows_of((x + LO) * reach + line), value))
        return stores

    each(LINES, LINES, along_y)
    each(LINES, LINES, along_x)
    fall_layers(
        n, parts, 0, EARLY, one, cell, wind_x, far_wind_x, wind_y, far_wind_y, wind_z, inner_second, second_edge, rate_ref, steps_ref,
        out_refs, second, fallen,
    )


def late_kernel(
    n, parts, one, cell, wind_x, far_wind_x, wind_y, far_wind_y, wind_z, inner_second, second_edge, rate_ref, steps_ref, *refs
):
    fall_layers(
        n, parts, EARLY, n, one, cell, wind_x, far_wind_x, wind_y, far_wind_y, wind_z, inner_second, second_edge, rate_ref, steps_ref,
        refs[:2], *refs[2:],
    )


def fall_layers(
    n, parts, begin, end, one, cell, wind_x, far_wind_x, wind_y, far_wind_y, wind_z, inner_second, second_edge, rate_ref, steps_ref,
    out_refs, second, fallen,
):
    width = groups(parts)[0]
    span, reach, count = n + PAD_LO + PAD_HI, n + LINES, end - begin
    ready = [x for x in range(LO, n - HI) if begin <= x < end]
    left = [x for x in range(begin, end) if x not in ready]
    if ready:
        second[rows_of((ready[0] - begin) * n, len(ready) * n)] = inner_second[rows_of((ready[0] - LO) * n, len(ready) * n)]

    second_y_z(n, width, left, begin, one, -LO, wind_y, far_wind_y, wind_z, second)

    def along_x(y):
        values = {}
        if begin == 0:
            cells = [one[rows_of((x + LO) * reach + LO + y)] for x in range(-LO, LO + 1)]
            winds = [far_wind_x[rows_of(LO * n + y)]] + [wind_x[rows_of(x * n + y)] for x in range(LO)]
            fluxes = line_fluxes(cells, winds) + [second_edge[rows_of(y)]]
            values |= zip(range(LO), changes(fluxes))
        if end == n:
            cells = [one[rows_of((x + LO) * reach + LO + y)] for x in range(n - 2 * HI, n + HI)]
            winds = [wind_x[rows_of(x * n + y)] for x in range(n - HI, n)] + [far_wind_x[rows_of((LO + 1) * n + y)]]
            fluxes = [second_edge[rows_of(n + y)]] + line_fluxes(cells, winds)
            values |= zip(range(n - HI, n), changes(fluxes))
        stores = []
        for x in range(begin, end):
            at = rows_of((x - begin) * n + y)
            value = second[at] + values[x] if x in values else second[at]
            value = one[rows_of((x + LO) * reach + LO + y)] + value
            value = 0.5 * cell[rows_of(x * span + PAD_LO + y)] + 0.5 * value
            stores.append((fallen, at, value))
        return stores

    each(n, 4, along_x)

    bins = LANES // 2 // parts
    ids = lax.axis_index("gz") * bins + lane_ids() % bins
    rates, steps = [
        pick(jnp.broadcast_to(jnp.concatenate([ref[...]] * 2, axis=1), (ROWS, LANES)), ids) for ref in (rate_ref, steps_ref)
    ]

    rain = []
    ahead = AHEAD[count]
    for some in [range(count)]:
        columns = [[fallen[eight(i * n, k)] for k in range(ROWS)] for i in some]
        drops = [jnp.zeros((ROWS, LANES), F32) for _ in some]
        for block in range(SUBS // ahead):
            columns = [column + [from_above(v, width) for v in column[:ahead]] for column in columns]
            for s in range(ahead):
                rate = jnp.where(block * ahead + s < steps, rates, 0.0)
                for i, column in enumerate(columns):
                    drops[i] = drops[i] + rate * column[0]
                    columns[i] = [v + rate * (u - v) for v, u in zip(column, column[1:])]
        for i, column in zip(some, columns):
            for k in range(ROWS):
                fallen[eight(i * n, k)] = column[k]
        rain += drops

    if parts == 2:
        send_ref, keep_ref = out_refs
        lower = is_even("gz")
        low = lane_ids() < 64
        half = count * n // 2
        for c in range(half):
            a, b = fallen[rows_of(c)], fallen[rows_of(half + c)]
            at = rows_of(c)
            keep_ref[at], send_ref[at] = order(jnp.where(low, a, turn(b, 64)), jnp.where(low, turn(a, 64), b), lower)
        for j in range(0, count, 4):
            four = (rain[j : j + 4] + rain[j:] * 3)[:4]
            value = by_quarter([turn(v, 32 * i) for i, v in enumerate(four)])
            keep_ref[rows_of(half + j // 4)] = value
            send_ref[rows_of(half + j // 4)] = value
    else:
        settled_ref, rain_ref = out_refs
        settled_ref[...] = fallen[...]
        for i in range(count):
            rain_ref[rows_of(i)] = rain[i]


def matrix_kernel(bins, gain_ref, loss_ref, pairs_ref, lost_ref, wide, tall):
    zero = jnp.zeros((bins, LANES - bins), F32)
    shifts = bins // 2

    @pl.loop(0, bins)
    def _(i):
        rows = gain_ref[pl.ds(i * bins, bins)].astype(F32)
        rows = jnp.concatenate([rows, zero], axis=1)
        wide[pl.ds(i * 2 * bins, bins)] = rows
        wide[pl.ds(i * 2 * bins + bins, bins)] = rows
        tall[pl.ds(i * bins, bins)] = rows

        @pl.when(i < shifts)
        def _():
            tall[pl.ds((i + bins) * bins, bins)] = rows

    for d in range(shifts + 1):
        rows = wide[pl.ds(d, bins, stride=2 * bins + 1)]
        if 0 < d < shifts:
            rows = rows + tall[pl.ds(d * bins, bins, stride=bins + 1)]
        pairs_ref[pl.ds(d * LANES, bins)] = rows.astype(jnp.bfloat16)
        pairs_ref[pl.ds(d * LANES + bins, bins)] = pltpu.roll(rows, bins, 1).astype(jnp.bfloat16)
    rows = jnp.concatenate([loss_ref[...].astype(F32), zero], axis=1)
    lost_ref[pl.ds(0, bins)] = rows.astype(jnp.bfloat16)
    lost_ref[pl.ds(bins, bins)] = pltpu.roll(rows, bins, 1).astype(jnp.bfloat16)


def breakup_rows(mass, pairs_ref, lost_ref, products):
    bins = LANES // 2
    count = mass.shape[0]
    lanes = lane_ids()
    rounded = mass.astype(jnp.bfloat16)
    wide = rounded.astype(F32)
    gained = None
    shifts = bins // 2 + 1
    for begin in range(0, shifts, 4):
        end = min(begin + 4, shifts)
        for d in range(begin, end):
            ids = lanes // bins * bins + (lanes + d) % bins
            for r in range(0, count, 2 * ROWS):
                halves = [wide[r + ROWS * k : r + ROWS * (k + 1)] for k in range(2)]
                halves = [v * pick(v, ids) if d else v * v for v in halves]
                both = jnp.concatenate(halves, axis=0).astype(jnp.bfloat16)
                products[pl.ds(r, 2 * ROWS), d * LANES : (d + 1) * LANES] = both
        part = jnp.dot(
            products[pl.ds(0, count), begin * LANES : end * LANES],
            pairs_ref[pl.ds(begin * LANES, (end - begin) * LANES)],
            preferred_element_type=F32,
        )
        gained = part if gained is None else gained + part
    loss = jnp.dot(rounded, lost_ref[...], preferred_element_type=F32)
    return mass + gained - mass * loss


def breakup_layers(n, count, keep_ref, got_ref, pairs_ref, lost_ref, columns, products):
    first = is_even("gz")
    half = count * n // 2
    for c in range(half):
        a, b = order(keep_ref[rows_of(c)], got_ref[rows_of(c)], first)
        columns[rows_of(c)] = by_quarter([a, turn(b, 32), turn(a, 32), turn(b, 64)])
        columns[rows_of(half + c)] = by_quarter([turn(a, -64), turn(b, -32), turn(a, -32), b])
    rain = []
    for i in range(count):
        a, b = order(keep_ref[rows_of(half + i // 4)], got_ref[rows_of(half + i // 4)], first)
        a, b = [jnp.where(first, v[: n // 2], v[n // 2 :])[:, 32 * (i % 4) : 32 * (i % 4) + 32] for v in (a, b)]
        rain.append(jnp.concatenate([a, b], axis=1))
    columns[...] = breakup_rows(columns[...], pairs_ref, lost_ref, products)
    return rain


def lay_out(columns, mass, n, count):
    for x in range(count):
        for y in range(n):
            value = columns[rows_of(x * n + y)]
            mass[x, y, 0:ROWS] = value[:, :64]
            mass[x, y, ROWS : 2 * ROWS] = value[:, 64:]


def breakup_first_kernel(n, keep_ref, got_ref, pairs_ref, lost_ref, mass_ref, rain_ref, columns, products):
    for i, value in enumerate(breakup_layers(n, EARLY, keep_ref, got_ref, pairs_ref, lost_ref, columns, products)):
        rain_ref[i] = value
    lay_out(columns, mass_ref, n, EARLY)


def breakup_last_kernel(
    n, keep_ref, got_ref, pairs_ref, lost_ref, early, early_rain, mass_out, rain_out, columns, products, mass, rain, sems
):
    early_copy = pltpu.make_async_copy(early, mass_out.at[pl.ds(0, EARLY)], sems.at[0])
    early_copy.start()
    late_rain = breakup_layers(n, n - EARLY, keep_ref, got_ref, pairs_ref, lost_ref, columns, products)
    for i in range(EARLY):
        rain[i] = early_rain[i]
    for i, value in enumerate(late_rain):
        rain[EARLY + i] = value
    rain_copy = pltpu.make_async_copy(rain, rain_out, sems.at[2])
    rain_copy.start()
    lay_out(columns, mass, n, n - EARLY)
    late_copy = pltpu.make_async_copy(mass, mass_out.at[pl.ds(EARLY, n - EARLY)], sems.at[1])
    late_copy.start()
    for copy in (early_copy, rain_copy, late_copy):
        copy.wait()


def breakup_plain_kernel(mass_ref, pairs_ref, lost_ref, out_ref, products):
    count = products.shape[0]

    @pl.loop(0, mass_ref.shape[0] // count)
    def _(i):
        start = pl.multiple_of(i * count, count)
        out_ref[pl.ds(start, count)] = breakup_rows(mass_ref[pl.ds(start, count)], pairs_ref, lost_ref, products)


def shape(*dims, dtype=F32):
    return jax.ShapeDtypeStruct(dims, dtype)


def tiles_of(count):
    return shape(count * ROWS, LANES)


def call(kernel, outs, args, scratch=(), micros=1.0, out_place=pltpu.VMEM, copies=0):
    scratch = [pltpu.VMEM(s.shape, s.dtype) for s in scratch]
    if copies:
        scratch.append(pltpu.SemaphoreType.DMA((copies,)))
    return pl.pallas_call(
        kernel,
        out_shape=outs,
        in_specs=[VMEM] * len(args),
        out_specs=jax.tree.map(lambda _: pl.BlockSpec(memory_space=out_place), outs),
        scratch_shapes=scratch,
        compiler_params=pltpu.CompilerParams(vmem_limit_bytes=40 << 20),
        cost_estimate=pl.CostEstimate(
            flops=int(micros * 1.1e9), bytes_accessed=int(micros * 3.6e6), transcendentals=0
        ),
    )(*args)


def swap_neighbours(axis, begin, message):
    axes = ("gx", "gy", "gz")
    sizes = [lax.axis_size(a) for a in axes]
    along, other = (0, 2) if axis == "gx" else (1, 0)

    def partner(place, start, count):
        to = start + ((place - start) ^ 1)
        return to if start <= place and to < count else place

    index = {place: i for i, place in enumerate(itertools.product(*map(range, sizes)))}
    pairs = []
    for place, i in index.items():
        to = list(place)
        to[along] = partner(place[along], begin, sizes[along])
        if to[along] == place[along]:
            to[other] = partner(place[other], 0, sizes[other])
        pairs.append((i, index[tuple(to)]))
    return lax.ppermute(message, axes, pairs)


def per_device(bin_mass, courant, sub_courant, fall_steps, frag_gain, collide):
    nx, ny, nz, bins = bin_mass.shape
    n = nx
    parts = lax.axis_size("gz")
    gz, gy = lax.axis_index("gz"), lax.axis_index("gy")
    width = bins // parts
    tiles = groups(parts)[2]
    winds = 3 * tiles

    pair_rows = (bins // 2 + 1) * LANES
    pairs, lost = call(
        functools.partial(matrix_kernel, bins),
        (shape(pair_rows, LANES, dtype=jnp.bfloat16), shape(LANES, LANES, dtype=jnp.bfloat16)),
        (frag_gain, collide),
        [shape(2 * bins * bins, LANES), shape(3 * bins * bins // 2, LANES)],
        micros=0.02,
    )

    y_message = tiles_of(n * PAD_LO + winds // 2)
    x_message = tiles_of(n * PAD_LO + winds // 2)
    if parts == 2:
        half = tiles_of(n * n // 2)
        send, keep = call(pack_kernel, (half, half), (bin_mass,), micros=0.3)
        got = lax.ppermute(send, "gz", [(0, 1), (1, 0)])
        own_wind = call(wind_kernel, tiles_of(3), (courant, keep), micros=0.1)
        got_wind = lax.ppermute(own_wind, "gz", [(0, 1), (1, 0)])
        block, *messages = call(
            merge_kernel,
            [tiles_of(n * n + winds), y_message, y_message, x_message, x_message],
            (keep, got, own_wind, got_wind, lost),
            micros=0.2,
        )
    else:
        split = bin_mass.reshape(nx, ny, nz // ROWS, ROWS, parts, width).transpose(4, 0, 1, 3, 2, 5)
        split = lax.all_to_all(split, "gz", split_axis=0, concat_axis=0, tiled=True)
        cube = split.transpose(1, 2, 3, 0, 4, 5).reshape(n, n, ROWS, LANES)
        air = courant.reshape(3, nx, ny, nz // ROWS, ROWS).transpose(0, 4, 3, 1, 2) * (1.0 / 12.0)
        air = lax.all_gather(air, "gz").reshape(parts, 3, ROWS, nz // ROWS, tiles, nx // tiles, ny)
        air = air.transpose(1, 4, 2, 0, 3, 5, 6).reshape(3, tiles, ROWS, LANES)
        block = jnp.concatenate([cube.reshape(-1, LANES), air.reshape(-1, LANES)])
        halves = [air[:, : tiles // 2], air[:, tiles // 2 :]]
        near = jnp.arange(LANES) % ROWS < ROWS // 2
        low_y = jnp.where(near, halves[0], jnp.roll(halves[1], ROWS // 2, axis=-1))
        high_y = jnp.where(near, jnp.roll(halves[0], -(ROWS // 2), axis=-1), halves[1])
        messages = []
        for layers, low_air, high_air, message, even in (
            (cube.transpose(1, 0, 2, 3), low_y, high_y, y_message, gy % 2 == 0),
            (cube, *halves, x_message, lax.axis_index("gx") % 2 == 0),
        ):
            up, down = layers[n - PAD_LO :], layers[:PAD_HI]
            if message is y_message:
                up, down = up.transpose(1, 0, 2, 3), down.transpose(1, 0, 2, 3)
            up = jnp.concatenate([up.reshape(-1, LANES), high_air.reshape(-1, LANES)])
            down = jnp.concatenate([down.reshape(-1, LANES), low_air.reshape(-1, LANES)])
            messages += order(up, jnp.pad(down, ((0, up.shape[0] - down.shape[0]), (0, 0))), even)

    from_y = swap_neighbours("gy", 0, messages[0]), swap_neighbours("gy", 1, messages[1])
    from_x = swap_neighbours("gx", 1, messages[3]), swap_neighbours("gx", 0, messages[2])
    wind_x, wind_y, wind_z, own_change, edge_x, edge_y = call(
        functools.partial(own_kernel, n, parts), [tiles_of(n * n)] * 4 + [tiles_of(2 * n)] * 2, (block,), micros=1.6
    )
    message = tiles_of(LO * LINES + 2 + tiles)
    corners = call(functools.partial(corner_kernel, n, parts), (message, message), (*from_y, own_change), micros=0.1)
    corners = swap_neighbours("gx", 1, corners[1]), swap_neighbours("gx", 0, corners[0])
    cell, change, halo_wind_x, far_wind_y = call(
        functools.partial(y_kernel, n, parts),
        [tiles_of(n * (n + PAD_LO + PAD_HI)), tiles_of(n * (n + LINES)), tiles_of(LINES * n), tiles_of(n * (LINES + 2))],
        (block, *from_y, wind_y, own_change, edge_y),
        [tiles_of(LINES * n)] * 2,
        micros=2.0,
    )
    reach, inner = n + LINES, n - LINES
    near = call(
        functools.partial(inner_kernel, n, parts),
        [tiles_of(inner * reach), tiles_of(2 * reach), tiles_of(inner * n)],
        (cell, change, halo_wind_x, wind_y, far_wind_y, wind_z, edge_x),
        micros=0.9,
    )
    mid, far_wind_x, side, side_wind_y, side_edge, ready_second, second_edge = call(
        functools.partial(x_kernel, n, parts),
        [tiles_of(count) for count in (reach * n, (LINES + 2) * n, LINES * n, LINES * n, 2 * LINES, inner * n, 2 * n)],
        (cell, change, wind_x, *near, *from_x),
        [tiles_of(LINES * n)] * 3,
        micros=1.7,
    )
    fall = sub_courant.reshape(1, bins), fall_steps.reshape(1, bins)

    def fallen(count):
        if parts == 2:
            return [tiles_of(n * count // 2 + (count + 3) // 4)] * 2
        return [tiles_of(n * count), tiles_of(count)]

    one, *early = call(
        functools.partial(main_kernel, n, parts),
        [tiles_of(reach * reach)] + fallen(EARLY),
        (
            *(cell, change, wind_x, wind_y, wind_z, halo_wind_x, far_wind_y, *near[:2]),
            *(mid, far_wind_x, side, side_wind_y, side_edge, ready_second, second_edge, *corners, *fall),
        ),
        [tiles_of(count) for count in (LINES * LINES, 2 * LINES, 2 * LINES, n * EARLY, n * EARLY)],
        micros=2.6,
    )
    if parts == 2:
        early_got = lax.ppermute(early[0], "gz", [(0, 1), (1, 0)])
    late = call(
        functools.partial(late_kernel, n, parts),
        fallen(n - EARLY),
        (one, cell, wind_x, far_wind_x, wind_y, far_wind_y, wind_z, ready_second, second_edge, *fall),
        [tiles_of(n * (n - EARLY))] * 2,
        micros=0.7,
    )

    def products(count):
        return shape(n * count * ROWS, pair_rows, dtype=jnp.bfloat16)

    if parts == 2:
        late_got = lax.ppermute(late[0], "gz", [(0, 1), (1, 0)])
        early = call(
            functools.partial(breakup_first_kernel, n),
            [shape(EARLY, ny, nz, bins), shape(EARLY, ny // parts, bins)],
            (early[1], early_got, pairs, lost),
            [tiles_of(n * EARLY), products(EARLY)],
            micros=1.8,
        )
        outs = [shape(nx, ny, nz, bins), shape(nx, ny // parts, bins)]
        return tuple(
            call(
                functools.partial(breakup_last_kernel, n),
                outs,
                (late[1], late_got, pairs, lost, *early),
                [tiles_of(n * (n - EARLY)), products(n - EARLY), shape(n - EARLY, ny, nz, bins), outs[1]],
                micros=1.2,
                out_place=pl.ANY,
                copies=3,
            )
        )

    settled, rain = [jnp.concatenate(halves) for halves in zip(early, late)]
    rain = rain.reshape(nx, ny, LANES)[:, :, :width]
    rain = lax.all_to_all(rain, "gz", split_axis=1, concat_axis=2, tiled=True)
    settled = settled.reshape(nx, ny, ROWS, parts, nz // ROWS, width).transpose(3, 0, 1, 4, 2, 5)
    settled = lax.all_to_all(settled, "gz", split_axis=0, concat_axis=0, tiled=True)
    settled = settled.transpose(1, 2, 3, 4, 0, 5).reshape(nx * ny, nz // ROWS, ROWS, bins)
    paired = settled.transpose(0, 2, 1, 3).reshape(-1, LANES)
    updated = call(breakup_plain_kernel, tiles_of(n * n), (paired, pairs, lost), [products(n // 2)], micros=3.0)
    updated = updated.reshape(nx, ny, ROWS, nz // ROWS, bins).transpose(0, 1, 3, 2, 4).reshape(nx, ny, nz, bins)
    return updated, rain


def solution(mesh):
    in_specs = (P("gx", "gy", "gz", None), P(None, "gx", "gy", "gz"), P(), P(), P(), P())
    out_specs = (P("gx", "gy", "gz", None), P("gx", ("gy", "gz"), None))
    return jax.shard_map(per_device, mesh=mesh, in_specs=in_specs, out_specs=out_specs, check_vma=False)
```
